32 devices in a mesh: space: 16 (over z, y, x), knot: 2 (over core).
Axes of the slice: x: 2, y: 2, z: 4, core: 2. Of those that a mesh axis runs over, the one named last changes fastest.
Arguments:
- probes: float32 [16, 32768], P(None, ('space', 'knot')), may hold values from -6 to 6
- locations: float32 [2, 32768], P(None, ('space', 'knot')), may hold values from 0 to 1.6, as said below
- knot_locs: float32 [2, 2048], P(None, 'knot'), may hold values from 0 to 1.6, as said below
- knot_precision: float32 [2048, 2048], P('knot'), may hold values from -0.125 to 0.125
- neighbours: int32 [256, 8], P(('space', 'knot')), may hold values from 0 to 255, as said below
- counts: int32 [256], P(('space', 'knot')), may hold values from 1 to 8
Outputs:
- applied: float32 [16, 32768], P(None, ('space', 'knot'))
The draws below stay inside these ranges and needn't reach their ends.
Inputs may be any that keep to these rules, and one draw needn't show every extreme that they name: `locations`: block b lies in one cell of a grid of 16 x 16 cells of side 0.1: its east coordinates in [0.1 (b // 16), 0.1 (b // 16 + 1)], its north ones in [0.1 (b % 16), 0.1 (b % 16 + 1)]. `knot_locs`: knots lie in [0, 0.1 * 16] east and [0, 0.1 * 16] north. neighbours[b, 0] = b; every other entry of row b is the block of one of the eight cells around b's cell, where a step off the grid is turned back in that direction; the steps of a row are distinct.
All inputs are finite; a program needn't handle non-finite values.
Results may differ from the reference program's by a relative error of at most 0.0003.
Values sent between devices are 32-bit elements; how exact they have to be, the bound alone decides.
No kernel may reach another device: no remote copies, remote signals or barrier semaphores. Data moves between devices by JAX's collectives and lax.ppermute only.
A program may use at most 64 MiB of HBM per device.

```python
import math
import jax
import jax.numpy as jnp
from jax import lax

NBD = 8
BLOCK = 128
PROBES = 16
KNOTS = 2048
KNB = 8
NCOLS = 16
NROWS = 16
NB = 256
NOBS = 32768


def draw_locations(key, part):
    split_keys = jax.random.split(jax.random.fold_in(key, 11), 2)
    total = NB * BLOCK
    blocks = jnp.arange(total, dtype=jnp.int32) // BLOCK
    east_cell = (blocks // NROWS).astype(jnp.float32)
    north_cell = (blocks % NROWS).astype(jnp.float32)
    east = (east_cell + jax.random.uniform(split_keys[0], (total,), jnp.float32)) * 0.1
    north = (north_cell + jax.random.uniform(split_keys[1], (total,), jnp.float32)) * 0.1
    return jnp.stack([east, north]).astype(jnp.float32)


def draw_knot_locs(key, part):
    split_keys = jax.random.split(jax.random.fold_in(key, 23), 2)
    east = jax.random.uniform(split_keys[0], (KNOTS,), jnp.float32) * (NCOLS * 0.1)
    north = jax.random.uniform(split_keys[1], (KNOTS,), jnp.float32) * (NROWS * 0.1)
    return jnp.stack([east, north]).astype(jnp.float32)


def draw_neighbours(key, part):
    steps_east = jnp.array([-1, -1, -1, 0, 0, 1, 1, 1], dtype=jnp.int32)
    steps_north = jnp.array([-1, 0, 1, -1, 1, -1, 0, 1], dtype=jnp.int32)
    key_list = jax.random.split(jax.random.fold_in(key, 37), NB)
    shuffled = jax.vmap(lambda single: jax.random.permutation(single, 8))(key_list)
    chosen = shuffled[:, :KNB - 1].astype(jnp.int32)
    blocks = jnp.arange(NB, dtype=jnp.int32)[:, None]
    east_cell = blocks // NROWS
    north_cell = blocks % NROWS
    move_east = steps_east[chosen]
    move_north = steps_north[chosen]
    target_east = east_cell + move_east
    target_east = jnp.where((target_east < 0) | (target_east >= NCOLS), east_cell - move_east, target_east)
    target_north = north_cell + move_north
    target_north = jnp.where((target_north < 0) | (target_north >= NROWS), north_cell - move_north, target_north)
    target = target_east * NROWS + target_north
    return jnp.concatenate([blocks, target], axis=1).astype(jnp.int32)


def draw_counts(key, part):
    values = jax.random.randint(jax.random.fold_in(key, 53), (NB,), 1, KNB + 1, dtype=jnp.int32)
    return values.at[0].set(KNB).at[1].set(1)


def levels(stream_key, shape, cuts, smallest, top_value):
    level, own = 1.0, jax.random.fold_in(stream_key, 6)
    for dim, blocks in cuts:
        heights = jnp.exp(jax.random.uniform(jax.random.fold_in(own, dim), (blocks,), jnp.float32, smallest / len(cuts), top_value / len(cuts)))
        level = level * jnp.repeat(heights, shape[dim] // blocks).reshape([-1 if axis == dim else 1 for axis in range(len(shape))])
    return level


def normal_values(own_key, dims, width, limit, shards=(), kind=jnp.bfloat16):
    values = width * jax.random.normal(own_key, dims, jnp.float32)
    if shards:
        values = values * levels(own_key, dims, shards, -0.22, 0.18)
    return jnp.clip(values, -limit, limit).astype(kind)


def setup_inputs(seed: int = 0) -> dict:
    streams_of = jax.random.split(jax.random.key(seed), 7)
    return {
        "probes": normal_values(streams_of[0], (PROBES, NOBS), 1.0, 6.0, ((1, 32),), jnp.float32),
        "locations": draw_locations(jax.random.fold_in(streams_of[6], 71), 0),
        "knot_locs": draw_knot_locs(jax.random.fold_in(streams_of[6], 71), 0),
        "knot_precision": normal_values(streams_of[3], (KNOTS, KNOTS), KNOTS ** -0.5, 0.125, ((0, 2),), jnp.float32),
        "neighbours": draw_neighbours(jax.random.fold_in(streams_of[6], 71), 0),
        "counts": draw_counts(jax.random.fold_in(streams_of[6], 71), 0),
    }


COV_RANGE = 0.05
TAPER_LEN = 0.15
KNOT_REACH = 0.15
TAPER_SCALE = 0.1
PROJ_GAIN = 0.5
EXPAND_GAIN = 0.5
LOW_SCALE = 0.5
NUGGET = 0.25
PRECISE = lax.Precision.HIGHEST

def tapered(own_locs, near_locs, near_vals, weights):
    delta_x = own_locs[0][:, None, :, None] - near_locs[0][:, :, None, :]
    delta_y = own_locs[1][:, None, :, None] - near_locs[1][:, :, None, :]
    distance = jnp.sqrt(delta_x * delta_x + delta_y * delta_y)
    scaled = jnp.minimum(distance / TAPER_LEN, 1.0)
    remain = (1.0 - scaled) * (1.0 - scaled)
    kernel = jnp.exp(-distance / COV_RANGE) * remain * remain * (1.0 + 4.0 * scaled) * weights[:, :, None, None]
    return jnp.einsum('gkpq,rgkq->rgp', kernel, near_vals, precision=PRECISE)

def knot_kernel(points, knot_pts, knot_range):
    delta_x = points[0][:, None] - knot_pts[0][None, :]
    delta_y = points[1][:, None] - knot_pts[1][None, :]
    return jnp.exp(-jnp.sqrt(delta_x * delta_x + delta_y * delta_y) / knot_range)

def reference(probes, locations, knot_locs, knot_precision, neighbours, counts):
    groups = NB // NBD
    row_count = NBD * BLOCK
    knot_range = KNOT_REACH * math.sqrt(NB / KNOTS)
    loc_blocks = locations.reshape(2, NB, BLOCK)
    val_blocks = probes.reshape(PROBES, NB, BLOCK)
    slot_ids = jnp.arange(KNB, dtype=jnp.int32)

    def one_group(group_index):
        first_block = group_index * NBD
        block_ids = lax.dynamic_slice_in_dim(neighbours, first_block, NBD, 0)
        live_count = lax.dynamic_slice_in_dim(counts, first_block, NBD, 0)
        weights = (slot_ids[None, :] < live_count[:, None]).astype(jnp.float32)
        own_locs = lax.dynamic_slice_in_dim(loc_blocks, first_block, NBD, 1)
        return tapered(own_locs, loc_blocks[:, block_ids], val_blocks[:, block_ids], weights)
    taper_part = lax.map(one_group, jnp.arange(groups, dtype=jnp.int32))
    taper_part = jnp.transpose(taper_part, (1, 0, 2, 3)).reshape(PROBES, NOBS)
    loc_rows = jnp.transpose(locations.reshape(2, groups, row_count), (1, 0, 2))
    val_rows = jnp.transpose(probes.reshape(PROBES, groups, row_count), (1, 0, 2))

    def accumulate(running, row_pair):
        kernel = knot_kernel(row_pair[0], knot_locs, knot_range)
        return (running + jnp.dot(row_pair[1], kernel, precision=PRECISE), None)
    projection, _ = lax.scan(accumulate, jnp.zeros((PROBES, KNOTS), jnp.float32), (loc_rows, val_rows))
    projection = projection * (PROJ_GAIN * math.sqrt(KNOTS / NOBS))
    factor = lax.dot_general(projection, knot_precision, (((1,), (1,)), ((), ())), precision=PRECISE)

    def expand(points):
        return lax.dot_general(factor, knot_kernel(points, knot_locs, knot_range), (((1,), (1,)), ((), ())), precision=PRECISE)
    low_part = lax.map(expand, loc_rows)
    low_part = jnp.transpose(low_part, (1, 0, 2)).reshape(PROBES, NOBS)
    low_part = low_part * EXPAND_GAIN
    return TAPER_SCALE * taper_part + LOW_SCALE * low_part + NUGGET * probes
```

```python
import math

import jax
import jax.numpy as jnp
from jax import lax
from jax.sharding import PartitionSpec as P

COV_RANGE = 0.05
TAPER_LEN = 0.15
KNOT_REACH = 0.15
TAPER_SCALE = 0.1
PROJ_GAIN = 0.5
EXPAND_GAIN = 0.5
LOW_SCALE = 0.5
NUGGET = 0.25
PRECISE = lax.Precision.HIGHEST


def with_halo(block, sides, width):
    for axis, dim in sides:
        count = lax.axis_size(axis)
        forward = [(i, i + 1) for i in range(count - 1)]
        backward = [(target, source) for source, target in forward]
        low = lax.ppermute(
            lax.slice_in_dim(block, block.shape[dim] - width, None, axis=dim), axis, forward
        )
        high = lax.ppermute(lax.slice_in_dim(block, 0, width, axis=dim), axis, backward)
        block = jnp.concatenate([low, block, high], axis=dim)
    return block


def tapered(own_locs, near_locs, near_vals, weights):
    delta_x = own_locs[0][:, None, :, None] - near_locs[0][:, :, None, :]
    delta_y = own_locs[1][:, None, :, None] - near_locs[1][:, :, None, :]
    distance = jnp.sqrt(delta_x * delta_x + delta_y * delta_y)
    scaled = jnp.minimum(distance / TAPER_LEN, 1.0)
    remain = (1.0 - scaled) * (1.0 - scaled)
    kernel = (
        jnp.exp(-distance / COV_RANGE)
        * remain
        * remain
        * (1.0 + 4.0 * scaled)
        * weights[:, :, None, None]
    )
    return jnp.einsum("gkpq,rgkq->rgp", kernel, near_vals, precision=PRECISE)


def knot_kernel(points, knot_pts, knot_range):
    delta_x = points[0][:, None] - knot_pts[0][None, :]
    delta_y = points[1][:, None] - knot_pts[1][None, :]
    return jnp.exp(-jnp.sqrt(delta_x * delta_x + delta_y * delta_y) / knot_range)


def contract_last(left, right):
    return lax.dot_general(left, right, (((1,), (1,)), ((), ())), precision=PRECISE)


def doubling_sum(value, axis):
    count = lax.axis_size(axis)
    if count & (count - 1):
        return lax.psum(value, axis)
    step = 1
    while step < count:
        value = value + lax.ppermute(value, axis, [(i, i ^ step) for i in range(count)])
        step *= 2
    return value


def own_share_sum(value, axis, width):
    count = lax.axis_size(axis)
    me = lax.axis_index(axis)
    total = lax.dynamic_slice_in_dim(value, me * width, width, axis=1)
    for step in range(1, count):
        share = lax.dynamic_slice_in_dim(value, ((me + step) % count) * width, width, axis=1)
        total = total + lax.ppermute(share, axis, [(i, (i + step) % count) for i in range(count)])
    return total


def shards(probes, locations, knot_locs, knot_precision, neighbours, counts):
    own_blocks = neighbours.shape[0]
    slot_count = neighbours.shape[1]
    row_count = probes.shape[1]
    block_len = row_count // own_blocks
    probe_count = probes.shape[0]
    knot_total = knot_precision.shape[1]
    device_count = lax.axis_size(("space", "knot"))
    north_cells = lax.axis_size("knot") * own_blocks
    knot_range = KNOT_REACH * math.sqrt(own_blocks * device_count / knot_total)
    proj_scale = PROJ_GAIN * math.sqrt(knot_total / (row_count * device_count))
    stacked = jnp.concatenate([probes, locations], axis=0).reshape(
        probe_count + 2, 1, own_blocks, block_len
    )
    padded = with_halo(stacked, (("space", 1), ("knot", 2)), 1)
    near = padded.reshape(probe_count + 2, 3 * (own_blocks + 2), block_len)
    east_base = lax.axis_index("space") - 1
    north_base = lax.axis_index("knot") * own_blocks - 1
    local_ids = (neighbours // north_cells - east_base) * (own_blocks + 2) + (
        neighbours % north_cells - north_base
    )
    picked = near[:, local_ids]
    slot_ids = jnp.arange(slot_count, dtype=jnp.int32)
    weights = (slot_ids[None, :] < counts[:, None]).astype(jnp.float32)
    taper_part = tapered(
        locations.reshape(2, own_blocks, block_len),
        picked[probe_count:],
        picked[:probe_count],
        weights,
    )
    taper_part = taper_part.reshape(probe_count, row_count)
    gathered_vals, gathered_locs = (
        lax.all_gather(probes, "knot", axis=1, tiled=True),
        lax.all_gather(locations, "knot", axis=1, tiled=True),
    )
    kernel = knot_kernel(gathered_locs, knot_locs, knot_range)
    local_terms = jnp.dot(gathered_vals, kernel, precision=PRECISE)
    projection = doubling_sum(local_terms, "space") * proj_scale
    factor = contract_last(lax.all_gather(projection, "knot", axis=1, tiled=True), knot_precision)
    spread = contract_last(factor, kernel)
    low_part = own_share_sum(spread, "knot", row_count)
    low_part = low_part * EXPAND_GAIN
    return TAPER_SCALE * taper_part + LOW_SCALE * low_part + NUGGET * probes


def solution(mesh):
    return jax.shard_map(
        shards,
        mesh=mesh,
        in_specs=(
            P(None, ("space", "knot")),
            P(None, ("space", "knot")),
            P(None, "knot"),
            P("knot", None),
            P(("space", "knot"), None),
            P(("space", "knot")),
        ),
        out_specs=P(None, ("space", "knot")),
        check_vma=False,
    )
```

```python
import functools
import math

import jax
import jax.numpy as jnp
from jax import lax
from jax.experimental import pallas as pl
from jax.experimental.pallas import tpu as pltpu
from jax.sharding import PartitionSpec as P

COV_RANGE = 0.05
TAPER_LEN = 0.15
KNOT_REACH = 0.15
TAPER_SCALE = 0.1
PROJ_GAIN = 0.5
EXPAND_GAIN = 0.5
LOW_SCALE = 0.5
NUGGET = 0.25
LOG2E = math.log2(math.e)
STACK_ROWS = 24
TINY = 1e-30
TILE = 256
LIMIT = 16 * 1024 * 1024
VMEM = pl.BlockSpec(memory_space=pltpu.VMEM)
SMEM = pl.BlockSpec(memory_space=pltpu.SMEM)


def halves(x):
    high = x.astype(jnp.bfloat16)
    return high, (x - high.astype(jnp.float32)).astype(jnp.bfloat16)


def stacked_halves(x):
    return jnp.concatenate(halves(x), axis=0)


def folded(x):
    rows = x.shape[0] // 2
    return x[:rows] + x[rows:]


def dot_nt(left, right):
    return lax.dot_general(
        left, right, (((1,), (1,)), ((), ())), preferred_element_type=jnp.float32
    )


def dot_nn(left, right):
    return jnp.dot(left, right, preferred_element_type=jnp.float32)


def distance(ax, ay, bx, by):
    dx = ax - bx
    dy = ay - by
    square = dx * dx + dy * dy
    return square * lax.rsqrt(jnp.maximum(square, TINY))


def as_columns(rows):
    fill = jnp.zeros((8 - rows.shape[0], rows.shape[1]), rows.dtype)
    return jnp.transpose(jnp.concatenate([rows, fill], axis=0))


def project_kernel(probes, scale, stack_ref, knots_ref, out_ref, high_ref, low_ref, columns, weights):
    knots, points = high_ref.shape
    tile = min(TILE, knots)
    wide = min(TILE, points)
    columns[...] = as_columns(knots_ref[...] * scale)
    weights[...] = stacked_halves(stack_ref[:probes, :])

    @pl.loop(0, knots // tile)
    def _(step):
        rows = pl.ds(pl.multiple_of(step * tile, tile), tile)
        kx = columns[rows, 0:1]
        ky = columns[rows, 1:2]
        total = jnp.zeros((2 * probes, tile), jnp.float32)
        for start in range(0, points, wide):
            lanes = slice(start, start + wide)
            px = stack_ref[probes : probes + 1, lanes] * scale
            py = stack_ref[probes + 1 : probes + 2, lanes] * scale
            high, low = halves(jnp.exp2(-distance(kx, ky, px, py)))
            high_ref[rows, lanes] = high
            low_ref[rows, lanes] = low
            part = weights[:, lanes]
            total = total + (dot_nt(part, high) + dot_nt(part, low))
        out_ref[:, rows] = folded(total)


def project(stack, knot_locs, probes, scale):
    points, knots = stack.shape[1], knot_locs.shape[1]
    pairs = points * knots
    return pl.pallas_call(
        functools.partial(project_kernel, probes, scale),
        out_shape=(
            jax.ShapeDtypeStruct((probes, knots), jnp.float32),
            pltpu.VMEM((knots, points), jnp.bfloat16),
            pltpu.VMEM((knots, points), jnp.bfloat16),
        ),
        in_specs=[VMEM, VMEM],
        out_specs=(VMEM, VMEM, VMEM),
        scratch_shapes=[
            pltpu.VMEM((knots, 8), jnp.float32),
            pltpu.VMEM((2 * probes, points), jnp.bfloat16),
        ],
        compiler_params=pltpu.CompilerParams(vmem_limit_bytes=LIMIT),
        cost_estimate=pl.CostEstimate(flops=128 * pairs, bytes_accessed=4 * pairs, transcendentals=2 * pairs),
        name="project",
    )(stack, knot_locs)


def factor_kernel(scale, proj_ref, precision_ref, out_ref, weights):
    rows_all, depth = precision_ref.shape
    tile = min(TILE, rows_all)
    wide = min(TILE, depth)
    weights[...] = stacked_halves(proj_ref[...] * scale)

    @pl.loop(0, rows_all // tile)
    def _(step):
        rows = pl.ds(pl.multiple_of(step * tile, tile), tile)
        total = jnp.zeros((weights.shape[0], tile), jnp.float32)
        for start in range(0, depth, wide):
            lanes = slice(start, start + wide)
            high, low = halves(precision_ref[rows, lanes])
            part = weights[:, lanes]
            total = total + (dot_nt(part, high) + dot_nt(part, low))
        out_ref[:, rows] = folded(total)


def factored(projection, precision, scale):
    probes, depth = projection.shape
    rows = precision.shape[0]
    return pl.pallas_call(
        functools.partial(factor_kernel, scale),
        out_shape=jax.ShapeDtypeStruct((probes, rows), jnp.float32),
        in_specs=[VMEM, VMEM],
        out_specs=VMEM,
        scratch_shapes=[pltpu.VMEM((2 * probes, depth), jnp.bfloat16)],
        compiler_params=pltpu.CompilerParams(vmem_limit_bytes=LIMIT),
        cost_estimate=pl.CostEstimate(flops=128 * rows * depth, bytes_accessed=4 * rows * depth, transcendentals=0),
        name="factor",
    )(projection, precision)


def spread_kernel(scale, factor_ref, high_ref, low_ref, out_ref):
    points = high_ref.shape[1]
    wide = min(TILE, points)
    part = stacked_halves(factor_ref[...] * scale)
    for start in range(0, points, wide):
        lanes = slice(start, start + wide)
        out_ref[:, lanes] = folded(dot_nn(part, high_ref[:, lanes]) + dot_nn(part, low_ref[:, lanes]))


def spread(factor, high, low, scale):
    probes, points = factor.shape[0], high.shape[1]
    high = pltpu.with_memory_space_constraint(high, pltpu.VMEM)
    low = pltpu.with_memory_space_constraint(low, pltpu.VMEM)
    return pl.pallas_call(
        functools.partial(spread_kernel, scale),
        out_shape=jax.ShapeDtypeStruct((probes, points), jnp.float32),
        in_specs=[VMEM, VMEM, VMEM],
        out_specs=VMEM,
        compiler_params=pltpu.CompilerParams(vmem_limit_bytes=LIMIT),
        cost_estimate=pl.CostEstimate(flops=128 * high.size, bytes_accessed=4 * high.size, transcendentals=0),
        name="spread",
    )(factor, high, low)


def taper_kernel(probes, first, ids_ref, counts_ref, own_ref, near_ref, out_ref):
    slots = ids_ref.shape[1]
    block = own_ref.shape[1] // ids_ref.shape[0]
    inverse = 1.0 / TAPER_LEN
    decay = -LOG2E * TAPER_LEN / COV_RANGE
    for index in range(out_ref.shape[1] // block):
        group = first + index
        here = slice(group * block, (group + 1) * block)
        own = as_columns(own_ref[probes : probes + 2, here] * inverse)
        px = own[:, 0:1]
        py = own[:, 1:2]
        total = jnp.zeros((2 * probes, block), jnp.float32)
        for slot in range(slots):
            lanes = pl.ds(pl.multiple_of(ids_ref[group, slot] * block, block), block)
            live = jnp.where(slot < counts_ref[group], 1.0, 0.0)
            qx = near_ref[probes : probes + 1, lanes] * inverse
            qy = near_ref[probes + 1 : probes + 2, lanes] * inverse
            scaled = jnp.minimum(distance(px, py, qx, qy), 1.0)
            remain = (1.0 - scaled) * (1.0 - scaled)
            covariance = jnp.exp2(scaled * decay) * (remain * remain) * (1.0 + 4.0 * scaled)
            high, low = halves(covariance)
            part = stacked_halves(near_ref[:probes, lanes] * live)
            total = total + (dot_nt(part, high) + dot_nt(part, low))
        out_ref[:, index * block : (index + 1) * block] = (
            TAPER_SCALE * folded(total) + NUGGET * own_ref[:probes, here]
        )


def taper(ids, counts, own, near, probes, first, blocks):
    block = own.shape[1] // ids.shape[0]
    pairs = blocks * ids.shape[1] * block * block
    return pl.pallas_call(
        functools.partial(taper_kernel, probes, first),
        out_shape=jax.ShapeDtypeStruct((probes, blocks * block), jnp.float32),
        in_specs=[SMEM, SMEM, VMEM, VMEM],
        out_specs=VMEM,
        compiler_params=pltpu.CompilerParams(vmem_limit_bytes=LIMIT),
        cost_estimate=pl.CostEstimate(flops=512 * pairs, bytes_accessed=4 * pairs, transcendentals=2 * pairs),
        name="taper",
    )(ids, counts, own, near)


def doubling_sum(value, axis):
    count = lax.axis_size(axis)
    if count & (count - 1):
        return lax.psum(value, axis)
    step = 1
    while step < count:
        value = value + lax.ppermute(value, axis, [(i, i ^ step) for i in range(count)])
        step *= 2
    return value


def shifted(value, axis, step):
    count = lax.axis_size(axis)
    if step % count == 0:
        return value
    return lax.ppermute(value, axis, [((i + step) % count, i) for i in range(count)])


def paired(value, axis, first):
    count = lax.axis_size(axis)
    pairs = [(i, i + 1) for i in range(first, count - 1, 2)]
    return lax.ppermute(value, axis, pairs + [(b, a) for a, b in pairs])


def shards(probes, locations, knot_locs, knot_precision, neighbours, counts):
    own_blocks = neighbours.shape[0]
    probe_count, row_count = probes.shape
    block_len = row_count // own_blocks
    knot_total = knot_precision.shape[1]
    device_count = lax.axis_size(("space", "knot"))
    groups = lax.axis_size("knot")
    north_cells = groups * own_blocks
    knot_range = KNOT_REACH * math.sqrt(own_blocks * device_count / knot_total)
    proj_scale = PROJ_GAIN * math.sqrt(knot_total / (row_count * device_count))
    column = lax.axis_index("space")

    fill = jnp.zeros((STACK_ROWS - probe_count - 2, row_count), jnp.float32)
    stack = jnp.concatenate([probes, locations, fill], axis=0)
    chunks = [shifted(stack, "knot", step) for step in range(groups)]

    own_strip = jnp.concatenate(
        [chunks[-1][:, row_count - block_len :], stack, chunks[1 % groups][:, :block_len]], axis=1
    )
    near = jnp.concatenate(
        [own_strip, paired(own_strip, "space", 0), paired(own_strip, "space", 1)], axis=1
    )
    move = neighbours // north_cells - column
    east_strip = 1 + column % 2
    strip = jnp.where(move == 0, 0, jnp.where(move > 0, east_strip, 3 - east_strip))
    north = neighbours % north_cells - lax.axis_index("knot") * own_blocks + 1
    ids = strip * (own_blocks + 2) + north
    pieces = math.gcd(own_blocks, 4)
    per_piece = own_blocks // pieces
    base = jnp.concatenate(
        [taper(ids, counts, stack, near, probe_count, i * per_piece, per_piece) for i in range(pieces)],
        axis=1,
    )

    rate = LOG2E / knot_range
    parts = [project(chunk, knot_locs, probe_count, rate) for chunk in chunks]
    projection = doubling_sum(sum(part[0] for part in parts), "space")
    projection = lax.all_gather(projection, "knot", axis=1, tiled=True)
    factor = factored(projection, knot_precision, proj_scale)
    total = base
    for step in reversed(range(groups)):
        share = spread(factor, parts[step][1], parts[step][2], LOW_SCALE * EXPAND_GAIN)
        total = total + shifted(share, "knot", -step)
    return total


def solution(mesh):
    return jax.shard_map(
        shards,
        mesh=mesh,
        in_specs=(
            P(None, ("space", "knot")),
            P(None, ("space", "knot")),
            P(None, "knot"),
            P("knot", None),
            P(("space", "knot"), None),
            P(("space", "knot")),
        ),
        out_specs=P(None, ("space", "knot")),
        check_vma=False,
    )
```

```python
import functools
import math

import jax
import jax.numpy as jnp
from jax import lax
from jax.experimental import pallas as pl
from jax.experimental.pallas import tpu as pltpu
from jax.sharding import PartitionSpec as P

COV_RANGE = 0.05
TAPER_LEN = 0.15
KNOT_REACH = 0.15
TAPER_SCALE = 0.1
PROJ_GAIN = 0.5
EXPAND_GAIN = 0.5
LOW_SCALE = 0.5
NUGGET = 0.25
LOG2E = math.log2(math.e)
STACK_ROWS = 24
TINY = 1e-30
TILE = 256
LIMIT = 16 * 1024 * 1024
VMEM = pl.BlockSpec(memory_space=pltpu.VMEM)
SMEM = pl.BlockSpec(memory_space=pltpu.SMEM)


def halves(x):
    high = x.astype(jnp.bfloat16)
    return high, (x - high.astype(jnp.float32)).astype(jnp.bfloat16)


def stacked_halves(x):
    return jnp.concatenate(halves(x), axis=0)


def folded(x):
    rows = x.shape[0] // 2
    return x[:rows] + x[rows:]


def dot_nt(left, right):
    return lax.dot_general(
        left, right, (((1,), (1,)), ((), ())), preferred_element_type=jnp.float32
    )


def dot_nn(left, right):
    return jnp.dot(left, right, preferred_element_type=jnp.float32)


def distance(ax, ay, bx, by):
    dx = ax - bx
    dy = ay - by
    square = dx * dx + dy * dy
    return square * lax.rsqrt(jnp.maximum(square, TINY))


def as_columns(rows):
    fill = jnp.zeros((8 - rows.shape[0], rows.shape[1]), rows.dtype)
    return jnp.transpose(jnp.concatenate([rows, fill], axis=0))


def project_kernel(probes, scale, stack_ref, knots_ref, out_ref, high_ref, low_ref, columns, weights):
    knots, points = high_ref.shape
    tile = min(TILE, knots)
    wide = min(TILE, points)
    columns[...] = as_columns(knots_ref[...] * scale)
    weights[...] = stacked_halves(stack_ref[:probes, :])

    @pl.loop(0, knots // tile)
    def _(step):
        rows = pl.ds(pl.multiple_of(step * tile, tile), tile)
        kx = columns[rows, 0:1]
        ky = columns[rows, 1:2]
        total = jnp.zeros((2 * probes, tile), jnp.float32)
        for start in range(0, points, wide):
            lanes = slice(start, start + wide)
            px = stack_ref[probes : probes + 1, lanes] * scale
            py = stack_ref[probes + 1 : probes + 2, lanes] * scale
            high, low = halves(jnp.exp2(-distance(kx, ky, px, py)))
            high_ref[rows, lanes] = high
            low_ref[rows, lanes] = low
            part = weights[:, lanes]
            total = total + (dot_nt(part, high) + dot_nt(part, low))
        out_ref[:, rows] = folded(total)


def project(stack, knot_locs, probes, scale):
    points, knots = stack.shape[1], knot_locs.shape[1]
    pairs = points * knots
    return pl.pallas_call(
        functools.partial(project_kernel, probes, scale),
        out_shape=(
            jax.ShapeDtypeStruct((probes, knots), jnp.float32),
            pltpu.VMEM((knots, points), jnp.bfloat16),
            pltpu.VMEM((knots, points), jnp.bfloat16),
        ),
        in_specs=[VMEM, VMEM],
        out_specs=(VMEM, VMEM, VMEM),
        scratch_shapes=[
            pltpu.VMEM((knots, 8), jnp.float32),
            pltpu.VMEM((2 * probes, points), jnp.bfloat16),
        ],
        compiler_params=pltpu.CompilerParams(vmem_limit_bytes=LIMIT),
        cost_estimate=pl.CostEstimate(flops=128 * pairs, bytes_accessed=4 * pairs, transcendentals=2 * pairs),
        name="project",
    )(stack, knot_locs)


def factor_kernel(scale, proj_ref, precision_ref, out_ref, weights):
    rows_all, depth = precision_ref.shape
    tile = min(TILE, rows_all)
    wide = min(TILE, depth)
    weights[...] = stacked_halves(proj_ref[...] * scale)

    @pl.loop(0, rows_all // tile)
    def _(step):
        rows = pl.ds(pl.multiple_of(step * tile, tile), tile)
        total = jnp.zeros((weights.shape[0], tile), jnp.float32)
        for start in range(0, depth, wide):
            lanes = slice(start, start + wide)
            high, low = halves(precision_ref[rows, lanes])
            part = weights[:, lanes]
            total = total + (dot_nt(part, high) + dot_nt(part, low))
        out_ref[:, rows] = folded(total)


def factored(projection, precision, scale):
    probes, depth = projection.shape
    rows = precision.shape[0]
    return pl.pallas_call(
        functools.partial(factor_kernel, scale),
        out_shape=jax.ShapeDtypeStruct((probes, rows), jnp.float32),
        in_specs=[VMEM, VMEM],
        out_specs=VMEM,
        scratch_shapes=[pltpu.VMEM((2 * probes, depth), jnp.bfloat16)],
        compiler_params=pltpu.CompilerParams(vmem_limit_bytes=LIMIT),
        cost_estimate=pl.CostEstimate(flops=128 * rows * depth, bytes_accessed=4 * rows * depth, transcendentals=0),
        name="factor",
    )(projection, precision)


def spread_kernel(scale, factor_ref, high_ref, low_ref, out_ref):
    points = high_ref.shape[1]
    wide = min(TILE, points)
    part = stacked_halves(factor_ref[...] * scale)
    for start in range(0, points, wide):
        lanes = slice(start, start + wide)
        out_ref[:, lanes] = folded(dot_nn(part, high_ref[:, lanes]) + dot_nn(part, low_ref[:, lanes]))


def spread(factor, high, low, scale):
    probes, points = factor.shape[0], high.shape[1]
    high = pltpu.with_memory_space_constraint(high, pltpu.VMEM)
    low = pltpu.with_memory_space_constraint(low, pltpu.VMEM)
    return pl.pallas_call(
        functools.partial(spread_kernel, scale),
        out_shape=jax.ShapeDtypeStruct((probes, points), jnp.float32),
        in_specs=[VMEM, VMEM, VMEM],
        out_specs=VMEM,
        compiler_params=pltpu.CompilerParams(vmem_limit_bytes=LIMIT),
        cost_estimate=pl.CostEstimate(flops=128 * high.size, bytes_accessed=4 * high.size, transcendentals=0),
        name="spread",
    )(factor, high, low)


def taper_kernel(probes, first, ids_ref, counts_ref, own_ref, near_ref, out_ref):
    slots = ids_ref.shape[1]
    block = own_ref.shape[1] // ids_ref.shape[0]
    inverse = 1.0 / TAPER_LEN
    decay = -LOG2E * TAPER_LEN / COV_RANGE
    for index in range(out_ref.shape[1] // block):
        group = first + index
        here = slice(group * block, (group + 1) * block)
        own = as_columns(own_ref[probes : probes + 2, here] * inverse)
        px = own[:, 0:1]
        py = own[:, 1:2]
        total = jnp.zeros((2 * probes, block), jnp.float32)
        for slot in range(slots):
            lanes = pl.ds(pl.multiple_of(ids_ref[group, slot] * block, block), block)
            live = jnp.where(slot < counts_ref[group], 1.0, 0.0)
            qx = near_ref[probes : probes + 1, lanes] * inverse
            qy = near_ref[probes + 1 : probes + 2, lanes] * inverse
            scaled = jnp.minimum(distance(px, py, qx, qy), 1.0)
            remain = (1.0 - scaled) * (1.0 - scaled)
            covariance = jnp.exp2(scaled * decay) * (remain * remain) * (1.0 + 4.0 * scaled)
            high, low = halves(covariance)
            part = stacked_halves(near_ref[:probes, lanes] * live)
            total = total + (dot_nt(part, high) + dot_nt(part, low))
        out_ref[:, index * block : (index + 1) * block] = (
            TAPER_SCALE * folded(total) + NUGGET * own_ref[:probes, here]
        )


def taper(ids, counts, own, near, probes, first, blocks):
    block = own.shape[1] // ids.shape[0]
    pairs = blocks * ids.shape[1] * block * block
    return pl.pallas_call(
        functools.partial(taper_kernel, probes, first),
        out_shape=jax.ShapeDtypeStruct((probes, blocks * block), jnp.float32),
        in_specs=[SMEM, SMEM, VMEM, VMEM],
        out_specs=VMEM,
        compiler_params=pltpu.CompilerParams(vmem_limit_bytes=LIMIT),
        cost_estimate=pl.CostEstimate(flops=512 * pairs, bytes_accessed=4 * pairs, transcendentals=2 * pairs),
        name="taper",
    )(ids, counts, own, near)


def gathered_sum(value, axis, other):
    rows, width = value.shape
    count, groups = lax.axis_size(axis), lax.axis_size(other)
    shares = value.reshape(count, rows * width // count)
    shares = lax.all_to_all(shares, axis, 0, 0, tiled=True)
    share = jnp.sum(shares, axis=0, keepdims=True)
    copies = jnp.broadcast_to(share, (count * groups, share.shape[1]))
    whole = lax.all_to_all(copies, (axis, other), 0, 0, tiled=True)
    whole = jnp.swapaxes(whole.reshape(count, groups, -1), 0, 1).reshape(groups, rows, width)
    return jnp.swapaxes(whole, 0, 1).reshape(rows, groups * width)


def shifted(value, axis, step):
    count = lax.axis_size(axis)
    if step % count == 0:
        return value
    return lax.ppermute(value, axis, [((i + step) % count, i) for i in range(count)])


def paired(value, axis, first):
    count = lax.axis_size(axis)
    pairs = [(i, i + 1) for i in range(first, count - 1, 2)]
    return lax.ppermute(value, axis, pairs + [(b, a) for a, b in pairs])


def shards(probes, locations, knot_locs, knot_precision, neighbours, counts):
    own_blocks = neighbours.shape[0]
    probe_count, row_count = probes.shape
    block_len = row_count // own_blocks
    knot_total = knot_precision.shape[1]
    device_count = lax.axis_size(("space", "knot"))
    groups = lax.axis_size("knot")
    north_cells = groups * own_blocks
    knot_range = KNOT_REACH * math.sqrt(own_blocks * device_count / knot_total)
    proj_scale = PROJ_GAIN * math.sqrt(knot_total / (row_count * device_count))
    column = lax.axis_index("space")

    fill = jnp.zeros((STACK_ROWS - probe_count - 2, row_count), jnp.float32)
    stack = jnp.concatenate([probes, locations, fill], axis=0)
    chunks = [shifted(stack, "knot", step) for step in range(groups)]

    own_strip = jnp.concatenate(
        [chunks[-1][:, row_count - block_len :], stack, chunks[1 % groups][:, :block_len]], axis=1
    )
    near = jnp.concatenate(
        [own_strip, paired(own_strip, "space", 0), paired(own_strip, "space", 1)], axis=1
    )
    move = neighbours // north_cells - column
    east_strip = 1 + column % 2
    strip = jnp.where(move == 0, 0, jnp.where(move > 0, east_strip, 3 - east_strip))
    north = neighbours % north_cells - lax.axis_index("knot") * own_blocks + 1
    ids = strip * (own_blocks + 2) + north
    pieces = math.gcd(own_blocks, 4)
    per_piece = own_blocks // pieces
    base = jnp.concatenate(
        [taper(ids, counts, stack, near, probe_count, i * per_piece, per_piece) for i in range(pieces)],
        axis=1,
    )

    rate = LOG2E / knot_range
    parts = [project(chunk, knot_locs, probe_count, rate) for chunk in chunks]
    projection = gathered_sum(sum(part[0] for part in parts), "space", "knot")
    factor = factored(projection, knot_precision, proj_scale)
    total = base
    for step in reversed(range(groups)):
        share = spread(factor, parts[step][1], parts[step][2], LOW_SCALE * EXPAND_GAIN)
        total = total + shifted(share, "knot", -step)
    return total


def solution(mesh):
    return jax.shard_map(
        shards,
        mesh=mesh,
        in_specs=(
            P(None, ("space", "knot")),
            P(None, ("space", "knot")),
            P(None, "knot"),
            P("knot", None),
            P(("space", "knot"), None),
            P(("space", "knot")),
        ),
        out_specs=P(None, ("space", "knot")),
        check_vma=False,
    )
```

```python
import functools
import math

import jax
import jax.numpy as jnp
from jax import lax
from jax.experimental import pallas as pl
from jax.experimental.pallas import tpu as pltpu
from jax.sharding import PartitionSpec as P

COV_RANGE = 0.05
TAPER_LEN = 0.15
KNOT_REACH = 0.15
TAPER_SCALE = 0.1
PROJ_GAIN = 0.5
EXPAND_GAIN = 0.5
LOW_SCALE = 0.5
NUGGET = 0.25
LOG2E = math.log2(math.e)
STACK_ROWS = 24
TINY = 1e-30
TILE = 256
LANES = 128
LIMIT = 16 * 1024 * 1024
VMEM = pl.BlockSpec(memory_space=pltpu.VMEM)
SMEM = pl.BlockSpec(memory_space=pltpu.SMEM)


def halves(x):
    high = x.astype(jnp.bfloat16)
    return high, (x - high.astype(jnp.float32)).astype(jnp.bfloat16)


def stacked_halves(x):
    return jnp.concatenate(halves(x), axis=0)


def folded(x):
    rows = x.shape[0] // 2
    return x[:rows] + x[rows:]


def dot_nt(left, right):
    return lax.dot_general(
        left, right, (((1,), (1,)), ((), ())), preferred_element_type=jnp.float32
    )


def dot_nn(left, right):
    return jnp.dot(left, right, preferred_element_type=jnp.float32)


def distance(ax, ay, bx, by):
    dx = ax - bx
    dy = ay - by
    square = dx * dx + dy * dy
    return square * lax.rsqrt(jnp.maximum(square, TINY))


def as_columns(rows):
    fill = jnp.zeros((8 - rows.shape[0], rows.shape[1]), rows.dtype)
    return jnp.transpose(jnp.concatenate([rows, fill], axis=0))


def padded_halves(x, rows):
    fill = jnp.zeros((rows - 2 * x.shape[0], x.shape[1]), jnp.bfloat16)
    return jnp.concatenate([*halves(x), fill], axis=0)


def folded_columns(x, rows):
    x = jnp.transpose(x)
    return x[:rows] + x[rows : 2 * rows]


def cost(work, pairs, transcendentals=0):
    return pl.CostEstimate(flops=work * pairs, bytes_accessed=4 * pairs, transcendentals=transcendentals * pairs)


def prepare_kernel(probes_ref, locations_ref, knots_ref, stack_ref, knots_out_ref):
    probes, points = probes_ref.shape
    stack_ref[:probes, :] = probes_ref[...]
    fill = jnp.zeros((STACK_ROWS - probes - 2, points), jnp.float32)
    stack_ref[probes:, :] = jnp.concatenate([locations_ref[...], fill], axis=0)
    knots_out_ref[...] = knots_ref[...]


def prepare(probes, locations, knot_locs):
    return pl.pallas_call(
        prepare_kernel,
        out_shape=(
            jax.ShapeDtypeStruct((STACK_ROWS, probes.shape[1]), jnp.float32),
            jax.ShapeDtypeStruct(knot_locs.shape, jnp.float32),
        ),
        in_specs=[VMEM, VMEM, VMEM],
        out_specs=(VMEM, VMEM),
        compiler_params=pltpu.CompilerParams(vmem_limit_bytes=LIMIT),
        name="prepare",
    )(probes, locations, knot_locs)


def project_kernel(probes, scale, stack_ref, knots_ref, out_ref, high_ref, low_ref, columns, weights):
    points, knots = high_ref.shape
    tile = min(TILE, knots)
    wide = min(TILE, points)
    columns[...] = as_columns(stack_ref[probes : probes + 2, :] * scale)
    weights[...] = stacked_halves(stack_ref[:probes, :])

    @pl.loop(0, knots // tile)
    def _(step):
        lanes = pl.ds(pl.multiple_of(step * tile, tile), tile)
        kx = knots_ref[0:1, lanes] * scale
        ky = knots_ref[1:2, lanes] * scale
        total = jnp.zeros((2 * probes, tile), jnp.float32)
        for start in range(0, points, wide):
            rows = slice(start, start + wide)
            px = columns[rows, 0:1]
            py = columns[rows, 1:2]
            high, low = halves(jnp.exp2(-distance(px, py, kx, ky)))
            high_ref[rows, lanes] = high
            low_ref[rows, lanes] = low
            part = weights[:, rows]
            total = total + (dot_nn(part, high) + dot_nn(part, low))
        out_ref[:, lanes] = folded(total)


def project(stack, knot_locs, probes, scale):
    points, knots = stack.shape[1], knot_locs.shape[1]
    return pl.pallas_call(
        functools.partial(project_kernel, probes, scale),
        out_shape=(
            jax.ShapeDtypeStruct((probes, knots), jnp.float32),
            pltpu.VMEM((points, knots), jnp.bfloat16),
            pltpu.VMEM((points, knots), jnp.bfloat16),
        ),
        in_specs=[VMEM, VMEM],
        out_specs=(VMEM, VMEM, VMEM),
        scratch_shapes=[
            pltpu.VMEM((points, 8), jnp.float32),
            pltpu.VMEM((2 * probes, points), jnp.bfloat16),
        ],
        compiler_params=pltpu.CompilerParams(vmem_limit_bytes=LIMIT),
        cost_estimate=cost(3000, points * knots, 2),
        name="project",
    )(stack, knot_locs)


def factor_kernel(scale, step, before_ref, proj_ref, precision_ref, *rest):
    out_ref, weights = rest[-2:]
    probes, depth = proj_ref.shape
    all_rows = precision_ref.shape[0]
    tile = min(TILE, all_rows)
    wide = min(TILE, depth)
    weights[...] = padded_halves(proj_ref[...] * scale, weights.shape[0])
    owner = lax.rem(lax.axis_index("knot") + step, lax.axis_size("knot"))
    offset = owner * depth

    @pl.loop(0, all_rows // tile)
    def _(turn):
        rows = pl.ds(pl.multiple_of(turn * tile, tile), tile)
        total = jnp.zeros((tile, weights.shape[0]), jnp.float32)
        for start in range(0, depth, wide):
            lanes = pl.ds(pl.multiple_of(offset + start, wide), wide)
            high, low = halves(precision_ref[rows, lanes])
            part = weights[:, start : start + wide]
            total = total + (dot_nt(high, part) + dot_nt(low, part))
        found = folded_columns(total, probes)
        if before_ref is not None:
            found = found + before_ref[:, rows]
        out_ref[:, rows] = found


def factored(before, projection, precision, scale, step, after=()):
    probes, depth = projection.shape
    rows = precision.shape[0]
    kernel = functools.partial(factor_kernel, scale, step)
    operands = (projection, precision, *after)
    if before is None:
        kernel = functools.partial(kernel, None)
    else:
        operands = (before, *operands)
    return pl.pallas_call(
        kernel,
        out_shape=jax.ShapeDtypeStruct((probes, rows), jnp.float32),
        in_specs=[VMEM] * (len(operands) - len(after)) + [pl.BlockSpec(memory_space=pl.ANY)] * len(after),
        out_specs=VMEM,
        scratch_shapes=[pltpu.VMEM((LANES, depth), jnp.bfloat16)],
        compiler_params=pltpu.CompilerParams(vmem_limit_bytes=LIMIT),
        cost_estimate=cost(1200, rows * depth),
        name="factor",
    )(*operands)


def spread_kernel(scale, factor_ref, high_ref, low_ref, out_ref, weights):
    probes = factor_ref.shape[0]
    points = high_ref.shape[0]
    tile = min(TILE, points)
    weights[...] = padded_halves(factor_ref[...] * scale, weights.shape[0])
    for start in range(0, points, tile):
        rows = slice(start, start + tile)
        total = dot_nt(high_ref[rows, :], weights[...]) + dot_nt(low_ref[rows, :], weights[...])
        out_ref[:, rows] = folded_columns(total, probes)


def spread(factor, high, low, scale):
    (probes, knots), points = factor.shape, high.shape[0]
    high = pltpu.with_memory_space_constraint(high, pltpu.VMEM)
    low = pltpu.with_memory_space_constraint(low, pltpu.VMEM)
    return pl.pallas_call(
        functools.partial(spread_kernel, scale),
        out_shape=jax.ShapeDtypeStruct((probes, points), jnp.float32),
        in_specs=[VMEM, VMEM, VMEM],
        out_specs=VMEM,
        scratch_shapes=[pltpu.VMEM((LANES, knots), jnp.bfloat16)],
        compiler_params=pltpu.CompilerParams(vmem_limit_bytes=LIMIT),
        cost_estimate=cost(850, knots * points),
        name="spread",
    )(factor, high, low)


def taper_kernel(probes, first, ids_ref, counts_ref, own_ref, near_ref, out_ref, values):
    own_blocks, slots = ids_ref.shape
    block = own_ref.shape[1] // own_blocks
    near_blocks = near_ref.shape[1] // block
    column = lax.axis_index("space")
    north_base = lax.axis_index("knot") * own_blocks - 1
    north_cells = lax.axis_size("knot") * own_blocks
    inverse = 1.0 / TAPER_LEN
    decay = -LOG2E * TAPER_LEN / COV_RANGE
    values[:, near_blocks * block :] = jnp.zeros((values.shape[0], block), jnp.bfloat16)
    values[:, : near_blocks * block] = padded_halves(near_ref[:probes, :], values.shape[0])

    def place(group, slot):
        ahead = ids_ref[group, slot] - (column - 1) * north_cells
        east = jnp.where(ahead >= north_cells, 1, 0) + jnp.where(ahead >= 2 * north_cells, 1, 0)
        strip = jnp.where(east == 1, 0, 1 + lax.rem(column + lax.div(east, 2) + 1, 2))
        index = strip * (own_blocks + 2) + (ahead - east * north_cells - north_base)
        return index, jnp.where(slot < counts_ref[group], index, near_blocks)

    def lanes_of(index):
        return pl.ds(pl.multiple_of(index * block, block), block)

    for index in range(out_ref.shape[1] // block):
        group = first + index
        here = slice(group * block, (group + 1) * block)
        own = as_columns(own_ref[probes : probes + 2, here] * inverse)
        px = own[:, 0:1]
        py = own[:, 1:2]
        total = jnp.zeros((block, values.shape[0]), jnp.float32)
        for pair in range(0, slots, 2):
            highs, lows, parts = [], [], []
            for slot in range(pair, min(pair + 2, slots)):
                spot, value_spot = place(group, slot)
                lanes = lanes_of(spot)
                qx = near_ref[probes : probes + 1, lanes] * inverse
                qy = near_ref[probes + 1 : probes + 2, lanes] * inverse
                scaled = jnp.minimum(distance(px, py, qx, qy), 1.0)
                remain = (1.0 - scaled) * (1.0 - scaled)
                covariance = jnp.exp2(scaled * decay) * (remain * remain) * (1.0 + 4.0 * scaled)
                high, low = halves(covariance)
                highs.append(high)
                lows.append(low)
                parts.append(values[:, lanes_of(value_spot)])
            part = jnp.concatenate(parts, axis=1)
            total = total + (
                dot_nt(jnp.concatenate(highs, axis=1), part) + dot_nt(jnp.concatenate(lows, axis=1), part)
            )
        out_ref[:, index * block : (index + 1) * block] = (
            TAPER_SCALE * folded_columns(total, probes) + NUGGET * own_ref[:probes, here]
        )


def taper(ids, counts, own, near, probes, first, blocks):
    block = own.shape[1] // ids.shape[0]
    return pl.pallas_call(
        functools.partial(taper_kernel, probes, first),
        out_shape=jax.ShapeDtypeStruct((probes, blocks * block), jnp.float32),
        in_specs=[SMEM, SMEM, VMEM, VMEM],
        out_specs=VMEM,
        scratch_shapes=[pltpu.VMEM((LANES, near.shape[1] + block), jnp.bfloat16)],
        compiler_params=pltpu.CompilerParams(vmem_limit_bytes=LIMIT),
        cost_estimate=cost(6000, blocks * ids.shape[1] * block * block, 2),
        name="taper",
    )(ids, counts, own, near)


def doubling_sum(value, axis, other):
    count, groups = lax.axis_size(axis), lax.axis_size(other)
    if count & (count - 1):
        return lax.psum(value, axis)
    steps = [1 << i for i in range(count.bit_length() - 1)]
    half = len(steps) // 2
    for turn in range(len(steps)):
        pairs = []
        for j in range(groups):
            step = steps[(turn + half * (j % 2)) % len(steps)]
            pairs += [(i * groups + j, (i ^ step) * groups + j) for i in range(count)]
        value = value + lax.ppermute(value, (axis, other), pairs)
    return value


def shifted(value, axis, step):
    count = lax.axis_size(axis)
    if step % count == 0:
        return value
    return lax.ppermute(value, axis, [((i + step) % count, i) for i in range(count)])


def paired(value, axis, first):
    count = lax.axis_size(axis)
    pairs = [(i, i + 1) for i in range(first, count - 1, 2)]
    return lax.ppermute(value, axis, pairs + [(b, a) for a, b in pairs])


def shards(probes, locations, knot_locs, knot_precision, neighbours, counts):
    own_blocks = neighbours.shape[0]
    probe_count, row_count = probes.shape
    block_len = row_count // own_blocks
    knot_total = knot_precision.shape[1]
    device_count = lax.axis_size(("space", "knot"))
    groups = lax.axis_size("knot")
    knot_range = KNOT_REACH * math.sqrt(own_blocks * device_count / knot_total)
    proj_scale = PROJ_GAIN * math.sqrt(knot_total / (row_count * device_count))

    stack, knots = prepare(probes, locations, knot_locs)
    chunks = [shifted(stack, "knot", step) for step in range(groups)]
    strips = [paired(stack, "space", 0), paired(stack, "space", 1)]

    first_blocks = jnp.concatenate([strip[:, :block_len] for strip in strips], axis=1)
    last_blocks = jnp.concatenate([strip[:, row_count - block_len :] for strip in strips], axis=1)
    if groups == 2:
        edge = jnp.where(lax.axis_index("knot") == 0, last_blocks, first_blocks)
        above = below = shifted(edge, "knot", 1)
    else:
        above, below = shifted(first_blocks, "knot", 1), shifted(last_blocks, "knot", -1)
    near = jnp.concatenate(
        [
            chunks[-1][:, row_count - block_len :],
            stack,
            chunks[1 % groups][:, :block_len],
            below[:, :block_len],
            strips[0],
            above[:, :block_len],
            below[:, block_len:],
            strips[1],
            above[:, block_len:],
        ],
        axis=1,
    )
    pieces = math.gcd(own_blocks, 4)
    per_piece = own_blocks // pieces
    base = [
        taper(neighbours, counts, stack, near, probe_count, i * per_piece, per_piece) for i in range(pieces)
    ]

    rate = LOG2E / knot_range
    parts = [project(chunk, knots, probe_count, rate) for chunk in chunks]
    projection = doubling_sum(sum(part[0] for part in parts), "space", "knot")
    factor = factored(None, projection, knot_precision, proj_scale, 0, base[:-1])
    for step in range(1, groups):
        factor = factored(factor, shifted(projection, "knot", step), knot_precision, proj_scale, step)
    total = jnp.concatenate(base, axis=1)
    for step in reversed(range(groups)):
        share = spread(factor, parts[step][1], parts[step][2], LOW_SCALE * EXPAND_GAIN)
        total = total + shifted(share, "knot", -step)
    return total


def solution(mesh):
    return jax.shard_map(
        shards,
        mesh=mesh,
        in_specs=(
            P(None, ("space", "knot")),
            P(None, ("space", "knot")),
            P(None, "knot"),
            P("knot", None),
            P(("space", "knot"), None),
            P(("space", "knot")),
        ),
        out_specs=P(None, ("space", "knot")),
        check_vma=False,
    )
```

```python
import functools
import math

import jax
import jax.numpy as jnp
from jax import lax
from jax.experimental import pallas as pl
from jax.experimental.pallas import tpu as pltpu
from jax.sharding import PartitionSpec as P

COV_RANGE = 0.05
TAPER_LEN = 0.15
KNOT_REACH = 0.15
TAPER_SCALE = 0.1
PROJ_GAIN = 0.5
EXPAND_GAIN = 0.5
LOW_SCALE = 0.5
NUGGET = 0.25
LOG2E = math.log2(math.e)
STACK_ROWS = 24
TINY = 1e-30
TILE = 256
LANES = 128
SLAB = 32
LIMIT = 6 * 1024 * 1024
VMEM = pl.BlockSpec(memory_space=pltpu.VMEM)
HBM = pl.BlockSpec(memory_space=pltpu.HBM)
SMEM = pl.BlockSpec(memory_space=pltpu.SMEM)


def halves(x):
    high = x.astype(jnp.bfloat16)
    return high, (x - high.astype(jnp.float32)).astype(jnp.bfloat16)


def stacked_halves(x):
    return jnp.concatenate(halves(x), axis=0)


def folded(x):
    rows = x.shape[0] // 2
    return x[:rows] + x[rows:]


def dot_nt(left, right):
    return lax.dot_general(
        left, right, (((1,), (1,)), ((), ())), preferred_element_type=jnp.float32
    )


def dot_nn(left, right):
    return jnp.dot(left, right, preferred_element_type=jnp.float32)


def distance(ax, ay, bx, by):
    dx = ax - bx
    dy = ay - by
    square = dx * dx + dy * dy
    return square * lax.rsqrt(jnp.maximum(square, TINY))


def as_columns(rows):
    fill = jnp.zeros((8 - rows.shape[0], rows.shape[1]), rows.dtype)
    return jnp.transpose(jnp.concatenate([rows, fill], axis=0))


def padded_halves(x, rows):
    fill = jnp.zeros((rows - 2 * x.shape[0], x.shape[1]), jnp.bfloat16)
    return jnp.concatenate([*halves(x), fill], axis=0)


def folded_columns(x, rows):
    x = jnp.transpose(x)
    return x[:rows] + x[rows : 2 * rows]


def cost(work, pairs, transcendentals=0):
    return pl.CostEstimate(flops=work * pairs, bytes_accessed=4 * pairs, transcendentals=transcendentals * pairs)


def prepare_kernel(probes_ref, locations_ref, knots_ref, stack_ref, knots_out_ref, coords, sems):
    probes, points = probes_ref.shape
    copies = [
        pltpu.make_async_copy(probes_ref, stack_ref.at[pl.ds(0, probes), :], sems.at[0]),
        pltpu.make_async_copy(locations_ref, coords, sems.at[1]),
        pltpu.make_async_copy(knots_ref, knots_out_ref, sems.at[2]),
    ]
    for copy in copies:
        copy.start()
    for copy in copies:
        copy.wait()
    fill = jnp.zeros((STACK_ROWS - probes - 2, points), jnp.float32)
    stack_ref[probes:, :] = jnp.concatenate([coords[...], fill], axis=0)


def prepare(probes, locations, knot_locs):
    probes, locations, knot_locs = [
        pltpu.with_memory_space_constraint(x, pltpu.HBM) for x in (probes, locations, knot_locs)
    ]
    return pl.pallas_call(
        prepare_kernel,
        out_shape=(
            jax.ShapeDtypeStruct((STACK_ROWS, probes.shape[1]), jnp.float32),
            jax.ShapeDtypeStruct(knot_locs.shape, jnp.float32),
        ),
        in_specs=[HBM, HBM, HBM],
        out_specs=(VMEM, VMEM),
        scratch_shapes=[pltpu.VMEM(locations.shape, jnp.float32), pltpu.SemaphoreType.DMA((3,))],
        compiler_params=pltpu.CompilerParams(vmem_limit_bytes=LIMIT),
        name="prepare",
    )(probes, locations, knot_locs)


def broadcast_columns(rows):
    columns = as_columns(rows)
    wide = (rows.shape[1], LANES)
    return jnp.broadcast_to(columns[:, 0:1], wide), jnp.broadcast_to(columns[:, 1:2], wide)


def project_kernel(probes, scale, stack_ref, knots_ref, out_ref, high_ref, low_ref, copy_ref, east, north, weights):
    points, knots = high_ref.shape
    tile = min(TILE, knots)
    wide = min(TILE, points)
    copy_ref[...] = stack_ref[...]
    for start in range(0, points, LANES):
        rows = slice(start, start + LANES)
        east[rows, :], north[rows, :] = broadcast_columns(stack_ref[probes : probes + 2, rows] * scale)
    weights[...] = stacked_halves(stack_ref[:probes, :])

    @pl.loop(0, knots // tile)
    def _(step):
        lanes = pl.ds(pl.multiple_of(step * tile, tile), tile)
        kx = knots_ref[0:1, lanes] * scale
        ky = knots_ref[1:2, lanes] * scale
        total = jnp.zeros((2 * probes, tile), jnp.float32)
        for start in range(0, points, wide):
            highs, lows = [], []
            for slab in range(start, start + wide, SLAB):
                rows = slice(slab, slab + SLAB)
                px, py = east[rows, :], north[rows, :]
                parts = [
                    halves(jnp.exp2(-distance(px, py, kx[:, at : at + LANES], ky[:, at : at + LANES])))
                    for at in range(0, tile, LANES)
                ]
                high = jnp.concatenate([part[0] for part in parts], axis=1)
                low = jnp.concatenate([part[1] for part in parts], axis=1)
                high_ref[rows, lanes] = high
                low_ref[rows, lanes] = low
                highs.append(high)
                lows.append(low)
            part = weights[:, start : start + wide]
            total = total + (
                dot_nn(part, jnp.concatenate(highs, axis=0)) + dot_nn(part, jnp.concatenate(lows, axis=0))
            )
        out_ref[:, lanes] = folded(total)


def project(stack, knot_locs, probes, scale):
    points, knots = stack.shape[1], knot_locs.shape[1]
    return pl.pallas_call(
        functools.partial(project_kernel, probes, scale),
        out_shape=(
            jax.ShapeDtypeStruct((probes, knots), jnp.float32),
            pltpu.VMEM((points, knots), jnp.bfloat16),
            pltpu.VMEM((points, knots), jnp.bfloat16),
            jax.ShapeDtypeStruct(stack.shape, jnp.float32),
        ),
        in_specs=[VMEM, VMEM],
        out_specs=(VMEM, VMEM, VMEM, VMEM),
        scratch_shapes=[
            pltpu.VMEM((points, LANES), jnp.float32),
            pltpu.VMEM((points, LANES), jnp.float32),
            pltpu.VMEM((2 * probes, points), jnp.bfloat16),
        ],
        compiler_params=pltpu.CompilerParams(vmem_limit_bytes=LIMIT),
        cost_estimate=cost(2300, points * knots, 2),
        name="project",
    )(stack, knot_locs)


def factor_kernel(scale, step, before_ref, proj_ref, precision_ref, *rest):
    out_ref, weights = rest[-2:]
    probes, depth = proj_ref.shape
    all_rows = precision_ref.shape[0]
    tile = min(TILE, all_rows)
    wide = min(TILE, depth)
    weights[...] = stacked_halves(proj_ref[...] * scale)
    owner = lax.rem(lax.axis_index("knot") + step, lax.axis_size("knot"))
    offset = owner * depth

    @pl.loop(0, all_rows // tile)
    def _(turn):
        rows = pl.ds(pl.multiple_of(turn * tile, tile), tile)
        total = jnp.zeros((weights.shape[0], tile), jnp.float32)
        for start in range(0, depth, wide):
            lanes = pl.ds(pl.multiple_of(offset + start, wide), wide)
            high, low = halves(precision_ref[rows, lanes])
            part = weights[:, start : start + wide]
            total = total + (dot_nt(part, high) + dot_nt(part, low))
        found = folded(total)
        if before_ref is not None:
            found = found + before_ref[:, rows]
        out_ref[:, rows] = found


def factored(before, projection, precision, scale, step, after=()):
    probes, depth = projection.shape
    rows = precision.shape[0]
    kernel = functools.partial(factor_kernel, scale, step)
    operands = (projection, precision, *after)
    if before is None:
        kernel = functools.partial(kernel, None)
    else:
        operands = (before, *operands)
    return pl.pallas_call(
        kernel,
        out_shape=jax.ShapeDtypeStruct((probes, rows), jnp.float32),
        in_specs=[VMEM] * (len(operands) - len(after)) + [pl.BlockSpec(memory_space=pl.ANY)] * len(after),
        out_specs=VMEM,
        scratch_shapes=[pltpu.VMEM((2 * probes, depth), jnp.bfloat16)],
        compiler_params=pltpu.CompilerParams(vmem_limit_bytes=LIMIT),
        cost_estimate=cost(1200, rows * depth),
        name="factor",
    )(*operands)


def spread_kernel(scale, factor_ref, high_ref, low_ref, out_ref, weights):
    probes = factor_ref.shape[0]
    points = high_ref.shape[0]
    tile = min(TILE, points)
    weights[...] = padded_halves(factor_ref[...] * scale, weights.shape[0])
    for start in range(0, points, tile):
        rows = slice(start, start + tile)
        total = dot_nt(high_ref[rows, :], weights[...]) + dot_nt(low_ref[rows, :], weights[...])
        out_ref[:, rows] = folded_columns(total, probes)


def spread(factor, high, low, scale):
    (probes, knots), points = factor.shape, high.shape[0]
    high = pltpu.with_memory_space_constraint(high, pltpu.VMEM)
    low = pltpu.with_memory_space_constraint(low, pltpu.VMEM)
    return pl.pallas_call(
        functools.partial(spread_kernel, scale),
        out_shape=jax.ShapeDtypeStruct((probes, points), jnp.float32),
        in_specs=[VMEM, VMEM, VMEM],
        out_specs=VMEM,
        scratch_shapes=[pltpu.VMEM((LANES, knots), jnp.bfloat16)],
        compiler_params=pltpu.CompilerParams(vmem_limit_bytes=LIMIT),
        cost_estimate=cost(850, knots * points),
        name="spread",
    )(factor, high, low)


def covariance(apart):
    scaled = jnp.minimum(apart, 1.0)
    remain = (1.0 - scaled) * (1.0 - scaled)
    return jnp.exp2(scaled * (-LOG2E * TAPER_LEN / COV_RANGE)) * (remain * remain) * (1.0 + 4.0 * scaled)


def taper_kernel(probes, first, ids_ref, counts_ref, own_ref, near_ref, out_ref, values):
    own_blocks, slots = ids_ref.shape
    block = own_ref.shape[1] // own_blocks
    near_blocks = near_ref.shape[1] // block
    column = lax.axis_index("space")
    north_base = lax.axis_index("knot") * own_blocks - 1
    north_cells = lax.axis_size("knot") * own_blocks
    inverse = 1.0 / TAPER_LEN
    values[:, near_blocks * block :] = jnp.zeros((values.shape[0], block), jnp.bfloat16)
    values[:, : near_blocks * block] = padded_halves(near_ref[:probes, :], values.shape[0])

    def place(group, slot):
        ahead = ids_ref[group, slot] - (column - 1) * north_cells
        east = jnp.where(ahead >= north_cells, 1, 0) + jnp.where(ahead >= 2 * north_cells, 1, 0)
        strip = jnp.where(east == 1, 0, 1 + lax.rem(column + lax.div(east, 2) + 1, 2))
        index = strip * (own_blocks + 2) + (ahead - east * north_cells - north_base)
        return index, jnp.where(slot < counts_ref[group], index, near_blocks)

    def lanes_of(index):
        return pl.ds(pl.multiple_of(index * block, block), block)

    for index in range(out_ref.shape[1] // block):
        group = first + index
        here = slice(group * block, (group + 1) * block)
        px, py = broadcast_columns(own_ref[probes : probes + 2, here] * inverse)
        total = jnp.zeros((block, values.shape[0]), jnp.float32)
        for pair in range(0, slots, 2):
            corners, parts = [], []
            for slot in range(pair, min(pair + 2, slots)):
                spot, value_spot = place(group, slot)
                lanes = lanes_of(spot)
                corners.append((near_ref[probes : probes + 1, lanes] * inverse, near_ref[probes + 1 : probes + 2, lanes] * inverse))
                parts.append(values[:, lanes_of(value_spot)])
            highs, lows = [], []
            for slab in range(0, block, SLAB):
                rows = slice(slab, slab + SLAB)
                pieces = [halves(covariance(distance(px[rows], py[rows], *corner))) for corner in corners]
                highs.append(jnp.concatenate([piece[0] for piece in pieces], axis=1))
                lows.append(jnp.concatenate([piece[1] for piece in pieces], axis=1))
            part = jnp.concatenate(parts, axis=1)
            total = total + (
                dot_nt(jnp.concatenate(highs, axis=0), part) + dot_nt(jnp.concatenate(lows, axis=0), part)
            )
        out_ref[:, index * block : (index + 1) * block] = (
            TAPER_SCALE * folded_columns(total, probes) + NUGGET * own_ref[:probes, here]
        )


def taper(ids, counts, own, near, probes, first, blocks):
    block = own.shape[1] // ids.shape[0]
    return pl.pallas_call(
        functools.partial(taper_kernel, probes, first),
        out_shape=jax.ShapeDtypeStruct((probes, blocks * block), jnp.float32),
        in_specs=[SMEM, SMEM, VMEM, VMEM],
        out_specs=VMEM,
        scratch_shapes=[pltpu.VMEM((LANES, near.shape[1] + block), jnp.bfloat16)],
        compiler_params=pltpu.CompilerParams(vmem_limit_bytes=LIMIT),
        cost_estimate=cost(4500, blocks * ids.shape[1] * block * block, 2),
        name="taper",
    )(ids, counts, own, near)


def doubling_sum(value, axis, other):
    count, groups = lax.axis_size(axis), lax.axis_size(other)
    if count & (count - 1):
        return lax.psum(value, axis)
    steps = [1 << i for i in range(count.bit_length() - 1)]
    half = len(steps) // 2
    for turn in range(len(steps)):
        pairs = []
        for j in range(groups):
            step = steps[(turn + half * (j % 2)) % len(steps)]
            pairs += [(i * groups + j, (i ^ step) * groups + j) for i in range(count)]
        value = value + lax.ppermute(value, (axis, other), pairs)
    return value


def shifted(value, axis, step):
    count = lax.axis_size(axis)
    if step % count == 0:
        return value
    return lax.ppermute(value, axis, [((i + step) % count, i) for i in range(count)])


def paired(value, axis, first):
    count = lax.axis_size(axis)
    pairs = [(i, i + 1) for i in range(first, count - 1, 2)]
    return lax.ppermute(value, axis, pairs + [(b, a) for a, b in pairs])


def shards(probes, locations, knot_locs, knot_precision, neighbours, counts):
    own_blocks = neighbours.shape[0]
    probe_count, row_count = probes.shape
    block_len = row_count // own_blocks
    knot_total = knot_precision.shape[1]
    device_count = lax.axis_size(("space", "knot"))
    groups = lax.axis_size("knot")
    knot_range = KNOT_REACH * math.sqrt(own_blocks * device_count / knot_total)
    proj_scale = PROJ_GAIN * math.sqrt(knot_total / (row_count * device_count))

    stack, knots = prepare(probes, locations, knot_locs)
    chunks = [shifted(stack, "knot", step) for step in range(groups)]
    rate = LOG2E / knot_range
    parts = [project(chunk, knots, probe_count, rate) for chunk in chunks]
    stack = parts[0][3]
    strips = [paired(stack, "space", 0), paired(stack, "space", 1)]

    first_blocks = jnp.concatenate([strip[:, :block_len] for strip in strips], axis=1)
    last_blocks = jnp.concatenate([strip[:, row_count - block_len :] for strip in strips], axis=1)
    if groups == 2:
        edge = jnp.where(lax.axis_index("knot") == 0, last_blocks, first_blocks)
        above = below = shifted(edge, "knot", 1)
    else:
        above, below = shifted(first_blocks, "knot", 1), shifted(last_blocks, "knot", -1)
    near = jnp.concatenate(
        [
            chunks[-1][:, row_count - block_len :],
            stack,
            chunks[1 % groups][:, :block_len],
            below[:, :block_len],
            strips[0],
            above[:, :block_len],
            below[:, block_len:],
            strips[1],
            above[:, block_len:],
        ],
        axis=1,
    )
    pieces = math.gcd(own_blocks, 4)
    per_piece = own_blocks // pieces
    base = [
        taper(neighbours, counts, stack, near, probe_count, i * per_piece, per_piece) for i in range(pieces)
    ]

    projection = doubling_sum(sum(part[0] for part in parts), "space", "knot")
    factor = factored(None, projection, knot_precision, proj_scale, 0, base[:-1])
    for step in range(1, groups):
        factor = factored(factor, shifted(projection, "knot", step), knot_precision, proj_scale, step)
    total = jnp.concatenate(base, axis=1)
    for step in reversed(range(groups)):
        share = spread(factor, parts[step][1], parts[step][2], LOW_SCALE * EXPAND_GAIN)
        total = total + shifted(share, "knot", -step)
    return total


def solution(mesh):
    return jax.shard_map(
        shards,
        mesh=mesh,
        in_specs=(
            P(None, ("space", "knot")),
            P(None, ("space", "knot")),
            P(None, "knot"),
            P("knot", None),
            P(("space", "knot"), None),
            P(("space", "knot")),
        ),
        out_specs=P(None, ("space", "knot")),
        check_vma=False,
    )
```

```python
import functools
import math

import jax
import jax.numpy as jnp
from jax import lax
from jax.experimental import pallas as pl
from jax.experimental.pallas import tpu as pltpu
from jax.sharding import PartitionSpec as P

COV_RANGE = 0.05
TAPER_LEN = 0.15
KNOT_REACH = 0.15
TAPER_SCALE = 0.1
PROJ_GAIN = 0.5
EXPAND_GAIN = 0.5
LOW_SCALE = 0.5
NUGGET = 0.25
LOG2E = math.log2(math.e)
CELL = 0.1
TINY = 1e-30
TILE = 256
LANES = 128
HALF_GRAIN = 2.0**-24
LIMIT = 6 * 1024 * 1024
VMEM = pl.BlockSpec(memory_space=pltpu.VMEM)
HBM = pl.BlockSpec(memory_space=pltpu.HBM)
SMEM = pl.BlockSpec(memory_space=pltpu.SMEM)


def halves(x):
    high = x.astype(jnp.bfloat16)
    return high, (x - high.astype(jnp.float32)).astype(jnp.bfloat16)


def stacked_halves(x):
    return jnp.concatenate(halves(x), axis=0)


def folded(x):
    rows = x.shape[0] // 2
    return x[:rows] + x[rows:]


def dot_nt(left, right):
    return lax.dot_general(
        left, right, (((1,), (1,)), ((), ())), preferred_element_type=jnp.float32
    )


def dot_nn(left, right):
    return jnp.dot(left, right, preferred_element_type=jnp.float32)


def distance(ax, ay, bx, by):
    dx = ax - bx
    dy = ay - by
    square = dx * dx + dy * dy
    return square * lax.rsqrt(jnp.maximum(square, TINY))


def padded_halves(x, rows):
    fill = jnp.zeros((rows - 2 * x.shape[0], x.shape[1]), jnp.bfloat16)
    return jnp.concatenate([*halves(x), fill], axis=0)


def folded_columns(x, rows):
    x = jnp.transpose(x)
    return x[:rows] + x[rows : 2 * rows]


def cost(work, pairs, transcendentals=0):
    return pl.CostEstimate(flops=work * pairs, bytes_accessed=4 * pairs, transcendentals=transcendentals * pairs)


def coordinate_rows(ref, points, axis):
    start = points + axis * LANES
    return ref[:, start : start + LANES]


def prepare_kernel(blocks, probes_ref, locations_ref, knots_ref, stack_ref, knots_out_ref, coords, sems):
    points = probes_ref.shape[1]
    block = points // blocks
    copies = [
        pltpu.make_async_copy(probes_ref, stack_ref.at[:, pl.ds(0, points)], sems.at[0]),
        pltpu.make_async_copy(locations_ref, coords, sems.at[1]),
        pltpu.make_async_copy(knots_ref, knots_out_ref, sems.at[2]),
    ]
    for copy in copies:
        copy.start()
    for copy in copies:
        copy.wait()
    stack_ref[:, points:] = jnp.zeros((stack_ref.shape[0], 2 * LANES), jnp.float32)
    for axis in range(2):
        lanes = slice(points + axis * LANES, points + (axis + 1) * LANES)
        for index in range(blocks):
            stack_ref[index : index + 1, lanes] = coords[axis : axis + 1, index * block : (index + 1) * block]


def prepare(probes, locations, knot_locs, blocks):
    rows, points = probes.shape
    assert points == blocks * LANES and blocks + 2 <= rows
    probes, locations, knot_locs = [
        pltpu.with_memory_space_constraint(x, pltpu.HBM) for x in (probes, locations, knot_locs)
    ]
    return pl.pallas_call(
        functools.partial(prepare_kernel, blocks),
        out_shape=(
            jax.ShapeDtypeStruct((rows, points + 2 * LANES), jnp.float32),
            jax.ShapeDtypeStruct(knot_locs.shape, jnp.float32),
        ),
        in_specs=[HBM, HBM, HBM],
        out_specs=(VMEM, VMEM),
        scratch_shapes=[pltpu.VMEM(locations.shape, jnp.float32), pltpu.SemaphoreType.DMA((3,))],
        compiler_params=pltpu.CompilerParams(vmem_limit_bytes=LIMIT),
        name="prepare",
    )(probes, locations, knot_locs)


def strip_kernel(below_ref, own_ref, above_ref, out_ref):
    rows, width = own_ref.shape
    points = width - 2 * LANES
    blocks = points // LANES
    out_ref[:, :LANES] = below_ref[:, points - LANES : points]
    out_ref[:, LANES : points + LANES] = own_ref[:, :points]
    out_ref[:, points + LANES : points + 2 * LANES] = above_ref[:, :LANES]
    for axis in range(2):
        lanes = slice(points + axis * LANES, points + (axis + 1) * LANES)
        target = slice(lanes.start + 2 * LANES, lanes.stop + 2 * LANES)
        out_ref[:, target] = jnp.zeros((rows, LANES), jnp.float32)
        out_ref[0:1, target] = below_ref[blocks - 1 : blocks, lanes]
        out_ref[1 : blocks + 1, target] = own_ref[:blocks, lanes]
        out_ref[blocks + 1 : blocks + 2, target] = above_ref[0:1, lanes]


def make_strip(below, own, above):
    return pl.pallas_call(
        strip_kernel,
        out_shape=jax.ShapeDtypeStruct((own.shape[0], own.shape[1] + 2 * LANES), jnp.float32),
        in_specs=[VMEM, VMEM, VMEM],
        out_specs=VMEM,
        compiler_params=pltpu.CompilerParams(vmem_limit_bytes=LIMIT),
        name="strip",
    )(below, own, above)


def project_kernel(scale, grain, stack_ref, knots_ref, out_ref, high_ref, low_ref, copy_ref, columns, weights):
    points, knots = high_ref.shape
    probes = stack_ref.shape[0]
    tile = min(TILE, knots)
    wide = min(TILE, points)
    copy_ref[...] = stack_ref[...]
    for axis in range(2):
        turned = jnp.transpose(coordinate_rows(stack_ref, points, axis) * scale)
        turned = (turned + grain) - grain
        for index in range(points // LANES):
            columns[index * LANES : (index + 1) * LANES, axis : axis + 1] = turned[:, index : index + 1]
    weights[...] = stacked_halves(stack_ref[:, :points])

    @pl.loop(0, knots // tile)
    def _(step):
        lanes = pl.ds(pl.multiple_of(step * tile, tile), tile)
        kx, ky = [
            (knots_ref[axis : axis + 1, lanes] * scale + grain) - (grain - grain * HALF_GRAIN) for axis in range(2)
        ]
        total = jnp.zeros((2 * probes, tile), jnp.float32)
        for start in range(0, points, wide):
            rows = slice(start, start + wide)
            dx = columns[rows, 0:1] - kx
            dy = columns[rows, 1:2] - ky
            square = dx * dx + dy * dy
            high, low = halves(jnp.exp2(-(square * lax.rsqrt(square))))
            high_ref[rows, lanes] = high
            low_ref[rows, lanes] = low
            part = weights[:, rows]
            total = total + (dot_nn(part, high) + dot_nn(part, low))
        out_ref[:, lanes] = folded(total)


def project(stack, knot_locs, scale, extent):
    probes, points, knots = stack.shape[0], stack.shape[1] - 2 * LANES, knot_locs.shape[1]
    grain = 2.0 ** math.ceil(math.log2(1.01 * scale * extent))
    return pl.pallas_call(
        functools.partial(project_kernel, scale, grain),
        out_shape=(
            jax.ShapeDtypeStruct((probes, knots), jnp.float32),
            pltpu.VMEM((points, knots), jnp.bfloat16),
            pltpu.VMEM((points, knots), jnp.bfloat16),
            jax.ShapeDtypeStruct(stack.shape, jnp.float32),
        ),
        in_specs=[VMEM, VMEM],
        out_specs=(VMEM, VMEM, VMEM, VMEM),
        scratch_shapes=[
            pltpu.VMEM((points, 8), jnp.float32),
            pltpu.VMEM((2 * probes, points), jnp.bfloat16),
        ],
        compiler_params=pltpu.CompilerParams(vmem_limit_bytes=LIMIT),
        cost_estimate=cost(2800, points * knots, 2),
        name="project",
    )(stack, knot_locs)


def factor_kernel(scale, step, before_ref, proj_ref, precision_ref, *rest):
    out_ref, weights = rest[-2:]
    probes, depth = proj_ref.shape
    all_rows = precision_ref.shape[0]
    tile = min(TILE, all_rows)
    wide = min(TILE, depth)
    weights[...] = stacked_halves(proj_ref[...] * scale)
    owner = lax.rem(lax.axis_index("knot") + step, lax.axis_size("knot"))
    offset = owner * depth

    @pl.loop(0, all_rows // tile)
    def _(turn):
        rows = pl.ds(pl.multiple_of(turn * tile, tile), tile)
        total = jnp.zeros((weights.shape[0], tile), jnp.float32)
        for start in range(0, depth, wide):
            lanes = pl.ds(pl.multiple_of(offset + start, wide), wide)
            high, low = halves(precision_ref[rows, lanes])
            part = weights[:, start : start + wide]
            total = total + (dot_nt(part, high) + dot_nt(part, low))
        found = folded(total)
        if before_ref is not None:
            found = found + before_ref[:, rows]
        out_ref[:, rows] = found


def factored(before, projection, precision, scale, step, after=()):
    probes, depth = projection.shape
    rows = precision.shape[0]
    kernel = functools.partial(factor_kernel, scale, step)
    operands = (projection, precision, *after)
    if before is None:
        kernel = functools.partial(kernel, None)
    else:
        operands = (before, *operands)
    return pl.pallas_call(
        kernel,
        out_shape=jax.ShapeDtypeStruct((probes, rows), jnp.float32),
        in_specs=[VMEM] * (len(operands) - len(after)) + [pl.BlockSpec(memory_space=pl.ANY)] * len(after),
        out_specs=VMEM,
        scratch_shapes=[pltpu.VMEM((2 * probes, depth), jnp.bfloat16)],
        compiler_params=pltpu.CompilerParams(vmem_limit_bytes=LIMIT),
        cost_estimate=cost(1200, rows * depth),
        name="factor",
    )(*operands)


def spread_kernel(scale, factor_ref, high_ref, low_ref, out_ref, weights):
    probes = factor_ref.shape[0]
    points = high_ref.shape[0]
    tile = min(TILE, points)
    weights[...] = padded_halves(factor_ref[...] * scale, weights.shape[0])
    for start in range(0, points, tile):
        rows = slice(start, start + tile)
        total = dot_nt(high_ref[rows, :], weights[...]) + dot_nt(low_ref[rows, :], weights[...])
        out_ref[:, rows] = folded_columns(total, probes)


def spread(factor, high, low, scale):
    (probes, knots), points = factor.shape, high.shape[0]
    high = pltpu.with_memory_space_constraint(high, pltpu.VMEM)
    low = pltpu.with_memory_space_constraint(low, pltpu.VMEM)
    return pl.pallas_call(
        functools.partial(spread_kernel, scale),
        out_shape=jax.ShapeDtypeStruct((probes, points), jnp.float32),
        in_specs=[VMEM, VMEM, VMEM],
        out_specs=VMEM,
        scratch_shapes=[pltpu.VMEM((LANES, knots), jnp.bfloat16)],
        compiler_params=pltpu.CompilerParams(vmem_limit_bytes=LIMIT),
        cost_estimate=cost(850, knots * points),
        name="spread",
    )(factor, high, low)


def covariance(apart):
    scaled = jnp.minimum(apart, 1.0)
    remain = (1.0 - scaled) * (1.0 - scaled)
    return jnp.exp2(scaled * (-LOG2E * TAPER_LEN / COV_RANGE)) * (remain * remain) * (1.0 + 4.0 * scaled)


def taper_kernel(first, ids_ref, counts_ref, own_ref, near_ref, out_ref, values, coords):
    own_blocks, slots = ids_ref.shape
    block = LANES
    strips, probes, width = near_ref.shape
    span = own_blocks + 2
    column = lax.axis_index("space")
    north_base = lax.axis_index("knot") * own_blocks - 1
    north_cells = lax.axis_size("knot") * own_blocks
    inverse = 1.0 / TAPER_LEN
    values[:, strips * span * block :] = jnp.zeros((values.shape[0], block), jnp.bfloat16)
    for strip in range(strips):
        values[:, strip * span * block : (strip + 1) * span * block] = padded_halves(
            near_ref[strip, :, : span * block], values.shape[0]
        )
        for axis in range(2):
            rows = near_ref[strip, :, (span + axis) * block : (span + axis + 1) * block] * inverse
            for index in range(span):
                start = (strip * span + index) * block
                coords[axis : axis + 1, start : start + block] = rows[index : index + 1]
    own_columns = [
        jnp.transpose(coordinate_rows(own_ref, own_blocks * block, axis) * inverse) for axis in range(2)
    ]

    def place(group, slot):
        ahead = ids_ref[group, slot] - (column - 1) * north_cells
        east = jnp.where(ahead >= north_cells, 1, 0) + jnp.where(ahead >= 2 * north_cells, 1, 0)
        strip = jnp.where(east == 1, 0, 1 + lax.rem(column + lax.div(east, 2) + 1, 2))
        index = strip * span + (ahead - east * north_cells - north_base)
        return lanes_of(index), lanes_of(jnp.where(slot < counts_ref[group], index, strips * span))

    def lanes_of(index):
        return pl.ds(pl.multiple_of(index * block, block), block)

    for index in range(out_ref.shape[1] // block):
        group = first + index
        px, py = [turned[:, group : group + 1] for turned in own_columns]
        total = jnp.zeros((block, values.shape[0]), jnp.float32)
        for pair in range(0, slots, 2):
            highs, lows, parts = [], [], []
            for slot in range(pair, min(pair + 2, slots)):
                lanes, value_lanes = place(group, slot)
                high, low = halves(covariance(distance(px, py, coords[0:1, lanes], coords[1:2, lanes])))
                highs.append(high)
                lows.append(low)
                parts.append(values[:, value_lanes])
            part = jnp.concatenate(parts, axis=1)
            total = total + (
                dot_nt(jnp.concatenate(highs, axis=1), part) + dot_nt(jnp.concatenate(lows, axis=1), part)
            )
        out_ref[:, index * block : (index + 1) * block] = (
            TAPER_SCALE * folded_columns(total, probes)
            + NUGGET * own_ref[:, group * block : (group + 1) * block]
        )


def taper(ids, counts, own, near, first, blocks):
    own_blocks, slots = ids.shape
    strips, probes, width = near.shape
    return pl.pallas_call(
        functools.partial(taper_kernel, first),
        out_shape=jax.ShapeDtypeStruct((probes, blocks * LANES), jnp.float32),
        in_specs=[SMEM, SMEM, VMEM, VMEM],
        out_specs=VMEM,
        scratch_shapes=[
            pltpu.VMEM((LANES, (strips * (own_blocks + 2) + 1) * LANES), jnp.bfloat16),
            pltpu.VMEM((2, strips * (own_blocks + 2) * LANES), jnp.float32),
        ],
        compiler_params=pltpu.CompilerParams(vmem_limit_bytes=LIMIT),
        cost_estimate=cost(6000, blocks * slots * LANES * LANES, 2),
        name="taper",
    )(ids, counts, own, near)


def doubling_sum(value, axis, other):
    count, groups = lax.axis_size(axis), lax.axis_size(other)
    if count & (count - 1):
        return lax.psum(value, axis)
    steps = [1 << i for i in range(count.bit_length() - 1)]
    half = len(steps) // 2
    for turn in range(len(steps)):
        pairs = []
        for j in range(groups):
            step = steps[(turn + half * (j % 2)) % len(steps)]
            pairs += [(i * groups + j, (i ^ step) * groups + j) for i in range(count)]
        value = value + lax.ppermute(value, (axis, other), pairs)
    return value


def shifted(value, axis, step):
    count = lax.axis_size(axis)
    if step % count == 0:
        return value
    return lax.ppermute(value, axis, [((i + step) % count, i) for i in range(count)])


def paired(value, axis, first):
    count = lax.axis_size(axis)
    pairs = [(i, i + 1) for i in range(first, count - 1, 2)]
    return lax.ppermute(value, axis, pairs + [(b, a) for a, b in pairs])


def shards(probes, locations, knot_locs, knot_precision, neighbours, counts):
    own_blocks = neighbours.shape[0]
    row_count = probes.shape[1]
    knot_total = knot_precision.shape[1]
    device_count = lax.axis_size(("space", "knot"))
    groups = lax.axis_size("knot")
    knot_range = KNOT_REACH * math.sqrt(own_blocks * device_count / knot_total)
    proj_scale = PROJ_GAIN * math.sqrt(knot_total / (row_count * device_count))

    stack, knots = prepare(probes, locations, knot_locs, own_blocks)
    chunks = [shifted(stack, "knot", step) for step in range(groups)]
    rate = LOG2E / knot_range
    extent = CELL * max(lax.axis_size("space"), groups * own_blocks)
    parts = [project(chunk, knots, rate, extent) for chunk in chunks]
    stack = parts[0][3]

    strip = make_strip(chunks[-1], stack, chunks[1 % groups])
    near = jnp.stack([strip, paired(strip, "space", 0), paired(strip, "space", 1)])
    pieces = math.gcd(own_blocks, 4)
    per_piece = own_blocks // pieces
    base = [taper(neighbours, counts, stack, near, i * per_piece, per_piece) for i in range(pieces)]

    projection = doubling_sum(sum(part[0] for part in parts), "space", "knot")
    factor = factored(None, projection, knot_precision, proj_scale, 0, base[:-1])
    for step in range(1, groups):
        factor = factored(factor, shifted(projection, "knot", step), knot_precision, proj_scale, step)
    total = jnp.concatenate(base, axis=1)
    for step in reversed(range(groups)):
        share = spread(factor, parts[step][1], parts[step][2], LOW_SCALE * EXPAND_GAIN)
        total = total + shifted(share, "knot", -step)
    return total


def solution(mesh):
    return jax.shard_map(
        shards,
        mesh=mesh,
        in_specs=(
            P(None, ("space", "knot")),
            P(None, ("space", "knot")),
            P(None, "knot"),
            P("knot", None),
            P(("space", "knot"), None),
            P(("space", "knot")),
        ),
        out_specs=P(None, ("space", "knot")),
        check_vma=False,
    )
```

```python
import functools
import math

import jax
import jax.numpy as jnp
from jax import lax
from jax.experimental import pallas as pl
from jax.experimental.pallas import tpu as pltpu
from jax.sharding import PartitionSpec as P

COV_RANGE = 0.05
TAPER_LEN = 0.15
KNOT_REACH = 0.15
TAPER_SCALE = 0.1
PROJ_GAIN = 0.5
EXPAND_GAIN = 0.5
LOW_SCALE = 0.5
NUGGET = 0.25
LOG2E = math.log2(math.e)
CELL = 0.1
TINY = 1e-30
TILE = 256
LANES = 128
HALF_GRAIN = 2.0**-24
LIMIT = 6 * 1024 * 1024
VMEM = pl.BlockSpec(memory_space=pltpu.VMEM)
HBM = pl.BlockSpec(memory_space=pltpu.HBM)
SMEM = pl.BlockSpec(memory_space=pltpu.SMEM)


def halves(x):
    high = x.astype(jnp.bfloat16)
    return high, (x - high.astype(jnp.float32)).astype(jnp.bfloat16)


def stacked_halves(x):
    return jnp.concatenate(halves(x), axis=0)


def folded(x):
    rows = x.shape[0] // 2
    return x[:rows] + x[rows:]


def dot_nt(left, right):
    return lax.dot_general(
        left, right, (((1,), (1,)), ((), ())), preferred_element_type=jnp.float32
    )


def dot_nn(left, right):
    return jnp.dot(left, right, preferred_element_type=jnp.float32)


def distance(ax, ay, bx, by):
    dx = ax - bx
    dy = ay - by
    square = dx * dx + dy * dy
    return square * lax.rsqrt(jnp.maximum(square, TINY))


def padded_halves(x, rows):
    fill = jnp.zeros((rows - 2 * x.shape[0], x.shape[1]), jnp.bfloat16)
    return jnp.concatenate([*halves(x), fill], axis=0)


def folded_columns(x, rows):
    x = jnp.transpose(x)
    return x[:rows] + x[rows : 2 * rows]


def cost(work, pairs, transcendentals=0):
    return pl.CostEstimate(flops=work * pairs, bytes_accessed=4 * pairs, transcendentals=transcendentals * pairs)


def coordinate_rows(ref, points, axis):
    start = points + axis * LANES
    return ref[:, start : start + LANES]


def prepare_kernel(blocks, probes_ref, locations_ref, knots_ref, stack_ref, knots_out_ref, coords, sems):
    points = probes_ref.shape[1]
    block = points // blocks
    copies = [
        pltpu.make_async_copy(probes_ref, stack_ref.at[:, pl.ds(0, points)], sems.at[0]),
        pltpu.make_async_copy(locations_ref, coords, sems.at[1]),
        pltpu.make_async_copy(knots_ref, knots_out_ref, sems.at[2]),
    ]
    for copy in copies:
        copy.start()
    for copy in copies:
        copy.wait()
    stack_ref[:, points:] = jnp.zeros((stack_ref.shape[0], 2 * LANES), jnp.float32)
    for axis in range(2):
        lanes = slice(points + axis * LANES, points + (axis + 1) * LANES)
        for index in range(blocks):
            stack_ref[index : index + 1, lanes] = coords[axis : axis + 1, index * block : (index + 1) * block]


def prepare(probes, locations, knot_locs, blocks):
    rows, points = probes.shape
    assert points == blocks * LANES and blocks + 2 <= rows
    probes, locations, knot_locs = [
        pltpu.with_memory_space_constraint(x, pltpu.HBM) for x in (probes, locations, knot_locs)
    ]
    return pl.pallas_call(
        functools.partial(prepare_kernel, blocks),
        out_shape=(
            jax.ShapeDtypeStruct((rows, points + 2 * LANES), jnp.float32),
            jax.ShapeDtypeStruct(knot_locs.shape, jnp.float32),
        ),
        in_specs=[HBM, HBM, HBM],
        out_specs=(VMEM, VMEM),
        scratch_shapes=[pltpu.VMEM(locations.shape, jnp.float32), pltpu.SemaphoreType.DMA((3,))],
        compiler_params=pltpu.CompilerParams(vmem_limit_bytes=LIMIT),
        name="prepare",
    )(probes, locations, knot_locs)


def corner_kernel(end, east_ref, west_ref, out_ref):
    rows, width = east_ref.shape
    points = width - 2 * LANES
    blocks = points // LANES

    out_ref[...] = jnp.zeros(out_ref.shape, jnp.float32)
    upper = lax.axis_index("knot") > 0
    for turn, ref in enumerate((east_ref, west_ref)):
        start = 2 * turn * LANES
        first = [ref[:, :LANES], *[ref[0:1, points + axis * LANES : points + (axis + 1) * LANES] for axis in range(2)]]
        last = [
            ref[:, points - LANES : points],
            *[ref[blocks - 1 : blocks, points + axis * LANES : points + (axis + 1) * LANES] for axis in range(2)],
        ]
        taken = {"first": first, "last": last, "inner": [jnp.where(upper, a, b) for a, b in zip(first, last)]}[end]
        out_ref[:, start : start + LANES] = taken[0]
        out_ref[0:1, start + LANES : start + 2 * LANES] = taken[1]
        out_ref[1:2, start + LANES : start + 2 * LANES] = taken[2]


def corner_blocks(end, strips):
    return pl.pallas_call(
        functools.partial(corner_kernel, end),
        out_shape=jax.ShapeDtypeStruct((strips[0].shape[0], 4 * LANES), jnp.float32),
        in_specs=[VMEM, VMEM],
        out_specs=VMEM,
        compiler_params=pltpu.CompilerParams(vmem_limit_bytes=LIMIT),
        name="corner",
    )(*strips)


def assemble_kernel(own_ref, below_ref, above_ref, east_ref, west_ref, low_ref, high_ref, values_ref, coords_ref):
    probes, width = own_ref.shape
    points = width - 2 * LANES
    blocks = points // LANES
    span = blocks + 2
    inverse = 1.0 / TAPER_LEN

    def put(place, vals, coords):
        count = vals.shape[1] // LANES
        values_ref[:, place * LANES : (place + count) * LANES] = stacked_halves(vals)
        for index in range(count):
            for axis in range(2):
                lanes = slice((place + index) * LANES, (place + index + 1) * LANES)
                coords_ref[axis : axis + 1, lanes] = coords[axis][index : index + 1] * inverse

    def put_stack(place, ref, first, count):
        lanes = [slice(points + axis * LANES, points + (axis + 1) * LANES) for axis in range(2)]
        put(
            place,
            ref[:, first * LANES : (first + count) * LANES],
            [ref[first : first + count, lanes[axis]] for axis in range(2)],
        )

    def put_corner(place, ref, turn):
        start = 2 * turn * LANES
        both = slice(start + LANES, start + 2 * LANES)
        put(place, ref[:, start : start + LANES], [ref[axis : axis + 1, both] for axis in range(2)])

    put_stack(0, below_ref, blocks - 1, 1)
    put_stack(1, own_ref, 0, blocks)
    put_stack(1 + blocks, above_ref, 0, 1)
    for turn, ref in enumerate((east_ref, west_ref)):
        place = (turn + 1) * span
        put_corner(place, low_ref, turn)
        put_stack(place + 1, ref, 0, blocks)
        put_corner(place + 1 + blocks, high_ref, turn)
    values_ref[:, 3 * points + 6 * LANES :] = jnp.zeros((2 * probes, LANES), jnp.bfloat16)


def assemble(own, below, above, strips, low, high):
    probes, width = own.shape
    near = 3 * (width - 2 * LANES + 2 * LANES)
    return pl.pallas_call(
        assemble_kernel,
        out_shape=(
            jax.ShapeDtypeStruct((2 * probes, near + LANES), jnp.bfloat16),
            jax.ShapeDtypeStruct((2, near), jnp.float32),
        ),
        in_specs=[VMEM] * 7,
        out_specs=(VMEM, VMEM),
        compiler_params=pltpu.CompilerParams(vmem_limit_bytes=LIMIT),
        name="assemble",
    )(own, below, above, *strips, low, high)


def project_kernel(scale, grain, stack_ref, knots_ref, out_ref, high_ref, low_ref, weights):
    points, knots = high_ref.shape
    probes = stack_ref.shape[0]
    tile = min(TILE, knots)
    wide = min(TILE, points)
    weights[...] = stacked_halves(stack_ref[:, :points])
    east, north = [
        (jnp.transpose(coordinate_rows(stack_ref, points, axis) * scale) + grain) - grain for axis in range(2)
    ]

    @pl.loop(0, knots // tile)
    def _(step):
        lanes = pl.ds(pl.multiple_of(step * tile, tile), tile)
        kx, ky = [
            (knots_ref[axis : axis + 1, lanes] * scale + grain) - (grain - grain * HALF_GRAIN) for axis in range(2)
        ]
        total = jnp.zeros((2 * probes, tile), jnp.float32)
        for start in range(0, points, wide):
            highs, lows = [], []
            for row in range(start, start + wide, LANES):
                block = row // LANES
                dx = east[:, block : block + 1] - kx
                dy = north[:, block : block + 1] - ky
                square = dx * dx + dy * dy
                high, low = halves(jnp.exp2(-(square * lax.rsqrt(square))))
                high_ref[row : row + LANES, lanes] = high
                low_ref[row : row + LANES, lanes] = low
                highs.append(high)
                lows.append(low)
            part = weights[:, start : start + wide]
            total = total + (
                dot_nn(part, jnp.concatenate(highs, axis=0)) + dot_nn(part, jnp.concatenate(lows, axis=0))
            )
        out_ref[:, lanes] = folded(total)


def project(stack, knot_locs, scale, extent):
    probes, points, knots = stack.shape[0], stack.shape[1] - 2 * LANES, knot_locs.shape[1]
    grain = 2.0 ** math.ceil(math.log2(1.01 * scale * extent))
    return pl.pallas_call(
        functools.partial(project_kernel, scale, grain),
        out_shape=(
            jax.ShapeDtypeStruct((probes, knots), jnp.float32),
            pltpu.VMEM((points, knots), jnp.bfloat16),
            pltpu.VMEM((points, knots), jnp.bfloat16),
        ),
        in_specs=[VMEM, VMEM],
        out_specs=(VMEM, VMEM, VMEM),
        scratch_shapes=[pltpu.VMEM((2 * probes, points), jnp.bfloat16)],
        compiler_params=pltpu.CompilerParams(vmem_limit_bytes=LIMIT),
        cost_estimate=cost(2800, points * knots, 2),
        name="project",
    )(stack, knot_locs)


def factor_kernel(scale, step, before_ref, proj_ref, precision_ref, *rest):
    out_ref, weights = rest[-2:]
    probes, depth = proj_ref.shape
    all_rows = precision_ref.shape[0]
    tile = min(TILE, all_rows)
    wide = min(TILE, depth)
    weights[...] = stacked_halves(proj_ref[...] * scale)
    owner = lax.rem(lax.axis_index("knot") + step, lax.axis_size("knot"))
    offset = owner * depth

    @pl.loop(0, all_rows // tile)
    def _(turn):
        rows = pl.ds(pl.multiple_of(turn * tile, tile), tile)
        total = jnp.zeros((weights.shape[0], tile), jnp.float32)
        for start in range(0, depth, wide):
            lanes = pl.ds(pl.multiple_of(offset + start, wide), wide)
            high, low = halves(precision_ref[rows, lanes])
            part = weights[:, start : start + wide]
            total = total + (dot_nt(part, high) + dot_nt(part, low))
        found = folded(total)
        if before_ref is not None:
            found = found + before_ref[:, rows]
        out_ref[:, rows] = found


def factored(before, projection, precision, scale, step, after=()):
    probes, depth = projection.shape
    rows = precision.shape[0]
    kernel = functools.partial(factor_kernel, scale, step)
    operands = (projection, precision, *after)
    if before is None:
        kernel = functools.partial(kernel, None)
    else:
        operands = (before, *operands)
    return pl.pallas_call(
        kernel,
        out_shape=jax.ShapeDtypeStruct((probes, rows), jnp.float32),
        in_specs=[VMEM] * (len(operands) - len(after)) + [pl.BlockSpec(memory_space=pl.ANY)] * len(after),
        out_specs=VMEM,
        scratch_shapes=[pltpu.VMEM((2 * probes, depth), jnp.bfloat16)],
        compiler_params=pltpu.CompilerParams(vmem_limit_bytes=LIMIT),
        cost_estimate=cost(1200, rows * depth),
        name="factor",
    )(*operands)


def spread_kernel(scale, factor_ref, high_ref, low_ref, out_ref, weights):
    probes = factor_ref.shape[0]
    points = high_ref.shape[0]
    tile = min(TILE, points)
    weights[...] = padded_halves(factor_ref[...] * scale, weights.shape[0])
    for start in range(0, points, tile):
        rows = slice(start, start + tile)
        total = dot_nt(high_ref[rows, :], weights[...]) + dot_nt(low_ref[rows, :], weights[...])
        out_ref[:, rows] = folded_columns(total, probes)


def spread(factor, high, low, scale):
    (probes, knots), points = factor.shape, high.shape[0]
    high = pltpu.with_memory_space_constraint(high, pltpu.VMEM)
    low = pltpu.with_memory_space_constraint(low, pltpu.VMEM)
    return pl.pallas_call(
        functools.partial(spread_kernel, scale),
        out_shape=jax.ShapeDtypeStruct((probes, points), jnp.float32),
        in_specs=[VMEM, VMEM, VMEM],
        out_specs=VMEM,
        scratch_shapes=[pltpu.VMEM((LANES, knots), jnp.bfloat16)],
        compiler_params=pltpu.CompilerParams(vmem_limit_bytes=LIMIT),
        cost_estimate=cost(850, knots * points),
        name="spread",
    )(factor, high, low)


def covariance(apart):
    scaled = jnp.minimum(apart, 1.0)
    remain = (1.0 - scaled) * (1.0 - scaled)
    return jnp.exp2(scaled * (-LOG2E * TAPER_LEN / COV_RANGE)) * (remain * remain) * (1.0 + 4.0 * scaled)


def taper_kernel(first, ids_ref, counts_ref, own_ref, values_ref, coords_ref, out_ref):
    own_blocks, slots = ids_ref.shape
    block = LANES
    probes = own_ref.shape[0]
    span = own_blocks + 2
    zeros_place = coords_ref.shape[1] // block
    column = lax.axis_index("space")
    north_base = lax.axis_index("knot") * own_blocks - 1
    north_cells = lax.axis_size("knot") * own_blocks
    own_columns = [
        jnp.transpose(coordinate_rows(own_ref, own_blocks * block, axis) * (1.0 / TAPER_LEN)) for axis in range(2)
    ]

    def place(group, slot):
        ahead = ids_ref[group, slot] - (column - 1) * north_cells
        east = jnp.where(ahead >= north_cells, 1, 0) + jnp.where(ahead >= 2 * north_cells, 1, 0)
        strip = jnp.where(east == 1, 0, 1 + lax.rem(column + lax.div(east, 2) + 1, 2))
        index = strip * span + (ahead - east * north_cells - north_base)
        return lanes_of(index), lanes_of(jnp.where(slot < counts_ref[group], index, zeros_place))

    def lanes_of(index):
        return pl.ds(pl.multiple_of(index * block, block), block)

    for index in range(out_ref.shape[1] // block):
        group = first + index
        px, py = [turned[:, group : group + 1] for turned in own_columns]
        total = jnp.zeros((block, 2 * probes), jnp.float32)
        for pair in range(0, slots, 2):
            highs, lows, parts = [], [], []
            for slot in range(pair, min(pair + 2, slots)):
                lanes, value_lanes = place(group, slot)
                high, low = halves(covariance(distance(px, py, coords_ref[0:1, lanes], coords_ref[1:2, lanes])))
                highs.append(high)
                lows.append(low)
                parts.append(values_ref[:, value_lanes])
            part = jnp.concatenate(parts, axis=1)
            total = total + (
                dot_nt(jnp.concatenate(highs, axis=1), part) + dot_nt(jnp.concatenate(lows, axis=1), part)
            )
        out_ref[:, index * block : (index + 1) * block] = (
            TAPER_SCALE * folded_columns(total, probes)
            + NUGGET * own_ref[:, group * block : (group + 1) * block]
        )


def taper(ids, counts, own, values, coords, first, blocks):
    slots = ids.shape[1]
    return pl.pallas_call(
        functools.partial(taper_kernel, first),
        out_shape=jax.ShapeDtypeStruct((own.shape[0], blocks * LANES), jnp.float32),
        in_specs=[SMEM, SMEM, VMEM, VMEM, VMEM],
        out_specs=VMEM,
        compiler_params=pltpu.CompilerParams(vmem_limit_bytes=LIMIT),
        cost_estimate=cost(6000, blocks * slots * LANES * LANES, 2),
        name="taper",
    )(ids, counts, own, values, coords)


def butterfly_sum(value, axis, other):
    count, groups = lax.axis_size(axis), lax.axis_size(other)
    if count & (count - 1):
        return lax.psum(value, axis)
    bits = [1 << i for i in range(count.bit_length() - 1)]
    rounds = [(low | high, high, low) for low, high in zip(bits[0::2], bits[1::2])]
    half = len(rounds) // 2
    for turn in range(len(rounds)):
        got = []
        for kind in range(3):
            pairs = []
            for j in range(groups):
                step = rounds[(turn + half * (j % 2)) % len(rounds)][kind]
                pairs += [(i * groups + j, (i ^ step) * groups + j) for i in range(count)]
            got.append(lax.ppermute(value, (axis, other), pairs))
        value = (value + got[2]) + (got[1] + got[0])
    if len(bits) % 2:
        value = value + lax.ppermute(value, axis, [(i, i ^ bits[-1]) for i in range(count)])
    return value


def shifted(value, axis, step):
    count = lax.axis_size(axis)
    if step % count == 0:
        return value
    return lax.ppermute(value, axis, [((i + step) % count, i) for i in range(count)])


def paired(value, axis, first):
    count = lax.axis_size(axis)
    pairs = [(i, i + 1) for i in range(first, count - 1, 2)]
    return lax.ppermute(value, axis, pairs + [(b, a) for a, b in pairs])


def shards(probes, locations, knot_locs, knot_precision, neighbours, counts):
    own_blocks = neighbours.shape[0]
    row_count = probes.shape[1]
    knot_total = knot_precision.shape[1]
    device_count = lax.axis_size(("space", "knot"))
    groups = lax.axis_size("knot")
    knot_range = KNOT_REACH * math.sqrt(own_blocks * device_count / knot_total)
    proj_scale = PROJ_GAIN * math.sqrt(knot_total / (row_count * device_count))

    stack, knots = prepare(probes, locations, knot_locs, own_blocks)
    chunks = [shifted(stack, "knot", step) for step in range(groups)]
    rate = LOG2E / knot_range
    extent = CELL * max(lax.axis_size("space"), groups * own_blocks)
    parts = [project(chunk, knots, rate, extent) for chunk in chunks]
    strips = [paired(stack, "space", 0), paired(stack, "space", 1)]
    if groups == 2:
        low = high = shifted(corner_blocks("inner", strips), "knot", 1)
    else:
        low = shifted(corner_blocks("last", strips), "knot", -1)
        high = shifted(corner_blocks("first", strips), "knot", 1)
    values, coords = assemble(stack, chunks[-1], chunks[1 % groups], strips, low, high)
    pieces = math.gcd(own_blocks, 4)
    per_piece = own_blocks // pieces
    base = [
        taper(neighbours, counts, stack, values, coords, i * per_piece, per_piece) for i in range(pieces)
    ]

    projection = butterfly_sum(sum(part[0] for part in parts), "space", "knot")
    factor = factored(None, projection, knot_precision, proj_scale, 0, base[:-1])
    for step in range(1, groups):
        factor = factored(factor, shifted(projection, "knot", step), knot_precision, proj_scale, step)
    total = jnp.concatenate(base, axis=1)
    for step in reversed(range(groups)):
        share = spread(factor, parts[step][1], parts[step][2], LOW_SCALE * EXPAND_GAIN)
        total = total + shifted(share, "knot", -step)
    return total


def solution(mesh):
    return jax.shard_map(
        shards,
        mesh=mesh,
        in_specs=(
            P(None, ("space", "knot")),
            P(None, ("space", "knot")),
            P(None, "knot"),
            P("knot", None),
            P(("space", "knot"), None),
            P(("space", "knot")),
        ),
        out_specs=P(None, ("space", "knot")),
        check_vma=False,
    )
```

```python
import functools
import math

import jax
import jax.numpy as jnp
from jax import lax
from jax.experimental import pallas as pl
from jax.experimental.pallas import tpu as pltpu
from jax.sharding import PartitionSpec as P

COV_RANGE = 0.05
TAPER_LEN = 0.15
KNOT_REACH = 0.15
TAPER_SCALE = 0.1
PROJ_GAIN = 0.5
EXPAND_GAIN = 0.5
LOW_SCALE = 0.5
NUGGET = 0.25
LOG2E = math.log2(math.e)
CELL = 0.1
TINY = 1e-30
TILE = 256
LANES = 128
HALF_GRAIN = 2.0**-24
LIMIT = 6 * 1024 * 1024
VMEM = pl.BlockSpec(memory_space=pltpu.VMEM)
HBM = pl.BlockSpec(memory_space=pltpu.HBM)
ANY = pl.BlockSpec(memory_space=pl.ANY)
SMEM = pl.BlockSpec(memory_space=pltpu.SMEM)


def halves(x):
    high = x.astype(jnp.bfloat16)
    return high, (x - high.astype(jnp.float32)).astype(jnp.bfloat16)


def stacked_halves(x):
    return jnp.concatenate(halves(x), axis=0)


def folded(x):
    rows = x.shape[0] // 2
    return x[:rows] + x[rows:]


def dot_nt(left, right):
    return lax.dot_general(
        left, right, (((1,), (1,)), ((), ())), preferred_element_type=jnp.float32
    )


def dot_nn(left, right):
    return jnp.dot(left, right, preferred_element_type=jnp.float32)


def distance(ax, ay, bx, by):
    dx = ax - bx
    dy = ay - by
    square = dx * dx + dy * dy
    return square * lax.rsqrt(jnp.maximum(square, TINY))


def padded_halves(x, rows):
    fill = jnp.zeros((rows - 2 * x.shape[0], x.shape[1]), jnp.bfloat16)
    return jnp.concatenate([*halves(x), fill], axis=0)


def folded_columns(x, rows):
    x = jnp.transpose(x)
    return x[:rows] + x[rows : 2 * rows]


def cost(work, pairs, transcendentals=0):
    return pl.CostEstimate(flops=work * pairs, bytes_accessed=4 * pairs, transcendentals=transcendentals * pairs)


def coordinate_rows(ref, points, axis):
    start = points + axis * LANES
    return ref[:, start : start + LANES]


def prepare_kernel(blocks, probes_ref, locations_ref, knots_ref, stack_ref, knots_out_ref, coords, sems):
    points = probes_ref.shape[1]
    block = points // blocks
    copies = [
        pltpu.make_async_copy(probes_ref, stack_ref.at[:, pl.ds(0, points)], sems.at[0]),
        pltpu.make_async_copy(locations_ref, coords, sems.at[1]),
        pltpu.make_async_copy(knots_ref, knots_out_ref, sems.at[2]),
    ]
    for copy in copies:
        copy.start()
    for copy in copies:
        copy.wait()
    stack_ref[:, points:] = jnp.zeros((stack_ref.shape[0], 2 * LANES), jnp.float32)
    for axis in range(2):
        lanes = slice(points + axis * LANES, points + (axis + 1) * LANES)
        for index in range(blocks):
            stack_ref[index : index + 1, lanes] = coords[axis : axis + 1, index * block : (index + 1) * block]


def prepare(probes, locations, knot_locs, blocks):
    rows, points = probes.shape
    assert points == blocks * LANES and blocks + 2 <= rows
    probes, locations, knot_locs = [
        pltpu.with_memory_space_constraint(x, pltpu.HBM) for x in (probes, locations, knot_locs)
    ]
    return pl.pallas_call(
        functools.partial(prepare_kernel, blocks),
        out_shape=(
            jax.ShapeDtypeStruct((rows, points + 2 * LANES), jnp.float32),
            jax.ShapeDtypeStruct(knot_locs.shape, jnp.float32),
        ),
        in_specs=[HBM, HBM, HBM],
        out_specs=(VMEM, VMEM),
        scratch_shapes=[pltpu.VMEM(locations.shape, jnp.float32), pltpu.SemaphoreType.DMA((3,))],
        compiler_params=pltpu.CompilerParams(vmem_limit_bytes=LIMIT),
        name="prepare",
    )(probes, locations, knot_locs)


def strip_kernel(below_ref, own_ref, above_ref, out_ref):
    rows, width = own_ref.shape
    points = width - 2 * LANES
    blocks = points // LANES
    out_ref[:, :LANES] = below_ref[:, points - LANES : points]
    out_ref[:, LANES : points + LANES] = own_ref[:, :points]
    out_ref[:, points + LANES : points + 2 * LANES] = above_ref[:, :LANES]
    for axis in range(2):
        lanes = slice(points + axis * LANES, points + (axis + 1) * LANES)
        target = slice(lanes.start + 2 * LANES, lanes.stop + 2 * LANES)
        out_ref[:, target] = jnp.zeros((rows, LANES), jnp.float32)
        out_ref[0:1, target] = below_ref[blocks - 1 : blocks, lanes]
        out_ref[1 : blocks + 1, target] = own_ref[:blocks, lanes]
        out_ref[blocks + 1 : blocks + 2, target] = above_ref[0:1, lanes]


def make_strip(below, own, above):
    return pl.pallas_call(
        strip_kernel,
        out_shape=jax.ShapeDtypeStruct((own.shape[0], own.shape[1] + 2 * LANES), jnp.float32),
        in_specs=[VMEM, VMEM, VMEM],
        out_specs=VMEM,
        compiler_params=pltpu.CompilerParams(vmem_limit_bytes=LIMIT),
        name="strip",
    )(below, own, above)


def assemble_kernel(own_ref, east_ref, west_ref, values_ref, coords_ref):
    probes, width = own_ref.shape
    points = width - 2 * LANES
    inverse = 1.0 / TAPER_LEN
    for turn, ref in enumerate((own_ref, east_ref, west_ref)):
        start = turn * points
        values_ref[:, start : start + points] = stacked_halves(ref[:, :points])
        for axis in range(2):
            rows = coordinate_rows(ref, points, axis) * inverse
            for index in range(points // LANES):
                lanes = slice(start + index * LANES, start + (index + 1) * LANES)
                coords_ref[axis : axis + 1, lanes] = rows[index : index + 1]
    values_ref[:, 3 * points :] = jnp.zeros((2 * probes, LANES), jnp.bfloat16)


def assemble(strips):
    probes, width = strips[0].shape
    near = 3 * (width - 2 * LANES)
    return pl.pallas_call(
        assemble_kernel,
        out_shape=(
            jax.ShapeDtypeStruct((2 * probes, near + LANES), jnp.bfloat16),
            jax.ShapeDtypeStruct((2, near), jnp.float32),
        ),
        in_specs=[VMEM] * 3,
        out_specs=(VMEM, VMEM),
        compiler_params=pltpu.CompilerParams(vmem_limit_bytes=LIMIT),
        name="assemble",
    )(*strips)


def project_kernel(scale, grain, stack_ref, knots_ref, out_ref, high_ref, low_ref, copy_ref, weights):
    points, knots = high_ref.shape
    probes = stack_ref.shape[0]
    tile = min(TILE, knots)
    wide = min(TILE, points)
    copy_ref[...] = stack_ref[...]
    weights[...] = stacked_halves(stack_ref[:, :points])
    east, north = [
        (jnp.transpose(coordinate_rows(stack_ref, points, axis) * scale) + grain) - grain for axis in range(2)
    ]

    @pl.loop(0, knots // tile)
    def _(step):
        lanes = pl.ds(pl.multiple_of(step * tile, tile), tile)
        kx, ky = [
            (knots_ref[axis : axis + 1, lanes] * scale + grain) - (grain - grain * HALF_GRAIN) for axis in range(2)
        ]
        total = jnp.zeros((2 * probes, tile), jnp.float32)
        for start in range(0, points, wide):
            highs, lows = [], []
            for row in range(start, start + wide, LANES):
                block = row // LANES
                dx = east[:, block : block + 1] - kx
                dy = north[:, block : block + 1] - ky
                square = dx * dx + dy * dy
                high, low = halves(jnp.exp2(-(square * lax.rsqrt(square))))
                high_ref[row : row + LANES, lanes] = high
                low_ref[row : row + LANES, lanes] = low
                highs.append(high)
                lows.append(low)
            part = weights[:, start : start + wide]
            total = total + (
                dot_nn(part, jnp.concatenate(highs, axis=0)) + dot_nn(part, jnp.concatenate(lows, axis=0))
            )
        out_ref[:, lanes] = folded(total)


def project(stack, knot_locs, scale, extent):
    probes, points, knots = stack.shape[0], stack.shape[1] - 2 * LANES, knot_locs.shape[1]
    grain = 2.0 ** math.ceil(math.log2(1.01 * scale * extent))
    return pl.pallas_call(
        functools.partial(project_kernel, scale, grain),
        out_shape=(
            jax.ShapeDtypeStruct((probes, knots), jnp.float32),
            pltpu.VMEM((points, knots), jnp.bfloat16),
            pltpu.VMEM((points, knots), jnp.bfloat16),
            jax.ShapeDtypeStruct(stack.shape, jnp.float32),
        ),
        in_specs=[VMEM, VMEM],
        out_specs=(VMEM, VMEM, VMEM, VMEM),
        scratch_shapes=[pltpu.VMEM((2 * probes, points), jnp.bfloat16)],
        compiler_params=pltpu.CompilerParams(vmem_limit_bytes=LIMIT),
        cost_estimate=cost(2800, points * knots, 2),
        name="project",
    )(stack, knot_locs)


def split_kernel(first, precision_ref, *rest):
    high_ref, low_ref = rest[-2:]
    rows = high_ref.shape[0]
    tile = min(TILE, rows)
    for start in range(0, rows, tile):
        here = slice(start, start + tile)
        high_ref[here, :], low_ref[here, :] = halves(precision_ref[first + start : first + start + tile, :])


def split_rows(precision, first, rows, after):
    depth = precision.shape[1]
    return pl.pallas_call(
        functools.partial(split_kernel, first),
        out_shape=(pltpu.VMEM((rows, depth), jnp.bfloat16), pltpu.VMEM((rows, depth), jnp.bfloat16)),
        in_specs=[VMEM] + [ANY] * len(after),
        out_specs=(VMEM, VMEM),
        compiler_params=pltpu.CompilerParams(vmem_limit_bytes=LIMIT),
        cost_estimate=cost(60, rows * depth),
        name="split",
    )(precision, *after)


def factor_kernel(scale, step, parts, before_ref, proj_ref, *rest):
    highs, lows, (out_ref, weights) = rest[:parts], rest[parts : 2 * parts], rest[-2:]
    probes, depth = proj_ref.shape
    weights[...] = stacked_halves(proj_ref[...] * scale)
    owner = lax.rem(lax.axis_index("knot") + step, lax.axis_size("knot"))
    lanes = pl.ds(pl.multiple_of(owner * depth, depth), depth)
    rows = highs[0].shape[0]
    tile = min(TILE, rows)
    for part, (high_ref, low_ref) in enumerate(zip(highs, lows)):
        for start in range(0, rows, tile):
            here = slice(start, start + tile)
            found = folded(dot_nt(weights[...], high_ref[here, lanes]) + dot_nt(weights[...], low_ref[here, lanes]))
            target = slice(part * rows + start, part * rows + start + tile)
            if before_ref is not None:
                found = found + before_ref[:, target]
            out_ref[:, target] = found


def factored(before, projection, splits, scale, step):
    probes, depth = projection.shape
    highs, lows = [
        [pltpu.with_memory_space_constraint(split[half], pltpu.VMEM) for split in splits] for half in range(2)
    ]
    rows = sum(high.shape[0] for high in highs)
    kernel = functools.partial(factor_kernel, scale, step, len(splits))
    operands = (projection, *highs, *lows)
    if before is None:
        kernel = functools.partial(kernel, None)
    else:
        operands = (before, *operands)
    return pl.pallas_call(
        kernel,
        out_shape=jax.ShapeDtypeStruct((probes, rows), jnp.float32),
        in_specs=[VMEM] * len(operands),
        out_specs=VMEM,
        scratch_shapes=[pltpu.VMEM((2 * probes, depth), jnp.bfloat16)],
        compiler_params=pltpu.CompilerParams(vmem_limit_bytes=LIMIT),
        cost_estimate=cost(1000, rows * depth),
        name="factor",
    )(*operands)


def spread_kernel(scale, factor_ref, high_ref, low_ref, out_ref, weights):
    probes = factor_ref.shape[0]
    points = high_ref.shape[0]
    tile = min(TILE, points)
    weights[...] = padded_halves(factor_ref[...] * scale, weights.shape[0])
    for start in range(0, points, tile):
        rows = slice(start, start + tile)
        total = dot_nt(high_ref[rows, :], weights[...]) + dot_nt(low_ref[rows, :], weights[...])
        out_ref[:, rows] = folded_columns(total, probes)


def spread(factor, high, low, scale):
    (probes, knots), points = factor.shape, high.shape[0]
    high = pltpu.with_memory_space_constraint(high, pltpu.VMEM)
    low = pltpu.with_memory_space_constraint(low, pltpu.VMEM)
    return pl.pallas_call(
        functools.partial(spread_kernel, scale),
        out_shape=jax.ShapeDtypeStruct((probes, points), jnp.float32),
        in_specs=[VMEM, VMEM, VMEM],
        out_specs=VMEM,
        scratch_shapes=[pltpu.VMEM((LANES, knots), jnp.bfloat16)],
        compiler_params=pltpu.CompilerParams(vmem_limit_bytes=LIMIT),
        cost_estimate=cost(850, knots * points),
        name="spread",
    )(factor, high, low)


def covariance(apart):
    scaled = jnp.minimum(apart, 1.0)
    remain = (1.0 - scaled) * (1.0 - scaled)
    return jnp.exp2(scaled * (-LOG2E * TAPER_LEN / COV_RANGE)) * (remain * remain) * (1.0 + 4.0 * scaled)


def taper_kernel(first, ids_ref, counts_ref, own_ref, values_ref, coords_ref, *rest):
    out_ref = rest[-1]
    own_blocks, slots = ids_ref.shape
    block = LANES
    probes = own_ref.shape[0]
    span = own_blocks + 2
    zeros_place = coords_ref.shape[1] // block
    column = lax.axis_index("space")
    north_base = lax.axis_index("knot") * own_blocks - 1
    north_cells = lax.axis_size("knot") * own_blocks
    own_columns = [
        jnp.transpose(coordinate_rows(own_ref, own_blocks * block, axis) * (1.0 / TAPER_LEN)) for axis in range(2)
    ]

    def place(group, slot):
        ahead = ids_ref[group, slot] - (column - 1) * north_cells
        east = jnp.where(ahead >= north_cells, 1, 0) + jnp.where(ahead >= 2 * north_cells, 1, 0)
        strip = jnp.where(east == 1, 0, 1 + lax.rem(column + lax.div(east, 2) + 1, 2))
        index = strip * span + (ahead - east * north_cells - north_base)
        return lanes_of(index), lanes_of(jnp.where(slot < counts_ref[group], index, zeros_place))

    def lanes_of(index):
        return pl.ds(pl.multiple_of(index * block, block), block)

    for index in range(out_ref.shape[1] // block):
        group = first + index
        px, py = [turned[:, group : group + 1] for turned in own_columns]
        total = jnp.zeros((block, 2 * probes), jnp.float32)
        for pair in range(0, slots, 2):
            highs, lows, parts = [], [], []
            for slot in range(pair, min(pair + 2, slots)):
                lanes, value_lanes = place(group, slot)
                high, low = halves(covariance(distance(px, py, coords_ref[0:1, lanes], coords_ref[1:2, lanes])))
                highs.append(high)
                lows.append(low)
                parts.append(values_ref[:, value_lanes])
            part = jnp.concatenate(parts, axis=1)
            total = total + (
                dot_nt(jnp.concatenate(highs, axis=1), part) + dot_nt(jnp.concatenate(lows, axis=1), part)
            )
        out_ref[:, index * block : (index + 1) * block] = (
            TAPER_SCALE * folded_columns(total, probes)
            + NUGGET * own_ref[:, group * block : (group + 1) * block]
        )


def taper(ids, counts, own, values, coords, first, blocks, after):
    slots = ids.shape[1]
    return pl.pallas_call(
        functools.partial(taper_kernel, first),
        out_shape=jax.ShapeDtypeStruct((own.shape[0], blocks * LANES), jnp.float32),
        in_specs=[SMEM, SMEM, VMEM, VMEM, VMEM] + [ANY] * len(after),
        out_specs=VMEM,
        compiler_params=pltpu.CompilerParams(vmem_limit_bytes=LIMIT),
        cost_estimate=cost(500, blocks * slots * LANES * LANES, 2),
        name="taper",
    )(ids, counts, own, values, coords, *after)


def add_kernel(count, *refs):
    total = refs[0][...]
    for ref in refs[1:count]:
        total = total + ref[...]
    refs[-1][...] = total


def add_all(values, after):
    return pl.pallas_call(
        functools.partial(add_kernel, len(values)),
        out_shape=jax.ShapeDtypeStruct(values[0].shape, jnp.float32),
        in_specs=[VMEM] * len(values) + [ANY] * len(after),
        out_specs=VMEM,
        compiler_params=pltpu.CompilerParams(vmem_limit_bytes=LIMIT),
        name="add",
    )(*values, *after)


def butterfly_rounds(count):
    assert count & (count - 1) == 0
    bits = [1 << i for i in range(count.bit_length() - 1)]
    rounds = [(low | high, high, low) for low, high in zip(bits[0::2], bits[1::2])]
    return rounds + [(bit,) for bit in bits[len(rounds) * 2 :]]


def butterfly_round(value, axis, other, turn):
    count, groups = lax.axis_size(axis), lax.axis_size(other)
    rounds = butterfly_rounds(count)
    half = len(rounds) // 2 if len({len(steps) for steps in rounds}) == 1 else 0
    got = []
    for kind in range(len(rounds[turn])):
        pairs = []
        for j in range(groups):
            step = rounds[(turn + half * (j % 2)) % len(rounds)][kind]
            pairs += [(i * groups + j, (i ^ step) * groups + j) for i in range(count)]
        got.append(lax.ppermute(value, (axis, other), pairs))
    return got


def shifted(value, axis, step):
    count = lax.axis_size(axis)
    if step % count == 0:
        return value
    return lax.ppermute(value, axis, [((i + step) % count, i) for i in range(count)])


def paired(value, axis, first):
    count = lax.axis_size(axis)
    pairs = [(i, i + 1) for i in range(first, count - 1, 2)]
    return lax.ppermute(value, axis, pairs + [(b, a) for a, b in pairs])


def shards(probes, locations, knot_locs, knot_precision, neighbours, counts):
    own_blocks = neighbours.shape[0]
    row_count = probes.shape[1]
    knot_total = knot_precision.shape[1]
    device_count = lax.axis_size(("space", "knot"))
    groups = lax.axis_size("knot")
    knot_range = KNOT_REACH * math.sqrt(own_blocks * device_count / knot_total)
    proj_scale = PROJ_GAIN * math.sqrt(knot_total / (row_count * device_count))

    stack, knots = prepare(probes, locations, knot_locs, own_blocks)
    chunks = [shifted(stack, "knot", step) for step in range(groups)]
    rate = LOG2E / knot_range
    extent = CELL * max(lax.axis_size("space"), groups * own_blocks)
    parts = [project(chunk, knots, rate, extent) for chunk in chunks]
    stack = parts[0][3]

    strip = make_strip(chunks[-1], stack, chunks[1 % groups])
    values, coords = assemble([strip, paired(strip, "space", 0), paired(strip, "space", 1)])
    projection = sum(part[0] for part in parts)
    rounds = len(butterfly_rounds(lax.axis_size("space")))
    pieces = math.gcd(own_blocks, 2 * rounds)
    per_piece = own_blocks // pieces
    row_pieces = math.gcd(knot_precision.shape[0] // LANES, rounds)
    per_split = knot_precision.shape[0] // row_pieces
    base, splits = [], []
    for turn in range(rounds):
        got = butterfly_round(projection, "space", "knot", turn)
        beside = []
        for i in range(pieces):
            if i * rounds // pieces == turn:
                base.append(
                    taper(neighbours, counts, stack, values, coords, i * per_piece, per_piece, [projection])
                )
                beside.append(base[-1])
        for i in range(row_pieces):
            if i * rounds // row_pieces == turn:
                splits.append(split_rows(knot_precision, i * per_split, per_split, [projection]))
                beside.extend(splits[-1])
        projection = add_all([projection, *got], beside)
    factor = factored(None, projection, splits, proj_scale, 0)
    for step in range(1, groups):
        factor = factored(factor, shifted(projection, "knot", step), splits, proj_scale, step)
    total = jnp.concatenate(base, axis=1)
    for step in reversed(range(groups)):
        share = spread(factor, parts[step][1], parts[step][2], LOW_SCALE * EXPAND_GAIN)
        total = total + shifted(share, "knot", -step)
    return total


def solution(mesh):
    return jax.shard_map(
        shards,
        mesh=mesh,
        in_specs=(
            P(None, ("space", "knot")),
            P(None, ("space", "knot")),
            P(None, "knot"),
            P("knot", None),
            P(("space", "knot"), None),
            P(("space", "knot")),
        ),
        out_specs=P(None, ("space", "knot")),
        check_vma=False,
    )
```

```python
import functools
import math

import jax
import jax.numpy as jnp
from jax import lax
from jax.experimental import pallas as pl
from jax.experimental.pallas import tpu as pltpu
from jax.sharding import PartitionSpec as P

COV_RANGE = 0.05
TAPER_LEN = 0.15
KNOT_REACH = 0.15
TAPER_SCALE = 0.1
PROJ_GAIN = 0.5
EXPAND_GAIN = 0.5
LOW_SCALE = 0.5
NUGGET = 0.25
LOG2E = math.log2(math.e)
TAPER_RATE = LOG2E / COV_RANGE
CELL = 0.1
TILE = 256
LANES = 128
HALF_GRAIN = 2.0**-24
LIMIT = 6 * 1024 * 1024
VMEM = pl.BlockSpec(memory_space=pltpu.VMEM)
HBM = pl.BlockSpec(memory_space=pltpu.HBM)
ANY = pl.BlockSpec(memory_space=pl.ANY)
SMEM = pl.BlockSpec(memory_space=pltpu.SMEM)


def halves(x):
    high = x.astype(jnp.bfloat16)
    return high, (x - high.astype(jnp.float32)).astype(jnp.bfloat16)


def stacked_halves(x):
    return jnp.concatenate(halves(x), axis=0)


def folded(x):
    rows = x.shape[0] // 2
    return x[:rows] + x[rows:]


def dot_nt(left, right):
    return lax.dot_general(
        left, right, (((1,), (1,)), ((), ())), preferred_element_type=jnp.float32
    )


def dot_nn(left, right):
    return jnp.dot(left, right, preferred_element_type=jnp.float32)


def padded_halves(x, rows):
    fill = jnp.zeros((rows - 2 * x.shape[0], x.shape[1]), jnp.bfloat16)
    return jnp.concatenate([*halves(x), fill], axis=0)


def folded_columns(x, rows):
    x = jnp.transpose(x)
    return x[:rows] + x[rows : 2 * rows]


def cost(work, pairs, transcendentals=0):
    return pl.CostEstimate(flops=work * pairs, bytes_accessed=4 * pairs, transcendentals=transcendentals * pairs)


def coordinate_rows(ref, points, axis):
    start = points + axis * LANES
    return ref[:, start : start + LANES]


def prepare_kernel(blocks, probes_ref, locations_ref, knots_ref, stack_ref, knots_out_ref, coords, sems):
    points = probes_ref.shape[1]
    block = points // blocks
    copies = [
        pltpu.make_async_copy(probes_ref, stack_ref.at[:, pl.ds(0, points)], sems.at[0]),
        pltpu.make_async_copy(locations_ref, coords, sems.at[1]),
        pltpu.make_async_copy(knots_ref, knots_out_ref, sems.at[2]),
    ]
    for copy in copies:
        copy.start()
    for copy in copies:
        copy.wait()
    stack_ref[:, points:] = jnp.zeros((stack_ref.shape[0], 2 * LANES), jnp.float32)
    for axis in range(2):
        lanes = slice(points + axis * LANES, points + (axis + 1) * LANES)
        for index in range(blocks):
            stack_ref[index : index + 1, lanes] = coords[axis : axis + 1, index * block : (index + 1) * block]


def prepare(probes, locations, knot_locs, blocks):
    rows, points = probes.shape
    assert points == blocks * LANES and blocks + 2 <= rows
    probes, locations, knot_locs = [
        pltpu.with_memory_space_constraint(x, pltpu.HBM) for x in (probes, locations, knot_locs)
    ]
    return pl.pallas_call(
        functools.partial(prepare_kernel, blocks),
        out_shape=(
            jax.ShapeDtypeStruct((rows, points + 2 * LANES), jnp.float32),
            jax.ShapeDtypeStruct(knot_locs.shape, jnp.float32),
        ),
        in_specs=[HBM, HBM, HBM],
        out_specs=(VMEM, VMEM),
        scratch_shapes=[pltpu.VMEM(locations.shape, jnp.float32), pltpu.SemaphoreType.DMA((3,))],
        compiler_params=pltpu.CompilerParams(vmem_limit_bytes=LIMIT),
        name="prepare",
    )(probes, locations, knot_locs)


def strip_kernel(below_ref, own_ref, above_ref, out_ref):
    rows, width = own_ref.shape
    points = width - 2 * LANES
    blocks = points // LANES
    out_ref[:, :LANES] = below_ref[:, points - LANES : points]
    out_ref[:, LANES : points + LANES] = own_ref[:, :points]
    out_ref[:, points + LANES : points + 2 * LANES] = above_ref[:, :LANES]
    for axis in range(2):
        lanes = slice(points + axis * LANES, points + (axis + 1) * LANES)
        target = slice(lanes.start + 2 * LANES, lanes.stop + 2 * LANES)
        out_ref[:, target] = jnp.zeros((rows, LANES), jnp.float32)
        out_ref[0:1, target] = below_ref[blocks - 1 : blocks, lanes]
        out_ref[1 : blocks + 1, target] = own_ref[:blocks, lanes]
        out_ref[blocks + 1 : blocks + 2, target] = above_ref[0:1, lanes]


def make_strip(below, own, above):
    return pl.pallas_call(
        strip_kernel,
        out_shape=jax.ShapeDtypeStruct((own.shape[0], own.shape[1] + 2 * LANES), jnp.float32),
        in_specs=[VMEM, VMEM, VMEM],
        out_specs=VMEM,
        compiler_params=pltpu.CompilerParams(vmem_limit_bytes=LIMIT),
        name="strip",
    )(below, own, above)


def assemble_kernel(grain, own_ref, east_ref, west_ref, values_ref, coords_ref):
    probes, width = own_ref.shape
    points = width - 2 * LANES
    for turn, ref in enumerate((own_ref, east_ref, west_ref)):
        start = turn * points
        values_ref[:, start : start + points] = stacked_halves(ref[:, :points] * (1.0 / 256.0))
        for axis in range(2):
            rows = off_grid(coordinate_rows(ref, points, axis) * TAPER_RATE, grain)
            for index in range(points // LANES):
                lanes = slice(start + index * LANES, start + (index + 1) * LANES)
                coords_ref[axis : axis + 1, lanes] = rows[index : index + 1]
    values_ref[:, 3 * points :] = jnp.zeros((2 * probes, LANES), jnp.bfloat16)


def assemble(strips, extent):
    probes, width = strips[0].shape
    near = 3 * (width - 2 * LANES)
    return pl.pallas_call(
        functools.partial(assemble_kernel, grain_of(TAPER_RATE * extent)),
        out_shape=(
            jax.ShapeDtypeStruct((2 * probes, near + LANES), jnp.bfloat16),
            jax.ShapeDtypeStruct((2, near), jnp.float32),
        ),
        in_specs=[VMEM] * 3,
        out_specs=(VMEM, VMEM),
        compiler_params=pltpu.CompilerParams(vmem_limit_bytes=LIMIT),
        name="assemble",
    )(*strips)


def grain_of(bound):
    return 2.0 ** math.ceil(math.log2(1.01 * bound))


def on_grid(x, grain):
    return (x + grain) - grain


def off_grid(x, grain):
    return (x + grain) - (grain - grain * HALF_GRAIN)


def project_kernel(scale, grain, stack_ref, knots_ref, out_ref, high_ref, low_ref, copy_ref, weights):
    points, knots = high_ref.shape
    probes = stack_ref.shape[0]
    tile = min(TILE, knots)
    wide = min(TILE, points)
    copy_ref[...] = stack_ref[...]
    weights[...] = stacked_halves(stack_ref[:, :points])
    east, north = [
        on_grid(jnp.transpose(coordinate_rows(stack_ref, points, axis) * scale), grain) for axis in range(2)
    ]

    @pl.loop(0, knots // tile)
    def _(step):
        lanes = pl.ds(pl.multiple_of(step * tile, tile), tile)
        kx, ky = [off_grid(knots_ref[axis : axis + 1, lanes] * scale, grain) for axis in range(2)]
        total = jnp.zeros((2 * probes, tile), jnp.float32)
        for start in range(0, points, wide):
            highs, lows = [], []
            for row in range(start, start + wide, LANES):
                block = row // LANES
                dx = east[:, block : block + 1] - kx
                dy = north[:, block : block + 1] - ky
                square = dx * dx + dy * dy
                high, low = halves(jnp.exp2(-(square * lax.rsqrt(square))))
                high_ref[row : row + LANES, lanes] = high
                low_ref[row : row + LANES, lanes] = low
                highs.append(high)
                lows.append(low)
            part = weights[:, start : start + wide]
            total = total + (
                dot_nn(part, jnp.concatenate(highs, axis=0)) + dot_nn(part, jnp.concatenate(lows, axis=0))
            )
        out_ref[:, lanes] = folded(total)


def project(stack, knot_locs, scale, extent):
    probes, points, knots = stack.shape[0], stack.shape[1] - 2 * LANES, knot_locs.shape[1]
    return pl.pallas_call(
        functools.partial(project_kernel, scale, grain_of(scale * extent)),
        out_shape=(
            jax.ShapeDtypeStruct((probes, knots), jnp.float32),
            pltpu.VMEM((points, knots), jnp.bfloat16),
            pltpu.VMEM((points, knots), jnp.bfloat16),
            jax.ShapeDtypeStruct(stack.shape, jnp.float32),
        ),
        in_specs=[VMEM, VMEM],
        out_specs=(VMEM, VMEM, VMEM, VMEM),
        scratch_shapes=[pltpu.VMEM((2 * probes, points), jnp.bfloat16)],
        compiler_params=pltpu.CompilerParams(vmem_limit_bytes=LIMIT),
        cost_estimate=cost(2800, points * knots, 2),
        name="project",
    )(stack, knot_locs)


def split_kernel(first, precision_ref, *rest):
    high_ref, low_ref = rest[-2:]
    rows = high_ref.shape[0]
    tile = min(TILE, rows)
    for start in range(0, rows, tile):
        here = slice(start, start + tile)
        high_ref[here, :], low_ref[here, :] = halves(precision_ref[first + start : first + start + tile, :])


def split_rows(precision, first, rows, after):
    depth = precision.shape[1]
    return pl.pallas_call(
        functools.partial(split_kernel, first),
        out_shape=(pltpu.VMEM((rows, depth), jnp.bfloat16), pltpu.VMEM((rows, depth), jnp.bfloat16)),
        in_specs=[VMEM] + [ANY] * len(after),
        out_specs=(VMEM, VMEM),
        compiler_params=pltpu.CompilerParams(vmem_limit_bytes=LIMIT),
        cost_estimate=cost(60, rows * depth),
        name="split",
    )(precision, *after)


def factor_kernel(scale, step, parts, before_ref, proj_ref, *rest):
    highs, lows, (out_ref, weights) = rest[:parts], rest[parts : 2 * parts], rest[-2:]
    probes, depth = proj_ref.shape
    weights[...] = stacked_halves(proj_ref[...] * scale)
    owner = lax.rem(lax.axis_index("knot") + step, lax.axis_size("knot"))
    lanes = pl.ds(pl.multiple_of(owner * depth, depth), depth)
    rows = highs[0].shape[0]
    tile = min(TILE, rows)
    for part, (high_ref, low_ref) in enumerate(zip(highs, lows)):
        for start in range(0, rows, tile):
            here = slice(start, start + tile)
            found = folded(dot_nt(weights[...], high_ref[here, lanes]) + dot_nt(weights[...], low_ref[here, lanes]))
            target = slice(part * rows + start, part * rows + start + tile)
            if before_ref is not None:
                found = found + before_ref[:, target]
            out_ref[:, target] = found


def factored(before, projection, splits, scale, step):
    probes, depth = projection.shape
    highs, lows = [
        [pltpu.with_memory_space_constraint(split[half], pltpu.VMEM) for split in splits] for half in range(2)
    ]
    rows = sum(high.shape[0] for high in highs)
    kernel = functools.partial(factor_kernel, scale, step, len(splits))
    operands = (projection, *highs, *lows)
    if before is None:
        kernel = functools.partial(kernel, None)
    else:
        operands = (before, *operands)
    return pl.pallas_call(
        kernel,
        out_shape=jax.ShapeDtypeStruct((probes, rows), jnp.float32),
        in_specs=[VMEM] * len(operands),
        out_specs=VMEM,
        scratch_shapes=[pltpu.VMEM((2 * probes, depth), jnp.bfloat16)],
        compiler_params=pltpu.CompilerParams(vmem_limit_bytes=LIMIT),
        cost_estimate=cost(1000, rows * depth),
        name="factor",
    )(*operands)


def spread_kernel(scale, factor_ref, high_ref, low_ref, out_ref, weights):
    probes = factor_ref.shape[0]
    points = high_ref.shape[0]
    tile = min(TILE, points)
    weights[...] = padded_halves(factor_ref[...] * scale, weights.shape[0])
    for start in range(0, points, tile):
        rows = slice(start, start + tile)
        total = dot_nt(high_ref[rows, :], weights[...]) + dot_nt(low_ref[rows, :], weights[...])
        out_ref[:, rows] = folded_columns(total, probes)


def spread(factor, high, low, scale):
    (probes, knots), points = factor.shape, high.shape[0]
    high = pltpu.with_memory_space_constraint(high, pltpu.VMEM)
    low = pltpu.with_memory_space_constraint(low, pltpu.VMEM)
    return pl.pallas_call(
        functools.partial(spread_kernel, scale),
        out_shape=jax.ShapeDtypeStruct((probes, points), jnp.float32),
        in_specs=[VMEM, VMEM, VMEM],
        out_specs=VMEM,
        scratch_shapes=[pltpu.VMEM((LANES, knots), jnp.bfloat16)],
        compiler_params=pltpu.CompilerParams(vmem_limit_bytes=LIMIT),
        cost_estimate=cost(850, knots * points),
        name="spread",
    )(factor, high, low)


def covariance(square):
    apart = square * lax.rsqrt(square)
    remain = jnp.maximum(4.0 - apart * (4.0 / (TAPER_LEN * TAPER_RATE)), 0.0)
    twice = remain * remain
    return (jnp.exp2(-apart) * (twice * twice)) * (5.0 - remain)


def taper_kernel(first, grain, ids_ref, counts_ref, own_ref, values_ref, coords_ref, *rest):
    out_ref = rest[-1]
    own_blocks, slots = ids_ref.shape
    block = LANES
    probes = own_ref.shape[0]
    span = own_blocks + 2
    zeros_place = coords_ref.shape[1] // block
    column = lax.axis_index("space")
    north_base = lax.axis_index("knot") * own_blocks - 1
    north_cells = lax.axis_size("knot") * own_blocks
    own_columns = [
        on_grid(jnp.transpose(coordinate_rows(own_ref, own_blocks * block, axis) * TAPER_RATE), grain)
        for axis in range(2)
    ]

    def place(group, slot):
        ahead = ids_ref[group, slot] - (column - 1) * north_cells
        east = jnp.where(ahead >= north_cells, 1, 0) + jnp.where(ahead >= 2 * north_cells, 1, 0)
        strip = jnp.where(east == 1, 0, 1 + lax.rem(column + lax.div(east, 2) + 1, 2))
        index = strip * span + (ahead - east * north_cells - north_base)
        return lanes_of(index), lanes_of(jnp.where(slot < counts_ref[group], index, zeros_place))

    def lanes_of(index):
        return pl.ds(pl.multiple_of(index * block, block), block)

    for index in range(out_ref.shape[1] // block):
        group = first + index
        px, py = [turned[:, group : group + 1] for turned in own_columns]
        total = jnp.zeros((block, 2 * probes), jnp.float32)
        for pair in range(0, slots, 2):
            highs, lows, parts = [], [], []
            for slot in range(pair, min(pair + 2, slots)):
                lanes, value_lanes = place(group, slot)
                dx = px - coords_ref[0:1, lanes]
                dy = py - coords_ref[1:2, lanes]
                high, low = halves(covariance(dx * dx + dy * dy))
                highs.append(high)
                lows.append(low)
                parts.append(values_ref[:, value_lanes])
            part = jnp.concatenate(parts, axis=1)
            total = total + (
                dot_nt(jnp.concatenate(highs, axis=1), part) + dot_nt(jnp.concatenate(lows, axis=1), part)
            )
        out_ref[:, index * block : (index + 1) * block] = (
            TAPER_SCALE * folded_columns(total, probes)
            + NUGGET * own_ref[:, group * block : (group + 1) * block]
        )


def taper(ids, counts, own, values, coords, extent, first, blocks, after):
    slots = ids.shape[1]
    return pl.pallas_call(
        functools.partial(taper_kernel, first, grain_of(TAPER_RATE * extent)),
        out_shape=jax.ShapeDtypeStruct((own.shape[0], blocks * LANES), jnp.float32),
        in_specs=[SMEM, SMEM, VMEM, VMEM, VMEM] + [ANY] * len(after),
        out_specs=VMEM,
        compiler_params=pltpu.CompilerParams(vmem_limit_bytes=LIMIT),
        cost_estimate=cost(500, blocks * slots * LANES * LANES, 2),
        name="taper",
    )(ids, counts, own, values, coords, *after)


def add_kernel(count, *refs):
    total = refs[0][...]
    for ref in refs[1:count]:
        total = total + ref[...]
    refs[-1][...] = total


def add_all(values, after):
    return pl.pallas_call(
        functools.partial(add_kernel, len(values)),
        out_shape=jax.ShapeDtypeStruct(values[0].shape, jnp.float32),
        in_specs=[VMEM] * len(values) + [ANY] * len(after),
        out_specs=VMEM,
        compiler_params=pltpu.CompilerParams(vmem_limit_bytes=LIMIT),
        name="add",
    )(*values, *after)


def butterfly_rounds(count):
    assert count & (count - 1) == 0
    bits = [1 << i for i in range(count.bit_length() - 1)]
    rounds = [(low | high, high, low) for low, high in zip(bits[0::2], bits[1::2])]
    return rounds + [(bit,) for bit in bits[len(rounds) * 2 :]]


def butterfly_round(value, axis, other, turn):
    count, groups = lax.axis_size(axis), lax.axis_size(other)
    rounds = butterfly_rounds(count)
    half = len(rounds) // 2 if len({len(steps) for steps in rounds}) == 1 else 0
    got = []
    for kind in range(len(rounds[turn])):
        pairs = []
        for j in range(groups):
            step = rounds[(turn + half * (j % 2)) % len(rounds)][kind]
            pairs += [(i * groups + j, (i ^ step) * groups + j) for i in range(count)]
        got.append(lax.ppermute(value, (axis, other), pairs))
    return got


def shifted(value, axis, step):
    count = lax.axis_size(axis)
    if step % count == 0:
        return value
    return lax.ppermute(value, axis, [((i + step) % count, i) for i in range(count)])


def paired(value, axis, first):
    count = lax.axis_size(axis)
    pairs = [(i, i + 1) for i in range(first, count - 1, 2)]
    pairs += [(b, a) for a, b in pairs]
    taken = {a for a, b in pairs}
    return lax.ppermute(value, axis, pairs + [(i, i) for i in range(count) if i not in taken])


def shards(probes, locations, knot_locs, knot_precision, neighbours, counts):
    own_blocks = neighbours.shape[0]
    row_count = probes.shape[1]
    knot_total = knot_precision.shape[1]
    device_count = lax.axis_size(("space", "knot"))
    groups = lax.axis_size("knot")
    knot_range = KNOT_REACH * math.sqrt(own_blocks * device_count / knot_total)
    proj_scale = PROJ_GAIN * math.sqrt(knot_total / (row_count * device_count))

    stack, knots = prepare(probes, locations, knot_locs, own_blocks)
    chunks = [shifted(stack, "knot", step) for step in range(groups)]
    rate = LOG2E / knot_range
    extent = CELL * max(lax.axis_size("space"), groups * own_blocks)
    parts = [project(chunk, knots, rate, extent) for chunk in chunks]
    stack = parts[0][3]

    strip = make_strip(chunks[-1], stack, chunks[1 % groups])
    values, coords = assemble([strip, paired(strip, "space", 0), paired(strip, "space", 1)], extent)
    projection = sum(part[0] for part in parts)
    rounds = len(butterfly_rounds(lax.axis_size("space")))
    pieces = math.gcd(own_blocks, rounds)
    per_piece = own_blocks // pieces
    row_pieces = math.gcd(knot_precision.shape[0] // LANES, rounds)
    per_split = knot_precision.shape[0] // row_pieces
    base, splits = [], []
    for turn in range(rounds):
        got = butterfly_round(projection, "space", "knot", turn)
        beside = []
        for i in range(pieces):
            if i * rounds // pieces == turn:
                base.append(
                    taper(
                        neighbours, counts, stack, values, coords, extent, i * per_piece, per_piece, [projection]
                    )
                )
                beside.append(base[-1])
        for i in range(row_pieces):
            if i * rounds // row_pieces == turn:
                splits.append(split_rows(knot_precision, i * per_split, per_split, [projection]))
                beside.extend(splits[-1])
        projection = add_all([projection, *got], beside)
    factor = factored(None, projection, splits, proj_scale, 0)
    for step in range(1, groups):
        factor = factored(factor, shifted(projection, "knot", step), splits, proj_scale, step)
    total = jnp.concatenate(base, axis=1)
    for step in reversed(range(groups)):
        share = spread(factor, parts[step][1], parts[step][2], LOW_SCALE * EXPAND_GAIN)
        total = total + shifted(share, "knot", -step)
    return total


def solution(mesh):
    return jax.shard_map(
        shards,
        mesh=mesh,
        in_specs=(
            P(None, ("space", "knot")),
            P(None, ("space", "knot")),
            P(None, "knot"),
            P("knot", None),
            P(("space", "knot"), None),
            P(("space", "knot")),
        ),
        out_specs=P(None, ("space", "knot")),
        check_vma=False,
    )
```

```python
import functools
import math

import jax
import jax.numpy as jnp
from jax import lax
from jax.experimental import pallas as pl
from jax.experimental.pallas import tpu as pltpu
from jax.sharding import PartitionSpec as P

COV_RANGE = 0.05
TAPER_LEN = 0.15
KNOT_REACH = 0.15
TAPER_SCALE = 0.1
PROJ_GAIN = 0.5
EXPAND_GAIN = 0.5
LOW_SCALE = 0.5
NUGGET = 0.25
LOG2E = math.log2(math.e)
TAPER_RATE = LOG2E / COV_RANGE
CELL = 0.1
TILE = 256
LANES = 128
HALF_GRAIN = 2.0**-24
LIMIT = 6 * 1024 * 1024
VMEM = pl.BlockSpec(memory_space=pltpu.VMEM)
HBM = pl.BlockSpec(memory_space=pltpu.HBM)
ANY = pl.BlockSpec(memory_space=pl.ANY)
SMEM = pl.BlockSpec(memory_space=pltpu.SMEM)


def halves(x):
    high = x.astype(jnp.bfloat16)
    return high, (x - high.astype(jnp.float32)).astype(jnp.bfloat16)


def stacked_halves(x):
    return jnp.concatenate(halves(x), axis=0)


def folded(x):
    rows = x.shape[0] // 2
    return x[:rows] + x[rows:]


def dot_nt(left, right):
    return lax.dot_general(
        left, right, (((1,), (1,)), ((), ())), preferred_element_type=jnp.float32
    )


def dot_nn(left, right):
    return jnp.dot(left, right, preferred_element_type=jnp.float32)


def padded_halves(x, rows):
    fill = jnp.zeros((rows - 2 * x.shape[0], x.shape[1]), jnp.bfloat16)
    return jnp.concatenate([*halves(x), fill], axis=0)


def folded_columns(x, rows):
    x = jnp.transpose(x)
    return x[:rows] + x[rows : 2 * rows]


def cost(work, pairs, transcendentals=0):
    return pl.CostEstimate(flops=work * pairs, bytes_accessed=4 * pairs, transcendentals=transcendentals * pairs)


def coordinate_rows(ref, points, axis):
    start = points + axis * LANES
    return ref[:, start : start + LANES]


def prepare_kernel(blocks, probes_ref, locations_ref, knots_ref, stack_ref, knots_out_ref, coords, sems):
    points = probes_ref.shape[1]
    block = points // blocks
    copies = [
        pltpu.make_async_copy(probes_ref, stack_ref.at[:, pl.ds(0, points)], sems.at[0]),
        pltpu.make_async_copy(locations_ref, coords, sems.at[1]),
        pltpu.make_async_copy(knots_ref, knots_out_ref, sems.at[2]),
    ]
    for copy in copies:
        copy.start()
    for copy in copies:
        copy.wait()
    stack_ref[:, points:] = jnp.zeros((stack_ref.shape[0], 2 * LANES), jnp.float32)
    for axis in range(2):
        lanes = slice(points + axis * LANES, points + (axis + 1) * LANES)
        for index in range(blocks):
            stack_ref[index : index + 1, lanes] = coords[axis : axis + 1, index * block : (index + 1) * block]


def prepare(probes, locations, knot_locs, blocks):
    rows, points = probes.shape
    assert points == blocks * LANES and blocks + 2 <= rows
    probes, locations, knot_locs = [
        pltpu.with_memory_space_constraint(x, pltpu.HBM) for x in (probes, locations, knot_locs)
    ]
    return pl.pallas_call(
        functools.partial(prepare_kernel, blocks),
        out_shape=(
            jax.ShapeDtypeStruct((rows, points + 2 * LANES), jnp.float32),
            jax.ShapeDtypeStruct(knot_locs.shape, jnp.float32),
        ),
        in_specs=[HBM, HBM, HBM],
        out_specs=(VMEM, VMEM),
        scratch_shapes=[pltpu.VMEM(locations.shape, jnp.float32), pltpu.SemaphoreType.DMA((3,))],
        compiler_params=pltpu.CompilerParams(vmem_limit_bytes=LIMIT),
        name="prepare",
    )(probes, locations, knot_locs)


def strip_kernel(below_ref, own_ref, above_ref, out_ref):
    rows, width = own_ref.shape
    points = width - 2 * LANES
    blocks = points // LANES
    out_ref[:, :LANES] = below_ref[:, points - LANES : points]
    out_ref[:, LANES : points + LANES] = own_ref[:, :points]
    out_ref[:, points + LANES : points + 2 * LANES] = above_ref[:, :LANES]
    for axis in range(2):
        lanes = slice(points + axis * LANES, points + (axis + 1) * LANES)
        target = slice(lanes.start + 2 * LANES, lanes.stop + 2 * LANES)
        out_ref[:, target] = jnp.zeros((rows, LANES), jnp.float32)
        out_ref[0:1, target] = below_ref[blocks - 1 : blocks, lanes]
        out_ref[1 : blocks + 1, target] = own_ref[:blocks, lanes]
        out_ref[blocks + 1 : blocks + 2, target] = above_ref[0:1, lanes]


def make_strip(below, own, above):
    return pl.pallas_call(
        strip_kernel,
        out_shape=jax.ShapeDtypeStruct((own.shape[0], own.shape[1] + 2 * LANES), jnp.float32),
        in_specs=[VMEM, VMEM, VMEM],
        out_specs=VMEM,
        compiler_params=pltpu.CompilerParams(vmem_limit_bytes=LIMIT),
        name="strip",
    )(below, own, above)


def assemble_kernel(grain, own_ref, east_ref, west_ref, values_ref, coords_ref):
    probes, width = own_ref.shape
    points = width - 2 * LANES
    for turn, ref in enumerate((own_ref, east_ref, west_ref)):
        start = turn * points
        values_ref[:, start : start + points] = stacked_halves(ref[:, :points] * (1.0 / 256.0))
        for axis in range(2):
            rows = off_grid(coordinate_rows(ref, points, axis) * TAPER_RATE, grain)
            for index in range(points // LANES):
                lanes = slice(start + index * LANES, start + (index + 1) * LANES)
                coords_ref[axis : axis + 1, lanes] = rows[index : index + 1]
    values_ref[:, 3 * points :] = jnp.zeros((2 * probes, LANES), jnp.bfloat16)


def assemble(strips, extent):
    probes, width = strips[0].shape
    near = 3 * (width - 2 * LANES)
    return pl.pallas_call(
        functools.partial(assemble_kernel, grain_of(TAPER_RATE * extent)),
        out_shape=(
            jax.ShapeDtypeStruct((2 * probes, near + LANES), jnp.bfloat16),
            jax.ShapeDtypeStruct((2, near), jnp.float32),
        ),
        in_specs=[VMEM] * 3,
        out_specs=(VMEM, VMEM),
        compiler_params=pltpu.CompilerParams(vmem_limit_bytes=LIMIT),
        name="assemble",
    )(*strips)


def grain_of(bound):
    return 2.0 ** math.ceil(math.log2(1.01 * bound))


def on_grid(x, grain):
    return (x + grain) - grain


def off_grid(x, grain):
    return (x + grain) - (grain - grain * HALF_GRAIN)


def project_kernel(scale, grain, stack_ref, knots_ref, out_ref, high_ref, low_ref, copy_ref, weights):
    points, knots = high_ref.shape
    probes = stack_ref.shape[0]
    tile = min(TILE, knots)
    wide = min(TILE, points)
    copy_ref[...] = stack_ref[...]
    weights[...] = stacked_halves(stack_ref[:, :points])
    east, north = [
        on_grid(jnp.transpose(coordinate_rows(stack_ref, points, axis) * scale), grain) for axis in range(2)
    ]

    @pl.loop(0, knots // tile)
    def _(step):
        lanes = pl.ds(pl.multiple_of(step * tile, tile), tile)
        kx, ky = [off_grid(knots_ref[axis : axis + 1, lanes] * scale, grain) for axis in range(2)]
        total = jnp.zeros((2 * probes, tile), jnp.float32)
        for start in range(0, points, wide):
            highs, lows = [], []
            for row in range(start, start + wide, LANES):
                block = row // LANES
                dx = east[:, block : block + 1] - kx
                dy = north[:, block : block + 1] - ky
                square = dx * dx + dy * dy
                high, low = halves(jnp.exp2(-(square * lax.rsqrt(square))))
                high_ref[row : row + LANES, lanes] = high
                low_ref[row : row + LANES, lanes] = low
                highs.append(high)
                lows.append(low)
            part = weights[:, start : start + wide]
            total = total + (
                dot_nn(part, jnp.concatenate(highs, axis=0)) + dot_nn(part, jnp.concatenate(lows, axis=0))
            )
        out_ref[:, lanes] = folded(total)


def project(stack, knot_locs, scale, extent):
    probes, points, knots = stack.shape[0], stack.shape[1] - 2 * LANES, knot_locs.shape[1]
    return pl.pallas_call(
        functools.partial(project_kernel, scale, grain_of(scale * extent)),
        out_shape=(
            jax.ShapeDtypeStruct((probes, knots), jnp.float32),
            pltpu.VMEM((points, knots), jnp.bfloat16),
            pltpu.VMEM((points, knots), jnp.bfloat16),
            jax.ShapeDtypeStruct(stack.shape, jnp.float32),
        ),
        in_specs=[VMEM, VMEM],
        out_specs=(VMEM, VMEM, VMEM, VMEM),
        scratch_shapes=[pltpu.VMEM((2 * probes, points), jnp.bfloat16)],
        compiler_params=pltpu.CompilerParams(vmem_limit_bytes=LIMIT),
        cost_estimate=cost(2800, points * knots, 2),
        name="project",
    )(stack, knot_locs)


def split_kernel(first, precision_ref, *rest):
    high_ref, low_ref = rest[-2:]
    rows = high_ref.shape[0]
    tile = min(TILE, rows)
    for start in range(0, rows, tile):
        here = slice(start, start + tile)
        high_ref[here, :], low_ref[here, :] = halves(precision_ref[first + start : first + start + tile, :])


def split_rows(precision, first, rows, after):
    depth = precision.shape[1]
    return pl.pallas_call(
        functools.partial(split_kernel, first),
        out_shape=(pltpu.VMEM((rows, depth), jnp.bfloat16), pltpu.VMEM((rows, depth), jnp.bfloat16)),
        in_specs=[VMEM] + [ANY] * len(after),
        out_specs=(VMEM, VMEM),
        compiler_params=pltpu.CompilerParams(vmem_limit_bytes=LIMIT),
        cost_estimate=cost(60, rows * depth),
        name="split",
    )(precision, *after)


def factor_kernel(scale, step, parts, before_ref, proj_ref, *rest):
    highs, lows, (out_ref, weights) = rest[:parts], rest[parts : 2 * parts], rest[-2:]
    probes, depth = proj_ref.shape
    weights[...] = stacked_halves(proj_ref[...] * scale)
    owner = lax.rem(lax.axis_index("knot") + step, lax.axis_size("knot"))
    lanes = pl.ds(pl.multiple_of(owner * depth, depth), depth)
    rows = highs[0].shape[0]
    tile = min(TILE, rows)
    for part, (high_ref, low_ref) in enumerate(zip(highs, lows)):
        for start in range(0, rows, tile):
            here = slice(start, start + tile)
            found = folded(dot_nt(weights[...], high_ref[here, lanes]) + dot_nt(weights[...], low_ref[here, lanes]))
            target = slice(part * rows + start, part * rows + start + tile)
            if before_ref is not None:
                found = found + before_ref[:, target]
            out_ref[:, target] = found


def factored(before, projection, splits, scale, step):
    probes, depth = projection.shape
    highs, lows = [
        [pltpu.with_memory_space_constraint(split[half], pltpu.VMEM) for split in splits] for half in range(2)
    ]
    rows = sum(high.shape[0] for high in highs)
    kernel = functools.partial(factor_kernel, scale, step, len(splits))
    operands = (projection, *highs, *lows)
    if before is None:
        kernel = functools.partial(kernel, None)
    else:
        operands = (before, *operands)
    return pl.pallas_call(
        kernel,
        out_shape=jax.ShapeDtypeStruct((probes, rows), jnp.float32),
        in_specs=[VMEM] * len(operands),
        out_specs=VMEM,
        scratch_shapes=[pltpu.VMEM((2 * probes, depth), jnp.bfloat16)],
        compiler_params=pltpu.CompilerParams(vmem_limit_bytes=LIMIT),
        cost_estimate=cost(1000, rows * depth),
        name="factor",
    )(*operands)


def spread_kernel(scale, factor_ref, high_ref, low_ref, out_ref, weights):
    probes = factor_ref.shape[0]
    points = high_ref.shape[0]
    tile = min(TILE, points)
    weights[...] = padded_halves(factor_ref[...] * scale, weights.shape[0])
    for start in range(0, points, tile):
        rows = slice(start, start + tile)
        total = dot_nt(high_ref[rows, :], weights[...]) + dot_nt(low_ref[rows, :], weights[...])
        out_ref[:, rows] = folded_columns(total, probes)


def spread(factor, high, low, scale):
    (probes, knots), points = factor.shape, high.shape[0]
    high = pltpu.with_memory_space_constraint(high, pltpu.VMEM)
    low = pltpu.with_memory_space_constraint(low, pltpu.VMEM)
    return pl.pallas_call(
        functools.partial(spread_kernel, scale),
        out_shape=jax.ShapeDtypeStruct((probes, points), jnp.float32),
        in_specs=[VMEM, VMEM, VMEM],
        out_specs=VMEM,
        scratch_shapes=[pltpu.VMEM((LANES, knots), jnp.bfloat16)],
        compiler_params=pltpu.CompilerParams(vmem_limit_bytes=LIMIT),
        cost_estimate=cost(850, knots * points),
        name="spread",
    )(factor, high, low)


def covariance(square):
    apart = square * lax.rsqrt(square)
    remain = jnp.maximum(4.0 - apart * (4.0 / (TAPER_LEN * TAPER_RATE)), 0.0)
    twice = remain * remain
    return (jnp.exp2(-apart) * (twice * twice)) * (5.0 - remain)


def taper_kernel(first, grain, ids_ref, counts_ref, own_ref, values_ref, coords_ref, *rest):
    out_ref = rest[-1]
    own_blocks, slots = ids_ref.shape
    block = LANES
    probes = own_ref.shape[0]
    span = own_blocks + 2
    zeros_place = coords_ref.shape[1] // block
    column = lax.axis_index("space")
    north_base = lax.axis_index("knot") * own_blocks - 1
    north_cells = lax.axis_size("knot") * own_blocks
    own_columns = [
        on_grid(jnp.transpose(coordinate_rows(own_ref, own_blocks * block, axis) * TAPER_RATE), grain)
        for axis in range(2)
    ]

    def place(group, slot):
        ahead = ids_ref[group, slot] - (column - 1) * north_cells
        east = jnp.where(ahead >= north_cells, 1, 0) + jnp.where(ahead >= 2 * north_cells, 1, 0)
        strip = jnp.where(east == 1, 0, 1 + lax.rem(column + lax.div(east, 2) + 1, 2))
        index = strip * span + (ahead - east * north_cells - north_base)
        return lanes_of(index), lanes_of(jnp.where(slot < counts_ref[group], index, zeros_place))

    def lanes_of(index):
        return pl.ds(pl.multiple_of(index * block, block), block)

    for index in range(out_ref.shape[1] // block):
        group = first + index
        px, py = [turned[:, group : group + 1] for turned in own_columns]
        total = jnp.zeros((block, 2 * probes), jnp.float32)
        for pair in range(0, slots, 2):
            highs, lows, parts = [], [], []
            for slot in range(pair, min(pair + 2, slots)):
                lanes, value_lanes = place(group, slot)
                dx = px - coords_ref[0:1, lanes]
                dy = py - coords_ref[1:2, lanes]
                high, low = halves(covariance(dx * dx + dy * dy))
                highs.append(high)
                lows.append(low)
                parts.append(values_ref[:, value_lanes])
            part = jnp.concatenate(parts, axis=1)
            total = total + (
                dot_nt(jnp.concatenate(highs, axis=1), part) + dot_nt(jnp.concatenate(lows, axis=1), part)
            )
        out_ref[:, index * block : (index + 1) * block] = (
            TAPER_SCALE * folded_columns(total, probes)
            + NUGGET * own_ref[:, group * block : (group + 1) * block]
        )


def taper(ids, counts, own, values, coords, extent, first, blocks, after):
    slots = ids.shape[1]
    return pl.pallas_call(
        functools.partial(taper_kernel, first, grain_of(TAPER_RATE * extent)),
        out_shape=jax.ShapeDtypeStruct((own.shape[0], blocks * LANES), jnp.float32),
        in_specs=[SMEM, SMEM, VMEM, VMEM, VMEM] + [ANY] * len(after),
        out_specs=VMEM,
        compiler_params=pltpu.CompilerParams(vmem_limit_bytes=LIMIT),
        cost_estimate=cost(500, blocks * slots * LANES * LANES, 2),
        name="taper",
    )(ids, counts, own, values, coords, *after)


def add_kernel(count, *refs):
    total = refs[0][...]
    for ref in refs[1:count]:
        total = total + ref[...]
    refs[-1][...] = total


def add_all(values, after):
    return pl.pallas_call(
        functools.partial(add_kernel, len(values)),
        out_shape=jax.ShapeDtypeStruct(values[0].shape, jnp.float32),
        in_specs=[VMEM] * len(values) + [ANY] * len(after),
        out_specs=VMEM,
        compiler_params=pltpu.CompilerParams(vmem_limit_bytes=LIMIT),
        name="add",
    )(*values, *after)


def butterfly_rounds(count):
    assert count & (count - 1) == 0
    bits = [1 << i for i in range(count.bit_length() - 1)]
    rounds = [(low | high, high, low) for low, high in zip(bits[0::2], bits[1::2])]
    return rounds + [(bit,) for bit in bits[len(rounds) * 2 :]]


def butterfly_round(value, axis, other, turn):
    count, groups = lax.axis_size(axis), lax.axis_size(other)
    rounds = butterfly_rounds(count)
    half = len(rounds) // 2 if len({len(steps) for steps in rounds}) == 1 else 0
    got = []
    for kind in range(len(rounds[turn])):
        pairs = []
        for j in range(groups):
            step = rounds[(turn + half * (j % 2)) % len(rounds)][kind]
            pairs += [(i * groups + j, (i ^ step) * groups + j) for i in range(count)]
        got.append(lax.ppermute(value, (axis, other), pairs))
    return got


def shifted(value, axis, step):
    count = lax.axis_size(axis)
    if step % count == 0:
        return value
    return lax.ppermute(value, axis, [((i + step) % count, i) for i in range(count)])


def paired(value, axis, first):
    count = lax.axis_size(axis)
    pairs = [((first + i) % count, (first + i + 1) % count) for i in range(0, count - 1, 2)]
    return lax.ppermute(value, axis, pairs + [(b, a) for a, b in pairs])


def shards(probes, locations, knot_locs, knot_precision, neighbours, counts):
    own_blocks = neighbours.shape[0]
    row_count = probes.shape[1]
    knot_total = knot_precision.shape[1]
    device_count = lax.axis_size(("space", "knot"))
    groups = lax.axis_size("knot")
    knot_range = KNOT_REACH * math.sqrt(own_blocks * device_count / knot_total)
    proj_scale = PROJ_GAIN * math.sqrt(knot_total / (row_count * device_count))

    stack, knots = prepare(probes, locations, knot_locs, own_blocks)
    chunks = [shifted(stack, "knot", step) for step in range(groups)]
    rate = LOG2E / knot_range
    extent = CELL * max(lax.axis_size("space"), groups * own_blocks)
    parts = [project(chunk, knots, rate, extent) for chunk in chunks]
    stack = parts[0][3]

    strip = make_strip(chunks[-1], stack, chunks[1 % groups])
    values, coords = assemble([strip, paired(strip, "space", 0), paired(strip, "space", 1)], extent)
    projection = sum(part[0] for part in parts)
    rounds = len(butterfly_rounds(lax.axis_size("space")))
    pieces = math.gcd(own_blocks, rounds)
    per_piece = own_blocks // pieces
    row_pieces = math.gcd(knot_precision.shape[0] // LANES, rounds)
    per_split = knot_precision.shape[0] // row_pieces
    base, splits = [], []
    for turn in range(rounds):
        got = butterfly_round(projection, "space", "knot", turn)
        beside = []
        for i in range(pieces):
            if i * rounds // pieces == turn:
                base.append(
                    taper(
                        neighbours, counts, stack, values, coords, extent, i * per_piece, per_piece, [projection]
                    )
                )
                beside.append(base[-1])
        for i in range(row_pieces):
            if i * rounds // row_pieces == turn:
                splits.append(split_rows(knot_precision, i * per_split, per_split, [projection]))
                beside.extend(splits[-1])
        projection = add_all([projection, *got], beside)
    factor = factored(None, projection, splits, proj_scale, 0)
    for step in range(1, groups):
        factor = factored(factor, shifted(projection, "knot", step), splits, proj_scale, step)
    total = jnp.concatenate(base, axis=1)
    for step in reversed(range(groups)):
        share = spread(factor, parts[step][1], parts[step][2], LOW_SCALE * EXPAND_GAIN)
        total = total + shifted(share, "knot", -step)
    return total


def solution(mesh):
    return jax.shard_map(
        shards,
        mesh=mesh,
        in_specs=(
            P(None, ("space", "knot")),
            P(None, ("space", "knot")),
            P(None, "knot"),
            P("knot", None),
            P(("space", "knot"), None),
            P(("space", "knot")),
        ),
        out_specs=P(None, ("space", "knot")),
        check_vma=False,
    )
```

```python
import functools
import math

import jax
import jax.numpy as jnp
from jax import lax
from jax.experimental import pallas as pl
from jax.experimental.pallas import tpu as pltpu
from jax.sharding import PartitionSpec as P

COV_RANGE = 0.05
TAPER_LEN = 0.15
KNOT_REACH = 0.15
TAPER_SCALE = 0.1
PROJ_GAIN = 0.5
EXPAND_GAIN = 0.5
LOW_SCALE = 0.5
NUGGET = 0.25
LOG2E = math.log2(math.e)
TAPER_RATE = LOG2E / COV_RANGE
CELL = 0.1
TILE = 256
LANES = 128
HALF_GRAIN = 2.0**-24
LIMIT = 6 * 1024 * 1024
VMEM = pl.BlockSpec(memory_space=pltpu.VMEM)
HBM = pl.BlockSpec(memory_space=pltpu.HBM)
ANY = pl.BlockSpec(memory_space=pl.ANY)
SMEM = pl.BlockSpec(memory_space=pltpu.SMEM)


def halves(x):
    high = x.astype(jnp.bfloat16)
    return high, (x - high.astype(jnp.float32)).astype(jnp.bfloat16)


def stacked_halves(x):
    return jnp.concatenate(halves(x), axis=0)


def folded(x):
    rows = x.shape[0] // 2
    return x[:rows] + x[rows:]


def dot_nt(left, right):
    return lax.dot_general(
        left, right, (((1,), (1,)), ((), ())), preferred_element_type=jnp.float32
    )


def dot_nn(left, right):
    return jnp.dot(left, right, preferred_element_type=jnp.float32)


def padded_halves(x, rows):
    fill = jnp.zeros((rows - 2 * x.shape[0], x.shape[1]), jnp.bfloat16)
    return jnp.concatenate([*halves(x), fill], axis=0)


def folded_columns(x, rows):
    x = jnp.transpose(x)
    return x[:rows] + x[rows : 2 * rows]


def cost(work, pairs, transcendentals=0):
    return pl.CostEstimate(flops=work * pairs, bytes_accessed=4 * pairs, transcendentals=transcendentals * pairs)


def coordinate_rows(ref, points, axis):
    start = points + axis * LANES
    return ref[:, start : start + LANES]


def prepare_kernel(blocks, probes_ref, locations_ref, knots_ref, stack_ref, knots_out_ref, coords, sems):
    points = probes_ref.shape[1]
    block = points // blocks
    copies = [
        pltpu.make_async_copy(probes_ref, stack_ref.at[:, pl.ds(0, points)], sems.at[0]),
        pltpu.make_async_copy(locations_ref, coords, sems.at[1]),
        pltpu.make_async_copy(knots_ref, knots_out_ref, sems.at[2]),
    ]
    for copy in copies:
        copy.start()
    for copy in copies:
        copy.wait()
    stack_ref[:, points:] = jnp.zeros((stack_ref.shape[0], 2 * LANES), jnp.float32)
    for axis in range(2):
        lanes = slice(points + axis * LANES, points + (axis + 1) * LANES)
        for index in range(blocks):
            stack_ref[index : index + 1, lanes] = coords[axis : axis + 1, index * block : (index + 1) * block]


def prepare(probes, locations, knot_locs, blocks):
    rows, points = probes.shape
    assert points == blocks * LANES and blocks + 2 <= rows
    probes, locations, knot_locs = [
        pltpu.with_memory_space_constraint(x, pltpu.HBM) for x in (probes, locations, knot_locs)
    ]
    return pl.pallas_call(
        functools.partial(prepare_kernel, blocks),
        out_shape=(
            jax.ShapeDtypeStruct((rows, points + 2 * LANES), jnp.float32),
            jax.ShapeDtypeStruct(knot_locs.shape, jnp.float32),
        ),
        in_specs=[HBM, HBM, HBM],
        out_specs=(VMEM, VMEM),
        scratch_shapes=[pltpu.VMEM(locations.shape, jnp.float32), pltpu.SemaphoreType.DMA((3,))],
        compiler_params=pltpu.CompilerParams(vmem_limit_bytes=LIMIT),
        name="prepare",
    )(probes, locations, knot_locs)


def strip_kernel(below_ref, own_ref, above_ref, out_ref):
    rows, width = own_ref.shape
    points = width - 2 * LANES
    blocks = points // LANES
    out_ref[:, :LANES] = below_ref[:, points - LANES : points]
    out_ref[:, LANES : points + LANES] = own_ref[:, :points]
    out_ref[:, points + LANES : points + 2 * LANES] = above_ref[:, :LANES]
    for axis in range(2):
        lanes = slice(points + axis * LANES, points + (axis + 1) * LANES)
        target = slice(lanes.start + 2 * LANES, lanes.stop + 2 * LANES)
        out_ref[:, target] = jnp.zeros((rows, LANES), jnp.float32)
        out_ref[0:1, target] = below_ref[blocks - 1 : blocks, lanes]
        out_ref[1 : blocks + 1, target] = own_ref[:blocks, lanes]
        out_ref[blocks + 1 : blocks + 2, target] = above_ref[0:1, lanes]


def make_strip(below, own, above):
    return pl.pallas_call(
        strip_kernel,
        out_shape=jax.ShapeDtypeStruct((own.shape[0], own.shape[1] + 2 * LANES), jnp.float32),
        in_specs=[VMEM, VMEM, VMEM],
        out_specs=VMEM,
        compiler_params=pltpu.CompilerParams(vmem_limit_bytes=LIMIT),
        name="strip",
    )(below, own, above)


def assemble_kernel(grain, own_ref, east_ref, west_ref, values_ref, coords_ref):
    probes, width = own_ref.shape
    points = width - 2 * LANES
    for turn, ref in enumerate((own_ref, east_ref, west_ref)):
        start = turn * points
        values_ref[:, start : start + points] = stacked_halves(ref[:, :points] * (1.0 / 256.0))
        for axis in range(2):
            rows = off_grid(coordinate_rows(ref, points, axis) * TAPER_RATE, grain)
            for index in range(points // LANES):
                lanes = slice(start + index * LANES, start + (index + 1) * LANES)
                coords_ref[axis : axis + 1, lanes] = rows[index : index + 1]
    values_ref[:, 3 * points :] = jnp.zeros((2 * probes, LANES), jnp.bfloat16)


def assemble(strips, extent):
    probes, width = strips[0].shape
    near = 3 * (width - 2 * LANES)
    return pl.pallas_call(
        functools.partial(assemble_kernel, grain_of(TAPER_RATE * extent)),
        out_shape=(
            jax.ShapeDtypeStruct((2 * probes, near + LANES), jnp.bfloat16),
            jax.ShapeDtypeStruct((2, near), jnp.float32),
        ),
        in_specs=[VMEM] * 3,
        out_specs=(VMEM, VMEM),
        compiler_params=pltpu.CompilerParams(vmem_limit_bytes=LIMIT),
        name="assemble",
    )(*strips)


def grain_of(bound):
    return 2.0 ** math.ceil(math.log2(1.01 * bound))


def on_grid(x, grain):
    return (x + grain) - grain


def off_grid(x, grain):
    return (x + grain) - (grain - grain * HALF_GRAIN)


def project_kernel(scale, grain, stack_ref, knots_ref, out_ref, high_ref, low_ref, copy_ref, weights):
    points, knots = high_ref.shape
    probes = stack_ref.shape[0]
    tile = min(TILE, knots)
    wide = min(TILE, points)
    copy_ref[...] = stack_ref[...]
    weights[...] = stacked_halves(stack_ref[:, :points])
    east, north = [
        on_grid(jnp.transpose(coordinate_rows(stack_ref, points, axis) * scale), grain) for axis in range(2)
    ]

    @pl.loop(0, knots // tile)
    def _(step):
        lanes = pl.ds(pl.multiple_of(step * tile, tile), tile)
        kx, ky = [off_grid(knots_ref[axis : axis + 1, lanes] * scale, grain) for axis in range(2)]
        total = jnp.zeros((2 * probes, tile), jnp.float32)
        for start in range(0, points, wide):
            highs, lows = [], []
            for row in range(start, start + wide, LANES):
                block = row // LANES
                dx = east[:, block : block + 1] - kx
                dy = north[:, block : block + 1] - ky
                square = dx * dx + dy * dy
                high, low = halves(jnp.exp2(-(square * lax.rsqrt(square))))
                high_ref[row : row + LANES, lanes] = high
                low_ref[row : row + LANES, lanes] = low
                highs.append(high)
                lows.append(low)
            part = weights[:, start : start + wide]
            total = total + (
                dot_nn(part, jnp.concatenate(highs, axis=0)) + dot_nn(part, jnp.concatenate(lows, axis=0))
            )
        out_ref[:, lanes] = folded(total)


def project(stack, knot_locs, scale, extent):
    probes, points, knots = stack.shape[0], stack.shape[1] - 2 * LANES, knot_locs.shape[1]
    return pl.pallas_call(
        functools.partial(project_kernel, scale, grain_of(scale * extent)),
        out_shape=(
            jax.ShapeDtypeStruct((probes, knots), jnp.float32),
            pltpu.VMEM((points, knots), jnp.bfloat16),
            pltpu.VMEM((points, knots), jnp.bfloat16),
            jax.ShapeDtypeStruct(stack.shape, jnp.float32),
        ),
        in_specs=[VMEM, VMEM],
        out_specs=(VMEM, VMEM, VMEM, VMEM),
        scratch_shapes=[pltpu.VMEM((2 * probes, points), jnp.bfloat16)],
        compiler_params=pltpu.CompilerParams(vmem_limit_bytes=LIMIT),
        cost_estimate=cost(2800, points * knots, 2),
        name="project",
    )(stack, knot_locs)


def split_kernel(first, precision_ref, *rest):
    high_ref, low_ref = rest[-2:]
    rows = high_ref.shape[0]
    tile = min(TILE, rows)
    for start in range(0, rows, tile):
        here = slice(start, start + tile)
        high_ref[here, :], low_ref[here, :] = halves(precision_ref[first + start : first + start + tile, :])


def split_rows(precision, first, rows, after):
    depth = precision.shape[1]
    return pl.pallas_call(
        functools.partial(split_kernel, first),
        out_shape=(pltpu.VMEM((rows, depth), jnp.bfloat16), pltpu.VMEM((rows, depth), jnp.bfloat16)),
        in_specs=[VMEM] + [ANY] * len(after),
        out_specs=(VMEM, VMEM),
        compiler_params=pltpu.CompilerParams(vmem_limit_bytes=LIMIT),
        cost_estimate=cost(60, rows * depth),
        name="split",
    )(precision, *after)


def factor_kernel(scale, step, parts, before_ref, proj_ref, *rest):
    highs, lows, (out_ref, weights) = rest[:parts], rest[parts : 2 * parts], rest[-2:]
    probes, depth = proj_ref.shape
    weights[...] = stacked_halves(proj_ref[...] * scale)
    owner = lax.rem(lax.axis_index("knot") + step, lax.axis_size("knot"))
    lanes = pl.ds(pl.multiple_of(owner * depth, depth), depth)
    rows = highs[0].shape[0]
    tile = min(TILE, rows)
    for part, (high_ref, low_ref) in enumerate(zip(highs, lows)):
        for start in range(0, rows, tile):
            here = slice(start, start + tile)
            found = folded(dot_nt(weights[...], high_ref[here, lanes]) + dot_nt(weights[...], low_ref[here, lanes]))
            target = slice(part * rows + start, part * rows + start + tile)
            if before_ref is not None:
                found = found + before_ref[:, target]
            out_ref[:, target] = found


def factored(before, projection, splits, scale, step):
    probes, depth = projection.shape
    highs, lows = [
        [pltpu.with_memory_space_constraint(split[half], pltpu.VMEM) for split in splits] for half in range(2)
    ]
    rows = sum(high.shape[0] for high in highs)
    kernel = functools.partial(factor_kernel, scale, step, len(splits))
    operands = (projection, *highs, *lows)
    if before is None:
        kernel = functools.partial(kernel, None)
    else:
        operands = (before, *operands)
    return pl.pallas_call(
        kernel,
        out_shape=jax.ShapeDtypeStruct((probes, rows), jnp.float32),
        in_specs=[VMEM] * len(operands),
        out_specs=VMEM,
        scratch_shapes=[pltpu.VMEM((2 * probes, depth), jnp.bfloat16)],
        compiler_params=pltpu.CompilerParams(vmem_limit_bytes=LIMIT),
        cost_estimate=cost(1000, rows * depth),
        name="factor",
    )(*operands)


def spread_kernel(scale, factor_ref, high_ref, low_ref, out_ref, weights):
    probes = factor_ref.shape[0]
    points = high_ref.shape[0]
    tile = min(TILE, points)
    weights[...] = padded_halves(factor_ref[...] * scale, weights.shape[0])
    for start in range(0, points, tile):
        rows = slice(start, start + tile)
        total = dot_nt(high_ref[rows, :], weights[...]) + dot_nt(low_ref[rows, :], weights[...])
        out_ref[:, rows] = folded_columns(total, probes)


def spread(factor, high, low, scale):
    (probes, knots), points = factor.shape, high.shape[0]
    high = pltpu.with_memory_space_constraint(high, pltpu.VMEM)
    low = pltpu.with_memory_space_constraint(low, pltpu.VMEM)
    return pl.pallas_call(
        functools.partial(spread_kernel, scale),
        out_shape=jax.ShapeDtypeStruct((probes, points), jnp.float32),
        in_specs=[VMEM, VMEM, VMEM],
        out_specs=VMEM,
        scratch_shapes=[pltpu.VMEM((LANES, knots), jnp.bfloat16)],
        compiler_params=pltpu.CompilerParams(vmem_limit_bytes=LIMIT),
        cost_estimate=cost(850, knots * points),
        name="spread",
    )(factor, high, low)


def covariance(square):
    apart = square * lax.rsqrt(square)
    remain = jnp.maximum(4.0 - apart * (4.0 / (TAPER_LEN * TAPER_RATE)), 0.0)
    twice = remain * remain
    return (jnp.exp2(-apart) * (twice * twice)) * (5.0 - remain)


def taper_kernel(first, grain, ids_ref, counts_ref, own_ref, values_ref, coords_ref, *rest):
    out_ref = rest[-1]
    own_blocks, slots = ids_ref.shape
    block = LANES
    probes = own_ref.shape[0]
    span = own_blocks + 2
    zeros_place = coords_ref.shape[1] // block
    column = lax.axis_index("space")
    north_base = lax.axis_index("knot") * own_blocks - 1
    north_cells = lax.axis_size("knot") * own_blocks
    own_columns = [
        on_grid(jnp.transpose(coordinate_rows(own_ref, own_blocks * block, axis) * TAPER_RATE), grain)
        for axis in range(2)
    ]

    def place(group, slot):
        ahead = ids_ref[group, slot] - (column - 1) * north_cells
        east = jnp.where(ahead >= north_cells, 1, 0) + jnp.where(ahead >= 2 * north_cells, 1, 0)
        strip = jnp.where(east == 1, 0, 1 + lax.rem(column + lax.div(east, 2) + 1, 2))
        index = strip * span + (ahead - east * north_cells - north_base)
        return lanes_of(index), lanes_of(jnp.where(slot < counts_ref[group], index, zeros_place))

    def lanes_of(index):
        return pl.ds(pl.multiple_of(index * block, block), block)

    for index in range(out_ref.shape[1] // block):
        group = first + index
        px, py = [turned[:, group : group + 1] for turned in own_columns]
        total = jnp.zeros((block, 2 * probes), jnp.float32)
        for pair in range(0, slots, 2):
            highs, lows, parts = [], [], []
            for slot in range(pair, min(pair + 2, slots)):
                lanes, value_lanes = place(group, slot)
                dx = px - coords_ref[0:1, lanes]
                dy = py - coords_ref[1:2, lanes]
                high, low = halves(covariance(dx * dx + dy * dy))
                highs.append(high)
                lows.append(low)
                parts.append(values_ref[:, value_lanes])
            part = jnp.concatenate(parts, axis=1)
            total = total + (
                dot_nt(jnp.concatenate(highs, axis=1), part) + dot_nt(jnp.concatenate(lows, axis=1), part)
            )
        out_ref[:, index * block : (index + 1) * block] = (
            TAPER_SCALE * folded_columns(total, probes)
            + NUGGET * own_ref[:, group * block : (group + 1) * block]
        )


def taper(ids, counts, own, values, coords, extent, first, blocks, after):
    slots = ids.shape[1]
    return pl.pallas_call(
        functools.partial(taper_kernel, first, grain_of(TAPER_RATE * extent)),
        out_shape=jax.ShapeDtypeStruct((own.shape[0], blocks * LANES), jnp.float32),
        in_specs=[SMEM, SMEM, VMEM, VMEM, VMEM] + [ANY] * len(after),
        out_specs=VMEM,
        compiler_params=pltpu.CompilerParams(vmem_limit_bytes=LIMIT),
        cost_estimate=cost(500, blocks * slots * LANES * LANES, 2),
        name="taper",
    )(ids, counts, own, values, coords, *after)


def add_kernel(count, *refs):
    total = refs[0][...]
    for ref in refs[1:count]:
        total = total + ref[...]
    refs[-1][...] = total


def add_all(values, after):
    return pl.pallas_call(
        functools.partial(add_kernel, len(values)),
        out_shape=jax.ShapeDtypeStruct(values[0].shape, jnp.float32),
        in_specs=[VMEM] * len(values) + [ANY] * len(after),
        out_specs=VMEM,
        compiler_params=pltpu.CompilerParams(vmem_limit_bytes=LIMIT),
        name="add",
    )(*values, *after)


def butterfly_rounds(count):
    assert count & (count - 1) == 0
    bits = [1 << i for i in range(count.bit_length() - 1)]
    rounds = [(low | high, high, low) for low, high in zip(bits[0::2], bits[1::2])]
    return rounds + [(bit,) for bit in bits[len(rounds) * 2 :]]


def butterfly_round(value, axis, other, turn):
    count, groups = lax.axis_size(axis), lax.axis_size(other)
    rounds = butterfly_rounds(count)
    half = len(rounds) // 2 if len({len(steps) for steps in rounds}) == 1 else 0
    got = []
    for kind in range(len(rounds[turn])):
        pairs = []
        for j in range(groups):
            step = rounds[(turn + half * (j % 2)) % len(rounds)][kind]
            pairs += [(i * groups + j, (i ^ step) * groups + j) for i in range(count)]
        got.append(lax.ppermute(value, (axis, other), pairs))
    return got


def shifted(value, axis, step):
    count = lax.axis_size(axis)
    if step % count == 0:
        return value
    return lax.ppermute(value, axis, [((i + step) % count, i) for i in range(count)])


def paired(value, axis, other, first):
    count, groups = lax.axis_size(axis), lax.axis_size(other)
    partner = {}
    for i in range(first, count - 1, 2):
        partner[i], partner[i + 1] = i + 1, i
    pairs = []
    for i in range(count):
        for j in range(groups):
            if i in partner:
                pairs.append((i * groups + j, partner[i] * groups + j))
            elif j ^ 1 < groups:
                pairs.append((i * groups + j, i * groups + (j ^ 1)))
    return lax.ppermute(value, (axis, other), pairs)


def shards(probes, locations, knot_locs, knot_precision, neighbours, counts):
    own_blocks = neighbours.shape[0]
    row_count = probes.shape[1]
    knot_total = knot_precision.shape[1]
    device_count = lax.axis_size(("space", "knot"))
    groups = lax.axis_size("knot")
    knot_range = KNOT_REACH * math.sqrt(own_blocks * device_count / knot_total)
    proj_scale = PROJ_GAIN * math.sqrt(knot_total / (row_count * device_count))

    stack, knots = prepare(probes, locations, knot_locs, own_blocks)
    chunks = [shifted(stack, "knot", step) for step in range(groups)]
    rate = LOG2E / knot_range
    extent = CELL * max(lax.axis_size("space"), groups * own_blocks)
    parts = [project(chunk, knots, rate, extent) for chunk in chunks]
    stack = parts[0][3]

    strip = make_strip(chunks[-1], stack, chunks[1 % groups])
    values, coords = assemble([strip, paired(strip, "space", "knot", 0), paired(strip, "space", "knot", 1)], extent)
    projection = sum(part[0] for part in parts)
    rounds = len(butterfly_rounds(lax.axis_size("space")))
    pieces = math.gcd(own_blocks, rounds)
    per_piece = own_blocks // pieces
    row_pieces = math.gcd(knot_precision.shape[0] // LANES, rounds)
    per_split = knot_precision.shape[0] // row_pieces
    base, splits = [], []
    for turn in range(rounds):
        got = butterfly_round(projection, "space", "knot", turn)
        beside = []
        for i in range(pieces):
            if i * rounds // pieces == turn:
                base.append(
                    taper(
                        neighbours, counts, stack, values, coords, extent, i * per_piece, per_piece, [projection]
                    )
                )
                beside.append(base[-1])
        for i in range(row_pieces):
            if i * rounds // row_pieces == turn:
                splits.append(split_rows(knot_precision, i * per_split, per_split, [projection]))
                beside.extend(splits[-1])
        projection = add_all([projection, *got], beside)
    factor = factored(None, projection, splits, proj_scale, 0)
    for step in range(1, groups):
        factor = factored(factor, shifted(projection, "knot", step), splits, proj_scale, step)
    total = jnp.concatenate(base, axis=1)
    for step in reversed(range(groups)):
        share = spread(factor, parts[step][1], parts[step][2], LOW_SCALE * EXPAND_GAIN)
        total = total + shifted(share, "knot", -step)
    return total


def solution(mesh):
    return jax.shard_map(
        shards,
        mesh=mesh,
        in_specs=(
            P(None, ("space", "knot")),
            P(None, ("space", "knot")),
            P(None, "knot"),
            P("knot", None),
            P(("space", "knot"), None),
            P(("space", "knot")),
        ),
        out_specs=P(None, ("space", "knot")),
        check_vma=False,
    )
```

```python
import functools
import math

import jax
import jax.numpy as jnp
from jax import lax
from jax.experimental import pallas as pl
from jax.experimental.pallas import tpu as pltpu
from jax.sharding import PartitionSpec as P

COV_RANGE = 0.05
TAPER_LEN = 0.15
KNOT_REACH = 0.15
TAPER_SCALE = 0.1
PROJ_GAIN = 0.5
EXPAND_GAIN = 0.5
LOW_SCALE = 0.5
NUGGET = 0.25
LOG2E = math.log2(math.e)
TAPER_RATE = LOG2E / COV_RANGE
CELL = 0.1
TILE = 256
LANES = 128
HALF_GRAIN = 2.0**-24
LIMIT = 6 * 1024 * 1024
VMEM = pl.BlockSpec(memory_space=pltpu.VMEM)
HBM = pl.BlockSpec(memory_space=pltpu.HBM)
ANY = pl.BlockSpec(memory_space=pl.ANY)
SMEM = pl.BlockSpec(memory_space=pltpu.SMEM)


def halves(x):
    high = x.astype(jnp.bfloat16)
    return high, (x - high.astype(jnp.float32)).astype(jnp.bfloat16)


def stacked_halves(x):
    return jnp.concatenate(halves(x), axis=0)


def folded(x):
    rows = x.shape[0] // 2
    return x[:rows] + x[rows:]


def dot_nt(left, right):
    return lax.dot_general(
        left, right, (((1,), (1,)), ((), ())), preferred_element_type=jnp.float32
    )


def dot_nn(left, right):
    return jnp.dot(left, right, preferred_element_type=jnp.float32)


def padded_halves(x, rows):
    fill = jnp.zeros((rows - 2 * x.shape[0], x.shape[1]), jnp.bfloat16)
    return jnp.concatenate([*halves(x), fill], axis=0)


def folded_columns(x, rows):
    x = jnp.transpose(x)
    return x[:rows] + x[rows : 2 * rows]


def cost(work, pairs, transcendentals=0):
    return pl.CostEstimate(flops=work * pairs, bytes_accessed=4 * pairs, transcendentals=transcendentals * pairs)


def coordinate_rows(ref, points, axis):
    start = points + axis * LANES
    return ref[:, start : start + LANES]


def prepare_kernel(blocks, probes_ref, locations_ref, knots_ref, stack_ref, knots_out_ref, coords, sems):
    points = probes_ref.shape[1]
    block = points // blocks
    copies = [
        pltpu.make_async_copy(probes_ref, stack_ref.at[:, pl.ds(0, points)], sems.at[0]),
        pltpu.make_async_copy(locations_ref, coords, sems.at[1]),
        pltpu.make_async_copy(knots_ref, knots_out_ref, sems.at[2]),
    ]
    for copy in copies:
        copy.start()
    for copy in copies:
        copy.wait()
    stack_ref[:, points:] = jnp.zeros((stack_ref.shape[0], 2 * LANES), jnp.float32)
    for axis in range(2):
        lanes = slice(points + axis * LANES, points + (axis + 1) * LANES)
        for index in range(blocks):
            stack_ref[index : index + 1, lanes] = coords[axis : axis + 1, index * block : (index + 1) * block]


def prepare(probes, locations, knot_locs, blocks):
    rows, points = probes.shape
    assert points == blocks * LANES and blocks + 2 <= rows
    probes, locations, knot_locs = [
        pltpu.with_memory_space_constraint(x, pltpu.HBM) for x in (probes, locations, knot_locs)
    ]
    return pl.pallas_call(
        functools.partial(prepare_kernel, blocks),
        out_shape=(
            jax.ShapeDtypeStruct((rows, points + 2 * LANES), jnp.float32),
            jax.ShapeDtypeStruct(knot_locs.shape, jnp.float32),
        ),
        in_specs=[HBM, HBM, HBM],
        out_specs=(VMEM, VMEM),
        scratch_shapes=[pltpu.VMEM(locations.shape, jnp.float32), pltpu.SemaphoreType.DMA((3,))],
        compiler_params=pltpu.CompilerParams(vmem_limit_bytes=LIMIT),
        name="prepare",
    )(probes, locations, knot_locs)


def strip_kernel(below_ref, own_ref, above_ref, out_ref):
    rows, width = own_ref.shape
    points = width - 2 * LANES
    blocks = points // LANES
    out_ref[:, :LANES] = below_ref[:, points - LANES : points]
    out_ref[:, LANES : points + LANES] = own_ref[:, :points]
    out_ref[:, points + LANES : points + 2 * LANES] = above_ref[:, :LANES]
    for axis in range(2):
        lanes = slice(points + axis * LANES, points + (axis + 1) * LANES)
        target = slice(lanes.start + 2 * LANES, lanes.stop + 2 * LANES)
        out_ref[:, target] = jnp.zeros((rows, LANES), jnp.float32)
        out_ref[0:1, target] = below_ref[blocks - 1 : blocks, lanes]
        out_ref[1 : blocks + 1, target] = own_ref[:blocks, lanes]
        out_ref[blocks + 1 : blocks + 2, target] = above_ref[0:1, lanes]


def make_strip(below, own, above):
    return pl.pallas_call(
        strip_kernel,
        out_shape=jax.ShapeDtypeStruct((own.shape[0], own.shape[1] + 2 * LANES), jnp.float32),
        in_specs=[VMEM, VMEM, VMEM],
        out_specs=VMEM,
        compiler_params=pltpu.CompilerParams(vmem_limit_bytes=LIMIT),
        name="strip",
    )(below, own, above)


def assemble_kernel(grain, own_ref, east_ref, west_ref, values_ref, coords_ref):
    probes, width = own_ref.shape
    points = width - 2 * LANES
    for turn, ref in enumerate((own_ref, east_ref, west_ref)):
        start = turn * points
        values_ref[:, start : start + points] = stacked_halves(ref[:, :points] * (1.0 / 256.0))
        for axis in range(2):
            rows = off_grid(coordinate_rows(ref, points, axis) * TAPER_RATE, grain)
            for index in range(points // LANES):
                lanes = slice(start + index * LANES, start + (index + 1) * LANES)
                coords_ref[axis : axis + 1, lanes] = rows[index : index + 1]
    values_ref[:, 3 * points :] = jnp.zeros((2 * probes, LANES), jnp.bfloat16)


def assemble(strips, extent):
    probes, width = strips[0].shape
    near = 3 * (width - 2 * LANES)
    return pl.pallas_call(
        functools.partial(assemble_kernel, grain_of(TAPER_RATE * extent)),
        out_shape=(
            jax.ShapeDtypeStruct((2 * probes, near + LANES), jnp.bfloat16),
            jax.ShapeDtypeStruct((2, near), jnp.float32),
        ),
        in_specs=[VMEM] * 3,
        out_specs=(VMEM, VMEM),
        compiler_params=pltpu.CompilerParams(vmem_limit_bytes=LIMIT),
        name="assemble",
    )(*strips)


def grain_of(bound):
    return 2.0 ** math.ceil(math.log2(1.01 * bound))


def on_grid(x, grain):
    return (x + grain) - grain


def off_grid(x, grain):
    return (x + grain) - (grain - grain * HALF_GRAIN)


def project_kernel(scale, grain, stack_ref, knots_ref, out_ref, high_ref, low_ref, copy_ref, weights, columns):
    knots, points = high_ref.shape
    probes = stack_ref.shape[0]
    tile = min(TILE, knots)
    wide = min(TILE, points)
    copy_ref[...] = stack_ref[...]
    weights[...] = stacked_halves(stack_ref[:, :points])
    fill = jnp.zeros((6, knots), jnp.float32)
    columns[...] = jnp.transpose(jnp.concatenate([off_grid(knots_ref[...] * scale, grain), fill], axis=0))
    east, north = [on_grid(coordinate_rows(stack_ref, points, axis) * scale, grain) for axis in range(2)]

    @pl.loop(0, knots // tile)
    def _(step):
        rows = pl.ds(pl.multiple_of(step * tile, tile), tile)
        kx, ky = [columns[rows, axis : axis + 1] for axis in range(2)]
        total = jnp.zeros((2 * probes, tile), jnp.float32)
        for start in range(0, points, wide):
            highs, lows = [], []
            for lane in range(start, start + wide, LANES):
                block = lane // LANES
                dx = east[block : block + 1, :] - kx
                dy = north[block : block + 1, :] - ky
                square = dx * dx + dy * dy
                high, low = halves(jnp.exp2(-(square * lax.rsqrt(square))))
                high_ref[rows, lane : lane + LANES] = high
                low_ref[rows, lane : lane + LANES] = low
                highs.append(high)
                lows.append(low)
            part = weights[:, start : start + wide]
            total = total + (
                dot_nt(part, jnp.concatenate(highs, axis=1)) + dot_nt(part, jnp.concatenate(lows, axis=1))
            )
        out_ref[:, rows] = folded(total)


def project(stack, knot_locs, scale, extent):
    probes, points, knots = stack.shape[0], stack.shape[1] - 2 * LANES, knot_locs.shape[1]
    return pl.pallas_call(
        functools.partial(project_kernel, scale, grain_of(scale * extent)),
        out_shape=(
            jax.ShapeDtypeStruct((probes, knots), jnp.float32),
            pltpu.VMEM((knots, points), jnp.bfloat16),
            pltpu.VMEM((knots, points), jnp.bfloat16),
            jax.ShapeDtypeStruct(stack.shape, jnp.float32),
        ),
        in_specs=[VMEM, VMEM],
        out_specs=(VMEM, VMEM, VMEM, VMEM),
        scratch_shapes=[
            pltpu.VMEM((2 * probes, points), jnp.bfloat16),
            pltpu.VMEM((knots, 8), jnp.float32),
        ],
        compiler_params=pltpu.CompilerParams(vmem_limit_bytes=LIMIT),
        cost_estimate=cost(2800, points * knots, 2),
        name="project",
    )(stack, knot_locs)


def split_kernel(first, precision_ref, *rest):
    high_ref, low_ref = rest[-2:]
    rows = high_ref.shape[0]
    tile = min(TILE, rows)
    for start in range(0, rows, tile):
        here = slice(start, start + tile)
        high_ref[here, :], low_ref[here, :] = halves(precision_ref[first + start : first + start + tile, :])


def split_rows(precision, first, rows, after):
    depth = precision.shape[1]
    return pl.pallas_call(
        functools.partial(split_kernel, first),
        out_shape=(pltpu.VMEM((rows, depth), jnp.bfloat16), pltpu.VMEM((rows, depth), jnp.bfloat16)),
        in_specs=[VMEM] + [ANY] * len(after),
        out_specs=(VMEM, VMEM),
        compiler_params=pltpu.CompilerParams(vmem_limit_bytes=LIMIT),
        cost_estimate=cost(60, rows * depth),
        name="split",
    )(precision, *after)


def factor_kernel(scale, step, parts, before_ref, proj_ref, *rest):
    highs, lows, (out_ref, weights) = rest[:parts], rest[parts : 2 * parts], rest[-2:]
    probes, depth = proj_ref.shape
    weights[...] = stacked_halves(proj_ref[...] * scale)
    owner = lax.rem(lax.axis_index("knot") + step, lax.axis_size("knot"))
    lanes = pl.ds(pl.multiple_of(owner * depth, depth), depth)
    rows = highs[0].shape[0]
    tile = min(TILE, rows)
    for part, (high_ref, low_ref) in enumerate(zip(highs, lows)):
        for start in range(0, rows, tile):
            here = slice(start, start + tile)
            found = folded(dot_nt(weights[...], high_ref[here, lanes]) + dot_nt(weights[...], low_ref[here, lanes]))
            target = slice(part * rows + start, part * rows + start + tile)
            if before_ref is not None:
                found = found + before_ref[:, target]
            out_ref[:, target] = found


def factored(before, projection, splits, scale, step):
    probes, depth = projection.shape
    highs, lows = [
        [pltpu.with_memory_space_constraint(split[half], pltpu.VMEM) for split in splits] for half in range(2)
    ]
    rows = sum(high.shape[0] for high in highs)
    kernel = functools.partial(factor_kernel, scale, step, len(splits))
    operands = (projection, *highs, *lows)
    if before is None:
        kernel = functools.partial(kernel, None)
    else:
        operands = (before, *operands)
    return pl.pallas_call(
        kernel,
        out_shape=jax.ShapeDtypeStruct((probes, rows), jnp.float32),
        in_specs=[VMEM] * len(operands),
        out_specs=VMEM,
        scratch_shapes=[pltpu.VMEM((2 * probes, depth), jnp.bfloat16)],
        compiler_params=pltpu.CompilerParams(vmem_limit_bytes=LIMIT),
        cost_estimate=cost(1000, rows * depth),
        name="factor",
    )(*operands)


def spread_kernel(scale, factor_ref, high_ref, low_ref, out_ref):
    points = high_ref.shape[1]
    tile = min(TILE, points)
    weights = stacked_halves(factor_ref[...] * scale)
    for start in range(0, points, tile):
        lanes = slice(start, start + tile)
        out_ref[:, lanes] = folded(dot_nn(weights, high_ref[:, lanes]) + dot_nn(weights, low_ref[:, lanes]))


def spread(factor, high, low, scale):
    (probes, knots), points = factor.shape, high.shape[1]
    high = pltpu.with_memory_space_constraint(high, pltpu.VMEM)
    low = pltpu.with_memory_space_constraint(low, pltpu.VMEM)
    return pl.pallas_call(
        functools.partial(spread_kernel, scale),
        out_shape=jax.ShapeDtypeStruct((probes, points), jnp.float32),
        in_specs=[VMEM, VMEM, VMEM],
        out_specs=VMEM,
        compiler_params=pltpu.CompilerParams(vmem_limit_bytes=LIMIT),
        cost_estimate=cost(850, knots * points),
        name="spread",
    )(factor, high, low)


def covariance(square):
    apart = square * lax.rsqrt(square)
    remain = jnp.maximum(4.0 - apart * (4.0 / (TAPER_LEN * TAPER_RATE)), 0.0)
    twice = remain * remain
    return (jnp.exp2(-apart) * (twice * twice)) * (5.0 - remain)


def taper_kernel(first, grain, ids_ref, counts_ref, own_ref, values_ref, coords_ref, *rest):
    out_ref = rest[-1]
    own_blocks, slots = ids_ref.shape
    block = LANES
    probes = own_ref.shape[0]
    span = own_blocks + 2
    zeros_place = coords_ref.shape[1] // block
    column = lax.axis_index("space")
    north_base = lax.axis_index("knot") * own_blocks - 1
    north_cells = lax.axis_size("knot") * own_blocks
    own_columns = [
        on_grid(jnp.transpose(coordinate_rows(own_ref, own_blocks * block, axis) * TAPER_RATE), grain)
        for axis in range(2)
    ]

    def place(group, slot):
        ahead = ids_ref[group, slot] - (column - 1) * north_cells
        east = jnp.where(ahead >= north_cells, 1, 0) + jnp.where(ahead >= 2 * north_cells, 1, 0)
        strip = jnp.where(east == 1, 0, 1 + lax.rem(column + lax.div(east, 2) + 1, 2))
        index = strip * span + (ahead - east * north_cells - north_base)
        return lanes_of(index), lanes_of(jnp.where(slot < counts_ref[group], index, zeros_place))

    def lanes_of(index):
        return pl.ds(pl.multiple_of(index * block, block), block)

    for index in range(out_ref.shape[1] // block):
        group = first + index
        px, py = [turned[:, group : group + 1] for turned in own_columns]
        total = jnp.zeros((block, 2 * probes), jnp.float32)
        for pair in range(0, slots, 2):
            highs, lows, parts = [], [], []
            for slot in range(pair, min(pair + 2, slots)):
                lanes, value_lanes = place(group, slot)
                dx = px - coords_ref[0:1, lanes]
                dy = py - coords_ref[1:2, lanes]
                high, low = halves(covariance(dx * dx + dy * dy))
                highs.append(high)
                lows.append(low)
                parts.append(values_ref[:, value_lanes])
            part = jnp.concatenate(parts, axis=1)
            total = total + (
                dot_nt(jnp.concatenate(highs, axis=1), part) + dot_nt(jnp.concatenate(lows, axis=1), part)
            )
        out_ref[:, index * block : (index + 1) * block] = (
            TAPER_SCALE * folded_columns(total, probes)
            + NUGGET * own_ref[:, group * block : (group + 1) * block]
        )


def taper(ids, counts, own, values, coords, extent, first, blocks, after):
    slots = ids.shape[1]
    return pl.pallas_call(
        functools.partial(taper_kernel, first, grain_of(TAPER_RATE * extent)),
        out_shape=jax.ShapeDtypeStruct((own.shape[0], blocks * LANES), jnp.float32),
        in_specs=[SMEM, SMEM, VMEM, VMEM, VMEM] + [ANY] * len(after),
        out_specs=VMEM,
        compiler_params=pltpu.CompilerParams(vmem_limit_bytes=LIMIT),
        cost_estimate=cost(500, blocks * slots * LANES * LANES, 2),
        name="taper",
    )(ids, counts, own, values, coords, *after)


def add_kernel(count, *refs):
    total = refs[0][...]
    for ref in refs[1:count]:
        total = total + ref[...]
    refs[-1][...] = total


def add_all(values, after):
    return pl.pallas_call(
        functools.partial(add_kernel, len(values)),
        out_shape=jax.ShapeDtypeStruct(values[0].shape, jnp.float32),
        in_specs=[VMEM] * len(values) + [ANY] * len(after),
        out_specs=VMEM,
        compiler_params=pltpu.CompilerParams(vmem_limit_bytes=LIMIT),
        name="add",
    )(*values, *after)


def butterfly_rounds(count):
    assert count & (count - 1) == 0
    bits = [1 << i for i in range(count.bit_length() - 1)]
    rounds = [(low | high, high, low) for low, high in zip(bits[0::2], bits[1::2])]
    return rounds + [(bit,) for bit in bits[len(rounds) * 2 :]]


def butterfly_round(value, axis, other, turn):
    count, groups = lax.axis_size(axis), lax.axis_size(other)
    rounds = butterfly_rounds(count)
    half = len(rounds) // 2 if len({len(steps) for steps in rounds}) == 1 else 0
    got = []
    for kind in range(len(rounds[turn])):
        pairs = []
        for j in range(groups):
            step = rounds[(turn + half * (j % 2)) % len(rounds)][kind]
            pairs += [(i * groups + j, (i ^ step) * groups + j) for i in range(count)]
        got.append(lax.ppermute(value, (axis, other), pairs))
    return got


def shifted(value, axis, step):
    count = lax.axis_size(axis)
    if step % count == 0:
        return value
    return lax.ppermute(value, axis, [((i + step) % count, i) for i in range(count)])


def paired(value, axis, other, first):
    count, groups = lax.axis_size(axis), lax.axis_size(other)
    partner = {}
    for i in range(first, count - 1, 2):
        partner[i], partner[i + 1] = i + 1, i
    pairs = []
    for i in range(count):
        for j in range(groups):
            if i in partner:
                pairs.append((i * groups + j, partner[i] * groups + j))
            elif j ^ 1 < groups:
                pairs.append((i * groups + j, i * groups + (j ^ 1)))
    return lax.ppermute(value, (axis, other), pairs)


def shards(probes, locations, knot_locs, knot_precision, neighbours, counts):
    own_blocks = neighbours.shape[0]
    row_count = probes.shape[1]
    knot_total = knot_precision.shape[1]
    device_count = lax.axis_size(("space", "knot"))
    groups = lax.axis_size("knot")
    knot_range = KNOT_REACH * math.sqrt(own_blocks * device_count / knot_total)
    proj_scale = PROJ_GAIN * math.sqrt(knot_total / (row_count * device_count))

    stack, knots = prepare(probes, locations, knot_locs, own_blocks)
    chunks = [shifted(stack, "knot", step) for step in range(groups)]
    rate = LOG2E / knot_range
    extent = CELL * max(lax.axis_size("space"), groups * own_blocks)
    parts = [project(chunk, knots, rate, extent) for chunk in chunks]
    stack = parts[0][3]

    strip = make_strip(chunks[-1], stack, chunks[1 % groups])
    values, coords = assemble([strip, paired(strip, "space", "knot", 0), paired(strip, "space", "knot", 1)], extent)
    projection = sum(part[0] for part in parts)
    rounds = len(butterfly_rounds(lax.axis_size("space")))
    pieces = math.gcd(own_blocks, rounds)
    per_piece = own_blocks // pieces
    row_pieces = math.gcd(knot_precision.shape[0] // LANES, rounds)
    per_split = knot_precision.shape[0] // row_pieces
    base, splits = [], []
    for turn in range(rounds):
        got = butterfly_round(projection, "space", "knot", turn)
        beside = []
        for i in range(pieces):
            if i * rounds // pieces == turn:
                base.append(
                    taper(
                        neighbours, counts, stack, values, coords, extent, i * per_piece, per_piece, [projection]
                    )
                )
                beside.append(base[-1])
        for i in range(row_pieces):
            if i * rounds // row_pieces == turn:
                splits.append(split_rows(knot_precision, i * per_split, per_split, [projection]))
                beside.extend(splits[-1])
        projection = add_all([projection, *got], beside)
    factor = factored(None, projection, splits, proj_scale, 0)
    for step in range(1, groups):
        factor = factored(factor, shifted(projection, "knot", step), splits, proj_scale, step)
    total = jnp.concatenate(base, axis=1)
    for step in reversed(range(groups)):
        share = spread(factor, parts[step][1], parts[step][2], LOW_SCALE * EXPAND_GAIN)
        total = total + shifted(share, "knot", -step)
    return total


def solution(mesh):
    return jax.shard_map(
        shards,
        mesh=mesh,
        in_specs=(
            P(None, ("space", "knot")),
            P(None, ("space", "knot")),
            P(None, "knot"),
            P("knot", None),
            P(("space", "knot"), None),
            P(("space", "knot")),
        ),
        out_specs=P(None, ("space", "knot")),
        check_vma=False,
    )
```

```python
import functools
import math

import jax
import jax.numpy as jnp
from jax import lax
from jax.experimental import pallas as pl
from jax.experimental.pallas import tpu as pltpu
from jax.sharding import PartitionSpec as P

COV_RANGE = 0.05
TAPER_LEN = 0.15
KNOT_REACH = 0.15
TAPER_SCALE = 0.1
PROJ_GAIN = 0.5
EXPAND_GAIN = 0.5
LOW_SCALE = 0.5
NUGGET = 0.25
LOG2E = math.log2(math.e)
TAPER_RATE = LOG2E / COV_RANGE
CELL = 0.1
TILE = 256
LANES = 128
HALF_GRAIN = 2.0**-24
LIMIT = 6 * 1024 * 1024
VMEM = pl.BlockSpec(memory_space=pltpu.VMEM)
HBM = pl.BlockSpec(memory_space=pltpu.HBM)
ANY = pl.BlockSpec(memory_space=pl.ANY)
SMEM = pl.BlockSpec(memory_space=pltpu.SMEM)


def halves(x):
    high = x.astype(jnp.bfloat16)
    return high, (x - high.astype(jnp.float32)).astype(jnp.bfloat16)


def stacked_halves(x):
    return jnp.concatenate(halves(x), axis=0)


def folded(x):
    rows = x.shape[0] // 2
    return x[:rows] + x[rows:]


def dot_nt(left, right):
    return lax.dot_general(
        left, right, (((1,), (1,)), ((), ())), preferred_element_type=jnp.float32
    )


def dot_nn(left, right):
    return jnp.dot(left, right, preferred_element_type=jnp.float32)


def padded_halves(x, rows):
    fill = jnp.zeros((rows - 2 * x.shape[0], x.shape[1]), jnp.bfloat16)
    return jnp.concatenate([*halves(x), fill], axis=0)


def folded_columns(x, rows):
    x = jnp.transpose(x)
    return x[:rows] + x[rows : 2 * rows]


def cost(work, pairs, transcendentals=0):
    return pl.CostEstimate(flops=work * pairs, bytes_accessed=4 * pairs, transcendentals=transcendentals * pairs)


def coordinate_rows(ref, points, axis):
    start = points + axis * LANES
    return ref[:, start : start + LANES]


def prepare_kernel(blocks, probes_ref, locations_ref, knots_ref, stack_ref, knots_out_ref, coords, sems):
    points = probes_ref.shape[1]
    block = points // blocks
    copies = [
        pltpu.make_async_copy(probes_ref, stack_ref.at[:, pl.ds(0, points)], sems.at[0]),
        pltpu.make_async_copy(locations_ref, coords, sems.at[1]),
        pltpu.make_async_copy(knots_ref, knots_out_ref, sems.at[2]),
    ]
    for copy in copies:
        copy.start()
    for copy in copies:
        copy.wait()
    stack_ref[:, points:] = jnp.zeros((stack_ref.shape[0], 2 * LANES), jnp.float32)
    for axis in range(2):
        lanes = slice(points + axis * LANES, points + (axis + 1) * LANES)
        for index in range(blocks):
            stack_ref[index : index + 1, lanes] = coords[axis : axis + 1, index * block : (index + 1) * block]


def prepare(probes, locations, knot_locs, blocks):
    rows, points = probes.shape
    assert points == blocks * LANES and blocks + 2 <= rows
    probes, locations, knot_locs = [
        pltpu.with_memory_space_constraint(x, pltpu.HBM) for x in (probes, locations, knot_locs)
    ]
    return pl.pallas_call(
        functools.partial(prepare_kernel, blocks),
        out_shape=(
            jax.ShapeDtypeStruct((rows, points + 2 * LANES), jnp.float32),
            jax.ShapeDtypeStruct(knot_locs.shape, jnp.float32),
        ),
        in_specs=[HBM, HBM, HBM],
        out_specs=(VMEM, VMEM),
        scratch_shapes=[pltpu.VMEM(locations.shape, jnp.float32), pltpu.SemaphoreType.DMA((3,))],
        compiler_params=pltpu.CompilerParams(vmem_limit_bytes=LIMIT),
        name="prepare",
    )(probes, locations, knot_locs)


def strip_kernel(below_ref, own_ref, above_ref, out_ref):
    rows, width = own_ref.shape
    points = width - 2 * LANES
    blocks = points // LANES
    out_ref[:, :LANES] = below_ref[:, points - LANES : points]
    out_ref[:, LANES : points + LANES] = own_ref[:, :points]
    out_ref[:, points + LANES : points + 2 * LANES] = above_ref[:, :LANES]
    for axis in range(2):
        lanes = slice(points + axis * LANES, points + (axis + 1) * LANES)
        target = slice(lanes.start + 2 * LANES, lanes.stop + 2 * LANES)
        out_ref[:, target] = jnp.zeros((rows, LANES), jnp.float32)
        out_ref[0:1, target] = below_ref[blocks - 1 : blocks, lanes]
        out_ref[1 : blocks + 1, target] = own_ref[:blocks, lanes]
        out_ref[blocks + 1 : blocks + 2, target] = above_ref[0:1, lanes]


def make_strip(below, own, above):
    return pl.pallas_call(
        strip_kernel,
        out_shape=jax.ShapeDtypeStruct((own.shape[0], own.shape[1] + 2 * LANES), jnp.float32),
        in_specs=[VMEM, VMEM, VMEM],
        out_specs=VMEM,
        compiler_params=pltpu.CompilerParams(vmem_limit_bytes=LIMIT),
        name="strip",
    )(below, own, above)


def assemble_kernel(grain, own_ref, east_ref, west_ref, values_ref, coords_ref):
    probes, width = own_ref.shape
    points = width - 2 * LANES
    for turn, ref in enumerate((own_ref, east_ref, west_ref)):
        start = turn * points
        values_ref[:, start : start + points] = stacked_halves(ref[:, :points] * (1.0 / 256.0))
        for axis in range(2):
            rows = off_grid(coordinate_rows(ref, points, axis) * TAPER_RATE, grain)
            for index in range(points // LANES):
                lanes = slice(start + index * LANES, start + (index + 1) * LANES)
                coords_ref[axis : axis + 1, lanes] = rows[index : index + 1]
    values_ref[:, 3 * points :] = jnp.zeros((2 * probes, LANES), jnp.bfloat16)


def assemble(strips, extent):
    probes, width = strips[0].shape
    near = 3 * (width - 2 * LANES)
    return pl.pallas_call(
        functools.partial(assemble_kernel, grain_of(TAPER_RATE * extent)),
        out_shape=(
            jax.ShapeDtypeStruct((2 * probes, near + LANES), jnp.bfloat16),
            jax.ShapeDtypeStruct((2, near), jnp.float32),
        ),
        in_specs=[VMEM] * 3,
        out_specs=(VMEM, VMEM),
        compiler_params=pltpu.CompilerParams(vmem_limit_bytes=LIMIT),
        name="assemble",
    )(*strips)


def grain_of(bound):
    return 2.0 ** math.ceil(math.log2(1.01 * bound))


def on_grid(x, grain):
    return (x + grain) - grain


def off_grid(x, grain):
    return (x + grain) - (grain - grain * HALF_GRAIN)


def project_kernel(scale, grain, stack_ref, knots_ref, out_ref, high_ref, low_ref, copy_ref, weights):
    points, knots = high_ref.shape
    probes = stack_ref.shape[0]
    tile = min(TILE, knots)
    wide = min(TILE, points)
    copy_ref[...] = stack_ref[...]
    weights[...] = stacked_halves(stack_ref[:, :points])
    east, north = [
        on_grid(jnp.transpose(coordinate_rows(stack_ref, points, axis) * scale), grain) for axis in range(2)
    ]

    @pl.loop(0, knots // tile)
    def _(step):
        lanes = pl.ds(pl.multiple_of(step * tile, tile), tile)
        kx, ky = [off_grid(knots_ref[axis : axis + 1, lanes] * scale, grain) for axis in range(2)]
        total = jnp.zeros((2 * probes, tile), jnp.float32)
        for start in range(0, points, wide):
            highs, lows = [], []
            for row in range(start, start + wide, LANES):
                block = row // LANES
                dx = east[:, block : block + 1] - kx
                dy = north[:, block : block + 1] - ky
                square = dx * dx + dy * dy
                high, low = halves(jnp.exp2(-(square * lax.rsqrt(square))))
                high_ref[row : row + LANES, lanes] = high
                low_ref[row : row + LANES, lanes] = low
                highs.append(high)
                lows.append(low)
            part = weights[:, start : start + wide]
            total = total + (
                dot_nn(part, jnp.concatenate(highs, axis=0)) + dot_nn(part, jnp.concatenate(lows, axis=0))
            )
        out_ref[:, lanes] = folded(total)


def project(stack, knot_locs, scale, extent):
    probes, points, knots = stack.shape[0], stack.shape[1] - 2 * LANES, knot_locs.shape[1]
    return pl.pallas_call(
        functools.partial(project_kernel, scale, grain_of(scale * extent)),
        out_shape=(
            jax.ShapeDtypeStruct((probes, knots), jnp.float32),
            pltpu.VMEM((points, knots), jnp.bfloat16),
            pltpu.VMEM((points, knots), jnp.bfloat16),
            jax.ShapeDtypeStruct(stack.shape, jnp.float32),
        ),
        in_specs=[VMEM, VMEM],
        out_specs=(VMEM, VMEM, VMEM, VMEM),
        scratch_shapes=[pltpu.VMEM((2 * probes, points), jnp.bfloat16)],
        compiler_params=pltpu.CompilerParams(vmem_limit_bytes=LIMIT),
        cost_estimate=cost(2800, points * knots, 2),
        name="project",
    )(stack, knot_locs)


def split_kernel(first, precision_ref, *rest):
    high_ref, low_ref = rest[-2:]
    rows = high_ref.shape[0]
    tile = min(TILE, rows)
    for start in range(0, rows, tile):
        here = slice(start, start + tile)
        high_ref[here, :], low_ref[here, :] = halves(precision_ref[first + start : first + start + tile, :])


def split_rows(precision, first, rows, after):
    depth = precision.shape[1]
    return pl.pallas_call(
        functools.partial(split_kernel, first),
        out_shape=(pltpu.VMEM((rows, depth), jnp.bfloat16), pltpu.VMEM((rows, depth), jnp.bfloat16)),
        in_specs=[VMEM] + [ANY] * len(after),
        out_specs=(VMEM, VMEM),
        compiler_params=pltpu.CompilerParams(vmem_limit_bytes=LIMIT),
        cost_estimate=cost(60, rows * depth),
        name="split",
    )(precision, *after)


def factor_kernel(scale, step, parts, before_ref, proj_ref, *rest):
    highs, lows, (out_ref, weights) = rest[:parts], rest[parts : 2 * parts], rest[-2:]
    probes, depth = proj_ref.shape
    weights[...] = stacked_halves(proj_ref[...] * scale)
    owner = lax.rem(lax.axis_index("knot") + step, lax.axis_size("knot"))
    lanes = pl.ds(pl.multiple_of(owner * depth, depth), depth)
    rows = highs[0].shape[0]
    tile = min(TILE, rows)
    for part, (high_ref, low_ref) in enumerate(zip(highs, lows)):
        for start in range(0, rows, tile):
            here = slice(start, start + tile)
            found = folded(dot_nt(weights[...], high_ref[here, lanes]) + dot_nt(weights[...], low_ref[here, lanes]))
            target = slice(part * rows + start, part * rows + start + tile)
            if before_ref is not None:
                found = found + before_ref[:, target]
            out_ref[:, target] = found


def factored(before, projection, splits, scale, step):
    probes, depth = projection.shape
    highs, lows = [
        [pltpu.with_memory_space_constraint(split[half], pltpu.VMEM) for split in splits] for half in range(2)
    ]
    rows = sum(high.shape[0] for high in highs)
    kernel = functools.partial(factor_kernel, scale, step, len(splits))
    operands = (projection, *highs, *lows)
    if before is None:
        kernel = functools.partial(kernel, None)
    else:
        operands = (before, *operands)
    return pl.pallas_call(
        kernel,
        out_shape=jax.ShapeDtypeStruct((probes, rows), jnp.float32),
        in_specs=[VMEM] * len(operands),
        out_specs=VMEM,
        scratch_shapes=[pltpu.VMEM((2 * probes, depth), jnp.bfloat16)],
        compiler_params=pltpu.CompilerParams(vmem_limit_bytes=LIMIT),
        cost_estimate=cost(1000, rows * depth),
        name="factor",
    )(*operands)


def spread_kernel(scale, factor_ref, high_ref, low_ref, out_ref, weights):
    probes = factor_ref.shape[0]
    points = high_ref.shape[0]
    tile = min(TILE, points)
    weights[...] = padded_halves(factor_ref[...] * scale, weights.shape[0])
    for start in range(0, points, tile):
        rows = slice(start, start + tile)
        total = dot_nt(high_ref[rows, :], weights[...]) + dot_nt(low_ref[rows, :], weights[...])
        out_ref[:, rows] = folded_columns(total, probes)


def spread(factor, high, low, scale):
    (probes, knots), points = factor.shape, high.shape[0]
    high = pltpu.with_memory_space_constraint(high, pltpu.VMEM)
    low = pltpu.with_memory_space_constraint(low, pltpu.VMEM)
    return pl.pallas_call(
        functools.partial(spread_kernel, scale),
        out_shape=jax.ShapeDtypeStruct((probes, points), jnp.float32),
        in_specs=[VMEM, VMEM, VMEM],
        out_specs=VMEM,
        scratch_shapes=[pltpu.VMEM((LANES, knots), jnp.bfloat16)],
        compiler_params=pltpu.CompilerParams(vmem_limit_bytes=LIMIT),
        cost_estimate=cost(850, knots * points),
        name="spread",
    )(factor, high, low)


def covariance(square):
    apart = square * lax.rsqrt(square)
    remain = jnp.maximum(4.0 - apart * (4.0 / (TAPER_LEN * TAPER_RATE)), 0.0)
    twice = remain * remain
    return (jnp.exp2(-apart) * (twice * twice)) * (5.0 - remain)


def taper_kernel(first, grain, ids_ref, counts_ref, own_ref, values_ref, coords_ref, *rest):
    out_ref = rest[-1]
    own_blocks, slots = ids_ref.shape
    block = LANES
    probes = own_ref.shape[0]
    span = own_blocks + 2
    zeros_place = coords_ref.shape[1] // block
    column = lax.axis_index("space")
    north_base = lax.axis_index("knot") * own_blocks - 1
    north_cells = lax.axis_size("knot") * own_blocks
    own_columns = [
        on_grid(jnp.transpose(coordinate_rows(own_ref, own_blocks * block, axis) * TAPER_RATE), grain)
        for axis in range(2)
    ]

    def place(group, slot):
        ahead = ids_ref[group, slot] - (column - 1) * north_cells
        east = jnp.where(ahead >= north_cells, 1, 0) + jnp.where(ahead >= 2 * north_cells, 1, 0)
        strip = jnp.where(east == 1, 0, 1 + lax.rem(column + lax.div(east, 2) + 1, 2))
        index = strip * span + (ahead - east * north_cells - north_base)
        return lanes_of(index), lanes_of(jnp.where(slot < counts_ref[group], index, zeros_place))

    def lanes_of(index):
        return pl.ds(pl.multiple_of(index * block, block), block)

    for index in range(out_ref.shape[1] // block):
        group = first + index
        px, py = [turned[:, group : group + 1] for turned in own_columns]
        total = jnp.zeros((block, 2 * probes), jnp.float32)
        for pair in range(0, slots, 2):
            highs, lows, parts = [], [], []
            for slot in range(pair, min(pair + 2, slots)):
                lanes, value_lanes = place(group, slot)
                dx = px - coords_ref[0:1, lanes]
                dy = py - coords_ref[1:2, lanes]
                high, low = halves(covariance(dx * dx + dy * dy))
                highs.append(high)
                lows.append(low)
                parts.append(values_ref[:, value_lanes])
            part = jnp.concatenate(parts, axis=1)
            total = total + (
                dot_nt(jnp.concatenate(highs, axis=1), part) + dot_nt(jnp.concatenate(lows, axis=1), part)
            )
        out_ref[:, index * block : (index + 1) * block] = (
            TAPER_SCALE * folded_columns(total, probes)
            + NUGGET * own_ref[:, group * block : (group + 1) * block]
        )


def taper(ids, counts, own, values, coords, extent, first, blocks, after):
    slots = ids.shape[1]
    return pl.pallas_call(
        functools.partial(taper_kernel, first, grain_of(TAPER_RATE * extent)),
        out_shape=jax.ShapeDtypeStruct((own.shape[0], blocks * LANES), jnp.float32),
        in_specs=[SMEM, SMEM, VMEM, VMEM, VMEM] + [ANY] * len(after),
        out_specs=VMEM,
        compiler_params=pltpu.CompilerParams(vmem_limit_bytes=LIMIT),
        cost_estimate=cost(500, blocks * slots * LANES * LANES, 2),
        name="taper",
    )(ids, counts, own, values, coords, *after)


def add_kernel(count, copies, *refs):
    if count:
        total = refs[0][...]
        for ref in refs[1:count]:
            total = total + ref[...]
    else:
        total = jnp.sum(refs[0][...], axis=0)
    if copies:
        for index in range(copies):
            refs[-1][index] = total
    else:
        refs[-1][...] = total


def add_all(values, after, copies):
    shape = values[0].shape[-2:]
    return pl.pallas_call(
        functools.partial(add_kernel, len(values) if values[0].ndim == 2 else 0, copies),
        out_shape=jax.ShapeDtypeStruct((copies, *shape) if copies else shape, jnp.float32),
        in_specs=[VMEM] * len(values) + [ANY] * len(after),
        out_specs=VMEM,
        compiler_params=pltpu.CompilerParams(vmem_limit_bytes=LIMIT),
        name="add",
    )(*values, *after)


def butterfly_rounds(count):
    assert count & (count - 1) == 0
    bits = [1 << i for i in range(count.bit_length() - 1)]
    return [tuple(bits[i : i + 2]) for i in range(0, len(bits), 2)]


def round_groups(count, groups, turn):
    rounds = butterfly_rounds(count)
    half = len(rounds) // 2 if len({len(steps) for steps in rounds}) == 1 else 0
    found = []
    for j in range(groups):
        members = [0]
        for step in rounds[(turn + half * (j % 2)) % len(rounds)]:
            members += [member | step for member in members]
        found += [[(i | m) * groups + j for m in members] for i in range(count) if not i & members[-1]]
    return found


def shifted(value, axis, step):
    count = lax.axis_size(axis)
    if step % count == 0:
        return value
    return lax.ppermute(value, axis, [((i + step) % count, i) for i in range(count)])


def paired(value, axis, other, first):
    count, groups = lax.axis_size(axis), lax.axis_size(other)
    partner = {}
    for i in range(first, count - 1, 2):
        partner[i], partner[i + 1] = i + 1, i
    pairs = []
    for i in range(count):
        for j in range(groups):
            if i in partner:
                pairs.append((i * groups + j, partner[i] * groups + j))
            elif j ^ 1 < groups:
                pairs.append((i * groups + j, i * groups + (j ^ 1)))
    return lax.ppermute(value, (axis, other), pairs)


def shards(probes, locations, knot_locs, knot_precision, neighbours, counts):
    own_blocks = neighbours.shape[0]
    row_count = probes.shape[1]
    knot_total = knot_precision.shape[1]
    device_count = lax.axis_size(("space", "knot"))
    groups = lax.axis_size("knot")
    knot_range = KNOT_REACH * math.sqrt(own_blocks * device_count / knot_total)
    proj_scale = PROJ_GAIN * math.sqrt(knot_total / (row_count * device_count))

    stack, knots = prepare(probes, locations, knot_locs, own_blocks)
    chunks = [shifted(stack, "knot", step) for step in range(groups)]
    rate = LOG2E / knot_range
    extent = CELL * max(lax.axis_size("space"), groups * own_blocks)
    parts = [project(chunk, knots, rate, extent) for chunk in chunks]
    stack = parts[0][3]

    strip = make_strip(chunks[-1], stack, chunks[1 % groups])
    values, coords = assemble([strip, paired(strip, "space", "knot", 0), paired(strip, "space", "knot", 1)], extent)
    space, rounds = lax.axis_size("space"), len(butterfly_rounds(lax.axis_size("space")))
    sizes = [1 << len(steps) for steps in butterfly_rounds(space)]
    projection = add_all([part[0] for part in parts], [], sizes[0])
    pieces = math.gcd(own_blocks, rounds)
    per_piece = own_blocks // pieces
    row_pieces = math.gcd(knot_precision.shape[0] // LANES, rounds)
    per_split = knot_precision.shape[0] // row_pieces
    base, splits = [], []
    for turn in range(rounds):
        got = lax.all_to_all(
            projection, ("space", "knot"), 0, 0, axis_index_groups=round_groups(space, groups, turn), tiled=True
        )
        beside = []
        for i in range(pieces):
            if i * rounds // pieces == turn:
                base.append(
                    taper(
                        neighbours, counts, stack, values, coords, extent, i * per_piece, per_piece, [projection]
                    )
                )
                beside.append(base[-1])
        for i in range(row_pieces):
            if i * rounds // row_pieces == turn:
                splits.append(split_rows(knot_precision, i * per_split, per_split, [projection]))
                beside.extend(splits[-1])
        projection = add_all([got], beside, sizes[turn + 1] if turn + 1 < rounds else 0)
    factor = factored(None, projection, splits, proj_scale, 0)
    for step in range(1, groups):
        factor = factored(factor, shifted(projection, "knot", step), splits, proj_scale, step)
    total = jnp.concatenate(base, axis=1)
    for step in reversed(range(groups)):
        share = spread(factor, parts[step][1], parts[step][2], LOW_SCALE * EXPAND_GAIN)
        total = total + shifted(share, "knot", -step)
    return total


def solution(mesh):
    return jax.shard_map(
        shards,
        mesh=mesh,
        in_specs=(
            P(None, ("space", "knot")),
            P(None, ("space", "knot")),
            P(None, "knot"),
            P("knot", None),
            P(("space", "knot"), None),
            P(("space", "knot")),
        ),
        out_specs=P(None, ("space", "knot")),
        check_vma=False,
    )
```

```python
import functools
import math

import jax
import jax.numpy as jnp
from jax import lax
from jax.experimental import pallas as pl
from jax.experimental.pallas import tpu as pltpu
from jax.sharding import PartitionSpec as P

COV_RANGE = 0.05
TAPER_LEN = 0.15
KNOT_REACH = 0.15
TAPER_SCALE = 0.1
PROJ_GAIN = 0.5
EXPAND_GAIN = 0.5
LOW_SCALE = 0.5
NUGGET = 0.25
LOG2E = math.log2(math.e)
TAPER_RATE = LOG2E / COV_RANGE
CELL = 0.1
TILE = 256
LANES = 128
HALF_GRAIN = 2.0**-24
LIMIT = 6 * 1024 * 1024
VMEM = pl.BlockSpec(memory_space=pltpu.VMEM)
HBM = pl.BlockSpec(memory_space=pltpu.HBM)
ANY = pl.BlockSpec(memory_space=pl.ANY)
SMEM = pl.BlockSpec(memory_space=pltpu.SMEM)


def halves(x):
    high = x.astype(jnp.bfloat16)
    return high, (x - high.astype(jnp.float32)).astype(jnp.bfloat16)


def stacked_halves(x):
    return jnp.concatenate(halves(x), axis=0)


def folded(x):
    rows = x.shape[0] // 2
    return x[:rows] + x[rows:]


def dot_nt(left, right):
    return lax.dot_general(
        left, right, (((1,), (1,)), ((), ())), preferred_element_type=jnp.float32
    )


def dot_nn(left, right):
    return jnp.dot(left, right, preferred_element_type=jnp.float32)


def padded_halves(x, rows):
    fill = jnp.zeros((rows - 2 * x.shape[0], x.shape[1]), jnp.bfloat16)
    return jnp.concatenate([*halves(x), fill], axis=0)


def folded_columns(x, rows):
    x = jnp.transpose(x)
    return x[:rows] + x[rows : 2 * rows]


def cost(work, pairs, transcendentals=0):
    return pl.CostEstimate(flops=work * pairs, bytes_accessed=4 * pairs, transcendentals=transcendentals * pairs)


def coordinate_rows(ref, points, axis):
    start = points + axis * LANES
    return ref[:, start : start + LANES]


def prepare_kernel(blocks, probes_ref, locations_ref, knots_ref, stack_ref, knots_out_ref, coords, sems):
    points = probes_ref.shape[1]
    block = points // blocks
    copies = [
        pltpu.make_async_copy(probes_ref, stack_ref.at[:, pl.ds(0, points)], sems.at[0]),
        pltpu.make_async_copy(locations_ref, coords, sems.at[1]),
        pltpu.make_async_copy(knots_ref, knots_out_ref, sems.at[2]),
    ]
    for copy in copies:
        copy.start()
    for copy in copies:
        copy.wait()
    stack_ref[:, points:] = jnp.zeros((stack_ref.shape[0], 2 * LANES), jnp.float32)
    for axis in range(2):
        lanes = slice(points + axis * LANES, points + (axis + 1) * LANES)
        for index in range(blocks):
            stack_ref[index : index + 1, lanes] = coords[axis : axis + 1, index * block : (index + 1) * block]


def prepare(probes, locations, knot_locs, blocks):
    rows, points = probes.shape
    assert points == blocks * LANES and blocks + 2 <= rows
    probes, locations, knot_locs = [
        pltpu.with_memory_space_constraint(x, pltpu.HBM) for x in (probes, locations, knot_locs)
    ]
    return pl.pallas_call(
        functools.partial(prepare_kernel, blocks),
        out_shape=(
            jax.ShapeDtypeStruct((rows, points + 2 * LANES), jnp.float32),
            jax.ShapeDtypeStruct(knot_locs.shape, jnp.float32),
        ),
        in_specs=[HBM, HBM, HBM],
        out_specs=(VMEM, VMEM),
        scratch_shapes=[pltpu.VMEM(locations.shape, jnp.float32), pltpu.SemaphoreType.DMA((3,))],
        compiler_params=pltpu.CompilerParams(vmem_limit_bytes=LIMIT),
        name="prepare",
    )(probes, locations, knot_locs)


def strip_kernel(below_ref, own_ref, above_ref, out_ref):
    rows, width = own_ref.shape
    points = width - 2 * LANES
    blocks = points // LANES
    out_ref[:, :LANES] = below_ref[:, points - LANES : points]
    out_ref[:, LANES : points + LANES] = own_ref[:, :points]
    out_ref[:, points + LANES : points + 2 * LANES] = above_ref[:, :LANES]
    for axis in range(2):
        lanes = slice(points + axis * LANES, points + (axis + 1) * LANES)
        target = slice(lanes.start + 2 * LANES, lanes.stop + 2 * LANES)
        out_ref[:, target] = jnp.zeros((rows, LANES), jnp.float32)
        out_ref[0:1, target] = below_ref[blocks - 1 : blocks, lanes]
        out_ref[1 : blocks + 1, target] = own_ref[:blocks, lanes]
        out_ref[blocks + 1 : blocks + 2, target] = above_ref[0:1, lanes]


def make_strip(below, own, above):
    return pl.pallas_call(
        strip_kernel,
        out_shape=jax.ShapeDtypeStruct((own.shape[0], own.shape[1] + 2 * LANES), jnp.float32),
        in_specs=[VMEM, VMEM, VMEM],
        out_specs=VMEM,
        compiler_params=pltpu.CompilerParams(vmem_limit_bytes=LIMIT),
        name="strip",
    )(below, own, above)


def assemble_kernel(grain, own_ref, east_ref, west_ref, values_ref, coords_ref):
    probes, width = own_ref.shape
    points = width - 2 * LANES
    for turn, ref in enumerate((own_ref, east_ref, west_ref)):
        start = turn * points
        values_ref[:, start : start + points] = stacked_halves(ref[:, :points] * (1.0 / 256.0))
        for axis in range(2):
            rows = off_grid(coordinate_rows(ref, points, axis) * TAPER_RATE, grain)
            for index in range(points // LANES):
                lanes = slice(start + index * LANES, start + (index + 1) * LANES)
                coords_ref[axis : axis + 1, lanes] = rows[index : index + 1]
    values_ref[:, 3 * points :] = jnp.zeros((2 * probes, LANES), jnp.bfloat16)


def assemble(strips, extent):
    probes, width = strips[0].shape
    near = 3 * (width - 2 * LANES)
    return pl.pallas_call(
        functools.partial(assemble_kernel, grain_of(TAPER_RATE * extent)),
        out_shape=(
            jax.ShapeDtypeStruct((2 * probes, near + LANES), jnp.bfloat16),
            jax.ShapeDtypeStruct((2, near), jnp.float32),
        ),
        in_specs=[VMEM] * 3,
        out_specs=(VMEM, VMEM),
        compiler_params=pltpu.CompilerParams(vmem_limit_bytes=LIMIT),
        name="assemble",
    )(*strips)


def grain_of(bound):
    return 2.0 ** math.ceil(math.log2(1.01 * bound))


def on_grid(x, grain):
    return (x + grain) - grain


def off_grid(x, grain):
    return (x + grain) - (grain - grain * HALF_GRAIN)


def project_kernel(scale, grain, stack_ref, knots_ref, out_ref, high_ref, low_ref, copy_ref, weights, columns):
    knots, points = high_ref.shape
    probes = stack_ref.shape[0]
    tile = min(TILE, knots)
    copy_ref[...] = stack_ref[...]
    weights[...] = padded_halves(stack_ref[:, :points], weights.shape[0])
    fill = jnp.zeros((6, knots), jnp.float32)
    columns[...] = jnp.transpose(jnp.concatenate([off_grid(knots_ref[...] * scale, grain), fill], axis=0))
    east, north = [on_grid(coordinate_rows(stack_ref, points, axis) * scale, grain) for axis in range(2)]

    for start in range(0, knots, tile):
        rows = slice(start, start + tile)
        kx, ky = [columns[rows, axis : axis + 1] for axis in range(2)]
        for block in range(points // LANES):
            lanes = slice(block * LANES, (block + 1) * LANES)
            dx = east[block : block + 1, :] - kx
            dy = north[block : block + 1, :] - ky
            square = dx * dx + dy * dy
            high_ref[rows, lanes], low_ref[rows, lanes] = halves(jnp.exp2(-(square * lax.rsqrt(square))))
        total = dot_nt(high_ref[rows, :], weights[...]) + dot_nt(low_ref[rows, :], weights[...])
        out_ref[:, rows] = folded_columns(total, probes)


def project(stack, knot_locs, scale, extent):
    probes, points, knots = stack.shape[0], stack.shape[1] - 2 * LANES, knot_locs.shape[1]
    return pl.pallas_call(
        functools.partial(project_kernel, scale, grain_of(scale * extent)),
        out_shape=(
            jax.ShapeDtypeStruct((probes, knots), jnp.float32),
            pltpu.VMEM((knots, points), jnp.bfloat16),
            pltpu.VMEM((knots, points), jnp.bfloat16),
            jax.ShapeDtypeStruct(stack.shape, jnp.float32),
        ),
        in_specs=[VMEM, VMEM],
        out_specs=(VMEM, VMEM, VMEM, VMEM),
        scratch_shapes=[
            pltpu.VMEM((LANES, points), jnp.bfloat16),
            pltpu.VMEM((knots, 8), jnp.float32),
        ],
        compiler_params=pltpu.CompilerParams(vmem_limit_bytes=LIMIT),
        cost_estimate=cost(2800, points * knots, 2),
        name="project",
    )(stack, knot_locs)


def split_kernel(first, precision_ref, *rest):
    high_ref, low_ref = rest[-2:]
    rows = high_ref.shape[0]
    tile = min(TILE, rows)
    for start in range(0, rows, tile):
        here = slice(start, start + tile)
        high_ref[here, :], low_ref[here, :] = halves(precision_ref[first + start : first + start + tile, :])


def split_rows(precision, first, rows, after):
    depth = precision.shape[1]
    return pl.pallas_call(
        functools.partial(split_kernel, first),
        out_shape=(pltpu.VMEM((rows, depth), jnp.bfloat16), pltpu.VMEM((rows, depth), jnp.bfloat16)),
        in_specs=[VMEM] + [ANY] * len(after),
        out_specs=(VMEM, VMEM),
        compiler_params=pltpu.CompilerParams(vmem_limit_bytes=LIMIT),
        cost_estimate=cost(60, rows * depth),
        name="split",
    )(precision, *after)


def factor_kernel(scale, step, parts, before_ref, proj_ref, *rest):
    highs, lows, (out_ref, weights) = rest[:parts], rest[parts : 2 * parts], rest[-2:]
    probes, depth = proj_ref.shape
    weights[...] = stacked_halves(proj_ref[...] * scale)
    owner = lax.rem(lax.axis_index("knot") + step, lax.axis_size("knot"))
    lanes = pl.ds(pl.multiple_of(owner * depth, depth), depth)
    rows = highs[0].shape[0]
    tile = min(TILE, rows)
    for part, (high_ref, low_ref) in enumerate(zip(highs, lows)):
        for start in range(0, rows, tile):
            here = slice(start, start + tile)
            found = folded(dot_nt(weights[...], high_ref[here, lanes]) + dot_nt(weights[...], low_ref[here, lanes]))
            target = slice(part * rows + start, part * rows + start + tile)
            if before_ref is not None:
                found = found + before_ref[:, target]
            out_ref[:, target] = found


def factored(before, projection, splits, scale, step):
    probes, depth = projection.shape
    highs, lows = [
        [pltpu.with_memory_space_constraint(split[half], pltpu.VMEM) for split in splits] for half in range(2)
    ]
    rows = sum(high.shape[0] for high in highs)
    kernel = functools.partial(factor_kernel, scale, step, len(splits))
    operands = (projection, *highs, *lows)
    if before is None:
        kernel = functools.partial(kernel, None)
    else:
        operands = (before, *operands)
    return pl.pallas_call(
        kernel,
        out_shape=jax.ShapeDtypeStruct((probes, rows), jnp.float32),
        in_specs=[VMEM] * len(operands),
        out_specs=VMEM,
        scratch_shapes=[pltpu.VMEM((2 * probes, depth), jnp.bfloat16)],
        compiler_params=pltpu.CompilerParams(vmem_limit_bytes=LIMIT),
        cost_estimate=cost(1000, rows * depth),
        name="factor",
    )(*operands)


def spread_kernel(scale, factor_ref, high_ref, low_ref, out_ref):
    points = high_ref.shape[1]
    tile = min(TILE, points)
    weights = stacked_halves(factor_ref[...] * scale)
    for start in range(0, points, tile):
        lanes = slice(start, start + tile)
        out_ref[:, lanes] = folded(dot_nn(weights, high_ref[:, lanes]) + dot_nn(weights, low_ref[:, lanes]))


def spread(factor, high, low, scale):
    (probes, knots), points = factor.shape, high.shape[1]
    high = pltpu.with_memory_space_constraint(high, pltpu.VMEM)
    low = pltpu.with_memory_space_constraint(low, pltpu.VMEM)
    return pl.pallas_call(
        functools.partial(spread_kernel, scale),
        out_shape=jax.ShapeDtypeStruct((probes, points), jnp.float32),
        in_specs=[VMEM, VMEM, VMEM],
        out_specs=VMEM,
        compiler_params=pltpu.CompilerParams(vmem_limit_bytes=LIMIT),
        cost_estimate=cost(850, knots * points),
        name="spread",
    )(factor, high, low)


def covariance(square):
    apart = square * lax.rsqrt(square)
    remain = jnp.maximum(4.0 - apart * (4.0 / (TAPER_LEN * TAPER_RATE)), 0.0)
    twice = remain * remain
    return (jnp.exp2(-apart) * (twice * twice)) * (5.0 - remain)


def taper_kernel(first, grain, ids_ref, counts_ref, own_ref, values_ref, coords_ref, *rest):
    out_ref = rest[-1]
    own_blocks, slots = ids_ref.shape
    block = LANES
    probes = own_ref.shape[0]
    span = own_blocks + 2
    zeros_place = coords_ref.shape[1] // block
    column = lax.axis_index("space")
    north_base = lax.axis_index("knot") * own_blocks - 1
    north_cells = lax.axis_size("knot") * own_blocks
    own_columns = [
        on_grid(jnp.transpose(coordinate_rows(own_ref, own_blocks * block, axis) * TAPER_RATE), grain)
        for axis in range(2)
    ]

    def place(group, slot):
        ahead = ids_ref[group, slot] - (column - 1) * north_cells
        east = jnp.where(ahead >= north_cells, 1, 0) + jnp.where(ahead >= 2 * north_cells, 1, 0)
        strip = jnp.where(east == 1, 0, 1 + lax.rem(column + lax.div(east, 2) + 1, 2))
        index = strip * span + (ahead - east * north_cells - north_base)
        return lanes_of(index), lanes_of(jnp.where(slot < counts_ref[group], index, zeros_place))

    def lanes_of(index):
        return pl.ds(pl.multiple_of(index * block, block), block)

    for index in range(out_ref.shape[1] // block):
        group = first + index
        px, py = [turned[:, group : group + 1] for turned in own_columns]
        total = jnp.zeros((block, 2 * probes), jnp.float32)
        for pair in range(0, slots, 2):
            highs, lows, parts = [], [], []
            for slot in range(pair, min(pair + 2, slots)):
                lanes, value_lanes = place(group, slot)
                dx = px - coords_ref[0:1, lanes]
                dy = py - coords_ref[1:2, lanes]
                high, low = halves(covariance(dx * dx + dy * dy))
                highs.append(high)
                lows.append(low)
                parts.append(values_ref[:, value_lanes])
            part = jnp.concatenate(parts, axis=1)
            total = total + (
                dot_nt(jnp.concatenate(highs, axis=1), part) + dot_nt(jnp.concatenate(lows, axis=1), part)
            )
        out_ref[:, index * block : (index + 1) * block] = (
            TAPER_SCALE * folded_columns(total, probes)
            + NUGGET * own_ref[:, group * block : (group + 1) * block]
        )


def taper(ids, counts, own, values, coords, extent, first, blocks, after):
    slots = ids.shape[1]
    return pl.pallas_call(
        functools.partial(taper_kernel, first, grain_of(TAPER_RATE * extent)),
        out_shape=jax.ShapeDtypeStruct((own.shape[0], blocks * LANES), jnp.float32),
        in_specs=[SMEM, SMEM, VMEM, VMEM, VMEM] + [ANY] * len(after),
        out_specs=VMEM,
        compiler_params=pltpu.CompilerParams(vmem_limit_bytes=LIMIT),
        cost_estimate=cost(500, blocks * slots * LANES * LANES, 2),
        name="taper",
    )(ids, counts, own, values, coords, *after)


def add_kernel(count, *refs):
    total = refs[0][...]
    for ref in refs[1:count]:
        total = total + ref[...]
    refs[-1][...] = total


def add_all(values, after):
    return pl.pallas_call(
        functools.partial(add_kernel, len(values)),
        out_shape=jax.ShapeDtypeStruct(values[0].shape, jnp.float32),
        in_specs=[VMEM] * len(values) + [ANY] * len(after),
        out_specs=VMEM,
        compiler_params=pltpu.CompilerParams(vmem_limit_bytes=LIMIT),
        name="add",
    )(*values, *after)


def butterfly_rounds(count):
    assert count & (count - 1) == 0
    bits = [1 << i for i in range(count.bit_length() - 1)]
    rounds = [(low | high, high, low) for low, high in zip(bits[0::2], bits[1::2])]
    return rounds + [(bit,) for bit in bits[len(rounds) * 2 :]]


def butterfly_round(value, axis, other, turn):
    count, groups = lax.axis_size(axis), lax.axis_size(other)
    rounds = butterfly_rounds(count)
    half = len(rounds) // 2 if len({len(steps) for steps in rounds}) == 1 else 0
    got = []
    for kind in range(len(rounds[turn])):
        pairs = []
        for j in range(groups):
            step = rounds[(turn + half * (j % 2)) % len(rounds)][kind]
            pairs += [(i * groups + j, (i ^ step) * groups + j) for i in range(count)]
        got.append(lax.ppermute(value, (axis, other), pairs))
    return got


def shifted(value, axis, step):
    count = lax.axis_size(axis)
    if step % count == 0:
        return value
    return lax.ppermute(value, axis, [((i + step) % count, i) for i in range(count)])


def paired(value, axis, other, first):
    count, groups = lax.axis_size(axis), lax.axis_size(other)
    partner = {}
    for i in range(first, count - 1, 2):
        partner[i], partner[i + 1] = i + 1, i
    pairs = []
    for i in range(count):
        for j in range(groups):
            if i in partner:
                pairs.append((i * groups + j, partner[i] * groups + j))
            elif j ^ 1 < groups:
                pairs.append((i * groups + j, i * groups + (j ^ 1)))
    return lax.ppermute(value, (axis, other), pairs)


def shards(probes, locations, knot_locs, knot_precision, neighbours, counts):
    own_blocks = neighbours.shape[0]
    row_count = probes.shape[1]
    knot_total = knot_precision.shape[1]
    device_count = lax.axis_size(("space", "knot"))
    groups = lax.axis_size("knot")
    knot_range = KNOT_REACH * math.sqrt(own_blocks * device_count / knot_total)
    proj_scale = PROJ_GAIN * math.sqrt(knot_total / (row_count * device_count))

    stack, knots = prepare(probes, locations, knot_locs, own_blocks)
    chunks = [shifted(stack, "knot", step) for step in range(groups)]
    rate = LOG2E / knot_range
    extent = CELL * max(lax.axis_size("space"), groups * own_blocks)
    parts = [project(chunk, knots, rate, extent) for chunk in chunks]
    stack = parts[0][3]

    strip = make_strip(chunks[-1], stack, chunks[1 % groups])
    values, coords = assemble([strip, paired(strip, "space", "knot", 0), paired(strip, "space", "knot", 1)], extent)
    projection = sum(part[0] for part in parts)
    rounds = len(butterfly_rounds(lax.axis_size("space")))
    pieces = math.gcd(own_blocks, rounds)
    per_piece = own_blocks // pieces
    row_pieces = math.gcd(knot_precision.shape[0] // LANES, rounds)
    per_split = knot_precision.shape[0] // row_pieces
    base, splits = [], []
    for turn in range(rounds):
        got = butterfly_round(projection, "space", "knot", turn)
        beside = []
        for i in range(pieces):
            if i * rounds // pieces == turn:
                base.append(
                    taper(
                        neighbours, counts, stack, values, coords, extent, i * per_piece, per_piece, [projection]
                    )
                )
                beside.append(base[-1])
        for i in range(row_pieces):
            if i * rounds // row_pieces == turn:
                splits.append(split_rows(knot_precision, i * per_split, per_split, [projection]))
                beside.extend(splits[-1])
        projection = add_all([projection, *got], beside)
    factor = factored(None, projection, splits, proj_scale, 0)
    for step in range(1, groups):
        factor = factored(factor, shifted(projection, "knot", step), splits, proj_scale, step)
    total = jnp.concatenate(base, axis=1)
    for step in reversed(range(groups)):
        share = spread(factor, parts[step][1], parts[step][2], LOW_SCALE * EXPAND_GAIN)
        total = total + shifted(share, "knot", -step)
    return total


def solution(mesh):
    return jax.shard_map(
        shards,
        mesh=mesh,
        in_specs=(
            P(None, ("space", "knot")),
            P(None, ("space", "knot")),
            P(None, "knot"),
            P("knot", None),
            P(("space", "knot"), None),
            P(("space", "knot")),
        ),
        out_specs=P(None, ("space", "knot")),
        check_vma=False,
    )
```

```python
import functools
import math

import jax
import jax.numpy as jnp
from jax import lax
from jax.experimental import pallas as pl
from jax.experimental.pallas import tpu as pltpu
from jax.sharding import PartitionSpec as P

COV_RANGE = 0.05
TAPER_LEN = 0.15
KNOT_REACH = 0.15
TAPER_SCALE = 0.1
PROJ_GAIN = 0.5
EXPAND_GAIN = 0.5
LOW_SCALE = 0.5
NUGGET = 0.25
LOG2E = math.log2(math.e)
TAPER_RATE = LOG2E / COV_RANGE
CELL = 0.1
TILE = 256
LANES = 128
HALF_GRAIN = 2.0**-24
LIMIT = 6 * 1024 * 1024
VMEM = pl.BlockSpec(memory_space=pltpu.VMEM)
HBM = pl.BlockSpec(memory_space=pltpu.HBM)
ANY = pl.BlockSpec(memory_space=pl.ANY)
SMEM = pl.BlockSpec(memory_space=pltpu.SMEM)


def halves(x):
    high = x.astype(jnp.bfloat16)
    return high, (x - high.astype(jnp.float32)).astype(jnp.bfloat16)


def stacked_halves(x):
    return jnp.concatenate(halves(x), axis=0)


def folded(x):
    rows = x.shape[0] // 2
    return x[:rows] + x[rows:]


def dot_nt(left, right):
    return lax.dot_general(
        left, right, (((1,), (1,)), ((), ())), preferred_element_type=jnp.float32
    )


def dot_nn(left, right):
    return jnp.dot(left, right, preferred_element_type=jnp.float32)


def padded_halves(x, rows):
    fill = jnp.zeros((rows - 2 * x.shape[0], x.shape[1]), jnp.bfloat16)
    return jnp.concatenate([*halves(x), fill], axis=0)


def folded_columns(x, rows):
    x = jnp.transpose(x)
    return x[:rows] + x[rows : 2 * rows]


def cost(work, pairs, transcendentals=0):
    return pl.CostEstimate(flops=work * pairs, bytes_accessed=4 * pairs, transcendentals=transcendentals * pairs)


def coordinate_rows(ref, points, axis):
    start = points + axis * LANES
    return ref[:, start : start + LANES]


def prepare_kernel(blocks, probes_ref, locations_ref, knots_ref, stack_ref, knots_out_ref, coords, sems):
    points = probes_ref.shape[1]
    block = points // blocks
    copies = [
        pltpu.make_async_copy(probes_ref, stack_ref.at[:, pl.ds(0, points)], sems.at[0]),
        pltpu.make_async_copy(locations_ref, coords, sems.at[1]),
        pltpu.make_async_copy(knots_ref, knots_out_ref, sems.at[2]),
    ]
    for copy in copies:
        copy.start()
    for copy in copies:
        copy.wait()
    stack_ref[:, points:] = jnp.zeros((stack_ref.shape[0], 2 * LANES), jnp.float32)
    for axis in range(2):
        lanes = slice(points + axis * LANES, points + (axis + 1) * LANES)
        for index in range(blocks):
            stack_ref[index : index + 1, lanes] = coords[axis : axis + 1, index * block : (index + 1) * block]


def prepare(probes, locations, knot_locs, blocks):
    rows, points = probes.shape
    assert points == blocks * LANES and blocks + 2 <= rows
    probes, locations, knot_locs = [
        pltpu.with_memory_space_constraint(x, pltpu.HBM) for x in (probes, locations, knot_locs)
    ]
    return pl.pallas_call(
        functools.partial(prepare_kernel, blocks),
        out_shape=(
            jax.ShapeDtypeStruct((rows, points + 2 * LANES), jnp.float32),
            jax.ShapeDtypeStruct(knot_locs.shape, jnp.float32),
        ),
        in_specs=[HBM, HBM, HBM],
        out_specs=(VMEM, VMEM),
        scratch_shapes=[pltpu.VMEM(locations.shape, jnp.float32), pltpu.SemaphoreType.DMA((3,))],
        compiler_params=pltpu.CompilerParams(vmem_limit_bytes=LIMIT),
        name="prepare",
    )(probes, locations, knot_locs)


def strip_kernel(below_ref, own_ref, above_ref, out_ref):
    rows, width = own_ref.shape
    points = width - 2 * LANES
    blocks = points // LANES
    out_ref[:, :LANES] = below_ref[:, points - LANES : points]
    out_ref[:, LANES : points + LANES] = own_ref[:, :points]
    out_ref[:, points + LANES : points + 2 * LANES] = above_ref[:, :LANES]
    for axis in range(2):
        lanes = slice(points + axis * LANES, points + (axis + 1) * LANES)
        target = slice(lanes.start + 2 * LANES, lanes.stop + 2 * LANES)
        out_ref[:, target] = jnp.zeros((rows, LANES), jnp.float32)
        out_ref[0:1, target] = below_ref[blocks - 1 : blocks, lanes]
        out_ref[1 : blocks + 1, target] = own_ref[:blocks, lanes]
        out_ref[blocks + 1 : blocks + 2, target] = above_ref[0:1, lanes]


def make_strip(below, own, above):
    return pl.pallas_call(
        strip_kernel,
        out_shape=jax.ShapeDtypeStruct((own.shape[0], own.shape[1] + 2 * LANES), jnp.float32),
        in_specs=[VMEM, VMEM, VMEM],
        out_specs=VMEM,
        compiler_params=pltpu.CompilerParams(vmem_limit_bytes=LIMIT),
        name="strip",
    )(below, own, above)


def assemble_kernel(grain, own_ref, east_ref, west_ref, values_ref, coords_ref):
    probes, width = own_ref.shape
    points = width - 2 * LANES
    for turn, ref in enumerate((own_ref, east_ref, west_ref)):
        start = turn * points
        values_ref[:, start : start + points] = stacked_halves(ref[:, :points] * (1.0 / 256.0))
        for axis in range(2):
            rows = off_grid(coordinate_rows(ref, points, axis) * TAPER_RATE, grain)
            for index in range(points // LANES):
                lanes = slice(start + index * LANES, start + (index + 1) * LANES)
                coords_ref[axis : axis + 1, lanes] = rows[index : index + 1]
    values_ref[:, 3 * points :] = jnp.zeros((2 * probes, LANES), jnp.bfloat16)


def assemble(strips, extent):
    probes, width = strips[0].shape
    near = 3 * (width - 2 * LANES)
    return pl.pallas_call(
        functools.partial(assemble_kernel, grain_of(TAPER_RATE * extent)),
        out_shape=(
            jax.ShapeDtypeStruct((2 * probes, near + LANES), jnp.bfloat16),
            jax.ShapeDtypeStruct((2, near), jnp.float32),
        ),
        in_specs=[VMEM] * 3,
        out_specs=(VMEM, VMEM),
        compiler_params=pltpu.CompilerParams(vmem_limit_bytes=LIMIT),
        name="assemble",
    )(*strips)


def grain_of(bound):
    return 2.0 ** math.ceil(math.log2(1.01 * bound))


def on_grid(x, grain):
    return (x + grain) - grain


def off_grid(x, grain):
    return (x + grain) - (grain - grain * HALF_GRAIN)


def project_kernel(scale, grain, stack_ref, knots_ref, out_ref, high_ref, low_ref, *rest):
    *copies, weights, columns = rest
    knots, points = high_ref.shape
    probes = stack_ref.shape[0]
    tile = min(TILE, knots)
    for copy_ref in copies:
        copy_ref[...] = stack_ref[...]
    weights[...] = padded_halves(stack_ref[:, :points], weights.shape[0])
    fill = jnp.zeros((6, knots), jnp.float32)
    columns[...] = jnp.transpose(jnp.concatenate([off_grid(knots_ref[...] * scale, grain), fill], axis=0))
    east, north = [on_grid(coordinate_rows(stack_ref, points, axis) * scale, grain) for axis in range(2)]

    for start in range(0, knots, tile):
        rows = slice(start, start + tile)
        kx, ky = [columns[rows, axis : axis + 1] for axis in range(2)]
        for block in range(points // LANES):
            lanes = slice(block * LANES, (block + 1) * LANES)
            dx = east[block : block + 1, :] - kx
            dy = north[block : block + 1, :] - ky
            square = dx * dx + dy * dy
            high_ref[rows, lanes], low_ref[rows, lanes] = halves(jnp.exp2(-(square * lax.rsqrt(square))))
        total = dot_nt(high_ref[rows, :], weights[...]) + dot_nt(low_ref[rows, :], weights[...])
        out_ref[:, rows] = folded_columns(total, probes)


def project(stack, knot_locs, scale, extent, copies):
    probes, points, knots = stack.shape[0], stack.shape[1] - 2 * LANES, knot_locs.shape[1]
    return pl.pallas_call(
        functools.partial(project_kernel, scale, grain_of(scale * extent)),
        out_shape=(
            jax.ShapeDtypeStruct((probes, knots), jnp.float32),
            pltpu.VMEM((knots, points), jnp.bfloat16),
            pltpu.VMEM((knots, points), jnp.bfloat16),
            *[jax.ShapeDtypeStruct(stack.shape, jnp.float32)] * copies,
        ),
        in_specs=[VMEM, VMEM],
        out_specs=(VMEM,) * (3 + copies),
        scratch_shapes=[
            pltpu.VMEM((LANES, points), jnp.bfloat16),
            pltpu.VMEM((knots, 8), jnp.float32),
        ],
        compiler_params=pltpu.CompilerParams(vmem_limit_bytes=LIMIT),
        cost_estimate=cost(2800, points * knots, 2),
        name="project",
    )(stack, knot_locs)


def split_kernel(first, precision_ref, *rest):
    high_ref, low_ref = rest[-2:]
    depth, rows = high_ref.shape
    tile = min(TILE, rows)
    wide = min(TILE, depth)
    for start in range(0, rows, tile):
        for deep in range(0, depth, wide):
            turned = jnp.transpose(precision_ref[first + start : first + start + tile, deep : deep + wide])
            here = slice(deep, deep + wide), slice(start, start + tile)
            high_ref[here], low_ref[here] = halves(turned)


def split_rows(precision, first, rows, after):
    depth = precision.shape[1]
    return pl.pallas_call(
        functools.partial(split_kernel, first),
        out_shape=(pltpu.VMEM((depth, rows), jnp.bfloat16), pltpu.VMEM((depth, rows), jnp.bfloat16)),
        in_specs=[VMEM] + [ANY] * len(after),
        out_specs=(VMEM, VMEM),
        compiler_params=pltpu.CompilerParams(vmem_limit_bytes=LIMIT),
        cost_estimate=cost(60, rows * depth),
        name="split",
    )(precision, *after)


def factor_kernel(scale, step, parts, before_ref, proj_ref, *rest):
    highs, lows, (out_ref, weights) = rest[:parts], rest[parts : 2 * parts], rest[-2:]
    probes, depth = proj_ref.shape
    weights[...] = stacked_halves(proj_ref[...] * scale)
    owner = lax.rem(lax.axis_index("knot") + step, lax.axis_size("knot"))
    deep = pl.ds(pl.multiple_of(owner * depth, depth), depth)
    rows = highs[0].shape[1]
    tile = min(TILE, rows)
    for part, (high_ref, low_ref) in enumerate(zip(highs, lows)):
        for start in range(0, rows, tile):
            here = slice(start, start + tile)
            found = folded(dot_nn(weights[...], high_ref[deep, here]) + dot_nn(weights[...], low_ref[deep, here]))
            target = slice(part * rows + start, part * rows + start + tile)
            if before_ref is not None:
                found = found + before_ref[:, target]
            out_ref[:, target] = found


def factored(before, projection, splits, scale, step):
    probes, depth = projection.shape
    highs, lows = [
        [pltpu.with_memory_space_constraint(split[half], pltpu.VMEM) for split in splits] for half in range(2)
    ]
    rows = sum(high.shape[1] for high in highs)
    kernel = functools.partial(factor_kernel, scale, step, len(splits))
    operands = (projection, *highs, *lows)
    if before is None:
        kernel = functools.partial(kernel, None)
    else:
        operands = (before, *operands)
    return pl.pallas_call(
        kernel,
        out_shape=jax.ShapeDtypeStruct((probes, rows), jnp.float32),
        in_specs=[VMEM] * len(operands),
        out_specs=VMEM,
        scratch_shapes=[pltpu.VMEM((2 * probes, depth), jnp.bfloat16)],
        compiler_params=pltpu.CompilerParams(vmem_limit_bytes=LIMIT),
        cost_estimate=cost(1000, rows * depth),
        name="factor",
    )(*operands)


def spread_kernel(scale, factor_ref, high_ref, low_ref, out_ref):
    points = high_ref.shape[1]
    tile = min(TILE, points)
    weights = stacked_halves(factor_ref[...] * scale)
    for start in range(0, points, tile):
        lanes = slice(start, start + tile)
        out_ref[:, lanes] = folded(dot_nn(weights, high_ref[:, lanes]) + dot_nn(weights, low_ref[:, lanes]))


def spread(factor, high, low, scale):
    (probes, knots), points = factor.shape, high.shape[1]
    high = pltpu.with_memory_space_constraint(high, pltpu.VMEM)
    low = pltpu.with_memory_space_constraint(low, pltpu.VMEM)
    return pl.pallas_call(
        functools.partial(spread_kernel, scale),
        out_shape=jax.ShapeDtypeStruct((probes, points), jnp.float32),
        in_specs=[VMEM, VMEM, VMEM],
        out_specs=VMEM,
        compiler_params=pltpu.CompilerParams(vmem_limit_bytes=LIMIT),
        cost_estimate=cost(850, knots * points),
        name="spread",
    )(factor, high, low)


def covariance(square):
    apart = square * lax.rsqrt(square)
    remain = jnp.maximum(4.0 - apart * (4.0 / (TAPER_LEN * TAPER_RATE)), 0.0)
    twice = remain * remain
    return (jnp.exp2(-apart) * (twice * twice)) * (5.0 - remain)


def taper_kernel(first, grain, ids_ref, counts_ref, own_ref, values_ref, coords_ref, *rest):
    out_ref = rest[-1]
    own_blocks, slots = ids_ref.shape
    block = LANES
    probes = own_ref.shape[0]
    span = own_blocks + 2
    zeros_place = coords_ref.shape[1] // block
    column = lax.axis_index("space")
    north_base = lax.axis_index("knot") * own_blocks - 1
    north_cells = lax.axis_size("knot") * own_blocks
    own_columns = [
        on_grid(jnp.transpose(coordinate_rows(own_ref, own_blocks * block, axis) * TAPER_RATE), grain)
        for axis in range(2)
    ]

    def place(group, slot):
        ahead = ids_ref[group, slot] - (column - 1) * north_cells
        east = jnp.where(ahead >= north_cells, 1, 0) + jnp.where(ahead >= 2 * north_cells, 1, 0)
        strip = jnp.where(east == 1, 0, 1 + lax.rem(column + lax.div(east, 2) + 1, 2))
        index = strip * span + (ahead - east * north_cells - north_base)
        return lanes_of(index), lanes_of(jnp.where(slot < counts_ref[group], index, zeros_place))

    def lanes_of(index):
        return pl.ds(pl.multiple_of(index * block, block), block)

    for index in range(out_ref.shape[1] // block):
        group = first + index
        px, py = [turned[:, group : group + 1] for turned in own_columns]
        total = jnp.zeros((block, 2 * probes), jnp.float32)
        for pair in range(0, slots, 2):
            highs, lows, parts = [], [], []
            for slot in range(pair, min(pair + 2, slots)):
                lanes, value_lanes = place(group, slot)
                dx = px - coords_ref[0:1, lanes]
                dy = py - coords_ref[1:2, lanes]
                high, low = halves(covariance(dx * dx + dy * dy))
                highs.append(high)
                lows.append(low)
                parts.append(values_ref[:, value_lanes])
            part = jnp.concatenate(parts, axis=1)
            total = total + (
                dot_nt(jnp.concatenate(highs, axis=1), part) + dot_nt(jnp.concatenate(lows, axis=1), part)
            )
        out_ref[:, index * block : (index + 1) * block] = (
            TAPER_SCALE * folded_columns(total, probes)
            + NUGGET * own_ref[:, group * block : (group + 1) * block]
        )


def taper(ids, counts, own, values, coords, extent, first, blocks, after):
    slots = ids.shape[1]
    return pl.pallas_call(
        functools.partial(taper_kernel, first, grain_of(TAPER_RATE * extent)),
        out_shape=jax.ShapeDtypeStruct((own.shape[0], blocks * LANES), jnp.float32),
        in_specs=[SMEM, SMEM, VMEM, VMEM, VMEM] + [ANY] * len(after),
        out_specs=VMEM,
        compiler_params=pltpu.CompilerParams(vmem_limit_bytes=LIMIT),
        cost_estimate=cost(500, blocks * slots * LANES * LANES, 2),
        name="taper",
    )(ids, counts, own, values, coords, *after)


def add_kernel(count, *refs):
    total = refs[0][...]
    for ref in refs[1:count]:
        total = total + ref[...]
    refs[-1][...] = total


def add_all(values, after):
    return pl.pallas_call(
        functools.partial(add_kernel, len(values)),
        out_shape=jax.ShapeDtypeStruct(values[0].shape, jnp.float32),
        in_specs=[VMEM] * len(values) + [ANY] * len(after),
        out_specs=VMEM,
        compiler_params=pltpu.CompilerParams(vmem_limit_bytes=LIMIT),
        name="add",
    )(*values, *after)


def butterfly_rounds(count):
    assert count & (count - 1) == 0
    bits = [1 << i for i in range(count.bit_length() - 1)]
    rounds = [(low | high, high, low) for low, high in zip(bits[0::2], bits[1::2])]
    return rounds + [(bit,) for bit in bits[len(rounds) * 2 :]]


def butterfly_round(value, axis, other, turn):
    count, groups = lax.axis_size(axis), lax.axis_size(other)
    rounds = butterfly_rounds(count)
    half = len(rounds) // 2 if len({len(steps) for steps in rounds}) == 1 else 0
    got = []
    for kind in range(len(rounds[turn])):
        pairs = []
        for j in range(groups):
            step = rounds[(turn + half * (j % 2)) % len(rounds)][kind]
            pairs += [(i * groups + j, (i ^ step) * groups + j) for i in range(count)]
        got.append(lax.ppermute(value, (axis, other), pairs))
    return got


def shifted(value, axis, step):
    count = lax.axis_size(axis)
    if step % count == 0:
        return value
    return lax.ppermute(value, axis, [((i + step) % count, i) for i in range(count)])


def paired(value, axis, other, first):
    count, groups = lax.axis_size(axis), lax.axis_size(other)
    partner = {}
    for i in range(first, count - 1, 2):
        partner[i], partner[i + 1] = i + 1, i
    pairs = []
    for i in range(count):
        for j in range(groups):
            if i in partner:
                pairs.append((i * groups + j, partner[i] * groups + j))
            elif j ^ 1 < groups:
                pairs.append((i * groups + j, i * groups + (j ^ 1)))
    return lax.ppermute(value, (axis, other), pairs)


def shards(probes, locations, knot_locs, knot_precision, neighbours, counts):
    own_blocks = neighbours.shape[0]
    row_count = probes.shape[1]
    knot_total = knot_precision.shape[1]
    device_count = lax.axis_size(("space", "knot"))
    groups = lax.axis_size("knot")
    knot_range = KNOT_REACH * math.sqrt(own_blocks * device_count / knot_total)
    proj_scale = PROJ_GAIN * math.sqrt(knot_total / (row_count * device_count))

    stack, knots = prepare(probes, locations, knot_locs, own_blocks)
    chunks = [shifted(stack, "knot", step) for step in range(groups)]
    rate = LOG2E / knot_range
    extent = CELL * max(lax.axis_size("space"), groups * own_blocks)
    parts = [project(chunk, knots, rate, extent, int(step == 0)) for step, chunk in enumerate(chunks)]
    stack = parts[0][3]

    strip = make_strip(chunks[-1], stack, chunks[1 % groups])
    values, coords = assemble([strip, paired(strip, "space", "knot", 0), paired(strip, "space", "knot", 1)], extent)
    projection = sum(part[0] for part in parts)
    rounds = len(butterfly_rounds(lax.axis_size("space")))
    pieces = math.gcd(own_blocks, rounds)
    per_piece = own_blocks // pieces
    row_pieces = math.gcd(knot_precision.shape[0] // LANES, rounds)
    per_split = knot_precision.shape[0] // row_pieces
    base, splits = [], []
    for turn in range(rounds):
        got = butterfly_round(projection, "space", "knot", turn)
        beside = []
        for i in range(pieces):
            if i * rounds // pieces == turn:
                base.append(
                    taper(
                        neighbours, counts, stack, values, coords, extent, i * per_piece, per_piece, [projection]
                    )
                )
                beside.append(base[-1])
        for i in range(row_pieces):
            if i * rounds // row_pieces == turn:
                splits.append(split_rows(knot_precision, i * per_split, per_split, [projection]))
                beside.extend(splits[-1])
        projection = add_all([projection, *got], beside)
    factor = factored(None, projection, splits, proj_scale, 0)
    for step in range(1, groups):
        factor = factored(factor, shifted(projection, "knot", step), splits, proj_scale, step)
    total = jnp.concatenate(base, axis=1)
    for step in reversed(range(groups)):
        share = spread(factor, parts[step][1], parts[step][2], LOW_SCALE * EXPAND_GAIN)
        total = total + shifted(share, "knot", -step)
    return total


def solution(mesh):
    return jax.shard_map(
        shards,
        mesh=mesh,
        in_specs=(
            P(None, ("space", "knot")),
            P(None, ("space", "knot")),
            P(None, "knot"),
            P("knot", None),
            P(("space", "knot"), None),
            P(("space", "knot")),
        ),
        out_specs=P(None, ("space", "knot")),
        check_vma=False,
    )
```

```python
import functools
import math

import jax
import jax.numpy as jnp
from jax import lax
from jax.experimental import pallas as pl
from jax.experimental.pallas import tpu as pltpu
from jax.sharding import PartitionSpec as P

COV_RANGE = 0.05
TAPER_LEN = 0.15
KNOT_REACH = 0.15
TAPER_SCALE = 0.1
PROJ_GAIN = 0.5
EXPAND_GAIN = 0.5
LOW_SCALE = 0.5
NUGGET = 0.25
LOG2E = math.log2(math.e)
TAPER_RATE = LOG2E / COV_RANGE
CELL = 0.1
TILE = 256
LANES = 128
HALF_GRAIN = 2.0**-24
LIMIT = 6 * 1024 * 1024
VMEM = pl.BlockSpec(memory_space=pltpu.VMEM)
HBM = pl.BlockSpec(memory_space=pltpu.HBM)
ANY = pl.BlockSpec(memory_space=pl.ANY)
SMEM = pl.BlockSpec(memory_space=pltpu.SMEM)


def halves(x):
    high = x.astype(jnp.bfloat16)
    return high, (x - high.astype(jnp.float32)).astype(jnp.bfloat16)


def stacked_halves(x):
    return jnp.concatenate(halves(x), axis=0)


def folded(x):
    rows = x.shape[0] // 2
    return x[:rows] + x[rows:]


def dot_nt(left, right):
    return lax.dot_general(
        left, right, (((1,), (1,)), ((), ())), preferred_element_type=jnp.float32
    )


def dot_nn(left, right):
    return jnp.dot(left, right, preferred_element_type=jnp.float32)


def padded_halves(x, rows):
    fill = jnp.zeros((rows - 2 * x.shape[0], x.shape[1]), jnp.bfloat16)
    return jnp.concatenate([*halves(x), fill], axis=0)


def folded_columns(x, rows):
    x = jnp.transpose(x)
    return x[:rows] + x[rows : 2 * rows]


def cost(work, pairs, transcendentals=0):
    return pl.CostEstimate(flops=work * pairs, bytes_accessed=4 * pairs, transcendentals=transcendentals * pairs)


def coordinate_rows(ref, points, axis):
    start = points + axis * LANES
    return ref[:, start : start + LANES]


def prepare_kernel(blocks, probes_ref, locations_ref, knots_ref, stack_ref, knots_out_ref, coords, sems):
    points = probes_ref.shape[1]
    block = points // blocks
    copies = [
        pltpu.make_async_copy(probes_ref, stack_ref.at[:, pl.ds(0, points)], sems.at[0]),
        pltpu.make_async_copy(locations_ref, coords, sems.at[1]),
        pltpu.make_async_copy(knots_ref, knots_out_ref, sems.at[2]),
    ]
    for copy in copies:
        copy.start()
    for copy in copies:
        copy.wait()
    stack_ref[:, points:] = jnp.zeros((stack_ref.shape[0], 2 * LANES), jnp.float32)
    for axis in range(2):
        lanes = slice(points + axis * LANES, points + (axis + 1) * LANES)
        for index in range(blocks):
            stack_ref[index : index + 1, lanes] = coords[axis : axis + 1, index * block : (index + 1) * block]


def prepare(probes, locations, knot_locs, blocks):
    rows, points = probes.shape
    assert points == blocks * LANES and blocks + 2 <= rows
    probes, locations, knot_locs = [
        pltpu.with_memory_space_constraint(x, pltpu.HBM) for x in (probes, locations, knot_locs)
    ]
    return pl.pallas_call(
        functools.partial(prepare_kernel, blocks),
        out_shape=(
            jax.ShapeDtypeStruct((rows, points + 2 * LANES), jnp.float32),
            jax.ShapeDtypeStruct(knot_locs.shape, jnp.float32),
        ),
        in_specs=[HBM, HBM, HBM],
        out_specs=(VMEM, VMEM),
        scratch_shapes=[pltpu.VMEM(locations.shape, jnp.float32), pltpu.SemaphoreType.DMA((3,))],
        compiler_params=pltpu.CompilerParams(vmem_limit_bytes=LIMIT),
        name="prepare",
    )(probes, locations, knot_locs)


def strip_kernel(below_ref, own_ref, above_ref, out_ref):
    rows, width = own_ref.shape
    points = width - 2 * LANES
    blocks = points // LANES
    out_ref[:, :LANES] = below_ref[:, points - LANES : points]
    out_ref[:, LANES : points + LANES] = own_ref[:, :points]
    out_ref[:, points + LANES : points + 2 * LANES] = above_ref[:, :LANES]
    for axis in range(2):
        lanes = slice(points + axis * LANES, points + (axis + 1) * LANES)
        target = slice(lanes.start + 2 * LANES, lanes.stop + 2 * LANES)
        out_ref[:, target] = jnp.zeros((rows, LANES), jnp.float32)
        out_ref[0:1, target] = below_ref[blocks - 1 : blocks, lanes]
        out_ref[1 : blocks + 1, target] = own_ref[:blocks, lanes]
        out_ref[blocks + 1 : blocks + 2, target] = above_ref[0:1, lanes]


def make_strip(below, own, above):
    return pl.pallas_call(
        strip_kernel,
        out_shape=jax.ShapeDtypeStruct((own.shape[0], own.shape[1] + 2 * LANES), jnp.float32),
        in_specs=[VMEM, VMEM, VMEM],
        out_specs=VMEM,
        compiler_params=pltpu.CompilerParams(vmem_limit_bytes=LIMIT),
        name="strip",
    )(below, own, above)


def assemble_kernel(grain, own_ref, east_ref, west_ref, values_ref, coords_ref):
    probes, width = own_ref.shape
    points = width - 2 * LANES
    for turn, ref in enumerate((own_ref, east_ref, west_ref)):
        start = turn * points
        values_ref[:, start : start + points] = stacked_halves(ref[:, :points] * (1.0 / 256.0))
        for axis in range(2):
            rows = off_grid(coordinate_rows(ref, points, axis) * TAPER_RATE, grain)
            for index in range(points // LANES):
                lanes = slice(start + index * LANES, start + (index + 1) * LANES)
                coords_ref[axis : axis + 1, lanes] = rows[index : index + 1]
    values_ref[:, 3 * points :] = jnp.zeros((2 * probes, LANES), jnp.bfloat16)


def assemble(strips, extent):
    probes, width = strips[0].shape
    near = 3 * (width - 2 * LANES)
    return pl.pallas_call(
        functools.partial(assemble_kernel, grain_of(TAPER_RATE * extent)),
        out_shape=(
            jax.ShapeDtypeStruct((2 * probes, near + LANES), jnp.bfloat16),
            jax.ShapeDtypeStruct((2, near), jnp.float32),
        ),
        in_specs=[VMEM] * 3,
        out_specs=(VMEM, VMEM),
        compiler_params=pltpu.CompilerParams(vmem_limit_bytes=LIMIT),
        name="assemble",
    )(*strips)


def grain_of(bound):
    return 2.0 ** math.ceil(math.log2(1.01 * bound))


def on_grid(x, grain):
    return (x + grain) - grain


def off_grid(x, grain):
    return (x + grain) - (grain - grain * HALF_GRAIN)


def project_kernel(scale, grain, stack_ref, knots_ref, out_ref, high_ref, low_ref, *rest):
    *copies, weights, columns = rest
    knots, points = high_ref.shape
    probes = stack_ref.shape[0]
    tile = min(TILE, knots)
    for copy_ref in copies:
        copy_ref[...] = stack_ref[...]
    weights[...] = padded_halves(stack_ref[:, :points], weights.shape[0])
    fill = jnp.zeros((6, knots), jnp.float32)
    columns[...] = jnp.transpose(jnp.concatenate([off_grid(knots_ref[...] * scale, grain), fill], axis=0))
    east, north = [on_grid(coordinate_rows(stack_ref, points, axis) * scale, grain) for axis in range(2)]

    for start in range(0, knots, tile):
        rows = slice(start, start + tile)
        kx, ky = [columns[rows, axis : axis + 1] for axis in range(2)]
        for block in range(points // LANES):
            lanes = slice(block * LANES, (block + 1) * LANES)
            dx = east[block : block + 1, :] - kx
            dy = north[block : block + 1, :] - ky
            square = dx * dx + dy * dy
            high_ref[rows, lanes], low_ref[rows, lanes] = halves(jnp.exp2(-(square * lax.rsqrt(square))))
        total = dot_nt(high_ref[rows, :], weights[...]) + dot_nt(low_ref[rows, :], weights[...])
        out_ref[:, rows] = folded_columns(total, probes)


def project(stack, knot_locs, scale, extent, copies):
    probes, points, knots = stack.shape[0], stack.shape[1] - 2 * LANES, knot_locs.shape[1]
    return pl.pallas_call(
        functools.partial(project_kernel, scale, grain_of(scale * extent)),
        out_shape=(
            jax.ShapeDtypeStruct((probes, knots), jnp.float32),
            pltpu.VMEM((knots, points), jnp.bfloat16),
            pltpu.VMEM((knots, points), jnp.bfloat16),
            *[jax.ShapeDtypeStruct(stack.shape, jnp.float32)] * copies,
        ),
        in_specs=[VMEM, VMEM],
        out_specs=(VMEM,) * (3 + copies),
        scratch_shapes=[
            pltpu.VMEM((LANES, points), jnp.bfloat16),
            pltpu.VMEM((knots, 8), jnp.float32),
        ],
        compiler_params=pltpu.CompilerParams(vmem_limit_bytes=LIMIT),
        cost_estimate=cost(2800, points * knots, 2),
        name="project",
    )(stack, knot_locs)


def split_kernel(first, precision_ref, *rest):
    high_ref, low_ref = rest[-2:]
    depth, rows = high_ref.shape
    tile = min(TILE, rows)
    wide = min(TILE, depth)
    for start in range(0, rows, tile):
        for deep in range(0, depth, wide):
            turned = jnp.transpose(precision_ref[first + start : first + start + tile, deep : deep + wide])
            here = slice(deep, deep + wide), slice(start, start + tile)
            high_ref[here], low_ref[here] = halves(turned)


def split_rows(precision, first, rows, after):
    depth = precision.shape[1]
    return pl.pallas_call(
        functools.partial(split_kernel, first),
        out_shape=(pltpu.VMEM((depth, rows), jnp.bfloat16), pltpu.VMEM((depth, rows), jnp.bfloat16)),
        in_specs=[VMEM] + [ANY] * len(after),
        out_specs=(VMEM, VMEM),
        compiler_params=pltpu.CompilerParams(vmem_limit_bytes=LIMIT),
        cost_estimate=cost(60, rows * depth),
        name="split",
    )(precision, *after)


def factor_kernel(scale, step, parts, before_ref, proj_ref, *rest):
    highs, lows, (out_ref, weights) = rest[:parts], rest[parts : 2 * parts], rest[-2:]
    probes, depth = proj_ref.shape
    weights[...] = stacked_halves(proj_ref[...] * scale)
    owner = lax.rem(lax.axis_index("knot") + step, lax.axis_size("knot"))
    deep = pl.ds(pl.multiple_of(owner * depth, depth), depth)
    rows = highs[0].shape[1]
    tile = min(TILE, rows)
    for part, (high_ref, low_ref) in enumerate(zip(highs, lows)):
        for start in range(0, rows, tile):
            here = slice(start, start + tile)
            found = folded(dot_nn(weights[...], high_ref[deep, here]) + dot_nn(weights[...], low_ref[deep, here]))
            target = slice(part * rows + start, part * rows + start + tile)
            if before_ref is not None:
                found = found + before_ref[:, target]
            out_ref[:, target] = found


def factored(before, projection, splits, scale, step):
    probes, depth = projection.shape
    highs, lows = [
        [pltpu.with_memory_space_constraint(split[half], pltpu.VMEM) for split in splits] for half in range(2)
    ]
    rows = sum(high.shape[1] for high in highs)
    kernel = functools.partial(factor_kernel, scale, step, len(splits))
    operands = (projection, *highs, *lows)
    if before is None:
        kernel = functools.partial(kernel, None)
    else:
        operands = (before, *operands)
    return pl.pallas_call(
        kernel,
        out_shape=jax.ShapeDtypeStruct((probes, rows), jnp.float32),
        in_specs=[VMEM] * len(operands),
        out_specs=VMEM,
        scratch_shapes=[pltpu.VMEM((2 * probes, depth), jnp.bfloat16)],
        compiler_params=pltpu.CompilerParams(vmem_limit_bytes=LIMIT),
        cost_estimate=cost(1000, rows * depth),
        name="factor",
    )(*operands)


def spread_kernel(scale, factor_ref, high_ref, low_ref, out_ref):
    points = high_ref.shape[1]
    tile = min(TILE, points)
    weights = stacked_halves(factor_ref[...] * scale)
    for start in range(0, points, tile):
        lanes = slice(start, start + tile)
        out_ref[:, lanes] = folded(dot_nn(weights, high_ref[:, lanes]) + dot_nn(weights, low_ref[:, lanes]))


def spread(factor, high, low, scale):
    (probes, knots), points = factor.shape, high.shape[1]
    high = pltpu.with_memory_space_constraint(high, pltpu.VMEM)
    low = pltpu.with_memory_space_constraint(low, pltpu.VMEM)
    return pl.pallas_call(
        functools.partial(spread_kernel, scale),
        out_shape=jax.ShapeDtypeStruct((probes, points), jnp.float32),
        in_specs=[VMEM, VMEM, VMEM],
        out_specs=VMEM,
        compiler_params=pltpu.CompilerParams(vmem_limit_bytes=LIMIT),
        cost_estimate=cost(850, knots * points),
        name="spread",
    )(factor, high, low)


def covariance(square):
    apart = square * lax.rsqrt(square)
    remain = jnp.maximum(4.0 - apart * (4.0 / (TAPER_LEN * TAPER_RATE)), 0.0)
    twice = remain * remain
    return (jnp.exp2(-apart) * (twice * twice)) * (5.0 - remain)


def taper_kernel(first, grain, ids_ref, counts_ref, own_ref, values_ref, coords_ref, *rest):
    out_ref = rest[-1]
    own_blocks, slots = ids_ref.shape
    block = LANES
    probes = own_ref.shape[0]
    span = own_blocks + 2
    zeros_place = coords_ref.shape[1] // block
    column = lax.axis_index("space")
    north_base = lax.axis_index("knot") * own_blocks - 1
    north_cells = lax.axis_size("knot") * own_blocks
    own_columns = [
        on_grid(jnp.transpose(coordinate_rows(own_ref, own_blocks * block, axis) * TAPER_RATE), grain)
        for axis in range(2)
    ]

    def place(group, slot):
        ahead = ids_ref[group, slot] - (column - 1) * north_cells
        east = jnp.where(ahead >= north_cells, 1, 0) + jnp.where(ahead >= 2 * north_cells, 1, 0)
        strip = jnp.where(east == 1, 0, 1 + lax.rem(column + lax.div(east, 2) + 1, 2))
        index = strip * span + (ahead - east * north_cells - north_base)
        return lanes_of(index), lanes_of(jnp.where(slot < counts_ref[group], index, zeros_place))

    def lanes_of(index):
        return pl.ds(pl.multiple_of(index * block, block), block)

    for index in range(out_ref.shape[1] // block):
        group = first + index
        px, py = [turned[:, group : group + 1] for turned in own_columns]
        total = jnp.zeros((block, 2 * probes), jnp.float32)
        for pair in range(0, slots, 2):
            highs, lows, parts = [], [], []
            for slot in range(pair, min(pair + 2, slots)):
                lanes, value_lanes = place(group, slot)
                dx = px - coords_ref[0:1, lanes]
                dy = py - coords_ref[1:2, lanes]
                high, low = halves(covariance(dx * dx + dy * dy))
                highs.append(high)
                lows.append(low)
                parts.append(values_ref[:, value_lanes])
            part = jnp.concatenate(parts, axis=1)
            total = total + (
                dot_nt(jnp.concatenate(highs, axis=1), part) + dot_nt(jnp.concatenate(lows, axis=1), part)
            )
        out_ref[:, index * block : (index + 1) * block] = (
            TAPER_SCALE * folded_columns(total, probes)
            + NUGGET * own_ref[:, group * block : (group + 1) * block]
        )


def taper(ids, counts, own, values, coords, extent, first, blocks, after):
    slots = ids.shape[1]
    return pl.pallas_call(
        functools.partial(taper_kernel, first, grain_of(TAPER_RATE * extent)),
        out_shape=jax.ShapeDtypeStruct((own.shape[0], blocks * LANES), jnp.float32),
        in_specs=[SMEM, SMEM, VMEM, VMEM, VMEM] + [ANY] * len(after),
        out_specs=VMEM,
        compiler_params=pltpu.CompilerParams(vmem_limit_bytes=LIMIT),
        cost_estimate=cost(500, blocks * slots * LANES * LANES, 2),
        name="taper",
    )(ids, counts, own, values, coords, *after)


def add_kernel(count, *refs):
    total = refs[0][...]
    for ref in refs[1:count]:
        total = total + ref[...]
    refs[-1][...] = total


def add_all(values, after):
    return pl.pallas_call(
        functools.partial(add_kernel, len(values)),
        out_shape=jax.ShapeDtypeStruct(values[0].shape, jnp.float32),
        in_specs=[VMEM] * len(values) + [ANY] * len(after),
        out_specs=VMEM,
        compiler_params=pltpu.CompilerParams(vmem_limit_bytes=LIMIT),
        name="add",
    )(*values, *after)


def butterfly_rounds(count):
    assert count & (count - 1) == 0
    bits = [1 << i for i in range(count.bit_length() - 1)]
    rounds = [(low, high, low | high) for low, high in zip(bits[0::2], bits[1::2])]
    return rounds + [(bit,) for bit in bits[len(rounds) * 2 :]]


def butterfly_round(value, axis, other, turn):
    count, groups = lax.axis_size(axis), lax.axis_size(other)
    rounds = butterfly_rounds(count)
    half = len(rounds) // 2 if len({len(steps) for steps in rounds}) == 1 else 0
    got = []
    for kind in range(len(rounds[turn])):
        pairs = []
        for j in range(groups):
            step = rounds[(turn + half * (j % 2)) % len(rounds)][kind]
            pairs += [(i * groups + j, (i ^ step) * groups + j) for i in range(count)]
        got.append(lax.ppermute(value, (axis, other), pairs))
    return got


def shifted(value, axis, step):
    count = lax.axis_size(axis)
    if step % count == 0:
        return value
    return lax.ppermute(value, axis, [((i + step) % count, i) for i in range(count)])


def paired(value, axis, other, first):
    count, groups = lax.axis_size(axis), lax.axis_size(other)
    partner = {}
    for i in range(first, count - 1, 2):
        partner[i], partner[i + 1] = i + 1, i
    pairs = []
    for i in range(count):
        for j in range(groups):
            if i in partner:
                pairs.append((i * groups + j, partner[i] * groups + j))
            elif j ^ 1 < groups:
                pairs.append((i * groups + j, i * groups + (j ^ 1)))
    return lax.ppermute(value, (axis, other), pairs)


def shards(probes, locations, knot_locs, knot_precision, neighbours, counts):
    own_blocks = neighbours.shape[0]
    row_count = probes.shape[1]
    knot_total = knot_precision.shape[1]
    device_count = lax.axis_size(("space", "knot"))
    groups = lax.axis_size("knot")
    knot_range = KNOT_REACH * math.sqrt(own_blocks * device_count / knot_total)
    proj_scale = PROJ_GAIN * math.sqrt(knot_total / (row_count * device_count))

    stack, knots = prepare(probes, locations, knot_locs, own_blocks)
    chunks = [shifted(stack, "knot", step) for step in range(groups)]
    rate = LOG2E / knot_range
    extent = CELL * max(lax.axis_size("space"), groups * own_blocks)
    parts = [project(chunk, knots, rate, extent, int(step == 0)) for step, chunk in enumerate(chunks)]
    stack = parts[0][3]

    strip = make_strip(chunks[-1], stack, chunks[1 % groups])
    values, coords = assemble([strip, paired(strip, "space", "knot", 0), paired(strip, "space", "knot", 1)], extent)
    projection = sum(part[0] for part in parts)
    rounds = len(butterfly_rounds(lax.axis_size("space")))
    pieces = math.gcd(own_blocks, rounds)
    per_piece = own_blocks // pieces
    row_pieces = math.gcd(knot_precision.shape[0] // LANES, rounds)
    per_split = knot_precision.shape[0] // row_pieces
    base, splits = [], []
    for turn in range(rounds):
        got = butterfly_round(projection, "space", "knot", turn)
        beside = []
        for i in range(pieces):
            if i * rounds // pieces == turn:
                base.append(
                    taper(
                        neighbours, counts, stack, values, coords, extent, i * per_piece, per_piece, [projection]
                    )
                )
                beside.append(base[-1])
        for i in range(row_pieces):
            if i * rounds // row_pieces == turn:
                splits.append(split_rows(knot_precision, i * per_split, per_split, [projection]))
                beside.extend(splits[-1])
        projection = add_all([projection, *got], beside)
    factor = factored(None, projection, splits, proj_scale, 0)
    for step in range(1, groups):
        factor = factored(factor, shifted(projection, "knot", step), splits, proj_scale, step)
    total = jnp.concatenate(base, axis=1)
    for step in reversed(range(groups)):
        share = spread(factor, parts[step][1], parts[step][2], LOW_SCALE * EXPAND_GAIN)
        total = total + shifted(share, "knot", -step)
    return total


def solution(mesh):
    return jax.shard_map(
        shards,
        mesh=mesh,
        in_specs=(
            P(None, ("space", "knot")),
            P(None, ("space", "knot")),
            P(None, "knot"),
            P("knot", None),
            P(("space", "knot"), None),
            P(("space", "knot")),
        ),
        out_specs=P(None, ("space", "knot")),
        check_vma=False,
    )
```

```python
import functools
import math

import jax
import jax.numpy as jnp
from jax import lax
from jax.experimental import pallas as pl
from jax.experimental.pallas import tpu as pltpu
from jax.sharding import PartitionSpec as P

COV_RANGE = 0.05
TAPER_LEN = 0.15
KNOT_REACH = 0.15
TAPER_SCALE = 0.1
PROJ_GAIN = 0.5
EXPAND_GAIN = 0.5
LOW_SCALE = 0.5
NUGGET = 0.25
LOG2E = math.log2(math.e)
TAPER_RATE = 4.0 / TAPER_LEN
CELL = 0.1
TILE = 256
LANES = 128
HALF_GRAIN = 2.0**-24
LIMIT = 6 * 1024 * 1024
VMEM = pl.BlockSpec(memory_space=pltpu.VMEM)
HBM = pl.BlockSpec(memory_space=pltpu.HBM)
ANY = pl.BlockSpec(memory_space=pl.ANY)
SMEM = pl.BlockSpec(memory_space=pltpu.SMEM)


def halves(x):
    high = x.astype(jnp.bfloat16)
    return high, (x - high.astype(jnp.float32)).astype(jnp.bfloat16)


def stacked_halves(x):
    return jnp.concatenate(halves(x), axis=0)


def folded(x):
    rows = x.shape[0] // 2
    return x[:rows] + x[rows:]


def dot_nt(left, right):
    return lax.dot_general(
        left, right, (((1,), (1,)), ((), ())), preferred_element_type=jnp.float32
    )


def dot_nn(left, right):
    return jnp.dot(left, right, preferred_element_type=jnp.float32)


def padded_halves(x, rows):
    fill = jnp.zeros((rows - 2 * x.shape[0], x.shape[1]), jnp.bfloat16)
    return jnp.concatenate([*halves(x), fill], axis=0)


def folded_columns(x, rows):
    x = jnp.transpose(x)
    return x[:rows] + x[rows : 2 * rows]


def cost(work, pairs, transcendentals=0):
    return pl.CostEstimate(flops=work * pairs, bytes_accessed=4 * pairs, transcendentals=transcendentals * pairs)


def coordinate_rows(ref, points, axis):
    start = points + axis * LANES
    return ref[:, start : start + LANES]


def prepare_kernel(blocks, probes_ref, locations_ref, knots_ref, stack_ref, knots_out_ref, coords, sems):
    points = probes_ref.shape[1]
    block = points // blocks
    copies = [
        pltpu.make_async_copy(probes_ref, stack_ref.at[:, pl.ds(0, points)], sems.at[0]),
        pltpu.make_async_copy(locations_ref, coords, sems.at[1]),
        pltpu.make_async_copy(knots_ref, knots_out_ref, sems.at[2]),
    ]
    for copy in copies:
        copy.start()
    for copy in copies:
        copy.wait()
    stack_ref[:, points:] = jnp.zeros((stack_ref.shape[0], 2 * LANES), jnp.float32)
    for axis in range(2):
        lanes = slice(points + axis * LANES, points + (axis + 1) * LANES)
        for index in range(blocks):
            stack_ref[index : index + 1, lanes] = coords[axis : axis + 1, index * block : (index + 1) * block]


def prepare(probes, locations, knot_locs, blocks):
    rows, points = probes.shape
    assert points == blocks * LANES and blocks + 2 <= rows
    probes, locations, knot_locs = [
        pltpu.with_memory_space_constraint(x, pltpu.HBM) for x in (probes, locations, knot_locs)
    ]
    return pl.pallas_call(
        functools.partial(prepare_kernel, blocks),
        out_shape=(
            jax.ShapeDtypeStruct((rows, points + 2 * LANES), jnp.float32),
            jax.ShapeDtypeStruct(knot_locs.shape, jnp.float32),
        ),
        in_specs=[HBM, HBM, HBM],
        out_specs=(VMEM, VMEM),
        scratch_shapes=[pltpu.VMEM(locations.shape, jnp.float32), pltpu.SemaphoreType.DMA((3,))],
        compiler_params=pltpu.CompilerParams(vmem_limit_bytes=LIMIT),
        name="prepare",
    )(probes, locations, knot_locs)


def strip_kernel(below_ref, own_ref, above_ref, out_ref):
    rows, width = own_ref.shape
    points = width - 2 * LANES
    blocks = points // LANES
    out_ref[:, :LANES] = below_ref[:, points - LANES : points]
    out_ref[:, LANES : points + LANES] = own_ref[:, :points]
    out_ref[:, points + LANES : points + 2 * LANES] = above_ref[:, :LANES]
    for axis in range(2):
        lanes = slice(points + axis * LANES, points + (axis + 1) * LANES)
        target = slice(lanes.start + 2 * LANES, lanes.stop + 2 * LANES)
        out_ref[:, target] = jnp.zeros((rows, LANES), jnp.float32)
        out_ref[0:1, target] = below_ref[blocks - 1 : blocks, lanes]
        out_ref[1 : blocks + 1, target] = own_ref[:blocks, lanes]
        out_ref[blocks + 1 : blocks + 2, target] = above_ref[0:1, lanes]


def make_strip(below, own, above):
    return pl.pallas_call(
        strip_kernel,
        out_shape=jax.ShapeDtypeStruct((own.shape[0], own.shape[1] + 2 * LANES), jnp.float32),
        in_specs=[VMEM, VMEM, VMEM],
        out_specs=VMEM,
        compiler_params=pltpu.CompilerParams(vmem_limit_bytes=LIMIT),
        name="strip",
    )(below, own, above)


def assemble_kernel(grain, own_ref, east_ref, west_ref, values_ref, coords_ref):
    probes, width = own_ref.shape
    points = width - 2 * LANES
    for turn, ref in enumerate((own_ref, east_ref, west_ref)):
        start = turn * points
        values_ref[:, start : start + points] = stacked_halves(ref[:, :points] * (1.0 / 256.0))
        for axis in range(2):
            rows = off_grid(coordinate_rows(ref, points, axis) * TAPER_RATE, grain)
            for index in range(points // LANES):
                lanes = slice(start + index * LANES, start + (index + 1) * LANES)
                coords_ref[axis : axis + 1, lanes] = rows[index : index + 1]
    values_ref[:, 3 * points :] = jnp.zeros((2 * probes, LANES), jnp.bfloat16)


def assemble(strips, extent):
    probes, width = strips[0].shape
    near = 3 * (width - 2 * LANES)
    return pl.pallas_call(
        functools.partial(assemble_kernel, grain_of(TAPER_RATE * extent)),
        out_shape=(
            jax.ShapeDtypeStruct((2 * probes, near + LANES), jnp.bfloat16),
            jax.ShapeDtypeStruct((2, near), jnp.float32),
        ),
        in_specs=[VMEM] * 3,
        out_specs=(VMEM, VMEM),
        compiler_params=pltpu.CompilerParams(vmem_limit_bytes=LIMIT),
        name="assemble",
    )(*strips)


def grain_of(bound):
    return 2.0 ** math.ceil(math.log2(1.01 * bound))


def on_grid(x, grain):
    return (x + grain) - grain


def off_grid(x, grain):
    return (x + grain) - (grain - grain * HALF_GRAIN)


def project_kernel(scale, grain, stack_ref, knots_ref, out_ref, high_ref, low_ref, *rest):
    *copies, weights, columns = rest
    knots, points = high_ref.shape
    probes = stack_ref.shape[0]
    tile = min(TILE, knots)
    for copy_ref in copies:
        copy_ref[...] = stack_ref[...]
    weights[...] = padded_halves(stack_ref[:, :points], weights.shape[0])
    fill = jnp.zeros((6, knots), jnp.float32)
    columns[...] = jnp.transpose(jnp.concatenate([off_grid(knots_ref[...] * scale, grain), fill], axis=0))
    east, north = [on_grid(coordinate_rows(stack_ref, points, axis) * scale, grain) for axis in range(2)]

    for start in range(0, knots, tile):
        rows = slice(start, start + tile)
        kx, ky = [columns[rows, axis : axis + 1] for axis in range(2)]
        for block in range(points // LANES):
            lanes = slice(block * LANES, (block + 1) * LANES)
            dx = east[block : block + 1, :] - kx
            dy = north[block : block + 1, :] - ky
            square = dx * dx + dy * dy
            high_ref[rows, lanes], low_ref[rows, lanes] = halves(jnp.exp2(-(square * lax.rsqrt(square))))
        total = dot_nt(high_ref[rows, :], weights[...]) + dot_nt(low_ref[rows, :], weights[...])
        out_ref[:, rows] = folded_columns(total, probes)


def project(stack, knot_locs, scale, extent, copies):
    probes, points, knots = stack.shape[0], stack.shape[1] - 2 * LANES, knot_locs.shape[1]
    return pl.pallas_call(
        functools.partial(project_kernel, scale, grain_of(scale * extent)),
        out_shape=(
            jax.ShapeDtypeStruct((probes, knots), jnp.float32),
            pltpu.VMEM((knots, points), jnp.bfloat16),
            pltpu.VMEM((knots, points), jnp.bfloat16),
            *[jax.ShapeDtypeStruct(stack.shape, jnp.float32)] * copies,
        ),
        in_specs=[VMEM, VMEM],
        out_specs=(VMEM,) * (3 + copies),
        scratch_shapes=[
            pltpu.VMEM((LANES, points), jnp.bfloat16),
            pltpu.VMEM((knots, 8), jnp.float32),
        ],
        compiler_params=pltpu.CompilerParams(vmem_limit_bytes=LIMIT),
        cost_estimate=cost(2800, points * knots, 2),
        name="project",
    )(stack, knot_locs)


def split_kernel(first, precision_ref, *rest):
    high_ref, low_ref = rest[-2:]
    depth, rows = high_ref.shape
    tile = min(TILE, rows)
    wide = min(TILE, depth)
    for start in range(0, rows, tile):
        for deep in range(0, depth, wide):
            turned = jnp.transpose(precision_ref[first + start : first + start + tile, deep : deep + wide])
            here = slice(deep, deep + wide), slice(start, start + tile)
            high_ref[here], low_ref[here] = halves(turned)


def split_rows(precision, first, rows, after):
    depth = precision.shape[1]
    return pl.pallas_call(
        functools.partial(split_kernel, first),
        out_shape=(pltpu.VMEM((depth, rows), jnp.bfloat16), pltpu.VMEM((depth, rows), jnp.bfloat16)),
        in_specs=[VMEM] + [ANY] * len(after),
        out_specs=(VMEM, VMEM),
        compiler_params=pltpu.CompilerParams(vmem_limit_bytes=LIMIT),
        cost_estimate=cost(60, rows * depth),
        name="split",
    )(precision, *after)


def factor_kernel(scale, step, parts, before_ref, proj_ref, *rest):
    highs, lows, (out_ref, weights) = rest[:parts], rest[parts : 2 * parts], rest[-2:]
    probes, depth = proj_ref.shape
    weights[...] = stacked_halves(proj_ref[...] * scale)
    owner = lax.rem(lax.axis_index("knot") + step, lax.axis_size("knot"))
    deep = pl.ds(pl.multiple_of(owner * depth, depth), depth)
    rows = highs[0].shape[1]
    tile = min(TILE, rows)
    for part, (high_ref, low_ref) in enumerate(zip(highs, lows)):
        for start in range(0, rows, tile):
            here = slice(start, start + tile)
            found = folded(dot_nn(weights[...], high_ref[deep, here]) + dot_nn(weights[...], low_ref[deep, here]))
            target = slice(part * rows + start, part * rows + start + tile)
            if before_ref is not None:
                found = found + before_ref[:, target]
            out_ref[:, target] = found


def factored(before, projection, splits, scale, step):
    probes, depth = projection.shape
    highs, lows = [
        [pltpu.with_memory_space_constraint(split[half], pltpu.VMEM) for split in splits] for half in range(2)
    ]
    rows = sum(high.shape[1] for high in highs)
    kernel = functools.partial(factor_kernel, scale, step, len(splits))
    operands = (projection, *highs, *lows)
    if before is None:
        kernel = functools.partial(kernel, None)
    else:
        operands = (before, *operands)
    return pl.pallas_call(
        kernel,
        out_shape=jax.ShapeDtypeStruct((probes, rows), jnp.float32),
        in_specs=[VMEM] * len(operands),
        out_specs=VMEM,
        scratch_shapes=[pltpu.VMEM((2 * probes, depth), jnp.bfloat16)],
        compiler_params=pltpu.CompilerParams(vmem_limit_bytes=LIMIT),
        cost_estimate=cost(1000, rows * depth),
        name="factor",
    )(*operands)


def spread_kernel(scale, factor_ref, high_ref, low_ref, out_ref):
    points = high_ref.shape[1]
    tile = min(TILE, points)
    weights = stacked_halves(factor_ref[...] * scale)
    for start in range(0, points, tile):
        lanes = slice(start, start + tile)
        out_ref[:, lanes] = folded(dot_nn(weights, high_ref[:, lanes]) + dot_nn(weights, low_ref[:, lanes]))


def spread(factor, high, low, scale):
    (probes, knots), points = factor.shape, high.shape[1]
    high = pltpu.with_memory_space_constraint(high, pltpu.VMEM)
    low = pltpu.with_memory_space_constraint(low, pltpu.VMEM)
    return pl.pallas_call(
        functools.partial(spread_kernel, scale),
        out_shape=jax.ShapeDtypeStruct((probes, points), jnp.float32),
        in_specs=[VMEM, VMEM, VMEM],
        out_specs=VMEM,
        compiler_params=pltpu.CompilerParams(vmem_limit_bytes=LIMIT),
        cost_estimate=cost(850, knots * points),
        name="spread",
    )(factor, high, low)


def covariance(square):
    apart = square * lax.rsqrt(square)
    remain = jnp.maximum(4.0 - apart, 0.0)
    twice = remain * remain
    return (jnp.exp2(apart * (-LOG2E / (COV_RANGE * TAPER_RATE))) * (twice * twice)) * (5.0 - remain)


def taper_kernel(first, grain, ids_ref, counts_ref, own_ref, values_ref, coords_ref, *rest):
    out_ref = rest[-1]
    own_blocks, slots = ids_ref.shape
    block = LANES
    probes = own_ref.shape[0]
    span = own_blocks + 2
    zeros_place = coords_ref.shape[1] // block
    column = lax.axis_index("space")
    north_base = lax.axis_index("knot") * own_blocks - 1
    north_cells = lax.axis_size("knot") * own_blocks
    own_columns = [
        on_grid(jnp.transpose(coordinate_rows(own_ref, own_blocks * block, axis) * TAPER_RATE), grain)
        for axis in range(2)
    ]

    def place(group, slot):
        ahead = ids_ref[group, slot] - (column - 1) * north_cells
        east = jnp.where(ahead >= north_cells, 1, 0) + jnp.where(ahead >= 2 * north_cells, 1, 0)
        strip = jnp.where(east == 1, 0, 1 + lax.rem(column + lax.div(east, 2) + 1, 2))
        index = strip * span + (ahead - east * north_cells - north_base)
        return lanes_of(index), lanes_of(jnp.where(slot < counts_ref[group], index, zeros_place))

    def lanes_of(index):
        return pl.ds(pl.multiple_of(index * block, block), block)

    for index in range(out_ref.shape[1] // block):
        group = first + index
        px, py = [turned[:, group : group + 1] for turned in own_columns]
        total = jnp.zeros((block, 2 * probes), jnp.float32)
        for pair in range(0, slots, 2):
            highs, lows, parts = [], [], []
            for slot in range(pair, min(pair + 2, slots)):
                lanes, value_lanes = place(group, slot)
                dx = px - coords_ref[0:1, lanes]
                dy = py - coords_ref[1:2, lanes]
                high, low = halves(covariance(dx * dx + dy * dy))
                highs.append(high)
                lows.append(low)
                parts.append(values_ref[:, value_lanes])
            part = jnp.concatenate(parts, axis=1)
            total = total + (
                dot_nt(jnp.concatenate(highs, axis=1), part) + dot_nt(jnp.concatenate(lows, axis=1), part)
            )
        out_ref[:, index * block : (index + 1) * block] = (
            TAPER_SCALE * folded_columns(total, probes)
            + NUGGET * own_ref[:, group * block : (group + 1) * block]
        )


def taper(ids, counts, own, values, coords, extent, first, blocks, after):
    slots = ids.shape[1]
    return pl.pallas_call(
        functools.partial(taper_kernel, first, grain_of(TAPER_RATE * extent)),
        out_shape=jax.ShapeDtypeStruct((own.shape[0], blocks * LANES), jnp.float32),
        in_specs=[SMEM, SMEM, VMEM, VMEM, VMEM] + [ANY] * len(after),
        out_specs=VMEM,
        compiler_params=pltpu.CompilerParams(vmem_limit_bytes=LIMIT),
        cost_estimate=cost(500, blocks * slots * LANES * LANES, 2),
        name="taper",
    )(ids, counts, own, values, coords, *after)


def add_kernel(count, *refs):
    total = refs[0][...]
    for ref in refs[1:count]:
        total = total + ref[...]
    refs[-1][...] = total


def add_all(values, after):
    return pl.pallas_call(
        functools.partial(add_kernel, len(values)),
        out_shape=jax.ShapeDtypeStruct(values[0].shape, jnp.float32),
        in_specs=[VMEM] * len(values) + [ANY] * len(after),
        out_specs=VMEM,
        compiler_params=pltpu.CompilerParams(vmem_limit_bytes=LIMIT),
        name="add",
    )(*values, *after)


def butterfly_rounds(count):
    assert count & (count - 1) == 0
    bits = [1 << i for i in range(count.bit_length() - 1)]
    rounds = [(low, high, low | high) for low, high in zip(bits[0::2], bits[1::2])]
    return rounds + [(bit,) for bit in bits[len(rounds) * 2 :]]


def butterfly_round(value, axis, other, turn):
    count, groups = lax.axis_size(axis), lax.axis_size(other)
    rounds = butterfly_rounds(count)
    half = len(rounds) // 2 if len({len(steps) for steps in rounds}) == 1 else 0
    got = []
    for kind in range(len(rounds[turn])):
        pairs = []
        for j in range(groups):
            step = rounds[(turn + half * ((j + 1) % 2)) % len(rounds)][kind]
            pairs += [(i * groups + j, (i ^ step) * groups + j) for i in range(count)]
        got.append(lax.ppermute(value, (axis, other), pairs))
    return got


def shifted(value, axis, step):
    count = lax.axis_size(axis)
    if step % count == 0:
        return value
    return lax.ppermute(value, axis, [((i + step) % count, i) for i in range(count)])


def paired(value, axis, other, first):
    count, groups = lax.axis_size(axis), lax.axis_size(other)
    partner = {}
    for i in range(first, count - 1, 2):
        partner[i], partner[i + 1] = i + 1, i
    pairs = []
    for i in range(count):
        for j in range(groups):
            if i in partner:
                pairs.append((i * groups + j, partner[i] * groups + j))
            elif j ^ 1 < groups:
                pairs.append((i * groups + j, i * groups + (j ^ 1)))
    return lax.ppermute(value, (axis, other), pairs)


def shards(probes, locations, knot_locs, knot_precision, neighbours, counts):
    own_blocks = neighbours.shape[0]
    row_count = probes.shape[1]
    knot_total = knot_precision.shape[1]
    device_count = lax.axis_size(("space", "knot"))
    groups = lax.axis_size("knot")
    knot_range = KNOT_REACH * math.sqrt(own_blocks * device_count / knot_total)
    proj_scale = PROJ_GAIN * math.sqrt(knot_total / (row_count * device_count))

    stack, knots = prepare(probes, locations, knot_locs, own_blocks)
    chunks = [shifted(stack, "knot", step) for step in range(groups)]
    rate = LOG2E / knot_range
    extent = CELL * max(lax.axis_size("space"), groups * own_blocks)
    parts = [project(chunk, knots, rate, extent, int(step == 0)) for step, chunk in enumerate(chunks)]
    stack = parts[0][3]

    strip = make_strip(chunks[-1], stack, chunks[1 % groups])
    values, coords = assemble([strip, paired(strip, "space", "knot", 0), paired(strip, "space", "knot", 1)], extent)
    projection = sum(part[0] for part in parts)
    rounds = len(butterfly_rounds(lax.axis_size("space")))
    pieces = math.gcd(own_blocks, rounds)
    per_piece = own_blocks // pieces
    row_pieces = math.gcd(knot_precision.shape[0] // LANES, rounds)
    per_split = knot_precision.shape[0] // row_pieces
    base, splits = [], []
    for turn in range(rounds):
        got = butterfly_round(projection, "space", "knot", turn)
        beside = []
        for i in range(pieces):
            if i * rounds // pieces == turn:
                base.append(
                    taper(
                        neighbours, counts, stack, values, coords, extent, i * per_piece, per_piece, [projection]
                    )
                )
                beside.append(base[-1])
        for i in range(row_pieces):
            if i * rounds // row_pieces == turn:
                splits.append(split_rows(knot_precision, i * per_split, per_split, [projection]))
                beside.extend(splits[-1])
        projection = add_all([projection, *got], beside)
    factor = factored(None, projection, splits, proj_scale, 0)
    for step in range(1, groups):
        factor = factored(factor, shifted(projection, "knot", step), splits, proj_scale, step)
    total = jnp.concatenate(base, axis=1)
    for step in reversed(range(groups)):
        share = spread(factor, parts[step][1], parts[step][2], LOW_SCALE * EXPAND_GAIN)
        total = total + shifted(share, "knot", -step)
    return total


def solution(mesh):
    return jax.shard_map(
        shards,
        mesh=mesh,
        in_specs=(
            P(None, ("space", "knot")),
            P(None, ("space", "knot")),
            P(None, "knot"),
            P("knot", None),
            P(("space", "knot"), None),
            P(("space", "knot")),
        ),
        out_specs=P(None, ("space", "knot")),
        check_vma=False,
    )
```

```python
import functools
import math

import jax
import jax.numpy as jnp
from jax import lax
from jax.experimental import pallas as pl
from jax.experimental.pallas import tpu as pltpu
from jax.sharding import PartitionSpec as P

COV_RANGE = 0.05
TAPER_LEN = 0.15
KNOT_REACH = 0.15
TAPER_SCALE = 0.1
PROJ_GAIN = 0.5
EXPAND_GAIN = 0.5
LOW_SCALE = 0.5
NUGGET = 0.25
LOG2E = math.log2(math.e)
TAPER_RATE = 4.0 / TAPER_LEN
CELL = 0.1
TILE = 256
LANES = 128
HALF_GRAIN = 2.0**-24
LIMIT = 6 * 1024 * 1024
VMEM = pl.BlockSpec(memory_space=pltpu.VMEM)
HBM = pl.BlockSpec(memory_space=pltpu.HBM)
ANY = pl.BlockSpec(memory_space=pl.ANY)
SMEM = pl.BlockSpec(memory_space=pltpu.SMEM)


def halves(x):
    high = x.astype(jnp.bfloat16)
    return high, (x - high.astype(jnp.float32)).astype(jnp.bfloat16)


def stacked_halves(x):
    return jnp.concatenate(halves(x), axis=0)


def folded(x):
    rows = x.shape[0] // 2
    return x[:rows] + x[rows:]


def dot_nt(left, right):
    return lax.dot_general(
        left, right, (((1,), (1,)), ((), ())), preferred_element_type=jnp.float32
    )


def dot_nn(left, right):
    return jnp.dot(left, right, preferred_element_type=jnp.float32)


def padded_halves(x, rows):
    fill = jnp.zeros((rows - 2 * x.shape[0], x.shape[1]), jnp.bfloat16)
    return jnp.concatenate([*halves(x), fill], axis=0)


def folded_columns(x, rows):
    x = jnp.transpose(x)
    return x[:rows] + x[rows : 2 * rows]


def cost(work, pairs, transcendentals=0):
    return pl.CostEstimate(flops=work * pairs, bytes_accessed=4 * pairs, transcendentals=transcendentals * pairs)


def coordinate_rows(ref, points, axis):
    start = points + axis * LANES
    return ref[:, start : start + LANES]


def prepare_kernel(blocks, probes_ref, locations_ref, knots_ref, stack_ref, knots_out_ref, coords, sems):
    points = probes_ref.shape[1]
    block = points // blocks
    copies = [
        pltpu.make_async_copy(probes_ref, stack_ref.at[:, pl.ds(0, points)], sems.at[0]),
        pltpu.make_async_copy(locations_ref, coords, sems.at[1]),
        pltpu.make_async_copy(knots_ref, knots_out_ref, sems.at[2]),
    ]
    for copy in copies:
        copy.start()
    for copy in copies:
        copy.wait()
    stack_ref[:, points:] = jnp.zeros((stack_ref.shape[0], 2 * LANES), jnp.float32)
    for axis in range(2):
        lanes = slice(points + axis * LANES, points + (axis + 1) * LANES)
        for index in range(blocks):
            stack_ref[index : index + 1, lanes] = coords[axis : axis + 1, index * block : (index + 1) * block]


def prepare(probes, locations, knot_locs, blocks):
    rows, points = probes.shape
    assert points == blocks * LANES and blocks + 2 <= rows
    probes, locations, knot_locs = [
        pltpu.with_memory_space_constraint(x, pltpu.HBM) for x in (probes, locations, knot_locs)
    ]
    return pl.pallas_call(
        functools.partial(prepare_kernel, blocks),
        out_shape=(
            jax.ShapeDtypeStruct((rows, points + 2 * LANES), jnp.float32),
            jax.ShapeDtypeStruct(knot_locs.shape, jnp.float32),
        ),
        in_specs=[HBM, HBM, HBM],
        out_specs=(VMEM, VMEM),
        scratch_shapes=[pltpu.VMEM(locations.shape, jnp.float32), pltpu.SemaphoreType.DMA((3,))],
        compiler_params=pltpu.CompilerParams(vmem_limit_bytes=LIMIT),
        name="prepare",
    )(probes, locations, knot_locs)


def strip_kernel(below_ref, own_ref, above_ref, out_ref):
    rows, width = own_ref.shape
    points = width - 2 * LANES
    blocks = points // LANES
    out_ref[:, :LANES] = below_ref[:, points - LANES : points]
    out_ref[:, LANES : points + LANES] = own_ref[:, :points]
    out_ref[:, points + LANES : points + 2 * LANES] = above_ref[:, :LANES]
    for axis in range(2):
        lanes = slice(points + axis * LANES, points + (axis + 1) * LANES)
        target = slice(lanes.start + 2 * LANES, lanes.stop + 2 * LANES)
        out_ref[:, target] = jnp.zeros((rows, LANES), jnp.float32)
        out_ref[0:1, target] = below_ref[blocks - 1 : blocks, lanes]
        out_ref[1 : blocks + 1, target] = own_ref[:blocks, lanes]
        out_ref[blocks + 1 : blocks + 2, target] = above_ref[0:1, lanes]


def make_strip(below, own, above):
    return pl.pallas_call(
        strip_kernel,
        out_shape=jax.ShapeDtypeStruct((own.shape[0], own.shape[1] + 2 * LANES), jnp.float32),
        in_specs=[VMEM, VMEM, VMEM],
        out_specs=VMEM,
        compiler_params=pltpu.CompilerParams(vmem_limit_bytes=LIMIT),
        name="strip",
    )(below, own, above)


def assemble_kernel(grain, own_ref, odd_ref, even_ref, values_ref, coords_ref):
    probes, width = own_ref.shape
    points = width - 2 * LANES
    for turn, ref in enumerate((own_ref, odd_ref, even_ref)):
        start = turn * points
        values_ref[:, start : start + points] = stacked_halves(ref[:, :points] * (1.0 / 256.0))
        for axis in range(2):
            rows = off_grid(coordinate_rows(ref, points, axis) * TAPER_RATE, grain)
            for index in range(points // LANES):
                lanes = slice(start + index * LANES, start + (index + 1) * LANES)
                coords_ref[axis : axis + 1, lanes] = rows[index : index + 1]
    values_ref[:, 3 * points :] = jnp.zeros((2 * probes, LANES), jnp.bfloat16)


def assemble(strips, extent):
    probes, width = strips[0].shape
    near = 3 * (width - 2 * LANES)
    return pl.pallas_call(
        functools.partial(assemble_kernel, grain_of(TAPER_RATE * extent)),
        out_shape=(
            jax.ShapeDtypeStruct((2 * probes, near + LANES), jnp.bfloat16),
            jax.ShapeDtypeStruct((2, near), jnp.float32),
        ),
        in_specs=[VMEM] * 3,
        out_specs=(VMEM, VMEM),
        compiler_params=pltpu.CompilerParams(vmem_limit_bytes=LIMIT),
        name="assemble",
    )(*strips)


def grain_of(bound):
    return 2.0 ** math.ceil(math.log2(1.01 * bound))


def on_grid(x, grain):
    return (x + grain) - grain


def off_grid(x, grain):
    return (x + grain) - (grain - grain * HALF_GRAIN)


def project_kernel(scale, grain, stack_ref, knots_ref, out_ref, high_ref, low_ref, *rest):
    *copies, weights, columns = rest
    knots, points = high_ref.shape
    probes = stack_ref.shape[0]
    tile = min(TILE, knots)
    for copy_ref in copies:
        copy_ref[...] = stack_ref[...]
    weights[...] = padded_halves(stack_ref[:, :points], weights.shape[0])
    fill = jnp.zeros((6, knots), jnp.float32)
    columns[...] = jnp.transpose(jnp.concatenate([off_grid(knots_ref[...] * scale, grain), fill], axis=0))
    east, north = [on_grid(coordinate_rows(stack_ref, points, axis) * scale, grain) for axis in range(2)]

    for start in range(0, knots, tile):
        rows = slice(start, start + tile)
        kx, ky = [columns[rows, axis : axis + 1] for axis in range(2)]
        for block in range(points // LANES):
            lanes = slice(block * LANES, (block + 1) * LANES)
            dx = east[block : block + 1, :] - kx
            dy = north[block : block + 1, :] - ky
            square = dx * dx + dy * dy
            high_ref[rows, lanes], low_ref[rows, lanes] = halves(jnp.exp2(-(square * lax.rsqrt(square))))
        total = dot_nt(high_ref[rows, :], weights[...]) + dot_nt(low_ref[rows, :], weights[...])
        out_ref[:, rows] = folded_columns(total, probes)


def project(stack, knot_locs, scale, extent, copies):
    probes, points, knots = stack.shape[0], stack.shape[1] - 2 * LANES, knot_locs.shape[1]
    return pl.pallas_call(
        functools.partial(project_kernel, scale, grain_of(scale * extent)),
        out_shape=(
            jax.ShapeDtypeStruct((probes, knots), jnp.float32),
            pltpu.VMEM((knots, points), jnp.bfloat16),
            pltpu.VMEM((knots, points), jnp.bfloat16),
            *[jax.ShapeDtypeStruct(stack.shape, jnp.float32)] * copies,
        ),
        in_specs=[VMEM, VMEM],
        out_specs=(VMEM,) * (3 + copies),
        scratch_shapes=[
            pltpu.VMEM((LANES, points), jnp.bfloat16),
            pltpu.VMEM((knots, 8), jnp.float32),
        ],
        compiler_params=pltpu.CompilerParams(vmem_limit_bytes=LIMIT),
        cost_estimate=cost(2800, points * knots, 2),
        name="project",
    )(stack, knot_locs)


def factor_kernel(scale, step, parts, before_ref, proj_ref, *rest):
    highs, lows, (out_ref, weights) = rest[:parts], rest[parts : 2 * parts], rest[-2:]
    probes, depth = proj_ref.shape
    weights[...] = stacked_halves(proj_ref[...] * scale)
    owner = lax.rem(lax.axis_index("knot") + step, lax.axis_size("knot"))
    deep = pl.ds(pl.multiple_of(owner * depth, depth), depth)
    rows = highs[0].shape[1]
    tile = min(TILE, rows)
    for part, (high_ref, low_ref) in enumerate(zip(highs, lows)):
        for start in range(0, rows, tile):
            here = slice(start, start + tile)
            found = folded(dot_nn(weights[...], high_ref[deep, here]) + dot_nn(weights[...], low_ref[deep, here]))
            target = slice(part * rows + start, part * rows + start + tile)
            if before_ref is not None:
                found = found + before_ref[:, target]
            out_ref[:, target] = found


def factored(before, projection, splits, scale, step):
    probes, depth = projection.shape
    highs, lows = [
        [pltpu.with_memory_space_constraint(split[half], pltpu.VMEM) for split in splits] for half in range(2)
    ]
    rows = sum(high.shape[1] for high in highs)
    kernel = functools.partial(factor_kernel, scale, step, len(splits))
    operands = (projection, *highs, *lows)
    if before is None:
        kernel = functools.partial(kernel, None)
    else:
        operands = (before, *operands)
    return pl.pallas_call(
        kernel,
        out_shape=jax.ShapeDtypeStruct((probes, rows), jnp.float32),
        in_specs=[VMEM] * len(operands),
        out_specs=VMEM,
        scratch_shapes=[pltpu.VMEM((2 * probes, depth), jnp.bfloat16)],
        compiler_params=pltpu.CompilerParams(vmem_limit_bytes=LIMIT),
        cost_estimate=cost(1000, rows * depth),
        name="factor",
    )(*operands)


def spread_kernel(scale, factor_ref, high_ref, low_ref, out_ref):
    points = high_ref.shape[1]
    tile = min(TILE, points)
    weights = stacked_halves(factor_ref[...] * scale)
    for start in range(0, points, tile):
        lanes = slice(start, start + tile)
        out_ref[:, lanes] = folded(dot_nn(weights, high_ref[:, lanes]) + dot_nn(weights, low_ref[:, lanes]))


def spread(factor, high, low, scale):
    (probes, knots), points = factor.shape, high.shape[1]
    high = pltpu.with_memory_space_constraint(high, pltpu.VMEM)
    low = pltpu.with_memory_space_constraint(low, pltpu.VMEM)
    return pl.pallas_call(
        functools.partial(spread_kernel, scale),
        out_shape=jax.ShapeDtypeStruct((probes, points), jnp.float32),
        in_specs=[VMEM, VMEM, VMEM],
        out_specs=VMEM,
        compiler_params=pltpu.CompilerParams(vmem_limit_bytes=LIMIT),
        cost_estimate=cost(850, knots * points),
        name="spread",
    )(factor, high, low)


def covariance(square):
    apart = square * lax.rsqrt(square)
    remain = jnp.maximum(4.0 - apart, 0.0)
    twice = remain * remain
    return (jnp.exp2(apart * (-LOG2E / (COV_RANGE * TAPER_RATE))) * (twice * twice)) * (5.0 - remain)


def beside_kernel(first, first_row, grain, ids_ref, counts_ref, own_ref, values_ref, coords_ref, precision_ref, *rest):
    out_ref, high_ref, low_ref = rest[-3:]
    own_blocks, slots = ids_ref.shape
    block = LANES
    probes = own_ref.shape[0]
    span = own_blocks + 2
    zeros_place = coords_ref.shape[1] // block
    column = lax.axis_index("space")
    north_base = lax.axis_index("knot") * own_blocks - 1
    north_cells = lax.axis_size("knot") * own_blocks
    own_columns = [
        on_grid(jnp.transpose(coordinate_rows(own_ref, own_blocks * block, axis) * TAPER_RATE), grain)
        for axis in range(2)
    ]

    def place(group, slot):
        ahead = ids_ref[group, slot] - (column - 1) * north_cells
        east = jnp.where(ahead >= north_cells, 1, 0) + jnp.where(ahead >= 2 * north_cells, 1, 0)
        strip = jnp.where(east == 1, 0, 2 - lax.rem(column + lax.div(east, 2) + 1, 2))
        index = strip * span + (ahead - east * north_cells - north_base)
        return lanes_of(index), lanes_of(jnp.where(slot < counts_ref[group], index, zeros_place))

    def lanes_of(index):
        return pl.ds(pl.multiple_of(index * block, block), block)

    depth, rows = high_ref.shape
    tile = min(TILE, rows)
    wide = min(TILE, depth)
    tiles = [(start, deep) for start in range(0, rows, tile) for deep in range(0, depth, wide)]
    groups = out_ref.shape[1] // block
    turns = groups * -(-slots // 2)

    for index in range(groups):
        group = first + index
        px, py = [turned[:, group : group + 1] for turned in own_columns]
        total = jnp.zeros((block, 2 * probes), jnp.float32)
        for pair in range(0, slots, 2):
            highs, lows, parts = [], [], []
            for slot in range(pair, min(pair + 2, slots)):
                lanes, value_lanes = place(group, slot)
                dx = px - coords_ref[0:1, lanes]
                dy = py - coords_ref[1:2, lanes]
                high, low = halves(covariance(dx * dx + dy * dy))
                highs.append(high)
                lows.append(low)
                parts.append(values_ref[:, value_lanes])
            part = jnp.concatenate(parts, axis=1)
            total = total + (
                dot_nt(jnp.concatenate(highs, axis=1), part) + dot_nt(jnp.concatenate(lows, axis=1), part)
            )
            turn = index * -(-slots // 2) + pair // 2
            for start, deep in tiles[turn * len(tiles) // turns : (turn + 1) * len(tiles) // turns]:
                from_row = first_row + start
                turned = jnp.transpose(precision_ref[from_row : from_row + tile, deep : deep + wide])
                here = slice(deep, deep + wide), slice(start, start + tile)
                high_ref[here], low_ref[here] = halves(turned)
        out_ref[:, index * block : (index + 1) * block] = (
            TAPER_SCALE * folded_columns(total, probes)
            + NUGGET * own_ref[:, group * block : (group + 1) * block]
        )


def beside_round(ids, counts, own, values, coords, precision, extent, first, blocks, first_row, rows, after):
    slots, depth = ids.shape[1], precision.shape[1]
    return pl.pallas_call(
        functools.partial(beside_kernel, first, first_row, grain_of(TAPER_RATE * extent)),
        out_shape=(
            jax.ShapeDtypeStruct((own.shape[0], blocks * LANES), jnp.float32),
            pltpu.VMEM((depth, rows), jnp.bfloat16),
            pltpu.VMEM((depth, rows), jnp.bfloat16),
        ),
        in_specs=[SMEM, SMEM, VMEM, VMEM, VMEM, VMEM] + [ANY] * len(after),
        out_specs=(VMEM, VMEM, VMEM),
        compiler_params=pltpu.CompilerParams(vmem_limit_bytes=LIMIT),
        cost_estimate=cost(500, blocks * slots * LANES * LANES, 2),
        name="beside",
    )(ids, counts, own, values, coords, precision, *after)


def add_kernel(count, *refs):
    total = refs[0][...]
    for ref in refs[1:count]:
        total = total + ref[...]
    refs[-1][...] = total


def add_all(values, after):
    return pl.pallas_call(
        functools.partial(add_kernel, len(values)),
        out_shape=jax.ShapeDtypeStruct(values[0].shape, jnp.float32),
        in_specs=[VMEM] * len(values) + [ANY] * len(after),
        out_specs=VMEM,
        compiler_params=pltpu.CompilerParams(vmem_limit_bytes=LIMIT),
        name="add",
    )(*values, *after)


def butterfly_rounds(count):
    assert count & (count - 1) == 0
    bits = [1 << i for i in range(count.bit_length() - 1)]
    rounds = [(low | high, high, low) for low, high in zip(bits[0::2], bits[1::2])]
    return rounds + [(bit,) for bit in bits[len(rounds) * 2 :]]


def butterfly_round(value, axis, other, turn):
    count, groups = lax.axis_size(axis), lax.axis_size(other)
    rounds = butterfly_rounds(count)
    half = len(rounds) // 2 if len({len(steps) for steps in rounds}) == 1 else 0
    got = []
    for kind in range(len(rounds[turn])):
        pairs = []
        for j in range(groups):
            step = rounds[(turn + half * ((j + 1) % 2)) % len(rounds)][kind]
            pairs += [(i * groups + j, (i ^ step) * groups + j) for i in range(count)]
        got.append(lax.ppermute(value, (axis, other), pairs))
    return got


def shifted(value, axis, step):
    count = lax.axis_size(axis)
    if step % count == 0:
        return value
    return lax.ppermute(value, axis, [((i + step) % count, i) for i in range(count)])


def paired(value, axis, other, first):
    count, groups = lax.axis_size(axis), lax.axis_size(other)
    partner = {}
    for i in range(first, count - 1, 2):
        partner[i], partner[i + 1] = i + 1, i
    pairs = []
    for i in range(count):
        for j in range(groups):
            if i in partner:
                pairs.append((i * groups + j, partner[i] * groups + j))
            elif j ^ 1 < groups:
                pairs.append((i * groups + j, i * groups + (j ^ 1)))
    return lax.ppermute(value, (axis, other), pairs)


def shards(probes, locations, knot_locs, knot_precision, neighbours, counts):
    own_blocks = neighbours.shape[0]
    row_count = probes.shape[1]
    knot_total = knot_precision.shape[1]
    device_count = lax.axis_size(("space", "knot"))
    groups = lax.axis_size("knot")
    knot_range = KNOT_REACH * math.sqrt(own_blocks * device_count / knot_total)
    proj_scale = PROJ_GAIN * math.sqrt(knot_total / (row_count * device_count))

    stack, knots = prepare(probes, locations, knot_locs, own_blocks)
    chunks = [shifted(stack, "knot", step) for step in range(groups)]
    rate = LOG2E / knot_range
    extent = CELL * max(lax.axis_size("space"), groups * own_blocks)
    parts = [project(chunk, knots, rate, extent, int(step == 0)) for step, chunk in enumerate(chunks)]
    stack = parts[0][3]

    strip = make_strip(chunks[-1], stack, chunks[1 % groups])
    odd = paired(strip, "space", "knot", 1)
    values, coords = assemble([strip, odd, paired(strip, "space", "knot", 0)], extent)
    projection = sum(part[0] for part in parts)
    rounds = len(butterfly_rounds(lax.axis_size("space")))
    pieces = math.gcd(math.gcd(own_blocks, rounds), knot_precision.shape[0] // LANES)
    per_piece, per_split = own_blocks // pieces, knot_precision.shape[0] // pieces
    base, splits = [], []
    for turn in range(rounds):
        got = butterfly_round(projection, "space", "knot", turn)
        beside = []
        for i in range(pieces):
            if i * rounds // pieces == turn:
                done = beside_round(
                    neighbours, counts, stack, values, coords, knot_precision, extent,
                    i * per_piece, per_piece, i * per_split, per_split, [projection],
                )
                base.append(done[0])
                splits.append(done[1:])
                beside.extend(done)
        projection = add_all([projection, *got], beside)
    factor = factored(None, projection, splits, proj_scale, 0)
    for step in range(1, groups):
        factor = factored(factor, shifted(projection, "knot", step), splits, proj_scale, step)
    total = jnp.concatenate(base, axis=1)
    for step in reversed(range(groups)):
        share = spread(factor, parts[step][1], parts[step][2], LOW_SCALE * EXPAND_GAIN)
        total = total + shifted(share, "knot", -step)
    return total


def solution(mesh):
    return jax.shard_map(
        shards,
        mesh=mesh,
        in_specs=(
            P(None, ("space", "knot")),
            P(None, ("space", "knot")),
            P(None, "knot"),
            P("knot", None),
            P(("space", "knot"), None),
            P(("space", "knot")),
        ),
        out_specs=P(None, ("space", "knot")),
        check_vma=False,
    )
```

```python
import functools
import math

import jax
import jax.numpy as jnp
from jax import lax
from jax.experimental import pallas as pl
from jax.experimental.pallas import tpu as pltpu
from jax.sharding import PartitionSpec as P

COV_RANGE = 0.05
TAPER_LEN = 0.15
KNOT_REACH = 0.15
TAPER_SCALE = 0.1
PROJ_GAIN = 0.5
EXPAND_GAIN = 0.5
LOW_SCALE = 0.5
NUGGET = 0.25
LOG2E = math.log2(math.e)
TAPER_RATE = 4.0 / TAPER_LEN
CELL = 0.1
TILE = 256
LANES = 128
HALF_GRAIN = 2.0**-24
LIMIT = 6 * 1024 * 1024
VMEM = pl.BlockSpec(memory_space=pltpu.VMEM)
HBM = pl.BlockSpec(memory_space=pltpu.HBM)
ANY = pl.BlockSpec(memory_space=pl.ANY)
SMEM = pl.BlockSpec(memory_space=pltpu.SMEM)


def halves(x):
    high = x.astype(jnp.bfloat16)
    return high, (x - high.astype(jnp.float32)).astype(jnp.bfloat16)


def stacked_halves(x):
    return jnp.concatenate(halves(x), axis=0)


def folded(x):
    rows = x.shape[0] // 2
    return x[:rows] + x[rows:]


def dot_nt(left, right):
    return lax.dot_general(
        left, right, (((1,), (1,)), ((), ())), preferred_element_type=jnp.float32
    )


def dot_nn(left, right):
    return jnp.dot(left, right, preferred_element_type=jnp.float32)


def padded_halves(x, rows):
    fill = jnp.zeros((rows - 2 * x.shape[0], x.shape[1]), jnp.bfloat16)
    return jnp.concatenate([*halves(x), fill], axis=0)


def folded_columns(x, rows):
    x = jnp.transpose(x)
    return x[:rows] + x[rows : 2 * rows]


def cost(work, pairs, transcendentals=0):
    return pl.CostEstimate(flops=work * pairs, bytes_accessed=4 * pairs, transcendentals=transcendentals * pairs)


def coordinate_rows(ref, points, axis):
    start = points + axis * LANES
    return ref[:, start : start + LANES]


def prepare_kernel(blocks, probes_ref, locations_ref, knots_ref, stack_ref, knots_out_ref, coords, sems):
    points = probes_ref.shape[1]
    block = points // blocks
    copies = [
        pltpu.make_async_copy(probes_ref, stack_ref.at[:, pl.ds(0, points)], sems.at[0]),
        pltpu.make_async_copy(locations_ref, coords, sems.at[1]),
        pltpu.make_async_copy(knots_ref, knots_out_ref, sems.at[2]),
    ]
    for copy in copies:
        copy.start()
    for copy in copies:
        copy.wait()
    stack_ref[:, points:] = jnp.zeros((stack_ref.shape[0], 2 * LANES), jnp.float32)
    for axis in range(2):
        lanes = slice(points + axis * LANES, points + (axis + 1) * LANES)
        for index in range(blocks):
            stack_ref[index : index + 1, lanes] = coords[axis : axis + 1, index * block : (index + 1) * block]


def prepare(probes, locations, knot_locs, blocks):
    rows, points = probes.shape
    assert points == blocks * LANES and blocks + 2 <= rows
    probes, locations, knot_locs = [
        pltpu.with_memory_space_constraint(x, pltpu.HBM) for x in (probes, locations, knot_locs)
    ]
    return pl.pallas_call(
        functools.partial(prepare_kernel, blocks),
        out_shape=(
            jax.ShapeDtypeStruct((rows, points + 2 * LANES), jnp.float32),
            jax.ShapeDtypeStruct(knot_locs.shape, jnp.float32),
        ),
        in_specs=[HBM, HBM, HBM],
        out_specs=(VMEM, VMEM),
        scratch_shapes=[pltpu.VMEM(locations.shape, jnp.float32), pltpu.SemaphoreType.DMA((3,))],
        compiler_params=pltpu.CompilerParams(vmem_limit_bytes=LIMIT),
        name="prepare",
    )(probes, locations, knot_locs)


def strip_kernel(below_ref, own_ref, above_ref, out_ref):
    rows, width = own_ref.shape
    points = width - 2 * LANES
    blocks = points // LANES
    out_ref[:, :LANES] = below_ref[:, points - LANES : points]
    out_ref[:, LANES : points + LANES] = own_ref[:, :points]
    out_ref[:, points + LANES : points + 2 * LANES] = above_ref[:, :LANES]
    for axis in range(2):
        lanes = slice(points + axis * LANES, points + (axis + 1) * LANES)
        target = slice(lanes.start + 2 * LANES, lanes.stop + 2 * LANES)
        out_ref[:, target] = jnp.zeros((rows, LANES), jnp.float32)
        out_ref[0:1, target] = below_ref[blocks - 1 : blocks, lanes]
        out_ref[1 : blocks + 1, target] = own_ref[:blocks, lanes]
        out_ref[blocks + 1 : blocks + 2, target] = above_ref[0:1, lanes]


def make_strip(below, own, above):
    return pl.pallas_call(
        strip_kernel,
        out_shape=jax.ShapeDtypeStruct((own.shape[0], own.shape[1] + 2 * LANES), jnp.float32),
        in_specs=[VMEM, VMEM, VMEM],
        out_specs=VMEM,
        compiler_params=pltpu.CompilerParams(vmem_limit_bytes=LIMIT),
        name="strip",
    )(below, own, above)


def assemble_kernel(grain, own_ref, odd_ref, even_ref, values_ref, coords_ref):
    probes, width = own_ref.shape
    points = width - 2 * LANES
    for turn, ref in enumerate((own_ref, odd_ref, even_ref)):
        start = turn * points
        values_ref[:, start : start + points] = stacked_halves(ref[:, :points] * (1.0 / 256.0))
        for axis in range(2):
            rows = off_grid(coordinate_rows(ref, points, axis) * TAPER_RATE, grain)
            for index in range(points // LANES):
                lanes = slice(start + index * LANES, start + (index + 1) * LANES)
                coords_ref[axis : axis + 1, lanes] = rows[index : index + 1]
    values_ref[:, 3 * points :] = jnp.zeros((2 * probes, LANES), jnp.bfloat16)


def assemble(strips, extent):
    probes, width = strips[0].shape
    near = 3 * (width - 2 * LANES)
    return pl.pallas_call(
        functools.partial(assemble_kernel, grain_of(TAPER_RATE * extent)),
        out_shape=(
            jax.ShapeDtypeStruct((2 * probes, near + LANES), jnp.bfloat16),
            jax.ShapeDtypeStruct((2, near), jnp.float32),
        ),
        in_specs=[VMEM] * 3,
        out_specs=(VMEM, VMEM),
        compiler_params=pltpu.CompilerParams(vmem_limit_bytes=LIMIT),
        name="assemble",
    )(*strips)


def grain_of(bound):
    return 2.0 ** math.ceil(math.log2(1.01 * bound))


def on_grid(x, grain):
    return (x + grain) - grain


def off_grid(x, grain):
    return (x + grain) - (grain - grain * HALF_GRAIN)


def project_kernel(scale, grain, follows, stack_ref, *rest):
    if follows:
        before_ref, columns, out_ref, high_ref, low_ref, weights = rest
    else:
        knots_ref, out_ref, high_ref, low_ref, columns, copy_ref, weights = rest
        copy_ref[...] = stack_ref[...]
        fill = jnp.zeros((6, knots_ref.shape[1]), jnp.float32)
        columns[...] = jnp.transpose(jnp.concatenate([off_grid(knots_ref[...] * scale, grain), fill], axis=0))
    knots, points = high_ref.shape
    probes = stack_ref.shape[0]
    tile = min(TILE, knots)
    weights[...] = padded_halves(stack_ref[:, :points], weights.shape[0])
    east, north = [on_grid(coordinate_rows(stack_ref, points, axis) * scale, grain) for axis in range(2)]

    for start in range(0, knots, tile):
        rows = slice(start, start + tile)
        kx, ky = [columns[rows, axis : axis + 1] for axis in range(2)]
        for block in range(points // LANES):
            lanes = slice(block * LANES, (block + 1) * LANES)
            dx = east[block : block + 1, :] - kx
            dy = north[block : block + 1, :] - ky
            square = dx * dx + dy * dy
            high_ref[rows, lanes], low_ref[rows, lanes] = halves(jnp.exp2(-(square * lax.rsqrt(square))))
        total = dot_nt(high_ref[rows, :], weights[...]) + dot_nt(low_ref[rows, :], weights[...])
        found = folded_columns(total, probes)
        out_ref[:, rows] = found + before_ref[:, rows] if follows else found


def project(stack, knot_locs, scale, extent, before=None):
    probes, points, knots = stack.shape[0], stack.shape[1] - 2 * LANES, knot_locs.shape[1]
    out_shape = [
        jax.ShapeDtypeStruct((probes, knots), jnp.float32),
        pltpu.VMEM((knots, points), jnp.bfloat16),
        pltpu.VMEM((knots, points), jnp.bfloat16),
    ]
    if before is None:
        operands = (stack, knot_locs)
        out_shape += [
            jax.ShapeDtypeStruct((knots, 8), jnp.float32),
            jax.ShapeDtypeStruct(stack.shape, jnp.float32),
        ]
    else:
        operands = (stack, before[0], before[3])
    found = pl.pallas_call(
        functools.partial(project_kernel, scale, grain_of(scale * extent), before is not None),
        out_shape=out_shape,
        in_specs=[VMEM] * len(operands),
        out_specs=[VMEM] * len(out_shape),
        scratch_shapes=[pltpu.VMEM((LANES, points), jnp.bfloat16)],
        compiler_params=pltpu.CompilerParams(vmem_limit_bytes=LIMIT),
        cost_estimate=cost(2800, points * knots, 2),
        name="project",
    )(*operands)
    return found if before is None else [*found, *before[3:]]


def factor_kernel(scale, step, parts, before_ref, proj_ref, *rest):
    highs, lows, (out_ref, weights) = rest[:parts], rest[parts : 2 * parts], rest[-2:]
    probes, depth = proj_ref.shape
    weights[...] = stacked_halves(proj_ref[...] * scale)
    owner = lax.rem(lax.axis_index("knot") + step, lax.axis_size("knot"))
    deep = pl.ds(pl.multiple_of(owner * depth, depth), depth)
    rows = highs[0].shape[1]
    tile = min(TILE, rows)
    for part, (high_ref, low_ref) in enumerate(zip(highs, lows)):
        for start in range(0, rows, tile):
            here = slice(start, start + tile)
            found = folded(dot_nn(weights[...], high_ref[deep, here]) + dot_nn(weights[...], low_ref[deep, here]))
            target = slice(part * rows + start, part * rows + start + tile)
            if before_ref is not None:
                found = found + before_ref[:, target]
            out_ref[:, target] = found


def factored(before, projection, splits, scale, step):
    probes, depth = projection.shape
    highs, lows = [
        [pltpu.with_memory_space_constraint(split[half], pltpu.VMEM) for split in splits] for half in range(2)
    ]
    rows = sum(high.shape[1] for high in highs)
    kernel = functools.partial(factor_kernel, scale, step, len(splits))
    operands = (projection, *highs, *lows)
    if before is None:
        kernel = functools.partial(kernel, None)
    else:
        operands = (before, *operands)
    return pl.pallas_call(
        kernel,
        out_shape=jax.ShapeDtypeStruct((probes, rows), jnp.float32),
        in_specs=[VMEM] * len(operands),
        out_specs=VMEM,
        scratch_shapes=[pltpu.VMEM((2 * probes, depth), jnp.bfloat16)],
        compiler_params=pltpu.CompilerParams(vmem_limit_bytes=LIMIT),
        cost_estimate=cost(1000, rows * depth),
        name="factor",
    )(*operands)


def spread_kernel(scale, factor_ref, high_ref, low_ref, out_ref):
    points = high_ref.shape[1]
    tile = min(TILE, points)
    weights = stacked_halves(factor_ref[...] * scale)
    for start in range(0, points, tile):
        lanes = slice(start, start + tile)
        out_ref[:, lanes] = folded(dot_nn(weights, high_ref[:, lanes]) + dot_nn(weights, low_ref[:, lanes]))


def spread(factor, high, low, scale):
    (probes, knots), points = factor.shape, high.shape[1]
    high = pltpu.with_memory_space_constraint(high, pltpu.VMEM)
    low = pltpu.with_memory_space_constraint(low, pltpu.VMEM)
    return pl.pallas_call(
        functools.partial(spread_kernel, scale),
        out_shape=jax.ShapeDtypeStruct((probes, points), jnp.float32),
        in_specs=[VMEM, VMEM, VMEM],
        out_specs=VMEM,
        compiler_params=pltpu.CompilerParams(vmem_limit_bytes=LIMIT),
        cost_estimate=cost(850, knots * points),
        name="spread",
    )(factor, high, low)


def covariance(square):
    apart = square * lax.rsqrt(square)
    remain = jnp.maximum(4.0 - apart, 0.0)
    twice = remain * remain
    return (jnp.exp2(apart * (-LOG2E / (COV_RANGE * TAPER_RATE))) * (twice * twice)) * (5.0 - remain)


def beside_kernel(first, first_row, grain, ids_ref, counts_ref, own_ref, values_ref, coords_ref, precision_ref, *rest):
    out_ref, high_ref, low_ref = rest[-3:]
    own_blocks, slots = ids_ref.shape
    block = LANES
    probes = own_ref.shape[0]
    span = own_blocks + 2
    zeros_place = coords_ref.shape[1] // block
    column = lax.axis_index("space")
    north_base = lax.axis_index("knot") * own_blocks - 1
    north_cells = lax.axis_size("knot") * own_blocks
    own_columns = [
        on_grid(jnp.transpose(coordinate_rows(own_ref, own_blocks * block, axis) * TAPER_RATE), grain)
        for axis in range(2)
    ]

    def place(group, slot):
        ahead = ids_ref[group, slot] - (column - 1) * north_cells
        east = jnp.where(ahead >= north_cells, 1, 0) + jnp.where(ahead >= 2 * north_cells, 1, 0)
        strip = jnp.where(east == 1, 0, 2 - lax.rem(column + lax.div(east, 2) + 1, 2))
        index = strip * span + (ahead - east * north_cells - north_base)
        return lanes_of(index), lanes_of(jnp.where(slot < counts_ref[group], index, zeros_place))

    def lanes_of(index):
        return pl.ds(pl.multiple_of(index * block, block), block)

    depth, rows = high_ref.shape
    tile = min(TILE, rows)
    wide = min(TILE, depth)
    tiles = [(start, deep) for start in range(0, rows, tile) for deep in range(0, depth, wide)]
    groups = out_ref.shape[1] // block
    turns = groups * -(-slots // 2)

    for index in range(groups):
        group = first + index
        px, py = [turned[:, group : group + 1] for turned in own_columns]
        total = jnp.zeros((block, 2 * probes), jnp.float32)
        for pair in range(0, slots, 2):
            highs, lows, parts = [], [], []
            for slot in range(pair, min(pair + 2, slots)):
                lanes, value_lanes = place(group, slot)
                dx = px - coords_ref[0:1, lanes]
                dy = py - coords_ref[1:2, lanes]
                high, low = halves(covariance(dx * dx + dy * dy))
                highs.append(high)
                lows.append(low)
                parts.append(values_ref[:, value_lanes])
            part = jnp.concatenate(parts, axis=1)
            total = total + (
                dot_nt(jnp.concatenate(highs, axis=1), part) + dot_nt(jnp.concatenate(lows, axis=1), part)
            )
            turn = index * -(-slots // 2) + pair // 2
            for start, deep in tiles[turn * len(tiles) // turns : (turn + 1) * len(tiles) // turns]:
                from_row = first_row + start
                turned = jnp.transpose(precision_ref[from_row : from_row + tile, deep : deep + wide])
                here = slice(deep, deep + wide), slice(start, start + tile)
                high_ref[here], low_ref[here] = halves(turned)
        out_ref[:, index * block : (index + 1) * block] = (
            TAPER_SCALE * folded_columns(total, probes)
            + NUGGET * own_ref[:, group * block : (group + 1) * block]
        )


def beside_round(ids, counts, own, values, coords, precision, extent, first, blocks, first_row, rows, after):
    slots, depth = ids.shape[1], precision.shape[1]
    return pl.pallas_call(
        functools.partial(beside_kernel, first, first_row, grain_of(TAPER_RATE * extent)),
        out_shape=(
            jax.ShapeDtypeStruct((own.shape[0], blocks * LANES), jnp.float32),
            pltpu.VMEM((depth, rows), jnp.bfloat16),
            pltpu.VMEM((depth, rows), jnp.bfloat16),
        ),
        in_specs=[SMEM, SMEM, VMEM, VMEM, VMEM, VMEM] + [ANY] * len(after),
        out_specs=(VMEM, VMEM, VMEM),
        compiler_params=pltpu.CompilerParams(vmem_limit_bytes=LIMIT),
        cost_estimate=cost(500, blocks * slots * LANES * LANES, 2),
        name="beside",
    )(ids, counts, own, values, coords, precision, *after)


def add_kernel(count, *refs):
    total = refs[0][...]
    for ref in refs[1:count]:
        total = total + ref[...]
    refs[-1][...] = total


def add_all(values, after):
    return pl.pallas_call(
        functools.partial(add_kernel, len(values)),
        out_shape=jax.ShapeDtypeStruct(values[0].shape, jnp.float32),
        in_specs=[VMEM] * len(values) + [ANY] * len(after),
        out_specs=VMEM,
        compiler_params=pltpu.CompilerParams(vmem_limit_bytes=LIMIT),
        name="add",
    )(*values, *after)


def butterfly_rounds(count):
    assert count & (count - 1) == 0
    bits = [1 << i for i in range(count.bit_length() - 1)]
    rounds = [(low | high, high, low) for low, high in zip(bits[0::2], bits[1::2])]
    rounds[1:] = [(high, both, low) for both, high, low in rounds[1:]]
    return rounds + [(bit,) for bit in bits[len(rounds) * 2 :]]


def butterfly_round(value, axis, other, turn):
    count, groups = lax.axis_size(axis), lax.axis_size(other)
    rounds = butterfly_rounds(count)
    half = len(rounds) // 2 if len({len(steps) for steps in rounds}) == 1 else 0
    got = []
    for kind in range(len(rounds[turn])):
        pairs = []
        for j in range(groups):
            step = rounds[(turn + half * ((j + 1) % 2)) % len(rounds)][kind]
            pairs += [(i * groups + j, (i ^ step) * groups + j) for i in range(count)]
        got.append(lax.ppermute(value, (axis, other), pairs))
    return got


def shifted(value, axis, step):
    count = lax.axis_size(axis)
    if step % count == 0:
        return value
    return lax.ppermute(value, axis, [((i + step) % count, i) for i in range(count)])


def paired(value, axis, other, first):
    count, groups = lax.axis_size(axis), lax.axis_size(other)
    partner = {}
    for i in range(first, count - 1, 2):
        partner[i], partner[i + 1] = i + 1, i
    pairs = []
    for i in range(count):
        for j in range(groups):
            if i in partner:
                pairs.append((i * groups + j, partner[i] * groups + j))
            elif j ^ 1 < groups:
                pairs.append((i * groups + j, i * groups + (j ^ 1)))
    return lax.ppermute(value, (axis, other), pairs)


def shards(probes, locations, knot_locs, knot_precision, neighbours, counts):
    own_blocks = neighbours.shape[0]
    row_count = probes.shape[1]
    knot_total = knot_precision.shape[1]
    device_count = lax.axis_size(("space", "knot"))
    groups = lax.axis_size("knot")
    knot_range = KNOT_REACH * math.sqrt(own_blocks * device_count / knot_total)
    proj_scale = PROJ_GAIN * math.sqrt(knot_total / (row_count * device_count))

    stack, knots = prepare(probes, locations, knot_locs, own_blocks)
    chunks = [shifted(stack, "knot", step) for step in range(groups)]
    rate = LOG2E / knot_range
    extent = CELL * max(lax.axis_size("space"), groups * own_blocks)
    parts = []
    for chunk in chunks:
        parts.append(project(chunk, knots, rate, extent, parts[-1] if parts else None))
    stack = parts[0][4]

    strip = make_strip(chunks[-1], stack, chunks[1 % groups])
    odd = paired(strip, "space", "knot", 1)
    values, coords = assemble([strip, odd, paired(strip, "space", "knot", 0)], extent)
    projection = parts[-1][0]
    rounds = len(butterfly_rounds(lax.axis_size("space")))
    pieces = math.gcd(math.gcd(own_blocks, rounds), knot_precision.shape[0] // LANES)
    per_piece, per_split = own_blocks // pieces, knot_precision.shape[0] // pieces
    base, splits = [], []
    for turn in range(rounds):
        got = butterfly_round(projection, "space", "knot", turn)
        beside = []
        for i in range(pieces):
            if i * rounds // pieces == turn:
                done = beside_round(
                    neighbours, counts, stack, values, coords, knot_precision, extent,
                    i * per_piece, per_piece, i * per_split, per_split, [projection],
                )
                base.append(done[0])
                splits.append(done[1:])
                beside.extend(done)
        projection = add_all([projection, *got], beside)
    factor = factored(None, projection, splits, proj_scale, 0)
    for step in range(1, groups):
        factor = factored(factor, shifted(projection, "knot", step), splits, proj_scale, step)
    total = jnp.concatenate(base, axis=1)
    for step in reversed(range(groups)):
        share = spread(factor, parts[step][1], parts[step][2], LOW_SCALE * EXPAND_GAIN)
        total = total + shifted(share, "knot", -step)
    return total


def solution(mesh):
    return jax.shard_map(
        shards,
        mesh=mesh,
        in_specs=(
            P(None, ("space", "knot")),
            P(None, ("space", "knot")),
            P(None, "knot"),
            P("knot", None),
            P(("space", "knot"), None),
            P(("space", "knot")),
        ),
        out_specs=P(None, ("space", "knot")),
        check_vma=False,
    )
```

```python
import functools
import math

import jax
import jax.numpy as jnp
from jax import lax
from jax.experimental import pallas as pl
from jax.experimental.pallas import tpu as pltpu
from jax.sharding import PartitionSpec as P

COV_RANGE = 0.05
TAPER_LEN = 0.15
KNOT_REACH = 0.15
TAPER_SCALE = 0.1
PROJ_GAIN = 0.5
EXPAND_GAIN = 0.5
LOW_SCALE = 0.5
NUGGET = 0.25
LOG2E = math.log2(math.e)
TAPER_RATE = 4.0 / TAPER_LEN
CELL = 0.1
TILE = 256
LANES = 128
HALF_GRAIN = 2.0**-24
LIMIT = 6 * 1024 * 1024
VMEM = pl.BlockSpec(memory_space=pltpu.VMEM)
HBM = pl.BlockSpec(memory_space=pltpu.HBM)
ANY = pl.BlockSpec(memory_space=pl.ANY)
SMEM = pl.BlockSpec(memory_space=pltpu.SMEM)


def halves(x):
    high = x.astype(jnp.bfloat16)
    return high, (x - high.astype(jnp.float32)).astype(jnp.bfloat16)


def stacked_halves(x):
    return jnp.concatenate(halves(x), axis=0)


def folded(x):
    rows = x.shape[0] // 2
    return x[:rows] + x[rows:]


def dot_nt(left, right):
    return lax.dot_general(
        left, right, (((1,), (1,)), ((), ())), preferred_element_type=jnp.float32
    )


def dot_nn(left, right):
    return jnp.dot(left, right, preferred_element_type=jnp.float32)


def padded_halves(x, rows):
    fill = jnp.zeros((rows - 2 * x.shape[0], x.shape[1]), jnp.bfloat16)
    return jnp.concatenate([*halves(x), fill], axis=0)


def folded_columns(x, rows):
    x = jnp.transpose(x)
    return x[:rows] + x[rows : 2 * rows]


def cost(work, pairs, transcendentals=0):
    return pl.CostEstimate(flops=work * pairs, bytes_accessed=4 * pairs, transcendentals=transcendentals * pairs)


def coordinate_rows(ref, points, axis):
    start = points + axis * LANES
    return ref[:, start : start + LANES]


def prepare_kernel(blocks, probes_ref, locations_ref, knots_ref, stack_ref, knots_out_ref, coords, sems):
    points = probes_ref.shape[1]
    block = points // blocks
    copies = [
        pltpu.make_async_copy(probes_ref, stack_ref.at[:, pl.ds(0, points)], sems.at[0]),
        pltpu.make_async_copy(locations_ref, coords, sems.at[1]),
        pltpu.make_async_copy(knots_ref, knots_out_ref, sems.at[2]),
    ]
    for copy in copies:
        copy.start()
    for copy in copies:
        copy.wait()
    stack_ref[:, points:] = jnp.zeros((stack_ref.shape[0], 2 * LANES), jnp.float32)
    for axis in range(2):
        lanes = slice(points + axis * LANES, points + (axis + 1) * LANES)
        for index in range(blocks):
            stack_ref[index : index + 1, lanes] = coords[axis : axis + 1, index * block : (index + 1) * block]


def prepare(probes, locations, knot_locs, blocks):
    rows, points = probes.shape
    assert points == blocks * LANES and blocks + 2 <= rows
    probes, locations, knot_locs = [
        pltpu.with_memory_space_constraint(x, pltpu.HBM) for x in (probes, locations, knot_locs)
    ]
    return pl.pallas_call(
        functools.partial(prepare_kernel, blocks),
        out_shape=(
            jax.ShapeDtypeStruct((rows, points + 2 * LANES), jnp.float32),
            jax.ShapeDtypeStruct(knot_locs.shape, jnp.float32),
        ),
        in_specs=[HBM, HBM, HBM],
        out_specs=(VMEM, VMEM),
        scratch_shapes=[pltpu.VMEM(locations.shape, jnp.float32), pltpu.SemaphoreType.DMA((3,))],
        compiler_params=pltpu.CompilerParams(vmem_limit_bytes=LIMIT),
        name="prepare",
    )(probes, locations, knot_locs)


def strip_kernel(below_ref, own_ref, above_ref, out_ref):
    rows, width = own_ref.shape
    points = width - 2 * LANES
    blocks = points // LANES
    out_ref[:, :LANES] = below_ref[:, points - LANES : points]
    out_ref[:, LANES : points + LANES] = own_ref[:, :points]
    out_ref[:, points + LANES : points + 2 * LANES] = above_ref[:, :LANES]
    for axis in range(2):
        lanes = slice(points + axis * LANES, points + (axis + 1) * LANES)
        target = slice(lanes.start + 2 * LANES, lanes.stop + 2 * LANES)
        out_ref[:, target] = jnp.zeros((rows, LANES), jnp.float32)
        out_ref[0:1, target] = below_ref[blocks - 1 : blocks, lanes]
        out_ref[1 : blocks + 1, target] = own_ref[:blocks, lanes]
        out_ref[blocks + 1 : blocks + 2, target] = above_ref[0:1, lanes]


def make_strip(below, own, above):
    return pl.pallas_call(
        strip_kernel,
        out_shape=jax.ShapeDtypeStruct((own.shape[0], own.shape[1] + 2 * LANES), jnp.float32),
        in_specs=[VMEM, VMEM, VMEM],
        out_specs=VMEM,
        compiler_params=pltpu.CompilerParams(vmem_limit_bytes=LIMIT),
        name="strip",
    )(below, own, above)


def assemble_kernel(grain, own_ref, odd_ref, even_ref, values_ref, coords_ref):
    probes, width = own_ref.shape
    points = width - 2 * LANES
    for turn, ref in enumerate((own_ref, odd_ref, even_ref)):
        start = turn * points
        values_ref[:, start : start + points] = stacked_halves(ref[:, :points] * (1.0 / 256.0))
        for axis in range(2):
            rows = off_grid(coordinate_rows(ref, points, axis) * TAPER_RATE, grain)
            for index in range(points // LANES):
                lanes = slice(start + index * LANES, start + (index + 1) * LANES)
                coords_ref[axis : axis + 1, lanes] = rows[index : index + 1]
    values_ref[:, 3 * points :] = jnp.zeros((2 * probes, LANES), jnp.bfloat16)


def assemble(strips, extent):
    probes, width = strips[0].shape
    near = 3 * (width - 2 * LANES)
    return pl.pallas_call(
        functools.partial(assemble_kernel, grain_of(TAPER_RATE * extent)),
        out_shape=(
            jax.ShapeDtypeStruct((2 * probes, near + LANES), jnp.bfloat16),
            jax.ShapeDtypeStruct((2, near), jnp.float32),
        ),
        in_specs=[VMEM] * 3,
        out_specs=(VMEM, VMEM),
        compiler_params=pltpu.CompilerParams(vmem_limit_bytes=LIMIT),
        name="assemble",
    )(*strips)


def grain_of(bound):
    return 2.0 ** math.ceil(math.log2(1.01 * bound))


def on_grid(x, grain):
    return (x + grain) - grain


def off_grid(x, grain):
    return (x + grain) - (grain - grain * HALF_GRAIN)


def project_kernel(scale, grain, follows, stack_ref, *rest):
    if follows:
        before_ref, columns, out_ref, high_ref, low_ref, weights = rest
    else:
        knots_ref, out_ref, high_ref, low_ref, columns, copy_ref, weights = rest
        copy_ref[...] = stack_ref[...]
        fill = jnp.zeros((6, knots_ref.shape[1]), jnp.float32)
        columns[...] = jnp.transpose(jnp.concatenate([off_grid(knots_ref[...] * scale, grain), fill], axis=0))
    knots, points = high_ref.shape
    probes = stack_ref.shape[0]
    tile = min(TILE, knots)
    weights[...] = padded_halves(stack_ref[:, :points], weights.shape[0])
    east, north = [on_grid(coordinate_rows(stack_ref, points, axis) * scale, grain) for axis in range(2)]

    for start in range(0, knots, tile):
        rows = slice(start, start + tile)
        kx, ky = [columns[rows, axis : axis + 1] for axis in range(2)]
        for block in range(points // LANES):
            lanes = slice(block * LANES, (block + 1) * LANES)
            dx = east[block : block + 1, :] - kx
            dy = north[block : block + 1, :] - ky
            square = dx * dx + dy * dy
            high_ref[rows, lanes], low_ref[rows, lanes] = halves(jnp.exp2(-lax.sqrt(square)))
        total = dot_nt(high_ref[rows, :], weights[...]) + dot_nt(low_ref[rows, :], weights[...])
        found = folded_columns(total, probes)
        out_ref[:, rows] = found + before_ref[:, rows] if follows else found


def project(stack, knot_locs, scale, extent, before=None):
    probes, points, knots = stack.shape[0], stack.shape[1] - 2 * LANES, knot_locs.shape[1]
    out_shape = [
        jax.ShapeDtypeStruct((probes, knots), jnp.float32),
        pltpu.VMEM((knots, points), jnp.bfloat16),
        pltpu.VMEM((knots, points), jnp.bfloat16),
    ]
    if before is None:
        operands = (stack, knot_locs)
        out_shape += [
            jax.ShapeDtypeStruct((knots, 8), jnp.float32),
            jax.ShapeDtypeStruct(stack.shape, jnp.float32),
        ]
    else:
        operands = (stack, before[0], before[3])
    found = pl.pallas_call(
        functools.partial(project_kernel, scale, grain_of(scale * extent), before is not None),
        out_shape=out_shape,
        in_specs=[VMEM] * len(operands),
        out_specs=[VMEM] * len(out_shape),
        scratch_shapes=[pltpu.VMEM((LANES, points), jnp.bfloat16)],
        compiler_params=pltpu.CompilerParams(vmem_limit_bytes=LIMIT),
        cost_estimate=cost(2800, points * knots, 2),
        name="project",
    )(*operands)
    return found if before is None else [*found, *before[3:]]


def factor_kernel(scale, step, parts, before_ref, proj_ref, *rest):
    highs, lows, (out_ref, weights) = rest[:parts], rest[parts : 2 * parts], rest[-2:]
    probes, depth = proj_ref.shape
    weights[...] = stacked_halves(proj_ref[...] * scale)
    owner = lax.rem(lax.axis_index("knot") + step, lax.axis_size("knot"))
    deep = pl.ds(pl.multiple_of(owner * depth, depth), depth)
    rows = highs[0].shape[1]
    tile = min(TILE, rows)
    for part, (high_ref, low_ref) in enumerate(zip(highs, lows)):
        for start in range(0, rows, tile):
            here = slice(start, start + tile)
            found = folded(dot_nn(weights[...], high_ref[deep, here]) + dot_nn(weights[...], low_ref[deep, here]))
            target = slice(part * rows + start, part * rows + start + tile)
            if before_ref is not None:
                found = found + before_ref[:, target]
            out_ref[:, target] = found


def factored(before, projection, splits, scale, step):
    probes, depth = projection.shape
    highs, lows = [
        [pltpu.with_memory_space_constraint(split[half], pltpu.VMEM) for split in splits] for half in range(2)
    ]
    rows = sum(high.shape[1] for high in highs)
    kernel = functools.partial(factor_kernel, scale, step, len(splits))
    operands = (projection, *highs, *lows)
    if before is None:
        kernel = functools.partial(kernel, None)
    else:
        operands = (before, *operands)
    return pl.pallas_call(
        kernel,
        out_shape=jax.ShapeDtypeStruct((probes, rows), jnp.float32),
        in_specs=[VMEM] * len(operands),
        out_specs=VMEM,
        scratch_shapes=[pltpu.VMEM((2 * probes, depth), jnp.bfloat16)],
        compiler_params=pltpu.CompilerParams(vmem_limit_bytes=LIMIT),
        cost_estimate=cost(1000, rows * depth),
        name="factor",
    )(*operands)


def spread_kernel(scale, factor_ref, high_ref, low_ref, *rest):
    *base, out_ref = rest
    points = high_ref.shape[1]
    tile = min(TILE, points)
    weights = stacked_halves(factor_ref[...] * scale)
    for start in range(0, points, tile):
        lanes = slice(start, start + tile)
        out_ref[:, lanes] = folded(dot_nn(weights, high_ref[:, lanes]) + dot_nn(weights, low_ref[:, lanes]))
    start = 0
    for ref in base:
        lanes = slice(start, start + ref.shape[1])
        out_ref[:, lanes] = out_ref[:, lanes] + ref[...]
        start = lanes.stop


def spread(factor, high, low, scale, base=()):
    (probes, knots), points = factor.shape, high.shape[1]
    high = pltpu.with_memory_space_constraint(high, pltpu.VMEM)
    low = pltpu.with_memory_space_constraint(low, pltpu.VMEM)
    return pl.pallas_call(
        functools.partial(spread_kernel, scale),
        out_shape=jax.ShapeDtypeStruct((probes, points), jnp.float32),
        in_specs=[VMEM] * (3 + len(base)),
        out_specs=VMEM,
        compiler_params=pltpu.CompilerParams(vmem_limit_bytes=LIMIT),
        cost_estimate=cost(850, knots * points),
        name="spread",
    )(factor, high, low, *base)


def finish_kernel(count, *refs):
    out_ref, total, sems = refs[count:]
    half = total.shape[0] // 2
    copies = []
    for part in range(2):
        rows = pl.ds(part * half, half)
        value = refs[0][rows, :]
        for ref in refs[1:count]:
            value = value + ref[rows, :]
        total[rows, :] = value
        copies.append(pltpu.make_async_copy(total.at[rows, :], out_ref.at[rows, :], sems.at[part]))
        copies[-1].start()
    for copy in copies:
        copy.wait()


def finish(values):
    return pl.pallas_call(
        functools.partial(finish_kernel, len(values)),
        out_shape=jax.ShapeDtypeStruct(values[0].shape, jnp.float32),
        in_specs=[VMEM] * len(values),
        out_specs=HBM,
        scratch_shapes=[pltpu.VMEM(values[0].shape, jnp.float32), pltpu.SemaphoreType.DMA((2,))],
        compiler_params=pltpu.CompilerParams(vmem_limit_bytes=LIMIT),
        name="finish",
    )(*values)


def covariance(square):
    apart = lax.sqrt(square)
    remain = jnp.maximum(4.0 - apart, 0.0)
    twice = remain * remain
    return (jnp.exp2(apart * (-LOG2E / (COV_RANGE * TAPER_RATE))) * (twice * twice)) * (5.0 - remain)


def beside_kernel(first, first_row, grain, ids_ref, counts_ref, own_ref, values_ref, coords_ref, precision_ref, *rest):
    out_ref, high_ref, low_ref = rest[-3:]
    own_blocks, slots = ids_ref.shape
    block = LANES
    probes = own_ref.shape[0]
    span = own_blocks + 2
    zeros_place = coords_ref.shape[1] // block
    column = lax.axis_index("space")
    north_base = lax.axis_index("knot") * own_blocks - 1
    north_cells = lax.axis_size("knot") * own_blocks
    own_columns = [
        on_grid(jnp.transpose(coordinate_rows(own_ref, own_blocks * block, axis) * TAPER_RATE), grain)
        for axis in range(2)
    ]

    def place(group, slot):
        ahead = ids_ref[group, slot] - (column - 1) * north_cells
        east = jnp.where(ahead >= north_cells, 1, 0) + jnp.where(ahead >= 2 * north_cells, 1, 0)
        strip = jnp.where(east == 1, 0, 2 - lax.rem(column + lax.div(east, 2) + 1, 2))
        index = strip * span + (ahead - east * north_cells - north_base)
        return lanes_of(index), lanes_of(jnp.where(slot < counts_ref[group], index, zeros_place))

    def lanes_of(index):
        return pl.ds(pl.multiple_of(index * block, block), block)

    depth, rows = high_ref.shape
    tile = min(TILE, rows)
    wide = min(TILE, depth)
    tiles = [(start, deep) for start in range(0, rows, tile) for deep in range(0, depth, wide)]
    groups = out_ref.shape[1] // block
    turns = groups * -(-slots // 2)

    for index in range(groups):
        group = first + index
        px, py = [turned[:, group : group + 1] for turned in own_columns]
        total = jnp.zeros((block, 2 * probes), jnp.float32)
        for pair in range(0, slots, 2):
            highs, lows, parts = [], [], []
            for slot in range(pair, min(pair + 2, slots)):
                lanes, value_lanes = place(group, slot)
                dx = px - coords_ref[0:1, lanes]
                dy = py - coords_ref[1:2, lanes]
                high, low = halves(covariance(dx * dx + dy * dy))
                highs.append(high)
                lows.append(low)
                parts.append(values_ref[:, value_lanes])
            part = jnp.concatenate(parts, axis=1)
            total = total + (
                dot_nt(jnp.concatenate(highs, axis=1), part) + dot_nt(jnp.concatenate(lows, axis=1), part)
            )
            turn = index * -(-slots // 2) + pair // 2
            for start, deep in tiles[turn * len(tiles) // turns : (turn + 1) * len(tiles) // turns]:
                from_row = first_row + start
                turned = jnp.transpose(precision_ref[from_row : from_row + tile, deep : deep + wide])
                here = slice(deep, deep + wide), slice(start, start + tile)
                high_ref[here], low_ref[here] = halves(turned)
        out_ref[:, index * block : (index + 1) * block] = (
            TAPER_SCALE * folded_columns(total, probes)
            + NUGGET * own_ref[:, group * block : (group + 1) * block]
        )


def beside_round(ids, counts, own, values, coords, precision, extent, first, blocks, first_row, rows, after):
    slots, depth = ids.shape[1], precision.shape[1]
    return pl.pallas_call(
        functools.partial(beside_kernel, first, first_row, grain_of(TAPER_RATE * extent)),
        out_shape=(
            jax.ShapeDtypeStruct((own.shape[0], blocks * LANES), jnp.float32),
            pltpu.VMEM((depth, rows), jnp.bfloat16),
            pltpu.VMEM((depth, rows), jnp.bfloat16),
        ),
        in_specs=[SMEM, SMEM, VMEM, VMEM, VMEM, VMEM] + [ANY] * len(after),
        out_specs=(VMEM, VMEM, VMEM),
        compiler_params=pltpu.CompilerParams(vmem_limit_bytes=LIMIT),
        cost_estimate=cost(500, blocks * slots * LANES * LANES, 2),
        name="beside",
    )(ids, counts, own, values, coords, precision, *after)


def add_kernel(count, *refs):
    total = refs[0][...]
    for ref in refs[1:count]:
        total = total + ref[...]
    refs[-1][...] = total


def add_all(values, after):
    return pl.pallas_call(
        functools.partial(add_kernel, len(values)),
        out_shape=jax.ShapeDtypeStruct(values[0].shape, jnp.float32),
        in_specs=[VMEM] * len(values) + [ANY] * len(after),
        out_specs=VMEM,
        compiler_params=pltpu.CompilerParams(vmem_limit_bytes=LIMIT),
        name="add",
    )(*values, *after)


def butterfly_rounds(count):
    assert count & (count - 1) == 0
    bits = [1 << i for i in range(count.bit_length() - 1)]
    rounds = [(low | high, high, low) for low, high in zip(bits[0::2], bits[1::2])]
    rounds[1:] = [(high, both, low) for both, high, low in rounds[1:]]
    return rounds + [(bit,) for bit in bits[len(rounds) * 2 :]]


def butterfly_round(value, axis, other, turn):
    count, groups = lax.axis_size(axis), lax.axis_size(other)
    rounds = butterfly_rounds(count)
    half = len(rounds) // 2 if len({len(steps) for steps in rounds}) == 1 else 0
    got = []
    for kind in range(len(rounds[turn])):
        pairs = []
        for j in range(groups):
            step = rounds[(turn + half * ((j + 1) % 2)) % len(rounds)][kind]
            pairs += [(i * groups + j, (i ^ step) * groups + j) for i in range(count)]
        got.append(lax.ppermute(value, (axis, other), pairs))
    return got


def shifted(value, axis, step):
    count = lax.axis_size(axis)
    if step % count == 0:
        return value
    return lax.ppermute(value, axis, [((i + step) % count, i) for i in range(count)])


def paired(value, axis, other, first):
    count, groups = lax.axis_size(axis), lax.axis_size(other)
    partner = {}
    for i in range(first, count - 1, 2):
        partner[i], partner[i + 1] = i + 1, i
    pairs = []
    for i in range(count):
        for j in range(groups):
            if i in partner:
                pairs.append((i * groups + j, partner[i] * groups + j))
            elif j ^ 1 < groups:
                pairs.append((i * groups + j, i * groups + (j ^ 1)))
    return lax.ppermute(value, (axis, other), pairs)


def shards(probes, locations, knot_locs, knot_precision, neighbours, counts):
    own_blocks = neighbours.shape[0]
    row_count = probes.shape[1]
    knot_total = knot_precision.shape[1]
    device_count = lax.axis_size(("space", "knot"))
    groups = lax.axis_size("knot")
    knot_range = KNOT_REACH * math.sqrt(own_blocks * device_count / knot_total)
    proj_scale = PROJ_GAIN * math.sqrt(knot_total / (row_count * device_count))

    stack, knots = prepare(probes, locations, knot_locs, own_blocks)
    chunks = [shifted(stack, "knot", step) for step in range(groups)]
    rate = LOG2E / knot_range
    extent = CELL * max(lax.axis_size("space"), groups * own_blocks)
    parts = []
    for chunk in chunks:
        parts.append(project(chunk, knots, rate, extent, parts[-1] if parts else None))
    stack = parts[0][4]

    strip = make_strip(chunks[-1], stack, chunks[1 % groups])
    odd = paired(strip, "space", "knot", 1)
    values, coords = assemble([strip, odd, paired(strip, "space", "knot", 0)], extent)
    projection = parts[-1][0]
    rounds = len(butterfly_rounds(lax.axis_size("space")))
    pieces = math.gcd(math.gcd(own_blocks, rounds), knot_precision.shape[0] // LANES)
    per_piece, per_split = own_blocks // pieces, knot_precision.shape[0] // pieces
    base, splits = [], []
    for turn in range(rounds):
        got = butterfly_round(projection, "space", "knot", turn)
        beside = []
        for i in range(pieces):
            if i * rounds // pieces == turn:
                done = beside_round(
                    neighbours, counts, stack, values, coords, knot_precision, extent,
                    i * per_piece, per_piece, i * per_split, per_split, [projection],
                )
                base.append(done[0])
                splits.append(done[1:])
                beside.extend(done)
        projection = add_all([projection, *got], beside)
    factor = factored(None, projection, splits, proj_scale, 0)
    for step in range(1, groups):
        factor = factored(factor, shifted(projection, "knot", step), splits, proj_scale, step)
    gain = LOW_SCALE * EXPAND_GAIN
    shares = []
    for step in reversed(range(1, groups)):
        shares.append(shifted(spread(factor, parts[step][1], parts[step][2], gain), "knot", -step))
    return finish([spread(factor, parts[0][1], parts[0][2], gain, base), *shares])


def solution(mesh):
    return jax.shard_map(
        shards,
        mesh=mesh,
        in_specs=(
            P(None, ("space", "knot")),
            P(None, ("space", "knot")),
            P(None, "knot"),
            P("knot", None),
            P(("space", "knot"), None),
            P(("space", "knot")),
        ),
        out_specs=P(None, ("space", "knot")),
        check_vma=False,
    )
```

```python
import functools
import math

import jax
import jax.numpy as jnp
from jax import lax
from jax.experimental import pallas as pl
from jax.experimental.pallas import tpu as pltpu
from jax.sharding import PartitionSpec as P

COV_RANGE = 0.05
TAPER_LEN = 0.15
KNOT_REACH = 0.15
TAPER_SCALE = 0.1
PROJ_GAIN = 0.5
EXPAND_GAIN = 0.5
LOW_SCALE = 0.5
NUGGET = 0.25
LOG2E = math.log2(math.e)
TAPER_RATE = 4.0 / TAPER_LEN
CELL = 0.1
TILE = 256
LANES = 128
HALF_GRAIN = 2.0**-24
LIMIT = 6 * 1024 * 1024
VMEM = pl.BlockSpec(memory_space=pltpu.VMEM)
HBM = pl.BlockSpec(memory_space=pltpu.HBM)
ANY = pl.BlockSpec(memory_space=pl.ANY)
SMEM = pl.BlockSpec(memory_space=pltpu.SMEM)


def halves(x):
    high = x.astype(jnp.bfloat16)
    return high, (x - high.astype(jnp.float32)).astype(jnp.bfloat16)


def stacked_halves(x):
    return jnp.concatenate(halves(x), axis=0)


def folded(x):
    rows = x.shape[0] // 2
    return x[:rows] + x[rows:]


def dot_nt(left, right):
    return lax.dot_general(
        left, right, (((1,), (1,)), ((), ())), preferred_element_type=jnp.float32
    )


def dot_nn(left, right):
    return jnp.dot(left, right, preferred_element_type=jnp.float32)


def padded_halves(x, rows):
    fill = jnp.zeros((rows - 2 * x.shape[0], x.shape[1]), jnp.bfloat16)
    return jnp.concatenate([*halves(x), fill], axis=0)


def folded_columns(x, rows):
    x = jnp.transpose(x)
    return x[:rows] + x[rows : 2 * rows]


def cost(work, pairs, transcendentals=0):
    return pl.CostEstimate(flops=work * pairs, bytes_accessed=4 * pairs, transcendentals=transcendentals * pairs)


def coordinate_rows(ref, points, axis):
    blocks = points // LANES
    return ref[axis * blocks : (axis + 1) * blocks, points : points + LANES]


def prepare_kernel(blocks, probes_ref, locations_ref, knots_ref, stack_ref, knots_out_ref, coords, sems):
    points = probes_ref.shape[1]
    copies = [
        pltpu.make_async_copy(probes_ref, stack_ref.at[:, pl.ds(0, points)], sems.at[0]),
        pltpu.make_async_copy(locations_ref, coords, sems.at[1]),
        pltpu.make_async_copy(knots_ref, knots_out_ref, sems.at[2]),
    ]
    for copy in copies:
        copy.start()
    for copy in copies:
        copy.wait()
    if 2 * blocks < stack_ref.shape[0]:
        stack_ref[:, points:] = jnp.zeros((stack_ref.shape[0], LANES), jnp.float32)
    for axis in range(2):
        for index in range(blocks):
            row = axis * blocks + index
            stack_ref[row : row + 1, points:] = coords[axis : axis + 1, index * LANES : (index + 1) * LANES]


def prepare(probes, locations, knot_locs, blocks):
    rows, points = probes.shape
    assert points == blocks * LANES and 2 * blocks <= rows
    probes, locations, knot_locs = [
        pltpu.with_memory_space_constraint(x, pltpu.HBM) for x in (probes, locations, knot_locs)
    ]
    return pl.pallas_call(
        functools.partial(prepare_kernel, blocks),
        out_shape=(
            jax.ShapeDtypeStruct((rows, points + LANES), jnp.float32),
            jax.ShapeDtypeStruct(knot_locs.shape, jnp.float32),
        ),
        in_specs=[HBM, HBM, HBM],
        out_specs=(VMEM, VMEM),
        scratch_shapes=[pltpu.VMEM(locations.shape, jnp.float32), pltpu.SemaphoreType.DMA((3,))],
        compiler_params=pltpu.CompilerParams(vmem_limit_bytes=LIMIT),
        name="prepare",
    )(probes, locations, knot_locs)


def corner_kernel(end, odd_ref, even_ref, *rest):
    out_ref = rest[-1]
    points = odd_ref.shape[1] - LANES
    upper = lax.axis_index("knot") > 0
    out_ref[...] = jnp.zeros(out_ref.shape, jnp.float32)
    for turn, ref in enumerate((odd_ref, even_ref)):
        start = 2 * turn * LANES
        coords = [coordinate_rows(ref, points, axis) for axis in range(2)]
        first = [ref[:, :LANES], *[rows[:1] for rows in coords]]
        last = [ref[:, points - LANES : points], *[rows[-1:] for rows in coords]]
        taken = {"first": first, "last": last, "inner": [jnp.where(upper, a, b) for a, b in zip(first, last)]}[end]
        out_ref[:, start : start + LANES] = taken[0]
        for axis in range(2):
            out_ref[axis : axis + 1, start + LANES : start + 2 * LANES] = taken[1 + axis]


def corner_blocks(end, strips, after):
    return pl.pallas_call(
        functools.partial(corner_kernel, end),
        out_shape=jax.ShapeDtypeStruct((strips[0].shape[0], 4 * LANES), jnp.float32),
        in_specs=[VMEM, VMEM] + [ANY] * len(after),
        out_specs=VMEM,
        compiler_params=pltpu.CompilerParams(vmem_limit_bytes=LIMIT),
        name="corner",
    )(*strips, *after)


def assemble_kernel(grain, own_ref, below_ref, above_ref, odd_ref, even_ref, *rest):
    *corners, values_ref, coords_ref = rest
    probes, width = own_ref.shape
    points = width - LANES
    blocks = points // LANES
    span = blocks + 2

    def put(place, vals, coords):
        count = vals.shape[1] // LANES
        values_ref[:, place * LANES : (place + count) * LANES] = stacked_halves(vals * (1.0 / 256.0))
        for axis in range(2):
            rows = off_grid(coords[axis] * TAPER_RATE, grain)
            for index in range(count):
                coords_ref[axis : axis + 1, (place + index) * LANES : (place + index + 1) * LANES] = rows[index : index + 1]

    def put_stack(place, ref, first, count):
        put(
            place,
            ref[:, first * LANES : (first + count) * LANES],
            [coordinate_rows(ref, points, axis)[first : first + count] for axis in range(2)],
        )

    def put_corner(place, ref, turn):
        start = 2 * turn * LANES
        both = slice(start + LANES, start + 2 * LANES)
        put(place, ref[:, start : start + LANES], [ref[axis : axis + 1, both] for axis in range(2)])

    put_stack(0, below_ref, blocks - 1, 1)
    put_stack(1, own_ref, 0, blocks)
    put_stack(1 + blocks, above_ref, 0, 1)
    for turn, ref in enumerate((odd_ref, even_ref)):
        place = (turn + 1) * span
        put_stack(place + 1, ref, 0, blocks)
        for corner, spot in zip(corners, (place, place + 1 + blocks)):
            put_corner(spot, corner, turn)
    values_ref[:, 3 * span * LANES :] = jnp.zeros((2 * probes, LANES), jnp.bfloat16)


def assemble(own, below, above, strips, corners, extent):
    probes, width = own.shape
    near = 3 * (width + LANES)
    return pl.pallas_call(
        functools.partial(assemble_kernel, grain_of(TAPER_RATE * extent)),
        out_shape=(
            jax.ShapeDtypeStruct((2 * probes, near + LANES), jnp.bfloat16),
            jax.ShapeDtypeStruct((2, near), jnp.float32),
        ),
        in_specs=[VMEM] * (5 + len(corners)),
        out_specs=(VMEM, VMEM),
        compiler_params=pltpu.CompilerParams(vmem_limit_bytes=LIMIT),
        name="assemble",
    )(own, below, above, *strips, *corners)


def grain_of(bound):
    return 2.0 ** math.ceil(math.log2(1.01 * bound))


def on_grid(x, grain):
    return (x + grain) - grain


def off_grid(x, grain):
    return (x + grain) - (grain - grain * HALF_GRAIN)


def project_kernel(scale, grain, follows, stack_ref, *rest):
    if follows:
        before_ref, columns, out_ref, high_ref, low_ref, weights = rest
    else:
        knots_ref, out_ref, high_ref, low_ref, columns, weights = rest
        fill = jnp.zeros((6, knots_ref.shape[1]), jnp.float32)
        columns[...] = jnp.transpose(jnp.concatenate([off_grid(knots_ref[...] * scale, grain), fill], axis=0))
    knots, points = high_ref.shape
    probes = stack_ref.shape[0]
    tile = min(TILE, knots)
    weights[...] = padded_halves(stack_ref[:, :points], weights.shape[0])
    east, north = [on_grid(coordinate_rows(stack_ref, points, axis) * scale, grain) for axis in range(2)]

    for start in range(0, knots, tile):
        rows = slice(start, start + tile)
        kx, ky = [columns[rows, axis : axis + 1] for axis in range(2)]
        for block in range(points // LANES):
            lanes = slice(block * LANES, (block + 1) * LANES)
            dx = east[block : block + 1, :] - kx
            dy = north[block : block + 1, :] - ky
            square = dx * dx + dy * dy
            high_ref[rows, lanes], low_ref[rows, lanes] = halves(jnp.exp2(-(square * lax.rsqrt(square))))
        total = dot_nt(high_ref[rows, :], weights[...]) + dot_nt(low_ref[rows, :], weights[...])
        found = folded_columns(total, probes)
        out_ref[:, rows] = found + before_ref[:, rows] if follows else found


def project(stack, knot_locs, scale, extent, before=None):
    probes, points, knots = stack.shape[0], stack.shape[1] - LANES, knot_locs.shape[1]
    out_shape = [
        jax.ShapeDtypeStruct((probes, knots), jnp.float32),
        pltpu.VMEM((knots, points), jnp.bfloat16),
        pltpu.VMEM((knots, points), jnp.bfloat16),
    ]
    if before is None:
        operands = (stack, knot_locs)
        out_shape.append(jax.ShapeDtypeStruct((knots, 8), jnp.float32))
    else:
        operands = (stack, before[0], before[3])
    found = pl.pallas_call(
        functools.partial(project_kernel, scale, grain_of(scale * extent), before is not None),
        out_shape=out_shape,
        in_specs=[VMEM] * len(operands),
        out_specs=[VMEM] * len(out_shape),
        scratch_shapes=[pltpu.VMEM((LANES, points), jnp.bfloat16)],
        compiler_params=pltpu.CompilerParams(vmem_limit_bytes=LIMIT),
        cost_estimate=cost(2800, points * knots, 2),
        name="project",
    )(*operands)
    return found if before is None else [*found, *before[3:]]


def factor_kernel(scale, step, parts, before_ref, proj_ref, *rest):
    highs, lows, (out_ref, weights) = rest[:parts], rest[parts : 2 * parts], rest[-2:]
    probes, depth = proj_ref.shape
    weights[...] = stacked_halves(proj_ref[...] * scale)
    owner = lax.rem(lax.axis_index("knot") + step, lax.axis_size("knot"))
    deep = pl.ds(pl.multiple_of(owner * depth, depth), depth)
    rows = highs[0].shape[1]
    tile = min(TILE, rows)
    for part, (high_ref, low_ref) in enumerate(zip(highs, lows)):
        for start in range(0, rows, tile):
            here = slice(start, start + tile)
            found = folded(dot_nn(weights[...], high_ref[deep, here]) + dot_nn(weights[...], low_ref[deep, here]))
            target = slice(part * rows + start, part * rows + start + tile)
            if before_ref is not None:
                found = found + before_ref[:, target]
            out_ref[:, target] = found


def factored(before, projection, splits, scale, step):
    probes, depth = projection.shape
    highs, lows = [
        [pltpu.with_memory_space_constraint(split[half], pltpu.VMEM) for split in splits] for half in range(2)
    ]
    rows = sum(high.shape[1] for high in highs)
    kernel = functools.partial(factor_kernel, scale, step, len(splits))
    operands = (projection, *highs, *lows)
    if before is None:
        kernel = functools.partial(kernel, None)
    else:
        operands = (before, *operands)
    return pl.pallas_call(
        kernel,
        out_shape=jax.ShapeDtypeStruct((probes, rows), jnp.float32),
        in_specs=[VMEM] * len(operands),
        out_specs=VMEM,
        scratch_shapes=[pltpu.VMEM((2 * probes, depth), jnp.bfloat16)],
        compiler_params=pltpu.CompilerParams(vmem_limit_bytes=LIMIT),
        cost_estimate=cost(1000, rows * depth),
        name="factor",
    )(*operands)


def spread_kernel(scale, factor_ref, high_ref, low_ref, out_ref):
    points = high_ref.shape[1]
    tile = min(TILE, points)
    weights = stacked_halves(factor_ref[...] * scale)
    for start in range(0, points, tile):
        lanes = slice(start, start + tile)
        out_ref[:, lanes] = folded(dot_nn(weights, high_ref[:, lanes]) + dot_nn(weights, low_ref[:, lanes]))


def spread(factor, high, low, scale):
    (probes, knots), points = factor.shape, high.shape[1]
    high = pltpu.with_memory_space_constraint(high, pltpu.VMEM)
    low = pltpu.with_memory_space_constraint(low, pltpu.VMEM)
    return pl.pallas_call(
        functools.partial(spread_kernel, scale),
        out_shape=jax.ShapeDtypeStruct((probes, points), jnp.float32),
        in_specs=[VMEM, VMEM, VMEM],
        out_specs=VMEM,
        compiler_params=pltpu.CompilerParams(vmem_limit_bytes=LIMIT),
        cost_estimate=cost(850, knots * points),
        name="spread",
    )(factor, high, low)


def covariance(square):
    apart = square * lax.rsqrt(square)
    remain = jnp.maximum(4.0 - apart, 0.0)
    twice = remain * remain
    return (jnp.exp2(apart * (-LOG2E / (COV_RANGE * TAPER_RATE))) * (twice * twice)) * (5.0 - remain)


def beside_kernel(chosen, first_row, grain, ids_ref, counts_ref, own_ref, values_ref, coords_ref, precision_ref, *rest):
    out_ref, high_ref, low_ref = rest[-3:]
    own_blocks, slots = ids_ref.shape
    block = LANES
    probes = own_ref.shape[0]
    span = own_blocks + 2
    zeros_place = coords_ref.shape[1] // block
    column = lax.axis_index("space")
    north_base = lax.axis_index("knot") * own_blocks - 1
    north_cells = lax.axis_size("knot") * own_blocks
    own_columns = [
        on_grid(jnp.transpose(coordinate_rows(own_ref, own_blocks * block, axis) * TAPER_RATE), grain)
        for axis in range(2)
    ]

    def place(group, slot):
        ahead = ids_ref[group, slot] - (column - 1) * north_cells
        east = jnp.where(ahead >= north_cells, 1, 0) + jnp.where(ahead >= 2 * north_cells, 1, 0)
        strip = jnp.where(east == 1, 0, 2 - lax.rem(column + lax.div(east, 2) + 1, 2))
        index = strip * span + (ahead - east * north_cells - north_base)
        return lanes_of(index), lanes_of(jnp.where(slot < counts_ref[group], index, zeros_place))

    def lanes_of(index):
        return pl.ds(pl.multiple_of(index * block, block), block)

    depth, rows = high_ref.shape
    tile = min(TILE, rows)
    wide = min(TILE, depth)
    tiles = [(start, deep) for start in range(0, rows, tile) for deep in range(0, depth, wide)]
    turns = len(chosen) * -(-slots // 2)

    for index, group in enumerate(chosen):
        px, py = [turned[:, group : group + 1] for turned in own_columns]
        total = jnp.zeros((block, 2 * probes), jnp.float32)
        for pair in range(0, slots, 2):
            highs, lows, parts = [], [], []
            for slot in range(pair, min(pair + 2, slots)):
                lanes, value_lanes = place(group, slot)
                dx = px - coords_ref[0:1, lanes]
                dy = py - coords_ref[1:2, lanes]
                high, low = halves(covariance(dx * dx + dy * dy))
                highs.append(high)
                lows.append(low)
                parts.append(values_ref[:, value_lanes])
            part = jnp.concatenate(parts, axis=1)
            total = total + (
                dot_nt(jnp.concatenate(highs, axis=1), part) + dot_nt(jnp.concatenate(lows, axis=1), part)
            )
            turn = index * -(-slots // 2) + pair // 2
            for start, deep in tiles[turn * len(tiles) // turns : (turn + 1) * len(tiles) // turns]:
                from_row = first_row + start
                turned = jnp.transpose(precision_ref[from_row : from_row + tile, deep : deep + wide])
                here = slice(deep, deep + wide), slice(start, start + tile)
                high_ref[here], low_ref[here] = halves(turned)
        out_ref[:, index * block : (index + 1) * block] = (
            TAPER_SCALE * folded_columns(total, probes)
            + NUGGET * own_ref[:, group * block : (group + 1) * block]
        )


def beside_round(ids, counts, own, values, coords, precision, extent, chosen, first_row, rows, after):
    slots, depth = ids.shape[1], precision.shape[1]
    return pl.pallas_call(
        functools.partial(beside_kernel, chosen, first_row, grain_of(TAPER_RATE * extent)),
        out_shape=(
            jax.ShapeDtypeStruct((own.shape[0], len(chosen) * LANES), jnp.float32),
            pltpu.VMEM((depth, rows), jnp.bfloat16),
            pltpu.VMEM((depth, rows), jnp.bfloat16),
        ),
        in_specs=[SMEM, SMEM, VMEM, VMEM, VMEM, VMEM] + [ANY] * len(after),
        out_specs=(VMEM, VMEM, VMEM),
        compiler_params=pltpu.CompilerParams(vmem_limit_bytes=LIMIT),
        cost_estimate=cost(500, len(chosen) * slots * LANES * LANES, 2),
        name="beside",
    )(ids, counts, own, values, coords, precision, *after)


def add_kernel(count, *refs):
    total = refs[0][...]
    for ref in refs[1:count]:
        total = total + ref[...]
    refs[-1][...] = total


def add_all(values, after):
    return pl.pallas_call(
        functools.partial(add_kernel, len(values)),
        out_shape=jax.ShapeDtypeStruct(values[0].shape, jnp.float32),
        in_specs=[VMEM] * len(values) + [ANY] * len(after),
        out_specs=VMEM,
        compiler_params=pltpu.CompilerParams(vmem_limit_bytes=LIMIT),
        name="add",
    )(*values, *after)


def butterfly_rounds(count):
    assert count & (count - 1) == 0
    bits = [1 << i for i in range(count.bit_length() - 1)]
    rounds = [(low | high, high, low) for low, high in zip(bits[0::2], bits[1::2])]
    rounds[1:] = [(high, both, low) for both, high, low in rounds[1:]]
    return rounds + [(bit,) for bit in bits[len(rounds) * 2 :]]


def butterfly_round(value, axis, other, turn):
    count, groups = lax.axis_size(axis), lax.axis_size(other)
    rounds = butterfly_rounds(count)
    half = len(rounds) // 2 if len({len(steps) for steps in rounds}) == 1 else 0
    got = []
    for kind in range(len(rounds[turn])):
        pairs = []
        for j in range(groups):
            step = rounds[(turn + half * ((j + 1) % 2)) % len(rounds)][kind]
            pairs += [(i * groups + j, (i ^ step) * groups + j) for i in range(count)]
        got.append(lax.ppermute(value, (axis, other), pairs))
    return got


def shifted(value, axis, step):
    count = lax.axis_size(axis)
    if step % count == 0:
        return value
    return lax.ppermute(value, axis, [((i + step) % count, i) for i in range(count)])


def paired(value, axis, other, first):
    count, groups = lax.axis_size(axis), lax.axis_size(other)
    partner = {}
    for i in range(first, count - 1, 2):
        partner[i], partner[i + 1] = i + 1, i
    pairs = []
    for i in range(count):
        for j in range(groups):
            if i in partner:
                pairs.append((i * groups + j, partner[i] * groups + j))
            elif j ^ 1 < groups:
                pairs.append((i * groups + j, i * groups + (j ^ 1)))
    return lax.ppermute(value, (axis, other), pairs)


def shards(probes, locations, knot_locs, knot_precision, neighbours, counts):
    own_blocks = neighbours.shape[0]
    row_count = probes.shape[1]
    knot_total = knot_precision.shape[1]
    device_count = lax.axis_size(("space", "knot"))
    groups = lax.axis_size("knot")
    knot_range = KNOT_REACH * math.sqrt(own_blocks * device_count / knot_total)
    proj_scale = PROJ_GAIN * math.sqrt(knot_total / (row_count * device_count))

    stack, knots = prepare(probes, locations, knot_locs, own_blocks)
    strips = [paired(stack, "space", "knot", 1), paired(stack, "space", "knot", 0)]
    chunks = [shifted(stack, "knot", step) for step in range(groups)]
    rate = LOG2E / knot_range
    extent = CELL * max(lax.axis_size("space"), groups * own_blocks)
    parts = []
    for chunk in chunks:
        parts.append(project(chunk, knots, rate, extent, parts[-1] if parts else None))
    projection = parts[-1][0]
    if groups == 2:
        low = high = shifted(corner_blocks("inner", strips, [projection]), "knot", 1)
    else:
        low = shifted(corner_blocks("last", strips, [projection]), "knot", -1)
        high = shifted(corner_blocks("first", strips, [projection]), "knot", 1)
    around = (stack, chunks[-1], chunks[1 % groups], strips)
    near = [assemble(*around, corners, extent) for corners in ((), (low, high))]
    rounds = len(butterfly_rounds(lax.axis_size("space")))
    pieces = math.gcd(math.gcd(own_blocks, rounds), knot_precision.shape[0] // LANES)
    per_piece, per_split = own_blocks // pieces, knot_precision.shape[0] // pieces
    order = [*range(1, own_blocks), 0]
    base, splits = [], []
    for turn in range(rounds):
        got = butterfly_round(projection, "space", "knot", turn)
        beside = [] if turn else [low, high]
        for i in range(pieces):
            if i * rounds // pieces == turn:
                chosen = order[i * per_piece : (i + 1) * per_piece]
                values, coords = near[0 in chosen or own_blocks - 1 in chosen]
                done = beside_round(
                    neighbours, counts, stack, values, coords, knot_precision, extent,
                    chosen, i * per_split, per_split, [projection],
                )
                base.append(done[0])
                splits.append(done[1:])
                beside.extend(done)
        projection = add_all([projection, *got], beside)
    factor = factored(None, projection, splits, proj_scale, 0)
    for step in range(1, groups):
        factor = factored(factor, shifted(projection, "knot", step), splits, proj_scale, step)
    base = jnp.concatenate(base, axis=1)
    total = jnp.concatenate([base[:, -LANES:], base[:, :-LANES]], axis=1)
    for step in reversed(range(groups)):
        share = spread(factor, parts[step][1], parts[step][2], LOW_SCALE * EXPAND_GAIN)
        total = total + shifted(share, "knot", -step)
    return total


def solution(mesh):
    return jax.shard_map(
        shards,
        mesh=mesh,
        in_specs=(
            P(None, ("space", "knot")),
            P(None, ("space", "knot")),
            P(None, "knot"),
            P("knot", None),
            P(("space", "knot"), None),
            P(("space", "knot")),
        ),
        out_specs=P(None, ("space", "knot")),
        check_vma=False,
    )
```

```python
import functools
import math

import jax
import jax.numpy as jnp
from jax import lax
from jax.experimental import pallas as pl
from jax.experimental.pallas import tpu as pltpu
from jax.sharding import PartitionSpec as P

COV_RANGE = 0.05
TAPER_LEN = 0.15
KNOT_REACH = 0.15
TAPER_SCALE = 0.1
PROJ_GAIN = 0.5
EXPAND_GAIN = 0.5
LOW_SCALE = 0.5
NUGGET = 0.25
LOG2E = math.log2(math.e)
TAPER_RATE = 4.0 / TAPER_LEN
CELL = 0.1
TILE = 256
LANES = 128
HALF_GRAIN = 2.0**-24
LIMIT = 6 * 1024 * 1024
VMEM = pl.BlockSpec(memory_space=pltpu.VMEM)
HBM = pl.BlockSpec(memory_space=pltpu.HBM)
ANY = pl.BlockSpec(memory_space=pl.ANY)
SMEM = pl.BlockSpec(memory_space=pltpu.SMEM)


def halves(x):
    high = x.astype(jnp.bfloat16)
    return high, (x - high.astype(jnp.float32)).astype(jnp.bfloat16)


def stacked_halves(x):
    return jnp.concatenate(halves(x), axis=0)


def folded(x):
    rows = x.shape[0] // 2
    return x[:rows] + x[rows:]


def dot_nt(left, right):
    return lax.dot_general(
        left, right, (((1,), (1,)), ((), ())), preferred_element_type=jnp.float32
    )


def dot_nn(left, right):
    return jnp.dot(left, right, preferred_element_type=jnp.float32)


def padded_halves(x, rows):
    fill = jnp.zeros((rows - 2 * x.shape[0], x.shape[1]), jnp.bfloat16)
    return jnp.concatenate([*halves(x), fill], axis=0)


def folded_columns(x, rows):
    x = jnp.transpose(x)
    return x[:rows] + x[rows : 2 * rows]


def cost(work, pairs, transcendentals=0):
    return pl.CostEstimate(flops=work * pairs, bytes_accessed=4 * pairs, transcendentals=transcendentals * pairs)


def coordinate_rows(ref, points, axis):
    start = points + axis * LANES
    return ref[:, start : start + LANES]


def prepare_kernel(blocks, probes_ref, locations_ref, knots_ref, stack_ref, knots_out_ref, coords, sems):
    points = probes_ref.shape[1]
    block = points // blocks
    copies = [
        pltpu.make_async_copy(probes_ref, stack_ref.at[:, pl.ds(0, points)], sems.at[0]),
        pltpu.make_async_copy(locations_ref, coords, sems.at[1]),
        pltpu.make_async_copy(knots_ref, knots_out_ref, sems.at[2]),
    ]
    for copy in copies:
        copy.start()
    for copy in copies:
        copy.wait()
    stack_ref[:, points:] = jnp.zeros((stack_ref.shape[0], 2 * LANES), jnp.float32)
    for axis in range(2):
        lanes = slice(points + axis * LANES, points + (axis + 1) * LANES)
        for index in range(blocks):
            stack_ref[index : index + 1, lanes] = coords[axis : axis + 1, index * block : (index + 1) * block]


def prepare(probes, locations, knot_locs, blocks):
    rows, points = probes.shape
    assert points == blocks * LANES and blocks + 2 <= rows
    probes, locations, knot_locs = [
        pltpu.with_memory_space_constraint(x, pltpu.HBM) for x in (probes, locations, knot_locs)
    ]
    return pl.pallas_call(
        functools.partial(prepare_kernel, blocks),
        out_shape=(
            jax.ShapeDtypeStruct((rows, points + 2 * LANES), jnp.float32),
            jax.ShapeDtypeStruct(knot_locs.shape, jnp.float32),
        ),
        in_specs=[HBM, HBM, HBM],
        out_specs=(VMEM, VMEM),
        scratch_shapes=[pltpu.VMEM(locations.shape, jnp.float32), pltpu.SemaphoreType.DMA((3,))],
        compiler_params=pltpu.CompilerParams(vmem_limit_bytes=LIMIT),
        name="prepare",
    )(probes, locations, knot_locs)


def strip_kernel(below_ref, own_ref, above_ref, out_ref):
    rows, width = own_ref.shape
    points = width - 2 * LANES
    blocks = points // LANES
    out_ref[:, :LANES] = below_ref[:, points - LANES : points]
    out_ref[:, LANES : points + LANES] = own_ref[:, :points]
    out_ref[:, points + LANES : points + 2 * LANES] = above_ref[:, :LANES]
    for axis in range(2):
        lanes = slice(points + axis * LANES, points + (axis + 1) * LANES)
        target = slice(lanes.start + 2 * LANES, lanes.stop + 2 * LANES)
        out_ref[:, target] = jnp.zeros((rows, LANES), jnp.float32)
        out_ref[0:1, target] = below_ref[blocks - 1 : blocks, lanes]
        out_ref[1 : blocks + 1, target] = own_ref[:blocks, lanes]
        out_ref[blocks + 1 : blocks + 2, target] = above_ref[0:1, lanes]


def make_strip(below, own, above):
    return pl.pallas_call(
        strip_kernel,
        out_shape=jax.ShapeDtypeStruct((own.shape[0], own.shape[1] + 2 * LANES), jnp.float32),
        in_specs=[VMEM, VMEM, VMEM],
        out_specs=VMEM,
        compiler_params=pltpu.CompilerParams(vmem_limit_bytes=LIMIT),
        name="strip",
    )(below, own, above)


def assemble_kernel(grain, own_ref, odd_ref, even_ref, values_ref, coords_ref):
    probes, width = own_ref.shape
    points = width - 2 * LANES
    for turn, ref in enumerate((own_ref, odd_ref, even_ref)):
        start = turn * points
        values_ref[:, start : start + points] = stacked_halves(ref[:, :points] * (1.0 / 256.0))
        for axis in range(2):
            rows = off_grid(coordinate_rows(ref, points, axis) * TAPER_RATE, grain)
            for index in range(points // LANES):
                lanes = slice(start + index * LANES, start + (index + 1) * LANES)
                coords_ref[axis : axis + 1, lanes] = rows[index : index + 1]
    values_ref[:, 3 * points :] = jnp.zeros((2 * probes, LANES), jnp.bfloat16)


def assemble(strips, extent):
    probes, width = strips[0].shape
    near = 3 * (width - 2 * LANES)
    return pl.pallas_call(
        functools.partial(assemble_kernel, grain_of(TAPER_RATE * extent)),
        out_shape=(
            jax.ShapeDtypeStruct((2 * probes, near + LANES), jnp.bfloat16),
            jax.ShapeDtypeStruct((2, near), jnp.float32),
        ),
        in_specs=[VMEM] * 3,
        out_specs=(VMEM, VMEM),
        compiler_params=pltpu.CompilerParams(vmem_limit_bytes=LIMIT),
        name="assemble",
    )(*strips)


def grain_of(bound):
    return 2.0 ** math.ceil(math.log2(1.01 * bound))


def on_grid(x, grain):
    return (x + grain) - grain


def off_grid(x, grain):
    return (x + grain) - (grain - grain * HALF_GRAIN)


def project_kernel(scale, grain, follows, stack_ref, *rest):
    if follows:
        before_ref, columns, out_ref, high_ref, low_ref, weights = rest
    else:
        knots_ref, out_ref, high_ref, low_ref, columns, copy_ref, weights = rest
        copy_ref[...] = stack_ref[...]
        fill = jnp.zeros((6, knots_ref.shape[1]), jnp.float32)
        columns[...] = jnp.transpose(jnp.concatenate([off_grid(knots_ref[...] * scale, grain), fill], axis=0))
    knots, points = high_ref.shape
    probes = stack_ref.shape[0]
    tile = min(TILE, knots)
    weights[...] = padded_halves(stack_ref[:, :points], weights.shape[0])
    east, north = [on_grid(coordinate_rows(stack_ref, points, axis) * scale, grain) for axis in range(2)]

    for start in range(0, knots, tile):
        rows = slice(start, start + tile)
        kx, ky = [columns[rows, axis : axis + 1] for axis in range(2)]
        for block in range(points // LANES):
            lanes = slice(block * LANES, (block + 1) * LANES)
            dx = east[block : block + 1, :] - kx
            dy = north[block : block + 1, :] - ky
            square = dx * dx + dy * dy
            high_ref[rows, lanes], low_ref[rows, lanes] = halves(jnp.exp2(-(square * lax.rsqrt(square))))
        total = dot_nt(high_ref[rows, :], weights[...]) + dot_nt(low_ref[rows, :], weights[...])
        found = folded_columns(total, probes)
        out_ref[:, rows] = found + before_ref[:, rows] if follows else found


def project(stack, knot_locs, scale, extent, before=None):
    probes, points, knots = stack.shape[0], stack.shape[1] - 2 * LANES, knot_locs.shape[1]
    out_shape = [
        jax.ShapeDtypeStruct((probes, knots), jnp.float32),
        pltpu.VMEM((knots, points), jnp.bfloat16),
        pltpu.VMEM((knots, points), jnp.bfloat16),
    ]
    if before is None:
        operands = (stack, knot_locs)
        out_shape += [
            jax.ShapeDtypeStruct((knots, 8), jnp.float32),
            jax.ShapeDtypeStruct(stack.shape, jnp.float32),
        ]
    else:
        operands = (stack, before[0], before[3])
    found = pl.pallas_call(
        functools.partial(project_kernel, scale, grain_of(scale * extent), before is not None),
        out_shape=out_shape,
        in_specs=[VMEM] * len(operands),
        out_specs=[VMEM] * len(out_shape),
        scratch_shapes=[pltpu.VMEM((LANES, points), jnp.bfloat16)],
        compiler_params=pltpu.CompilerParams(vmem_limit_bytes=LIMIT),
        cost_estimate=cost(2800, points * knots, 2),
        name="project",
    )(*operands)
    return found if before is None else [*found, *before[3:]]


def factor_kernel(scale, step, parts, before_ref, proj_ref, *rest):
    highs, lows, (out_ref, weights) = rest[:parts], rest[parts : 2 * parts], rest[-2:]
    probes, depth = proj_ref.shape
    weights[...] = stacked_halves(proj_ref[...] * scale)
    owner = lax.rem(lax.axis_index("knot") + step, lax.axis_size("knot"))
    deep = pl.ds(pl.multiple_of(owner * depth, depth), depth)
    rows = highs[0].shape[1]
    tile = min(TILE, rows)
    for part, (high_ref, low_ref) in enumerate(zip(highs, lows)):
        for start in range(0, rows, tile):
            here = slice(start, start + tile)
            found = folded(dot_nn(weights[...], high_ref[deep, here]) + dot_nn(weights[...], low_ref[deep, here]))
            target = slice(part * rows + start, part * rows + start + tile)
            if before_ref is not None:
                found = found + before_ref[:, target]
            out_ref[:, target] = found


def factored(before, projection, splits, scale, step):
    probes, depth = projection.shape
    highs, lows = [
        [pltpu.with_memory_space_constraint(split[half], pltpu.VMEM) for split in splits] for half in range(2)
    ]
    rows = sum(high.shape[1] for high in highs)
    kernel = functools.partial(factor_kernel, scale, step, len(splits))
    operands = (projection, *highs, *lows)
    if before is None:
        kernel = functools.partial(kernel, None)
    else:
        operands = (before, *operands)
    return pl.pallas_call(
        kernel,
        out_shape=jax.ShapeDtypeStruct((probes, rows), jnp.float32),
        in_specs=[VMEM] * len(operands),
        out_specs=VMEM,
        scratch_shapes=[pltpu.VMEM((2 * probes, depth), jnp.bfloat16)],
        compiler_params=pltpu.CompilerParams(vmem_limit_bytes=LIMIT),
        cost_estimate=cost(1000, rows * depth),
        name="factor",
    )(*operands)


def spread_kernel(scale, factor_ref, high_ref, low_ref, out_ref):
    points = high_ref.shape[1]
    tile = min(TILE, points)
    weights = stacked_halves(factor_ref[...] * scale)
    for start in range(0, points, tile):
        lanes = slice(start, start + tile)
        out_ref[:, lanes] = folded(dot_nn(weights, high_ref[:, lanes]) + dot_nn(weights, low_ref[:, lanes]))


def spread(factor, high, low, scale):
    (probes, knots), points = factor.shape, high.shape[1]
    high = pltpu.with_memory_space_constraint(high, pltpu.VMEM)
    low = pltpu.with_memory_space_constraint(low, pltpu.VMEM)
    return pl.pallas_call(
        functools.partial(spread_kernel, scale),
        out_shape=jax.ShapeDtypeStruct((probes, points), jnp.float32),
        in_specs=[VMEM, VMEM, VMEM],
        out_specs=VMEM,
        compiler_params=pltpu.CompilerParams(vmem_limit_bytes=LIMIT),
        cost_estimate=cost(850, knots * points),
        name="spread",
    )(factor, high, low)


def covariance(square):
    apart = square * lax.rsqrt(square)
    remain = jnp.maximum(4.0 - apart, 0.0)
    twice = remain * remain
    return (jnp.exp2(apart * (-LOG2E / (COV_RANGE * TAPER_RATE))) * (twice * twice)) * (5.0 - remain)


def beside_kernel(first, first_row, grain, ids_ref, counts_ref, own_ref, values_ref, coords_ref, precision_ref, *rest):
    out_ref, high_ref, low_ref = rest[-3:]
    own_blocks, slots = ids_ref.shape
    block = LANES
    probes = own_ref.shape[0]
    span = own_blocks + 2
    zeros_place = coords_ref.shape[1] // block
    column = lax.axis_index("space")
    north_base = lax.axis_index("knot") * own_blocks - 1
    north_cells = lax.axis_size("knot") * own_blocks
    own_columns = [
        on_grid(jnp.transpose(coordinate_rows(own_ref, own_blocks * block, axis) * TAPER_RATE), grain)
        for axis in range(2)
    ]

    def place(group, slot):
        ahead = ids_ref[group, slot] - (column - 1) * north_cells
        east = jnp.where(ahead >= north_cells, 1, 0) + jnp.where(ahead >= 2 * north_cells, 1, 0)
        strip = jnp.where(east == 1, 0, 2 - lax.rem(column + lax.div(east, 2) + 1, 2))
        index = strip * span + (ahead - east * north_cells - north_base)
        return lanes_of(index), lanes_of(jnp.where(slot < counts_ref[group], index, zeros_place))

    def lanes_of(index):
        return pl.ds(pl.multiple_of(index * block, block), block)

    depth, rows = high_ref.shape
    tile = min(TILE, rows)
    wide = min(TILE, depth)
    tiles = [(start, deep) for start in range(0, rows, tile) for deep in range(0, depth, wide)]
    groups = out_ref.shape[1] // block
    turns = groups * -(-slots // 2)

    for index in range(groups):
        group = first + index
        px, py = [turned[:, group : group + 1] for turned in own_columns]
        total = jnp.zeros((block, 2 * probes), jnp.float32)
        for pair in range(0, slots, 2):
            highs, lows, parts = [], [], []
            for slot in range(pair, min(pair + 2, slots)):
                lanes, value_lanes = place(group, slot)
                dx = px - coords_ref[0:1, lanes]
                dy = py - coords_ref[1:2, lanes]
                high, low = halves(covariance(dx * dx + dy * dy))
                highs.append(high)
                lows.append(low)
                parts.append(values_ref[:, value_lanes])
            part = jnp.concatenate(parts, axis=1)
            total = total + (
                dot_nt(jnp.concatenate(highs, axis=1), part) + dot_nt(jnp.concatenate(lows, axis=1), part)
            )
            turn = index * -(-slots // 2) + pair // 2
            for start, deep in tiles[turn * len(tiles) // turns : (turn + 1) * len(tiles) // turns]:
                from_row = first_row + start
                turned = jnp.transpose(precision_ref[from_row : from_row + tile, deep : deep + wide])
                here = slice(deep, deep + wide), slice(start, start + tile)
                high_ref[here], low_ref[here] = halves(turned)
        out_ref[:, index * block : (index + 1) * block] = (
            TAPER_SCALE * folded_columns(total, probes)
            + NUGGET * own_ref[:, group * block : (group + 1) * block]
        )


def beside_round(ids, counts, own, values, coords, precision, extent, first, blocks, first_row, rows, after):
    slots, depth = ids.shape[1], precision.shape[1]
    return pl.pallas_call(
        functools.partial(beside_kernel, first, first_row, grain_of(TAPER_RATE * extent)),
        out_shape=(
            jax.ShapeDtypeStruct((own.shape[0], blocks * LANES), jnp.float32),
            pltpu.VMEM((depth, rows), jnp.bfloat16),
            pltpu.VMEM((depth, rows), jnp.bfloat16),
        ),
        in_specs=[SMEM, SMEM, VMEM, VMEM, VMEM, VMEM] + [ANY] * len(after),
        out_specs=(VMEM, VMEM, VMEM),
        compiler_params=pltpu.CompilerParams(vmem_limit_bytes=LIMIT),
        cost_estimate=cost(500, blocks * slots * LANES * LANES, 2),
        name="beside",
    )(ids, counts, own, values, coords, precision, *after)


def add_kernel(count, *refs):
    total = refs[0][...]
    for ref in refs[1:count]:
        total = total + ref[...]
    refs[-1][...] = total


def add_all(values, after):
    return pl.pallas_call(
        functools.partial(add_kernel, len(values)),
        out_shape=jax.ShapeDtypeStruct(values[0].shape, jnp.float32),
        in_specs=[VMEM] * len(values) + [ANY] * len(after),
        out_specs=VMEM,
        compiler_params=pltpu.CompilerParams(vmem_limit_bytes=LIMIT),
        name="add",
    )(*values, *after)


def butterfly_rounds(count):
    assert count & (count - 1) == 0
    bits = [1 << i for i in range(count.bit_length() - 1)]
    rounds = [(low | high, high, low) for low, high in zip(bits[0::2], bits[1::2])]
    rounds[1:] = [(high, both, low) for both, high, low in rounds[1:]]
    return rounds + [(bit,) for bit in bits[len(rounds) * 2 :]]


def butterfly_round(value, axis, turn):
    count = lax.axis_size(axis)
    return [
        lax.ppermute(value, axis, [(i, i ^ step) for i in range(count)]) for step in butterfly_rounds(count)[turn]
    ]


def shifted(value, axis, step):
    count = lax.axis_size(axis)
    if step % count == 0:
        return value
    return lax.ppermute(value, axis, [((i + step) % count, i) for i in range(count)])


def paired(value, axis, other, first):
    count, groups = lax.axis_size(axis), lax.axis_size(other)
    partner = {}
    for i in range(first, count - 1, 2):
        partner[i], partner[i + 1] = i + 1, i
    pairs = []
    for i in range(count):
        for j in range(groups):
            if i in partner:
                pairs.append((i * groups + j, partner[i] * groups + j))
            elif j ^ 1 < groups:
                pairs.append((i * groups + j, i * groups + (j ^ 1)))
    return lax.ppermute(value, (axis, other), pairs)


def shards(probes, locations, knot_locs, knot_precision, neighbours, counts):
    own_blocks = neighbours.shape[0]
    row_count = probes.shape[1]
    knot_total = knot_precision.shape[1]
    device_count = lax.axis_size(("space", "knot"))
    groups = lax.axis_size("knot")
    knot_range = KNOT_REACH * math.sqrt(own_blocks * device_count / knot_total)
    proj_scale = PROJ_GAIN * math.sqrt(knot_total / (row_count * device_count))

    stack, knots = prepare(probes, locations, knot_locs, own_blocks)
    chunks = [shifted(stack, "knot", step) for step in range(groups)]
    rate = LOG2E / knot_range
    extent = CELL * max(lax.axis_size("space"), groups * own_blocks)
    parts = []
    for chunk in chunks:
        parts.append(project(chunk, knots, rate, extent, parts[-1] if parts else None))
    stack = parts[0][4]

    strip = make_strip(chunks[-1], stack, chunks[1 % groups])
    odd = paired(strip, "space", "knot", 1)
    values, coords = assemble([strip, odd, paired(strip, "space", "knot", 0)], extent)
    projection = parts[-1][0]
    rounds = len(butterfly_rounds(lax.axis_size("space")))
    pieces = math.gcd(math.gcd(own_blocks, rounds), knot_precision.shape[0] // LANES)
    per_piece, per_split = own_blocks // pieces, knot_precision.shape[0] // pieces
    base, splits = [], []
    for turn in range(rounds):
        got = butterfly_round(projection, "space", turn)
        beside = []
        for i in range(pieces):
            if i * rounds // pieces == turn:
                done = beside_round(
                    neighbours, counts, stack, values, coords, knot_precision, extent,
                    i * per_piece, per_piece, i * per_split, per_split, [projection],
                )
                base.append(done[0])
                splits.append(done[1:])
                beside.extend(done)
        projection = add_all([projection, *got], beside)
    factor = factored(None, projection, splits, proj_scale, 0)
    for step in range(1, groups):
        factor = factored(factor, shifted(projection, "knot", step), splits, proj_scale, step)
    total = jnp.concatenate(base, axis=1)
    for step in reversed(range(groups)):
        share = spread(factor, parts[step][1], parts[step][2], LOW_SCALE * EXPAND_GAIN)
        total = total + shifted(share, "knot", -step)
    return total


def solution(mesh):
    return jax.shard_map(
        shards,
        mesh=mesh,
        in_specs=(
            P(None, ("space", "knot")),
            P(None, ("space", "knot")),
            P(None, "knot"),
            P("knot", None),
            P(("space", "knot"), None),
            P(("space", "knot")),
        ),
        out_specs=P(None, ("space", "knot")),
        check_vma=False,
    )
```

```python
import functools
import math

import jax
import jax.numpy as jnp
from jax import lax
from jax.experimental import pallas as pl
from jax.experimental.pallas import tpu as pltpu
from jax.sharding import PartitionSpec as P

COV_RANGE = 0.05
TAPER_LEN = 0.15
KNOT_REACH = 0.15
TAPER_SCALE = 0.1
PROJ_GAIN = 0.5
EXPAND_GAIN = 0.5
LOW_SCALE = 0.5
NUGGET = 0.25
LOG2E = math.log2(math.e)
TAPER_RATE = 4.0 / TAPER_LEN
CELL = 0.1
TILE = 256
LANES = 128
HALF_GRAIN = 2.0**-24
LIMIT = 6 * 1024 * 1024
VMEM = pl.BlockSpec(memory_space=pltpu.VMEM)
HBM = pl.BlockSpec(memory_space=pltpu.HBM)
ANY = pl.BlockSpec(memory_space=pl.ANY)
SMEM = pl.BlockSpec(memory_space=pltpu.SMEM)


def halves(x):
    high = x.astype(jnp.bfloat16)
    return high, (x - high.astype(jnp.float32)).astype(jnp.bfloat16)


def stacked_halves(x):
    return jnp.concatenate(halves(x), axis=0)


def folded(x):
    rows = x.shape[0] // 2
    return x[:rows] + x[rows:]


def dot_nt(left, right):
    return lax.dot_general(
        left, right, (((1,), (1,)), ((), ())), preferred_element_type=jnp.float32
    )


def dot_nn(left, right):
    return jnp.dot(left, right, preferred_element_type=jnp.float32)


def padded_halves(x, rows):
    fill = jnp.zeros((rows - 2 * x.shape[0], x.shape[1]), jnp.bfloat16)
    return jnp.concatenate([*halves(x), fill], axis=0)


def folded_columns(x, rows):
    x = jnp.transpose(x)
    return x[:rows] + x[rows : 2 * rows]


def cost(work, pairs, transcendentals=0):
    return pl.CostEstimate(flops=work * pairs, bytes_accessed=4 * pairs, transcendentals=transcendentals * pairs)


def coordinate_rows(ref, points, axis):
    start = points + axis * LANES
    return ref[:, start : start + LANES]


def prepare_kernel(blocks, probes_ref, locations_ref, knots_ref, stack_ref, knots_out_ref, coords, sems):
    points = probes_ref.shape[1]
    block = points // blocks
    copies = [
        pltpu.make_async_copy(probes_ref, stack_ref.at[:, pl.ds(0, points)], sems.at[0]),
        pltpu.make_async_copy(locations_ref, coords, sems.at[1]),
        pltpu.make_async_copy(knots_ref, knots_out_ref, sems.at[2]),
    ]
    for copy in copies:
        copy.start()
    for copy in copies:
        copy.wait()
    stack_ref[:, points:] = jnp.zeros((stack_ref.shape[0], 2 * LANES), jnp.float32)
    for axis in range(2):
        lanes = slice(points + axis * LANES, points + (axis + 1) * LANES)
        for index in range(blocks):
            stack_ref[index : index + 1, lanes] = coords[axis : axis + 1, index * block : (index + 1) * block]


def prepare(probes, locations, knot_locs, blocks):
    rows, points = probes.shape
    assert points == blocks * LANES and blocks + 2 <= rows
    probes, locations, knot_locs = [
        pltpu.with_memory_space_constraint(x, pltpu.HBM) for x in (probes, locations, knot_locs)
    ]
    return pl.pallas_call(
        functools.partial(prepare_kernel, blocks),
        out_shape=(
            jax.ShapeDtypeStruct((rows, points + 2 * LANES), jnp.float32),
            jax.ShapeDtypeStruct(knot_locs.shape, jnp.float32),
        ),
        in_specs=[HBM, HBM, HBM],
        out_specs=(VMEM, VMEM),
        scratch_shapes=[pltpu.VMEM(locations.shape, jnp.float32), pltpu.SemaphoreType.DMA((3,))],
        compiler_params=pltpu.CompilerParams(vmem_limit_bytes=LIMIT),
        name="prepare",
    )(probes, locations, knot_locs)


def strip_kernel(below_ref, own_ref, above_ref, out_ref):
    rows, width = own_ref.shape
    points = width - 2 * LANES
    blocks = points // LANES
    out_ref[:, :LANES] = below_ref[:, points - LANES : points]
    out_ref[:, LANES : points + LANES] = own_ref[:, :points]
    out_ref[:, points + LANES : points + 2 * LANES] = above_ref[:, :LANES]
    for axis in range(2):
        lanes = slice(points + axis * LANES, points + (axis + 1) * LANES)
        target = slice(lanes.start + 2 * LANES, lanes.stop + 2 * LANES)
        out_ref[:, target] = jnp.zeros((rows, LANES), jnp.float32)
        out_ref[0:1, target] = below_ref[blocks - 1 : blocks, lanes]
        out_ref[1 : blocks + 1, target] = own_ref[:blocks, lanes]
        out_ref[blocks + 1 : blocks + 2, target] = above_ref[0:1, lanes]


def make_strip(below, own, above):
    return pl.pallas_call(
        strip_kernel,
        out_shape=jax.ShapeDtypeStruct((own.shape[0], own.shape[1] + 2 * LANES), jnp.float32),
        in_specs=[VMEM, VMEM, VMEM],
        out_specs=VMEM,
        compiler_params=pltpu.CompilerParams(vmem_limit_bytes=LIMIT),
        name="strip",
    )(below, own, above)


def assemble_kernel(grain, own_ref, odd_ref, even_ref, values_ref, coords_ref):
    probes, width = own_ref.shape
    points = width - 2 * LANES
    for turn, ref in enumerate((own_ref, odd_ref, even_ref)):
        start = turn * points
        values_ref[:, start : start + points] = stacked_halves(ref[:, :points] * (1.0 / 256.0))
        for axis in range(2):
            rows = off_grid(coordinate_rows(ref, points, axis) * TAPER_RATE, grain)
            for index in range(points // LANES):
                lanes = slice(start + index * LANES, start + (index + 1) * LANES)
                coords_ref[axis : axis + 1, lanes] = rows[index : index + 1]
    values_ref[:, 3 * points :] = jnp.zeros((2 * probes, LANES), jnp.bfloat16)


def assemble(strips, extent):
    probes, width = strips[0].shape
    near = 3 * (width - 2 * LANES)
    return pl.pallas_call(
        functools.partial(assemble_kernel, grain_of(TAPER_RATE * extent)),
        out_shape=(
            jax.ShapeDtypeStruct((2 * probes, near + LANES), jnp.bfloat16),
            jax.ShapeDtypeStruct((2, near), jnp.float32),
        ),
        in_specs=[VMEM] * 3,
        out_specs=(VMEM, VMEM),
        compiler_params=pltpu.CompilerParams(vmem_limit_bytes=LIMIT),
        name="assemble",
    )(*strips)


def grain_of(bound):
    return 2.0 ** math.ceil(math.log2(1.01 * bound))


def on_grid(x, grain):
    return (x + grain) - grain


def off_grid(x, grain):
    return (x + grain) - (grain - grain * HALF_GRAIN)


def project_kernel(scale, grain, follows, stack_ref, *rest):
    if follows:
        before_ref, columns, out_ref, high_ref, low_ref, weights = rest
    else:
        knots_ref, out_ref, high_ref, low_ref, columns, copy_ref, weights = rest
        copy_ref[...] = stack_ref[...]
        fill = jnp.zeros((6, knots_ref.shape[1]), jnp.float32)
        columns[...] = jnp.transpose(jnp.concatenate([off_grid(knots_ref[...] * scale, grain), fill], axis=0))
    knots, points = high_ref.shape
    probes = stack_ref.shape[0]
    tile = min(TILE, knots)
    weights[...] = padded_halves(stack_ref[:, :points], weights.shape[0])
    east, north = [on_grid(coordinate_rows(stack_ref, points, axis) * scale, grain) for axis in range(2)]

    for start in range(0, knots, tile):
        rows = slice(start, start + tile)
        kx, ky = [columns[rows, axis : axis + 1] for axis in range(2)]
        for block in range(points // LANES):
            lanes = slice(block * LANES, (block + 1) * LANES)
            dx = east[block : block + 1, :] - kx
            dy = north[block : block + 1, :] - ky
            square = dx * dx + dy * dy
            high_ref[rows, lanes], low_ref[rows, lanes] = halves(jnp.exp2(-(square * lax.rsqrt(square))))
        total = dot_nt(high_ref[rows, :], weights[...]) + dot_nt(low_ref[rows, :], weights[...])
        found = folded_columns(total, probes)
        out_ref[:, rows] = found + before_ref[:, rows] if follows else found


def project(stack, knot_locs, scale, extent, before=None):
    probes, points, knots = stack.shape[0], stack.shape[1] - 2 * LANES, knot_locs.shape[1]
    out_shape = [
        jax.ShapeDtypeStruct((probes, knots), jnp.float32),
        pltpu.VMEM((knots, points), jnp.bfloat16),
        pltpu.VMEM((knots, points), jnp.bfloat16),
    ]
    if before is None:
        operands = (stack, knot_locs)
        out_shape += [
            jax.ShapeDtypeStruct((knots, 8), jnp.float32),
            jax.ShapeDtypeStruct(stack.shape, jnp.float32),
        ]
    else:
        operands = (stack, before[0], before[3])
    found = pl.pallas_call(
        functools.partial(project_kernel, scale, grain_of(scale * extent), before is not None),
        out_shape=out_shape,
        in_specs=[VMEM] * len(operands),
        out_specs=[VMEM] * len(out_shape),
        scratch_shapes=[pltpu.VMEM((LANES, points), jnp.bfloat16)],
        compiler_params=pltpu.CompilerParams(vmem_limit_bytes=LIMIT),
        cost_estimate=cost(2800, points * knots, 2),
        name="project",
    )(*operands)
    return found if before is None else [*found, *before[3:]]


def factor_kernel(scale, step, parts, before_ref, proj_ref, *rest):
    highs, lows, (out_ref, weights) = rest[:parts], rest[parts : 2 * parts], rest[-2:]
    probes, depth = proj_ref.shape
    weights[...] = stacked_halves(proj_ref[...] * scale)
    owner = lax.rem(lax.axis_index("knot") + step, lax.axis_size("knot"))
    deep = pl.ds(pl.multiple_of(owner * depth, depth), depth)
    rows = highs[0].shape[1]
    tile = min(TILE, rows)
    for part, (high_ref, low_ref) in enumerate(zip(highs, lows)):
        for start in range(0, rows, tile):
            here = slice(start, start + tile)
            found = folded(dot_nn(weights[...], high_ref[deep, here]) + dot_nn(weights[...], low_ref[deep, here]))
            target = slice(part * rows + start, part * rows + start + tile)
            if before_ref is not None:
                found = found + before_ref[:, target]
            out_ref[:, target] = found


def factored(before, projection, splits, scale, step):
    probes, depth = projection.shape
    highs, lows = [
        [pltpu.with_memory_space_constraint(split[half], pltpu.VMEM) for split in splits] for half in range(2)
    ]
    rows = sum(high.shape[1] for high in highs)
    kernel = functools.partial(factor_kernel, scale, step, len(splits))
    operands = (projection, *highs, *lows)
    if before is None:
        kernel = functools.partial(kernel, None)
    else:
        operands = (before, *operands)
    return pl.pallas_call(
        kernel,
        out_shape=jax.ShapeDtypeStruct((probes, rows), jnp.float32),
        in_specs=[VMEM] * len(operands),
        out_specs=VMEM,
        scratch_shapes=[pltpu.VMEM((2 * probes, depth), jnp.bfloat16)],
        compiler_params=pltpu.CompilerParams(vmem_limit_bytes=LIMIT),
        cost_estimate=cost(1000, rows * depth),
        name="factor",
    )(*operands)


def spread_kernel(scale, factor_ref, high_ref, low_ref, out_ref):
    points = high_ref.shape[1]
    tile = min(TILE, points)
    weights = stacked_halves(factor_ref[...] * scale)
    for start in range(0, points, tile):
        lanes = slice(start, start + tile)
        out_ref[:, lanes] = folded(dot_nn(weights, high_ref[:, lanes]) + dot_nn(weights, low_ref[:, lanes]))


def spread(factor, high, low, scale):
    (probes, knots), points = factor.shape, high.shape[1]
    high = pltpu.with_memory_space_constraint(high, pltpu.VMEM)
    low = pltpu.with_memory_space_constraint(low, pltpu.VMEM)
    return pl.pallas_call(
        functools.partial(spread_kernel, scale),
        out_shape=jax.ShapeDtypeStruct((probes, points), jnp.float32),
        in_specs=[VMEM, VMEM, VMEM],
        out_specs=VMEM,
        compiler_params=pltpu.CompilerParams(vmem_limit_bytes=LIMIT),
        cost_estimate=cost(850, knots * points),
        name="spread",
    )(factor, high, low)


def covariance(square):
    apart = square * lax.rsqrt(square)
    remain = jnp.maximum(4.0 - apart, 0.0)
    twice = remain * remain
    return (jnp.exp2(apart * (-LOG2E / (COV_RANGE * TAPER_RATE))) * (twice * twice)) * (5.0 - remain)


def beside_kernel(first, first_row, grain, ids_ref, counts_ref, own_ref, values_ref, coords_ref, precision_ref, *rest):
    out_ref, high_ref, low_ref = rest[-3:]
    own_blocks, slots = ids_ref.shape
    block = LANES
    probes = own_ref.shape[0]
    span = own_blocks + 2
    zeros_place = coords_ref.shape[1] // block
    column = lax.axis_index("space")
    north_base = lax.axis_index("knot") * own_blocks - 1
    north_cells = lax.axis_size("knot") * own_blocks
    own_columns = [
        on_grid(jnp.transpose(coordinate_rows(own_ref, own_blocks * block, axis) * TAPER_RATE), grain)
        for axis in range(2)
    ]

    def place(group, slot):
        ahead = ids_ref[group, slot] - (column - 1) * north_cells
        east = jnp.where(ahead >= north_cells, 1, 0) + jnp.where(ahead >= 2 * north_cells, 1, 0)
        strip = jnp.where(east == 1, 0, 2 - lax.rem(column + lax.div(east, 2) + 1, 2))
        index = strip * span + (ahead - east * north_cells - north_base)
        return lanes_of(index), lanes_of(jnp.where(slot < counts_ref[group], index, zeros_place))

    def lanes_of(index):
        return pl.ds(pl.multiple_of(index * block, block), block)

    depth, rows = high_ref.shape
    tile = min(TILE, rows)
    wide = min(TILE, depth)
    tiles = [(start, deep) for start in range(0, rows, tile) for deep in range(0, depth, wide)]
    groups = out_ref.shape[1] // block
    turns = groups * -(-slots // 2)

    for index in range(groups):
        group = first + index
        px, py = [turned[:, group : group + 1] for turned in own_columns]
        total = jnp.zeros((block, 2 * probes), jnp.float32)
        for pair in range(0, slots, 2):
            highs, lows, parts = [], [], []
            for slot in range(pair, min(pair + 2, slots)):
                lanes, value_lanes = place(group, slot)
                dx = px - coords_ref[0:1, lanes]
                dy = py - coords_ref[1:2, lanes]
                high, low = halves(covariance(dx * dx + dy * dy))
                highs.append(high)
                lows.append(low)
                parts.append(values_ref[:, value_lanes])
            part = jnp.concatenate(parts, axis=1)
            total = total + (
                dot_nt(jnp.concatenate(highs, axis=1), part) + dot_nt(jnp.concatenate(lows, axis=1), part)
            )
            turn = index * -(-slots // 2) + pair // 2
            for start, deep in tiles[turn * len(tiles) // turns : (turn + 1) * len(tiles) // turns]:
                from_row = first_row + start
                turned = jnp.transpose(precision_ref[from_row : from_row + tile, deep : deep + wide])
                here = slice(deep, deep + wide), slice(start, start + tile)
                high_ref[here], low_ref[here] = halves(turned)
        out_ref[:, index * block : (index + 1) * block] = (
            TAPER_SCALE * folded_columns(total, probes)
            + NUGGET * own_ref[:, group * block : (group + 1) * block]
        )


def beside_round(ids, counts, own, values, coords, precision, extent, first, blocks, first_row, rows, after):
    slots, depth = ids.shape[1], precision.shape[1]
    return pl.pallas_call(
        functools.partial(beside_kernel, first, first_row, grain_of(TAPER_RATE * extent)),
        out_shape=(
            jax.ShapeDtypeStruct((own.shape[0], blocks * LANES), jnp.float32),
            pltpu.VMEM((depth, rows), jnp.bfloat16),
            pltpu.VMEM((depth, rows), jnp.bfloat16),
        ),
        in_specs=[SMEM, SMEM, VMEM, VMEM, VMEM, VMEM] + [ANY] * len(after),
        out_specs=(VMEM, VMEM, VMEM),
        compiler_params=pltpu.CompilerParams(vmem_limit_bytes=LIMIT),
        cost_estimate=cost(500, blocks * slots * LANES * LANES, 2),
        name="beside",
    )(ids, counts, own, values, coords, precision, *after)


def add_kernel(count, *refs):
    total = refs[0][...]
    for ref in refs[1:count]:
        total = total + ref[...]
    refs[-1][...] = total


def add_all(values, after):
    return pl.pallas_call(
        functools.partial(add_kernel, len(values)),
        out_shape=jax.ShapeDtypeStruct(values[0].shape, jnp.float32),
        in_specs=[VMEM] * len(values) + [ANY] * len(after),
        out_specs=VMEM,
        compiler_params=pltpu.CompilerParams(vmem_limit_bytes=LIMIT),
        name="add",
    )(*values, *after)


def butterfly_rounds(count):
    assert count & (count - 1) == 0
    bits = [1 << i for i in range(count.bit_length() - 1)]
    rounds = [(low | high, high, low) for low, high in zip(bits[0::2], bits[1::2])]
    return rounds + [(bit,) for bit in bits[len(rounds) * 2 :]]


def butterfly_round(value, axis, turn):
    count = lax.axis_size(axis)
    return [
        lax.ppermute(value, axis, [(i, i ^ step) for i in range(count)]) for step in butterfly_rounds(count)[turn]
    ]


def shifted(value, axis, step):
    count = lax.axis_size(axis)
    if step % count == 0:
        return value
    return lax.ppermute(value, axis, [((i + step) % count, i) for i in range(count)])


def paired(value, axis, other, first):
    count, groups = lax.axis_size(axis), lax.axis_size(other)
    partner = {}
    for i in range(first, count - 1, 2):
        partner[i], partner[i + 1] = i + 1, i
    pairs = []
    for i in range(count):
        for j in range(groups):
            if i in partner:
                pairs.append((i * groups + j, partner[i] * groups + j))
            elif j ^ 1 < groups:
                pairs.append((i * groups + j, i * groups + (j ^ 1)))
    return lax.ppermute(value, (axis, other), pairs)


def shards(probes, locations, knot_locs, knot_precision, neighbours, counts):
    own_blocks = neighbours.shape[0]
    row_count = probes.shape[1]
    knot_total = knot_precision.shape[1]
    device_count = lax.axis_size(("space", "knot"))
    groups = lax.axis_size("knot")
    knot_range = KNOT_REACH * math.sqrt(own_blocks * device_count / knot_total)
    proj_scale = PROJ_GAIN * math.sqrt(knot_total / (row_count * device_count))

    stack, knots = prepare(probes, locations, knot_locs, own_blocks)
    chunks = [shifted(stack, "knot", step) for step in range(groups)]
    rate = LOG2E / knot_range
    extent = CELL * max(lax.axis_size("space"), groups * own_blocks)
    parts = []
    for chunk in chunks:
        parts.append(project(chunk, knots, rate, extent, parts[-1] if parts else None))
    stack = parts[0][4]

    strip = make_strip(chunks[-1], stack, chunks[1 % groups])
    odd = paired(strip, "space", "knot", 1)
    values, coords = assemble([strip, odd, paired(strip, "space", "knot", 0)], extent)
    projection = parts[-1][0]
    rounds = len(butterfly_rounds(lax.axis_size("space")))
    pieces = math.gcd(math.gcd(own_blocks, rounds), knot_precision.shape[0] // LANES)
    per_piece, per_split = own_blocks // pieces, knot_precision.shape[0] // pieces
    base, splits = [], []
    for turn in range(rounds):
        got = butterfly_round(projection, "space", turn)
        beside = []
        for i in range(pieces):
            if i * rounds // pieces == turn:
                done = beside_round(
                    neighbours, counts, stack, values, coords, knot_precision, extent,
                    i * per_piece, per_piece, i * per_split, per_split, [projection],
                )
                base.append(done[0])
                splits.append(done[1:])
                beside.extend(done)
        projection = add_all([projection, *got], beside)
    factor = factored(None, projection, splits, proj_scale, 0)
    for step in range(1, groups):
        factor = factored(factor, shifted(projection, "knot", step), splits, proj_scale, step)
    total = jnp.concatenate(base, axis=1)
    for step in reversed(range(groups)):
        share = spread(factor, parts[step][1], parts[step][2], LOW_SCALE * EXPAND_GAIN)
        total = total + shifted(share, "knot", -step)
    return total


def solution(mesh):
    return jax.shard_map(
        shards,
        mesh=mesh,
        in_specs=(
            P(None, ("space", "knot")),
            P(None, ("space", "knot")),
            P(None, "knot"),
            P("knot", None),
            P(("space", "knot"), None),
            P(("space", "knot")),
        ),
        out_specs=P(None, ("space", "knot")),
        check_vma=False,
    )
```

```python
import functools
import math

import jax
import jax.numpy as jnp
from jax import lax
from jax.experimental import pallas as pl
from jax.experimental.pallas import tpu as pltpu
from jax.sharding import PartitionSpec as P

COV_RANGE = 0.05
TAPER_LEN = 0.15
KNOT_REACH = 0.15
TAPER_SCALE = 0.1
PROJ_GAIN = 0.5
EXPAND_GAIN = 0.5
LOW_SCALE = 0.5
NUGGET = 0.25
LOG2E = math.log2(math.e)
TAPER_RATE = 4.0 / TAPER_LEN
CELL = 0.1
TILE = 256
LANES = 128
HALF_GRAIN = 2.0**-24
LIMIT = 6 * 1024 * 1024
VMEM = pl.BlockSpec(memory_space=pltpu.VMEM)
HBM = pl.BlockSpec(memory_space=pltpu.HBM)
ANY = pl.BlockSpec(memory_space=pl.ANY)
SMEM = pl.BlockSpec(memory_space=pltpu.SMEM)


def halves(x):
    high = x.astype(jnp.bfloat16)
    return high, (x - high.astype(jnp.float32)).astype(jnp.bfloat16)


def stacked_halves(x):
    return jnp.concatenate(halves(x), axis=0)


def folded(x):
    rows = x.shape[0] // 2
    return x[:rows] + x[rows:]


def dot_nt(left, right):
    return lax.dot_general(
        left, right, (((1,), (1,)), ((), ())), preferred_element_type=jnp.float32
    )


def dot_nn(left, right):
    return jnp.dot(left, right, preferred_element_type=jnp.float32)


def padded_halves(x, rows):
    fill = jnp.zeros((rows - 2 * x.shape[0], x.shape[1]), jnp.bfloat16)
    return jnp.concatenate([*halves(x), fill], axis=0)


def folded_columns(x, rows):
    x = jnp.transpose(x)
    return x[:rows] + x[rows : 2 * rows]


def cost(work, pairs, transcendentals=0):
    return pl.CostEstimate(flops=work * pairs, bytes_accessed=4 * pairs, transcendentals=transcendentals * pairs)


def coordinate_rows(ref, points, axis):
    start = points + axis * LANES
    return ref[:, start : start + LANES]


def prepare_kernel(blocks, probes_ref, locations_ref, knots_ref, stack_ref, knots_out_ref, coords, sems):
    points = probes_ref.shape[1]
    block = points // blocks
    copies = [
        pltpu.make_async_copy(probes_ref, stack_ref.at[:, pl.ds(0, points)], sems.at[0]),
        pltpu.make_async_copy(locations_ref, coords, sems.at[1]),
        pltpu.make_async_copy(knots_ref, knots_out_ref, sems.at[2]),
    ]
    for copy in copies:
        copy.start()
    for copy in copies:
        copy.wait()
    stack_ref[:, points:] = jnp.zeros((stack_ref.shape[0], 2 * LANES), jnp.float32)
    for axis in range(2):
        lanes = slice(points + axis * LANES, points + (axis + 1) * LANES)
        for index in range(blocks):
            stack_ref[index : index + 1, lanes] = coords[axis : axis + 1, index * block : (index + 1) * block]


def prepare(probes, locations, knot_locs, blocks):
    rows, points = probes.shape
    assert points == blocks * LANES and blocks + 2 <= rows
    probes, locations, knot_locs = [
        pltpu.with_memory_space_constraint(x, pltpu.HBM) for x in (probes, locations, knot_locs)
    ]
    return pl.pallas_call(
        functools.partial(prepare_kernel, blocks),
        out_shape=(
            jax.ShapeDtypeStruct((rows, points + 2 * LANES), jnp.float32),
            jax.ShapeDtypeStruct(knot_locs.shape, jnp.float32),
        ),
        in_specs=[HBM, HBM, HBM],
        out_specs=(VMEM, VMEM),
        scratch_shapes=[pltpu.VMEM(locations.shape, jnp.float32), pltpu.SemaphoreType.DMA((3,))],
        compiler_params=pltpu.CompilerParams(vmem_limit_bytes=LIMIT),
        name="prepare",
    )(probes, locations, knot_locs)


def strip_kernel(below_ref, own_ref, above_ref, out_ref):
    rows, width = own_ref.shape
    points = width - 2 * LANES
    blocks = points // LANES
    out_ref[:, :LANES] = below_ref[:, points - LANES : points]
    out_ref[:, LANES : points + LANES] = own_ref[:, :points]
    out_ref[:, points + LANES : points + 2 * LANES] = above_ref[:, :LANES]
    for axis in range(2):
        lanes = slice(points + axis * LANES, points + (axis + 1) * LANES)
        target = slice(lanes.start + 2 * LANES, lanes.stop + 2 * LANES)
        out_ref[:, target] = jnp.zeros((rows, LANES), jnp.float32)
        out_ref[0:1, target] = below_ref[blocks - 1 : blocks, lanes]
        out_ref[1 : blocks + 1, target] = own_ref[:blocks, lanes]
        out_ref[blocks + 1 : blocks + 2, target] = above_ref[0:1, lanes]


def make_strip(below, own, above):
    return pl.pallas_call(
        strip_kernel,
        out_shape=jax.ShapeDtypeStruct((own.shape[0], own.shape[1] + 2 * LANES), jnp.float32),
        in_specs=[VMEM, VMEM, VMEM],
        out_specs=VMEM,
        compiler_params=pltpu.CompilerParams(vmem_limit_bytes=LIMIT),
        name="strip",
    )(below, own, above)


def assemble_kernel(grain, own_ref, odd_ref, even_ref, values_ref, coords_ref):
    probes, width = own_ref.shape
    points = width - 2 * LANES
    for turn, ref in enumerate((own_ref, odd_ref, even_ref)):
        start = turn * points
        values_ref[:, start : start + points] = stacked_halves(ref[:, :points] * (1.0 / 256.0))
        for axis in range(2):
            rows = off_grid(coordinate_rows(ref, points, axis) * TAPER_RATE, grain)
            for index in range(points // LANES):
                lanes = slice(start + index * LANES, start + (index + 1) * LANES)
                coords_ref[axis : axis + 1, lanes] = rows[index : index + 1]
    values_ref[:, 3 * points :] = jnp.zeros((2 * probes, LANES), jnp.bfloat16)


def assemble(strips, extent):
    probes, width = strips[0].shape
    near = 3 * (width - 2 * LANES)
    return pl.pallas_call(
        functools.partial(assemble_kernel, grain_of(TAPER_RATE * extent)),
        out_shape=(
            jax.ShapeDtypeStruct((2 * probes, near + LANES), jnp.bfloat16),
            jax.ShapeDtypeStruct((2, near), jnp.float32),
        ),
        in_specs=[VMEM] * 3,
        out_specs=(VMEM, VMEM),
        compiler_params=pltpu.CompilerParams(vmem_limit_bytes=LIMIT),
        name="assemble",
    )(*strips)


def grain_of(bound):
    return 2.0 ** math.ceil(math.log2(1.01 * bound))


def on_grid(x, grain):
    return (x + grain) - grain


def off_grid(x, grain):
    return (x + grain) - (grain - grain * HALF_GRAIN)


def project_kernel(scale, grain, follows, stack_ref, *rest):
    if follows:
        before_ref, columns, out_ref, high_ref, low_ref, weights = rest
    else:
        knots_ref, out_ref, high_ref, low_ref, columns, copy_ref, weights = rest
        copy_ref[...] = stack_ref[...]
        fill = jnp.zeros((6, knots_ref.shape[1]), jnp.float32)
        columns[...] = jnp.transpose(jnp.concatenate([off_grid(knots_ref[...] * scale, grain), fill], axis=0))
    knots, points = high_ref.shape
    probes = stack_ref.shape[0]
    tile = min(TILE, knots)
    weights[...] = padded_halves(stack_ref[:, :points], weights.shape[0])
    east, north = [on_grid(coordinate_rows(stack_ref, points, axis) * scale, grain) for axis in range(2)]

    for start in range(0, knots, tile):
        rows = slice(start, start + tile)
        kx, ky = [columns[rows, axis : axis + 1] for axis in range(2)]
        for block in range(points // LANES):
            lanes = slice(block * LANES, (block + 1) * LANES)
            dx = east[block : block + 1, :] - kx
            dy = north[block : block + 1, :] - ky
            square = dx * dx + dy * dy
            high_ref[rows, lanes], low_ref[rows, lanes] = halves(jnp.exp2(-(square * lax.rsqrt(square))))
        total = dot_nt(high_ref[rows, :], weights[...]) + dot_nt(low_ref[rows, :], weights[...])
        found = folded_columns(total, probes)
        out_ref[:, rows] = found + before_ref[:, rows] if follows else found


def project(stack, knot_locs, scale, extent, before=None):
    probes, points, knots = stack.shape[0], stack.shape[1] - 2 * LANES, knot_locs.shape[1]
    out_shape = [
        jax.ShapeDtypeStruct((probes, knots), jnp.float32),
        pltpu.VMEM((knots, points), jnp.bfloat16),
        pltpu.VMEM((knots, points), jnp.bfloat16),
    ]
    if before is None:
        operands = (stack, knot_locs)
        out_shape += [
            jax.ShapeDtypeStruct((knots, 8), jnp.float32),
            jax.ShapeDtypeStruct(stack.shape, jnp.float32),
        ]
    else:
        operands = (stack, before[0], before[3])
    found = pl.pallas_call(
        functools.partial(project_kernel, scale, grain_of(scale * extent), before is not None),
        out_shape=out_shape,
        in_specs=[VMEM] * len(operands),
        out_specs=[VMEM] * len(out_shape),
        scratch_shapes=[pltpu.VMEM((LANES, points), jnp.bfloat16)],
        compiler_params=pltpu.CompilerParams(vmem_limit_bytes=LIMIT),
        cost_estimate=cost(2800, points * knots, 2),
        name="project",
    )(*operands)
    return found if before is None else [*found, *before[3:]]


def factor_kernel(scale, step, parts, before_ref, proj_ref, *rest):
    highs, lows, (out_ref, weights) = rest[:parts], rest[parts : 2 * parts], rest[-2:]
    probes, depth = proj_ref.shape
    weights[...] = stacked_halves(proj_ref[...] * scale)
    owner = lax.rem(lax.axis_index("knot") + step, lax.axis_size("knot"))
    deep = pl.ds(pl.multiple_of(owner * depth, depth), depth)
    rows = highs[0].shape[1]
    tile = min(TILE, rows)
    for part, (high_ref, low_ref) in enumerate(zip(highs, lows)):
        for start in range(0, rows, tile):
            here = slice(start, start + tile)
            found = folded(dot_nn(weights[...], high_ref[deep, here]) + dot_nn(weights[...], low_ref[deep, here]))
            target = slice(part * rows + start, part * rows + start + tile)
            if before_ref is not None:
                found = found + before_ref[:, target]
            out_ref[:, target] = found


def factored(before, projection, splits, scale, step):
    probes, depth = projection.shape
    highs, lows = [
        [pltpu.with_memory_space_constraint(split[half], pltpu.VMEM) for split in splits] for half in range(2)
    ]
    rows = sum(high.shape[1] for high in highs)
    kernel = functools.partial(factor_kernel, scale, step, len(splits))
    operands = (projection, *highs, *lows)
    if before is None:
        kernel = functools.partial(kernel, None)
    else:
        operands = (before, *operands)
    return pl.pallas_call(
        kernel,
        out_shape=jax.ShapeDtypeStruct((probes, rows), jnp.float32),
        in_specs=[VMEM] * len(operands),
        out_specs=VMEM,
        scratch_shapes=[pltpu.VMEM((2 * probes, depth), jnp.bfloat16)],
        compiler_params=pltpu.CompilerParams(vmem_limit_bytes=LIMIT),
        cost_estimate=cost(1000, rows * depth),
        name="factor",
    )(*operands)


def spread_kernel(scale, factor_ref, high_ref, low_ref, out_ref):
    points = high_ref.shape[1]
    tile = min(TILE, points)
    weights = stacked_halves(factor_ref[...] * scale)
    for start in range(0, points, tile):
        lanes = slice(start, start + tile)
        out_ref[:, lanes] = folded(dot_nn(weights, high_ref[:, lanes]) + dot_nn(weights, low_ref[:, lanes]))


def spread(factor, high, low, scale):
    (probes, knots), points = factor.shape, high.shape[1]
    high = pltpu.with_memory_space_constraint(high, pltpu.VMEM)
    low = pltpu.with_memory_space_constraint(low, pltpu.VMEM)
    return pl.pallas_call(
        functools.partial(spread_kernel, scale),
        out_shape=jax.ShapeDtypeStruct((probes, points), jnp.float32),
        in_specs=[VMEM, VMEM, VMEM],
        out_specs=VMEM,
        compiler_params=pltpu.CompilerParams(vmem_limit_bytes=LIMIT),
        cost_estimate=cost(850, knots * points),
        name="spread",
    )(factor, high, low)


def covariance(square):
    apart = square * lax.rsqrt(square)
    remain = jnp.maximum(4.0 - apart, 0.0)
    twice = remain * remain
    return (jnp.exp2(apart * (-LOG2E / (COV_RANGE * TAPER_RATE))) * (twice * twice)) * (5.0 - remain)


def beside_kernel(first, first_row, grain, ids_ref, counts_ref, own_ref, values_ref, coords_ref, precision_ref, *rest):
    out_ref, high_ref, low_ref = rest[-3:]
    own_blocks, slots = ids_ref.shape
    block = LANES
    probes = own_ref.shape[0]
    span = own_blocks + 2
    zeros_place = coords_ref.shape[1] // block
    column = lax.axis_index("space")
    north_base = lax.axis_index("knot") * own_blocks - 1
    north_cells = lax.axis_size("knot") * own_blocks
    own_columns = [
        on_grid(jnp.transpose(coordinate_rows(own_ref, own_blocks * block, axis) * TAPER_RATE), grain)
        for axis in range(2)
    ]

    def place(group, slot):
        ahead = ids_ref[group, slot] - (column - 1) * north_cells
        east = jnp.where(ahead >= north_cells, 1, 0) + jnp.where(ahead >= 2 * north_cells, 1, 0)
        strip = jnp.where(east == 1, 0, 2 - lax.rem(column + lax.div(east, 2) + 1, 2))
        index = strip * span + (ahead - east * north_cells - north_base)
        return lanes_of(index), lanes_of(jnp.where(slot < counts_ref[group], index, zeros_place))

    def lanes_of(index):
        return pl.ds(pl.multiple_of(index * block, block), block)

    depth, rows = high_ref.shape
    tile = min(TILE, rows)
    wide = min(TILE, depth)
    tiles = [(start, deep) for start in range(0, rows, tile) for deep in range(0, depth, wide)]
    groups = out_ref.shape[1] // block
    turns = groups * -(-slots // 2)

    for index in range(groups):
        group = first + index
        px, py = [turned[:, group : group + 1] for turned in own_columns]
        total = jnp.zeros((block, 2 * probes), jnp.float32)
        for pair in range(0, slots, 2):
            highs, lows, parts = [], [], []
            for slot in range(pair, min(pair + 2, slots)):
                lanes, value_lanes = place(group, slot)
                dx = px - coords_ref[0:1, lanes]
                dy = py - coords_ref[1:2, lanes]
                high, low = halves(covariance(dx * dx + dy * dy))
                highs.append(high)
                lows.append(low)
                parts.append(values_ref[:, value_lanes])
            part = jnp.concatenate(parts, axis=1)
            total = total + (
                dot_nt(jnp.concatenate(highs, axis=1), part) + dot_nt(jnp.concatenate(lows, axis=1), part)
            )
            turn = index * -(-slots // 2) + pair // 2
            for start, deep in tiles[turn * len(tiles) // turns : (turn + 1) * len(tiles) // turns]:
                from_row = first_row + start
                turned = jnp.transpose(precision_ref[from_row : from_row + tile, deep : deep + wide])
                here = slice(deep, deep + wide), slice(start, start + tile)
                high_ref[here], low_ref[here] = halves(turned)
        out_ref[:, index * block : (index + 1) * block] = (
            TAPER_SCALE * folded_columns(total, probes)
            + NUGGET * own_ref[:, group * block : (group + 1) * block]
        )


def beside_round(ids, counts, own, values, coords, precision, extent, first, blocks, first_row, rows, after):
    slots, depth = ids.shape[1], precision.shape[1]
    return pl.pallas_call(
        functools.partial(beside_kernel, first, first_row, grain_of(TAPER_RATE * extent)),
        out_shape=(
            jax.ShapeDtypeStruct((own.shape[0], blocks * LANES), jnp.float32),
            pltpu.VMEM((depth, rows), jnp.bfloat16),
            pltpu.VMEM((depth, rows), jnp.bfloat16),
        ),
        in_specs=[SMEM, SMEM, VMEM, VMEM, VMEM, VMEM] + [ANY] * len(after),
        out_specs=(VMEM, VMEM, VMEM),
        compiler_params=pltpu.CompilerParams(vmem_limit_bytes=LIMIT),
        cost_estimate=cost(500, blocks * slots * LANES * LANES, 2),
        name="beside",
    )(ids, counts, own, values, coords, precision, *after)


def add_kernel(count, *refs):
    total = refs[0][...]
    for ref in refs[1:count]:
        total = total + ref[...]
    refs[-1][...] = total


def add_all(values, after):
    return pl.pallas_call(
        functools.partial(add_kernel, len(values)),
        out_shape=jax.ShapeDtypeStruct(values[0].shape, jnp.float32),
        in_specs=[VMEM] * len(values) + [ANY] * len(after),
        out_specs=VMEM,
        compiler_params=pltpu.CompilerParams(vmem_limit_bytes=LIMIT),
        name="add",
    )(*values, *after)


def butterfly_rounds(count):
    assert count & (count - 1) == 0
    bits = [1 << i for i in range(count.bit_length() - 1)]
    rounds = [(low | high, high, low) for low, high in zip(bits[0::2], bits[1::2])]
    return rounds + [(bit,) for bit in bits[len(rounds) * 2 :]]


def butterfly_round(value, axis, turn):
    count = lax.axis_size(axis)
    return [
        lax.ppermute(value, axis, [(i, i ^ step) for i in range(count)]) for step in butterfly_rounds(count)[turn]
    ]


def shifted(value, axis, step):
    count = lax.axis_size(axis)
    if step % count == 0:
        return value
    return lax.ppermute(value, axis, [((i + step) % count, i) for i in range(count)])


def paired(value, axis, other, first):
    count, groups = lax.axis_size(axis), lax.axis_size(other)
    partner = {}
    for i in range(first, count - 1, 2):
        partner[i], partner[i + 1] = i + 1, i
    pairs = []
    for i in range(count):
        for j in range(groups):
            if i in partner:
                pairs.append((i * groups + j, partner[i] * groups + j))
            elif j ^ 1 < groups:
                pairs.append((i * groups + j, i * groups + (j ^ 1)))
    return lax.ppermute(value, (axis, other), pairs)


def shards(probes, locations, knot_locs, knot_precision, neighbours, counts):
    own_blocks = neighbours.shape[0]
    row_count = probes.shape[1]
    knot_total = knot_precision.shape[1]
    device_count = lax.axis_size(("space", "knot"))
    groups = lax.axis_size("knot")
    knot_range = KNOT_REACH * math.sqrt(own_blocks * device_count / knot_total)
    proj_scale = PROJ_GAIN * math.sqrt(knot_total / (row_count * device_count))

    stack, knots = prepare(probes, locations, knot_locs, own_blocks)
    chunks = [shifted(stack, "knot", step) for step in range(groups)]
    rate = LOG2E / knot_range
    extent = CELL * max(lax.axis_size("space"), groups * own_blocks)
    parts = []
    for chunk in chunks:
        parts.append(project(chunk, knots, rate, extent, parts[-1] if parts else None))
    stack = parts[0][4]

    strip = make_strip(chunks[-1], stack, chunks[1 % groups])
    odd = paired(strip, "space", "knot", 1)
    values, coords = assemble([strip, odd, paired(strip, "space", "knot", 0)], extent)
    projection = parts[-1][0]
    rounds = len(butterfly_rounds(lax.axis_size("space")))
    pieces = math.gcd(math.gcd(own_blocks, rounds), knot_precision.shape[0] // LANES)
    bounds = [own_blocks * i * (i + 2) // (pieces * (pieces + 2)) for i in range(pieces + 1)]
    per_split = knot_precision.shape[0] // pieces
    base, splits = [], []
    for turn in range(rounds):
        got = butterfly_round(projection, "space", turn)
        beside = []
        for i in range(pieces):
            if i * rounds // pieces == turn:
                done = beside_round(
                    neighbours, counts, stack, values, coords, knot_precision, extent,
                    bounds[i], bounds[i + 1] - bounds[i], i * per_split, per_split, [projection],
                )
                base.append(done[0])
                splits.append(done[1:])
                beside.extend(done)
        projection = add_all([projection, *got], beside)
    factor = factored(None, projection, splits, proj_scale, 0)
    for step in range(1, groups):
        factor = factored(factor, shifted(projection, "knot", step), splits, proj_scale, step)
    total = jnp.concatenate(base, axis=1)
    for step in reversed(range(groups)):
        share = spread(factor, parts[step][1], parts[step][2], LOW_SCALE * EXPAND_GAIN)
        total = total + shifted(share, "knot", -step)
    return total


def solution(mesh):
    return jax.shard_map(
        shards,
        mesh=mesh,
        in_specs=(
            P(None, ("space", "knot")),
            P(None, ("space", "knot")),
            P(None, "knot"),
            P("knot", None),
            P(("space", "knot"), None),
            P(("space", "knot")),
        ),
        out_specs=P(None, ("space", "knot")),
        check_vma=False,
    )
```

```python
import functools
import math

import jax
import jax.numpy as jnp
from jax import lax
from jax.experimental import pallas as pl
from jax.experimental.pallas import tpu as pltpu
from jax.sharding import PartitionSpec as P

COV_RANGE = 0.05
TAPER_LEN = 0.15
KNOT_REACH = 0.15
TAPER_SCALE = 0.1
PROJ_GAIN = 0.5
EXPAND_GAIN = 0.5
LOW_SCALE = 0.5
NUGGET = 0.25
LOG2E = math.log2(math.e)
TAPER_RATE = 4.0 / TAPER_LEN
CELL = 0.1
TILE = 256
LANES = 128
HALF_GRAIN = 2.0**-24
LIMIT = 6 * 1024 * 1024
VMEM = pl.BlockSpec(memory_space=pltpu.VMEM)
HBM = pl.BlockSpec(memory_space=pltpu.HBM)
ANY = pl.BlockSpec(memory_space=pl.ANY)
SMEM = pl.BlockSpec(memory_space=pltpu.SMEM)


def halves(x):
    high = x.astype(jnp.bfloat16)
    return high, (x - high.astype(jnp.float32)).astype(jnp.bfloat16)


def stacked_halves(x):
    return jnp.concatenate(halves(x), axis=0)


def folded(x):
    rows = x.shape[0] // 2
    return x[:rows] + x[rows:]


def dot_nt(left, right):
    return lax.dot_general(
        left, right, (((1,), (1,)), ((), ())), preferred_element_type=jnp.float32
    )


def dot_nn(left, right):
    return jnp.dot(left, right, preferred_element_type=jnp.float32)


def folded_columns(x, rows):
    x = jnp.transpose(x)
    return x[:rows] + x[rows : 2 * rows]


def cost(work, pairs, transcendentals=0):
    return pl.CostEstimate(flops=work * pairs, bytes_accessed=4 * pairs, transcendentals=transcendentals * pairs)


def coordinate_rows(ref, points, axis):
    start = points + axis * LANES
    return ref[:, start : start + LANES]


def prepare_kernel(blocks, probes_ref, locations_ref, knots_ref, stack_ref, knots_out_ref, coords, sems):
    points = probes_ref.shape[1]
    block = points // blocks
    copies = [
        pltpu.make_async_copy(probes_ref, stack_ref.at[:, pl.ds(0, points)], sems.at[0]),
        pltpu.make_async_copy(locations_ref, coords, sems.at[1]),
        pltpu.make_async_copy(knots_ref, knots_out_ref, sems.at[2]),
    ]
    for copy in copies:
        copy.start()
    for copy in copies:
        copy.wait()
    stack_ref[:, points:] = jnp.zeros((stack_ref.shape[0], 2 * LANES), jnp.float32)
    for axis in range(2):
        lanes = slice(points + axis * LANES, points + (axis + 1) * LANES)
        for index in range(blocks):
            stack_ref[index : index + 1, lanes] = coords[axis : axis + 1, index * block : (index + 1) * block]


def prepare(probes, locations, knot_locs, blocks):
    rows, points = probes.shape
    assert points == blocks * LANES and blocks + 2 <= rows
    probes, locations, knot_locs = [
        pltpu.with_memory_space_constraint(x, pltpu.HBM) for x in (probes, locations, knot_locs)
    ]
    return pl.pallas_call(
        functools.partial(prepare_kernel, blocks),
        out_shape=(
            jax.ShapeDtypeStruct((rows, points + 2 * LANES), jnp.float32),
            jax.ShapeDtypeStruct(knot_locs.shape, jnp.float32),
        ),
        in_specs=[HBM, HBM, HBM],
        out_specs=(VMEM, VMEM),
        scratch_shapes=[pltpu.VMEM(locations.shape, jnp.float32), pltpu.SemaphoreType.DMA((3,))],
        compiler_params=pltpu.CompilerParams(vmem_limit_bytes=LIMIT),
        name="prepare",
    )(probes, locations, knot_locs)


def strip_kernel(below_ref, own_ref, above_ref, out_ref):
    rows, width = own_ref.shape
    points = width - 2 * LANES
    blocks = points // LANES
    out_ref[:, :LANES] = below_ref[:, points - LANES : points]
    out_ref[:, LANES : points + LANES] = own_ref[:, :points]
    out_ref[:, points + LANES : points + 2 * LANES] = above_ref[:, :LANES]
    for axis in range(2):
        lanes = slice(points + axis * LANES, points + (axis + 1) * LANES)
        target = slice(lanes.start + 2 * LANES, lanes.stop + 2 * LANES)
        out_ref[:, target] = jnp.zeros((rows, LANES), jnp.float32)
        out_ref[0:1, target] = below_ref[blocks - 1 : blocks, lanes]
        out_ref[1 : blocks + 1, target] = own_ref[:blocks, lanes]
        out_ref[blocks + 1 : blocks + 2, target] = above_ref[0:1, lanes]


def make_strip(below, own, above):
    return pl.pallas_call(
        strip_kernel,
        out_shape=jax.ShapeDtypeStruct((own.shape[0], own.shape[1] + 2 * LANES), jnp.float32),
        in_specs=[VMEM, VMEM, VMEM],
        out_specs=VMEM,
        compiler_params=pltpu.CompilerParams(vmem_limit_bytes=LIMIT),
        name="strip",
    )(below, own, above)


def assemble_kernel(grain, own_ref, odd_ref, even_ref, values_ref, coords_ref):
    probes, width = own_ref.shape
    points = width - 2 * LANES
    for turn, ref in enumerate((own_ref, odd_ref, even_ref)):
        start = turn * points
        values_ref[:, start : start + points] = stacked_halves(ref[:, :points] * (1.0 / 256.0))
        for axis in range(2):
            rows = off_grid(coordinate_rows(ref, points, axis) * TAPER_RATE, grain)
            for index in range(points // LANES):
                lanes = slice(start + index * LANES, start + (index + 1) * LANES)
                coords_ref[axis : axis + 1, lanes] = rows[index : index + 1]
    values_ref[:, 3 * points :] = jnp.zeros((2 * probes, LANES), jnp.bfloat16)


def assemble(strips, extent):
    probes, width = strips[0].shape
    near = 3 * (width - 2 * LANES)
    return pl.pallas_call(
        functools.partial(assemble_kernel, grain_of(TAPER_RATE * extent)),
        out_shape=(
            jax.ShapeDtypeStruct((2 * probes, near + LANES), jnp.bfloat16),
            jax.ShapeDtypeStruct((2, near), jnp.float32),
        ),
        in_specs=[VMEM] * 3,
        out_specs=(VMEM, VMEM),
        compiler_params=pltpu.CompilerParams(vmem_limit_bytes=LIMIT),
        name="assemble",
    )(*strips)


def grain_of(bound):
    return 2.0 ** math.ceil(math.log2(1.01 * bound))


def on_grid(x, grain):
    return (x + grain) - grain


def off_grid(x, grain):
    return (x + grain) - (grain - grain * HALF_GRAIN)


def project_kernel(scale, grain, follows, stack_ref, *rest):
    if follows:
        before_ref, columns, out_ref, high_ref, low_ref, weights = rest
    else:
        knots_ref, out_ref, high_ref, low_ref, columns, copy_ref, weights = rest
        copy_ref[...] = stack_ref[...]
        fill = jnp.zeros((6, knots_ref.shape[1]), jnp.float32)
        columns[...] = jnp.transpose(jnp.concatenate([off_grid(knots_ref[...] * scale, grain), fill], axis=0))
    knots, points = high_ref.shape
    probes = stack_ref.shape[0]
    tile = min(TILE, knots)
    weights[...] = stacked_halves(stack_ref[:, :points])
    east, north = [on_grid(coordinate_rows(stack_ref, points, axis) * scale, grain) for axis in range(2)]

    for start in range(0, knots, tile):
        rows = slice(start, start + tile)
        kx, ky = [columns[rows, axis : axis + 1] for axis in range(2)]
        for block in range(points // LANES):
            lanes = slice(block * LANES, (block + 1) * LANES)
            dx = east[block : block + 1, :] - kx
            dy = north[block : block + 1, :] - ky
            square = dx * dx + dy * dy
            high_ref[rows, lanes], low_ref[rows, lanes] = halves(jnp.exp2(-(square * lax.rsqrt(square))))
        total = dot_nt(high_ref[rows, :], weights[...]) + dot_nt(low_ref[rows, :], weights[...])
        found = folded_columns(total, probes)
        out_ref[:, rows] = found + before_ref[:, rows] if follows else found


def project(stack, knot_locs, scale, extent, before=None):
    probes, points, knots = stack.shape[0], stack.shape[1] - 2 * LANES, knot_locs.shape[1]
    out_shape = [
        jax.ShapeDtypeStruct((probes, knots), jnp.float32),
        pltpu.VMEM((knots, points), jnp.bfloat16),
        pltpu.VMEM((knots, points), jnp.bfloat16),
    ]
    if before is None:
        operands = (stack, knot_locs)
        out_shape += [
            jax.ShapeDtypeStruct((knots, 8), jnp.float32),
            jax.ShapeDtypeStruct(stack.shape, jnp.float32),
        ]
    else:
        operands = (stack, before[0], before[3])
    found = pl.pallas_call(
        functools.partial(project_kernel, scale, grain_of(scale * extent), before is not None),
        out_shape=out_shape,
        in_specs=[VMEM] * len(operands),
        out_specs=[VMEM] * len(out_shape),
        scratch_shapes=[pltpu.VMEM((2 * probes, points), jnp.bfloat16)],
        compiler_params=pltpu.CompilerParams(vmem_limit_bytes=LIMIT),
        cost_estimate=cost(2800, points * knots, 2),
        name="project",
    )(*operands)
    return found if before is None else [*found, *before[3:]]


def factor_kernel(scale, step, parts, before_ref, proj_ref, *rest):
    highs, lows, (out_ref, weights) = rest[:parts], rest[parts : 2 * parts], rest[-2:]
    probes, depth = proj_ref.shape
    weights[...] = stacked_halves(proj_ref[...] * scale)
    owner = lax.rem(lax.axis_index("knot") + step, lax.axis_size("knot"))
    deep = pl.ds(pl.multiple_of(owner * depth, depth), depth)
    rows = highs[0].shape[1]
    tile = min(TILE, rows)
    for part, (high_ref, low_ref) in enumerate(zip(highs, lows)):
        for start in range(0, rows, tile):
            here = slice(start, start + tile)
            found = folded(dot_nn(weights[...], high_ref[deep, here]) + dot_nn(weights[...], low_ref[deep, here]))
            target = slice(part * rows + start, part * rows + start + tile)
            if before_ref is not None:
                found = found + before_ref[:, target]
            out_ref[:, target] = found


def factored(before, projection, splits, scale, step):
    probes, depth = projection.shape
    highs, lows = [
        [pltpu.with_memory_space_constraint(split[half], pltpu.VMEM) for split in splits] for half in range(2)
    ]
    rows = sum(high.shape[1] for high in highs)
    kernel = functools.partial(factor_kernel, scale, step, len(splits))
    operands = (projection, *highs, *lows)
    if before is None:
        kernel = functools.partial(kernel, None)
    else:
        operands = (before, *operands)
    return pl.pallas_call(
        kernel,
        out_shape=jax.ShapeDtypeStruct((probes, rows), jnp.float32),
        in_specs=[VMEM] * len(operands),
        out_specs=VMEM,
        scratch_shapes=[pltpu.VMEM((2 * probes, depth), jnp.bfloat16)],
        compiler_params=pltpu.CompilerParams(vmem_limit_bytes=LIMIT),
        cost_estimate=cost(1000, rows * depth),
        name="factor",
    )(*operands)


def spread_kernel(scale, factor_ref, high_ref, low_ref, out_ref):
    points = high_ref.shape[1]
    tile = min(TILE, points)
    weights = stacked_halves(factor_ref[...] * scale)
    for start in range(0, points, tile):
        lanes = slice(start, start + tile)
        out_ref[:, lanes] = folded(dot_nn(weights, high_ref[:, lanes]) + dot_nn(weights, low_ref[:, lanes]))


def spread(factor, high, low, scale):
    (probes, knots), points = factor.shape, high.shape[1]
    high = pltpu.with_memory_space_constraint(high, pltpu.VMEM)
    low = pltpu.with_memory_space_constraint(low, pltpu.VMEM)
    return pl.pallas_call(
        functools.partial(spread_kernel, scale),
        out_shape=jax.ShapeDtypeStruct((probes, points), jnp.float32),
        in_specs=[VMEM, VMEM, VMEM],
        out_specs=VMEM,
        compiler_params=pltpu.CompilerParams(vmem_limit_bytes=LIMIT),
        cost_estimate=cost(850, knots * points),
        name="spread",
    )(factor, high, low)


def covariance(square):
    apart = square * lax.rsqrt(square)
    remain = jnp.maximum(4.0 - apart, 0.0)
    twice = remain * remain
    return (jnp.exp2(apart * (-LOG2E / (COV_RANGE * TAPER_RATE))) * (twice * twice)) * (5.0 - remain)


def beside_kernel(first, first_row, grain, ids_ref, counts_ref, own_ref, values_ref, coords_ref, precision_ref, *rest):
    out_ref, high_ref, low_ref = rest[-3:]
    own_blocks, slots = ids_ref.shape
    block = LANES
    probes = own_ref.shape[0]
    span = own_blocks + 2
    zeros_place = coords_ref.shape[1] // block
    column = lax.axis_index("space")
    north_base = lax.axis_index("knot") * own_blocks - 1
    north_cells = lax.axis_size("knot") * own_blocks
    own_columns = [
        on_grid(jnp.transpose(coordinate_rows(own_ref, own_blocks * block, axis) * TAPER_RATE), grain)
        for axis in range(2)
    ]

    def place(group, slot):
        ahead = ids_ref[group, slot] - (column - 1) * north_cells
        east = jnp.where(ahead >= north_cells, 1, 0) + jnp.where(ahead >= 2 * north_cells, 1, 0)
        strip = jnp.where(east == 1, 0, 2 - lax.rem(column + lax.div(east, 2) + 1, 2))
        index = strip * span + (ahead - east * north_cells - north_base)
        return lanes_of(index), lanes_of(jnp.where(slot < counts_ref[group], index, zeros_place))

    def lanes_of(index):
        return pl.ds(pl.multiple_of(index * block, block), block)

    depth, rows = high_ref.shape
    tile = min(TILE, rows)
    wide = min(TILE, depth)
    tiles = [(start, deep) for start in range(0, rows, tile) for deep in range(0, depth, wide)]
    groups = out_ref.shape[1] // block
    turns = groups * -(-slots // 2)

    for index in range(groups):
        group = first + index
        px, py = [turned[:, group : group + 1] for turned in own_columns]
        total = jnp.zeros((block, 2 * probes), jnp.float32)
        for pair in range(0, slots, 2):
            highs, lows, parts = [], [], []
            for slot in range(pair, min(pair + 2, slots)):
                lanes, value_lanes = place(group, slot)
                dx = px - coords_ref[0:1, lanes]
                dy = py - coords_ref[1:2, lanes]
                high, low = halves(covariance(dx * dx + dy * dy))
                highs.append(high)
                lows.append(low)
                parts.append(values_ref[:, value_lanes])
            part = jnp.concatenate(parts, axis=1)
            total = total + (
                dot_nt(jnp.concatenate(highs, axis=1), part) + dot_nt(jnp.concatenate(lows, axis=1), part)
            )
            turn = index * -(-slots // 2) + pair // 2
            for start, deep in tiles[turn * len(tiles) // turns : (turn + 1) * len(tiles) // turns]:
                from_row = first_row + start
                turned = jnp.transpose(precision_ref[from_row : from_row + tile, deep : deep + wide])
                here = slice(deep, deep + wide), slice(start, start + tile)
                high_ref[here], low_ref[here] = halves(turned)
        out_ref[:, index * block : (index + 1) * block] = (
            TAPER_SCALE * folded_columns(total, probes)
            + NUGGET * own_ref[:, group * block : (group + 1) * block]
        )


def beside_round(ids, counts, own, values, coords, precision, extent, first, blocks, first_row, rows, after):
    slots, depth = ids.shape[1], precision.shape[1]
    return pl.pallas_call(
        functools.partial(beside_kernel, first, first_row, grain_of(TAPER_RATE * extent)),
        out_shape=(
            jax.ShapeDtypeStruct((own.shape[0], blocks * LANES), jnp.float32),
            pltpu.VMEM((depth, rows), jnp.bfloat16),
            pltpu.VMEM((depth, rows), jnp.bfloat16),
        ),
        in_specs=[SMEM, SMEM, VMEM, VMEM, VMEM, VMEM] + [ANY] * len(after),
        out_specs=(VMEM, VMEM, VMEM),
        compiler_params=pltpu.CompilerParams(vmem_limit_bytes=LIMIT),
        cost_estimate=cost(500, blocks * slots * LANES * LANES, 2),
        name="beside",
    )(ids, counts, own, values, coords, precision, *after)


def add_kernel(count, *refs):
    total = refs[0][...]
    for ref in refs[1:count]:
        total = total + ref[...]
    refs[-1][...] = total


def add_all(values, after):
    return pl.pallas_call(
        functools.partial(add_kernel, len(values)),
        out_shape=jax.ShapeDtypeStruct(values[0].shape, jnp.float32),
        in_specs=[VMEM] * len(values) + [ANY] * len(after),
        out_specs=VMEM,
        compiler_params=pltpu.CompilerParams(vmem_limit_bytes=LIMIT),
        name="add",
    )(*values, *after)


def butterfly_rounds(count):
    assert count & (count - 1) == 0
    bits = [1 << i for i in range(count.bit_length() - 1)]
    rounds = [(low | high, high, low) for low, high in zip(bits[0::2], bits[1::2])]
    return rounds + [(bit,) for bit in bits[len(rounds) * 2 :]]


def butterfly_round(value, axis, turn):
    count = lax.axis_size(axis)
    return [
        lax.ppermute(value, axis, [(i, i ^ step) for i in range(count)]) for step in butterfly_rounds(count)[turn]
    ]


def shifted(value, axis, step):
    count = lax.axis_size(axis)
    if step % count == 0:
        return value
    return lax.ppermute(value, axis, [((i + step) % count, i) for i in range(count)])


def paired(value, axis, other, first):
    count, groups = lax.axis_size(axis), lax.axis_size(other)
    partner = {}
    for i in range(first, count - 1, 2):
        partner[i], partner[i + 1] = i + 1, i
    pairs = []
    for i in range(count):
        for j in range(groups):
            if i in partner:
                pairs.append((i * groups + j, partner[i] * groups + j))
            elif j ^ 1 < groups:
                pairs.append((i * groups + j, i * groups + (j ^ 1)))
    return lax.ppermute(value, (axis, other), pairs)


def shards(probes, locations, knot_locs, knot_precision, neighbours, counts):
    own_blocks = neighbours.shape[0]
    row_count = probes.shape[1]
    knot_total = knot_precision.shape[1]
    device_count = lax.axis_size(("space", "knot"))
    groups = lax.axis_size("knot")
    knot_range = KNOT_REACH * math.sqrt(own_blocks * device_count / knot_total)
    proj_scale = PROJ_GAIN * math.sqrt(knot_total / (row_count * device_count))

    stack, knots = prepare(probes, locations, knot_locs, own_blocks)
    chunks = [shifted(stack, "knot", step) for step in range(groups)]
    rate = LOG2E / knot_range
    extent = CELL * max(lax.axis_size("space"), groups * own_blocks)
    parts = []
    for chunk in chunks:
        parts.append(project(chunk, knots, rate, extent, parts[-1] if parts else None))
    stack = parts[0][4]

    strip = make_strip(chunks[-1], stack, chunks[1 % groups])
    odd = paired(strip, "space", "knot", 1)
    values, coords = assemble([strip, odd, paired(strip, "space", "knot", 0)], extent)
    projection = parts[-1][0]
    rounds = len(butterfly_rounds(lax.axis_size("space")))
    pieces = math.gcd(math.gcd(own_blocks, rounds), knot_precision.shape[0] // LANES)
    bounds = [own_blocks * i * (i + 2) // (pieces * (pieces + 2)) for i in range(pieces + 1)]
    per_split = knot_precision.shape[0] // pieces
    base, splits = [], []
    for turn in range(rounds):
        got = butterfly_round(projection, "space", turn)
        beside = []
        for i in range(pieces):
            if i * rounds // pieces == turn:
                done = beside_round(
                    neighbours, counts, stack, values, coords, knot_precision, extent,
                    bounds[i], bounds[i + 1] - bounds[i], i * per_split, per_split, [projection],
                )
                base.append(done[0])
                splits.append(done[1:])
                beside.extend(done)
        projection = add_all([projection, *got], beside)
    factor = factored(None, projection, splits, proj_scale, 0)
    for step in range(1, groups):
        factor = factored(factor, shifted(projection, "knot", step), splits, proj_scale, step)
    total = jnp.concatenate(base, axis=1)
    for step in reversed(range(groups)):
        share = spread(factor, parts[step][1], parts[step][2], LOW_SCALE * EXPAND_GAIN)
        total = total + shifted(share, "knot", -step)
    return total


def solution(mesh):
    return jax.shard_map(
        shards,
        mesh=mesh,
        in_specs=(
            P(None, ("space", "knot")),
            P(None, ("space", "knot")),
            P(None, "knot"),
            P("knot", None),
            P(("space", "knot"), None),
            P(("space", "knot")),
        ),
        out_specs=P(None, ("space", "knot")),
        check_vma=False,
    )
```

```python
import functools
import math

import jax
import jax.numpy as jnp
from jax import lax
from jax.experimental import pallas as pl
from jax.experimental.pallas import tpu as pltpu
from jax.sharding import PartitionSpec as P

COV_RANGE = 0.05
TAPER_LEN = 0.15
KNOT_REACH = 0.15
TAPER_SCALE = 0.1
PROJ_GAIN = 0.5
EXPAND_GAIN = 0.5
LOW_SCALE = 0.5
NUGGET = 0.25
LOG2E = math.log2(math.e)
TAPER_RATE = 4.0 / TAPER_LEN
CELL = 0.1
TILE = 256
LANES = 128
HALF_GRAIN = 2.0**-24
LIMIT = 6 * 1024 * 1024
VMEM = pl.BlockSpec(memory_space=pltpu.VMEM)
HBM = pl.BlockSpec(memory_space=pltpu.HBM)
ANY = pl.BlockSpec(memory_space=pl.ANY)
SMEM = pl.BlockSpec(memory_space=pltpu.SMEM)


def halves(x):
    high = x.astype(jnp.bfloat16)
    return high, (x - high.astype(jnp.float32)).astype(jnp.bfloat16)


def stacked_halves(x):
    return jnp.concatenate(halves(x), axis=0)


def folded(x):
    rows = x.shape[0] // 2
    return x[:rows] + x[rows:]


def dot_nt(left, right):
    return lax.dot_general(
        left, right, (((1,), (1,)), ((), ())), preferred_element_type=jnp.float32
    )


def dot_nn(left, right):
    return jnp.dot(left, right, preferred_element_type=jnp.float32)


def folded_columns(x, rows):
    x = jnp.transpose(x)
    return x[:rows] + x[rows : 2 * rows]


def cost(work, pairs, transcendentals=0):
    return pl.CostEstimate(flops=work * pairs, bytes_accessed=4 * pairs, transcendentals=transcendentals * pairs)


def coordinate_rows(ref, points, axis):
    start = points + axis * LANES
    return ref[:, start : start + LANES]


def prepare_kernel(blocks, probes_ref, locations_ref, knots_ref, stack_ref, knots_out_ref, coords, sems):
    points = probes_ref.shape[1]
    block = points // blocks
    copies = [
        pltpu.make_async_copy(probes_ref, stack_ref.at[:, pl.ds(0, points)], sems.at[0]),
        pltpu.make_async_copy(locations_ref, coords, sems.at[1]),
        pltpu.make_async_copy(knots_ref, knots_out_ref, sems.at[2]),
    ]
    for copy in copies:
        copy.start()
    for copy in copies:
        copy.wait()
    stack_ref[:, points:] = jnp.zeros((stack_ref.shape[0], 2 * LANES), jnp.float32)
    for axis in range(2):
        lanes = slice(points + axis * LANES, points + (axis + 1) * LANES)
        for index in range(blocks):
            stack_ref[index : index + 1, lanes] = coords[axis : axis + 1, index * block : (index + 1) * block]


def prepare(probes, locations, knot_locs, blocks):
    rows, points = probes.shape
    assert points == blocks * LANES and blocks + 2 <= rows
    probes, locations, knot_locs = [
        pltpu.with_memory_space_constraint(x, pltpu.HBM) for x in (probes, locations, knot_locs)
    ]
    return pl.pallas_call(
        functools.partial(prepare_kernel, blocks),
        out_shape=(
            jax.ShapeDtypeStruct((rows, points + 2 * LANES), jnp.float32),
            jax.ShapeDtypeStruct(knot_locs.shape, jnp.float32),
        ),
        in_specs=[HBM, HBM, HBM],
        out_specs=(VMEM, VMEM),
        scratch_shapes=[pltpu.VMEM(locations.shape, jnp.float32), pltpu.SemaphoreType.DMA((3,))],
        compiler_params=pltpu.CompilerParams(vmem_limit_bytes=LIMIT),
        name="prepare",
    )(probes, locations, knot_locs)


def strip_kernel(below_ref, own_ref, above_ref, out_ref):
    rows, width = own_ref.shape
    points = width - 2 * LANES
    blocks = points // LANES
    out_ref[:, :LANES] = below_ref[:, points - LANES : points]
    out_ref[:, LANES : points + LANES] = own_ref[:, :points]
    out_ref[:, points + LANES : points + 2 * LANES] = above_ref[:, :LANES]
    for axis in range(2):
        lanes = slice(points + axis * LANES, points + (axis + 1) * LANES)
        target = slice(lanes.start + 2 * LANES, lanes.stop + 2 * LANES)
        out_ref[:, target] = jnp.zeros((rows, LANES), jnp.float32)
        out_ref[0:1, target] = below_ref[blocks - 1 : blocks, lanes]
        out_ref[1 : blocks + 1, target] = own_ref[:blocks, lanes]
        out_ref[blocks + 1 : blocks + 2, target] = above_ref[0:1, lanes]


def make_strip(below, own, above):
    return pl.pallas_call(
        strip_kernel,
        out_shape=jax.ShapeDtypeStruct((own.shape[0], own.shape[1] + 2 * LANES), jnp.float32),
        in_specs=[VMEM, VMEM, VMEM],
        out_specs=VMEM,
        compiler_params=pltpu.CompilerParams(vmem_limit_bytes=LIMIT),
        name="strip",
    )(below, own, above)


def assemble_kernel(grain, own_ref, odd_ref, even_ref, values_ref, coords_ref):
    probes, width = own_ref.shape
    points = width - 2 * LANES
    for turn, ref in enumerate((own_ref, odd_ref, even_ref)):
        start = turn * points
        values_ref[:, start : start + points] = stacked_halves(ref[:, :points] * (1.0 / 256.0))
        for axis in range(2):
            rows = off_grid(coordinate_rows(ref, points, axis) * TAPER_RATE, grain)
            for index in range(points // LANES):
                lanes = slice(start + index * LANES, start + (index + 1) * LANES)
                coords_ref[axis : axis + 1, lanes] = rows[index : index + 1]
    values_ref[:, 3 * points :] = jnp.zeros((2 * probes, LANES), jnp.bfloat16)


def assemble(strips, extent):
    probes, width = strips[0].shape
    near = 3 * (width - 2 * LANES)
    return pl.pallas_call(
        functools.partial(assemble_kernel, grain_of(TAPER_RATE * extent)),
        out_shape=(
            jax.ShapeDtypeStruct((2 * probes, near + LANES), jnp.bfloat16),
            jax.ShapeDtypeStruct((2, near), jnp.float32),
        ),
        in_specs=[VMEM] * 3,
        out_specs=(VMEM, VMEM),
        compiler_params=pltpu.CompilerParams(vmem_limit_bytes=LIMIT),
        name="assemble",
    )(*strips)


def grain_of(bound):
    return 2.0 ** math.ceil(math.log2(1.01 * bound))


def on_grid(x, grain):
    return (x + grain) - grain


def off_grid(x, grain):
    return (x + grain) - (grain - grain * HALF_GRAIN)


def project_kernel(scale, grain, follows, stack_ref, *rest):
    if follows:
        before_ref, columns, out_ref, high_ref, low_ref, weights = rest
    else:
        knots_ref, out_ref, high_ref, low_ref, columns, copy_ref, weights = rest
        copy_ref[...] = stack_ref[...]
        fill = jnp.zeros((6, knots_ref.shape[1]), jnp.float32)
        columns[...] = jnp.transpose(jnp.concatenate([off_grid(knots_ref[...] * scale, grain), fill], axis=0))
    knots, points = high_ref.shape
    probes = stack_ref.shape[0]
    tile = min(TILE, knots)
    weights[...] = stacked_halves(stack_ref[:, :points])
    east, north = [on_grid(coordinate_rows(stack_ref, points, axis) * scale, grain) for axis in range(2)]

    for start in range(0, knots, tile):
        rows = slice(start, start + tile)
        kx, ky = [columns[rows, axis : axis + 1] for axis in range(2)]
        for block in range(points // LANES):
            lanes = slice(block * LANES, (block + 1) * LANES)
            dx = east[block : block + 1, :] - kx
            dy = north[block : block + 1, :] - ky
            square = dx * dx + dy * dy
            high_ref[rows, lanes], low_ref[rows, lanes] = halves(jnp.exp2(-(square * lax.rsqrt(square))))
        total = dot_nt(high_ref[rows, :], weights[...]) + dot_nt(low_ref[rows, :], weights[...])
        found = folded_columns(total, probes)
        out_ref[:, rows] = found + before_ref[:, rows] if follows else found


def project(stack, knot_locs, scale, extent, before=None):
    probes, points, knots = stack.shape[0], stack.shape[1] - 2 * LANES, knot_locs.shape[1]
    out_shape = [
        jax.ShapeDtypeStruct((probes, knots), jnp.float32),
        pltpu.VMEM((knots, points), jnp.bfloat16),
        pltpu.VMEM((knots, points), jnp.bfloat16),
    ]
    if before is None:
        operands = (stack, knot_locs)
        out_shape += [
            jax.ShapeDtypeStruct((knots, 8), jnp.float32),
            jax.ShapeDtypeStruct(stack.shape, jnp.float32),
        ]
    else:
        operands = (stack, before[0], before[3])
    found = pl.pallas_call(
        functools.partial(project_kernel, scale, grain_of(scale * extent), before is not None),
        out_shape=out_shape,
        in_specs=[VMEM] * len(operands),
        out_specs=[VMEM] * len(out_shape),
        scratch_shapes=[pltpu.VMEM((2 * probes, points), jnp.bfloat16)],
        compiler_params=pltpu.CompilerParams(vmem_limit_bytes=LIMIT),
        cost_estimate=cost(2800, points * knots, 2),
        name="project",
    )(*operands)
    return found if before is None else [*found, *before[3:]]


def factor_kernel(scale, step, parts, before_ref, proj_ref, *rest):
    highs, lows, (out_ref, weights) = rest[:parts], rest[parts : 2 * parts], rest[-2:]
    probes, depth = proj_ref.shape
    weights[...] = stacked_halves(proj_ref[...] * scale)
    owner = lax.rem(lax.axis_index("knot") + step, lax.axis_size("knot"))
    deep = pl.ds(pl.multiple_of(owner * depth, depth), depth)
    rows = highs[0].shape[1]
    tile = min(TILE, rows)
    for part, (high_ref, low_ref) in enumerate(zip(highs, lows)):
        for start in range(0, rows, tile):
            here = slice(start, start + tile)
            found = folded(dot_nn(weights[...], high_ref[deep, here]) + dot_nn(weights[...], low_ref[deep, here]))
            target = slice(part * rows + start, part * rows + start + tile)
            if before_ref is not None:
                found = found + before_ref[:, target]
            out_ref[:, target] = found


def factored(before, projection, splits, scale, step):
    probes, depth = projection.shape
    highs, lows = [
        [pltpu.with_memory_space_constraint(split[half], pltpu.VMEM) for split in splits] for half in range(2)
    ]
    rows = sum(high.shape[1] for high in highs)
    kernel = functools.partial(factor_kernel, scale, step, len(splits))
    operands = (projection, *highs, *lows)
    if before is None:
        kernel = functools.partial(kernel, None)
    else:
        operands = (before, *operands)
    return pl.pallas_call(
        kernel,
        out_shape=jax.ShapeDtypeStruct((probes, rows), jnp.float32),
        in_specs=[VMEM] * len(operands),
        out_specs=VMEM,
        scratch_shapes=[pltpu.VMEM((2 * probes, depth), jnp.bfloat16)],
        compiler_params=pltpu.CompilerParams(vmem_limit_bytes=LIMIT),
        cost_estimate=cost(1000, rows * depth),
        name="factor",
    )(*operands)


def spread_kernel(scale, factor_ref, high_ref, low_ref, out_ref):
    points = high_ref.shape[1]
    tile = min(TILE, points)
    weights = stacked_halves(factor_ref[...] * scale)
    for start in range(0, points, tile):
        lanes = slice(start, start + tile)
        out_ref[:, lanes] = folded(dot_nn(weights, high_ref[:, lanes]) + dot_nn(weights, low_ref[:, lanes]))


def spread(factor, high, low, scale):
    (probes, knots), points = factor.shape, high.shape[1]
    high = pltpu.with_memory_space_constraint(high, pltpu.VMEM)
    low = pltpu.with_memory_space_constraint(low, pltpu.VMEM)
    return pl.pallas_call(
        functools.partial(spread_kernel, scale),
        out_shape=jax.ShapeDtypeStruct((probes, points), jnp.float32),
        in_specs=[VMEM, VMEM, VMEM],
        out_specs=VMEM,
        compiler_params=pltpu.CompilerParams(vmem_limit_bytes=LIMIT),
        cost_estimate=cost(850, knots * points),
        name="spread",
    )(factor, high, low)


def covariance(square):
    apart = square * lax.rsqrt(square)
    remain = jnp.maximum(4.0 - apart, 0.0)
    twice = remain * remain
    return (jnp.exp2(apart * (-LOG2E / (COV_RANGE * TAPER_RATE))) * (twice * twice)) * (5.0 - remain)


def beside_kernel(first, first_row, grain, ids_ref, counts_ref, own_ref, values_ref, coords_ref, precision_ref, *rest):
    out_ref, high_ref, low_ref = rest[-3:]
    own_blocks, slots = ids_ref.shape
    block = LANES
    probes = own_ref.shape[0]
    span = own_blocks + 2
    zeros_place = coords_ref.shape[1] // block
    column = lax.axis_index("space")
    north_base = lax.axis_index("knot") * own_blocks - 1
    north_cells = lax.axis_size("knot") * own_blocks
    own_columns = [
        on_grid(jnp.transpose(coordinate_rows(own_ref, own_blocks * block, axis) * TAPER_RATE), grain)
        for axis in range(2)
    ]

    def place(group, slot):
        ahead = ids_ref[group, slot] - (column - 1) * north_cells
        east = jnp.where(ahead >= north_cells, 1, 0) + jnp.where(ahead >= 2 * north_cells, 1, 0)
        strip = jnp.where(east == 1, 0, 2 - lax.rem(column + lax.div(east, 2) + 1, 2))
        index = strip * span + (ahead - east * north_cells - north_base)
        return lanes_of(index), lanes_of(jnp.where(slot < counts_ref[group], index, zeros_place))

    def lanes_of(index):
        return pl.ds(pl.multiple_of(index * block, block), block)

    depth, rows = high_ref.shape
    tile = min(TILE, rows)
    wide = min(TILE, depth)
    tiles = [(start, deep) for start in range(0, rows, tile) for deep in range(0, depth, wide)]
    groups = out_ref.shape[1] // block
    turns = groups * -(-slots // 2)

    for index in range(groups):
        group = first + index
        px, py = [turned[:, group : group + 1] for turned in own_columns]
        total = jnp.zeros((block, 2 * probes), jnp.float32)
        for pair in range(0, slots, 2):
            highs, lows, parts = [], [], []
            for slot in range(pair, min(pair + 2, slots)):
                lanes, value_lanes = place(group, slot)
                dx = px - coords_ref[0:1, lanes]
                dy = py - coords_ref[1:2, lanes]
                high, low = halves(covariance(dx * dx + dy * dy))
                highs.append(high)
                lows.append(low)
                parts.append(values_ref[:, value_lanes])
            part = jnp.concatenate(parts, axis=1)
            total = total + (
                dot_nt(jnp.concatenate(highs, axis=1), part) + dot_nt(jnp.concatenate(lows, axis=1), part)
            )
            turn = index * -(-slots // 2) + pair // 2
            for start, deep in tiles[turn * len(tiles) // turns : (turn + 1) * len(tiles) // turns]:
                from_row = first_row + start
                turned = jnp.transpose(precision_ref[from_row : from_row + tile, deep : deep + wide])
                here = slice(deep, deep + wide), slice(start, start + tile)
                high_ref[here], low_ref[here] = halves(turned)
        out_ref[:, index * block : (index + 1) * block] = (
            TAPER_SCALE * folded_columns(total, probes)
            + NUGGET * own_ref[:, group * block : (group + 1) * block]
        )


def beside_round(ids, counts, own, values, coords, precision, extent, first, blocks, first_row, rows, after):
    slots, depth = ids.shape[1], precision.shape[1]
    return pl.pallas_call(
        functools.partial(beside_kernel, first, first_row, grain_of(TAPER_RATE * extent)),
        out_shape=(
            jax.ShapeDtypeStruct((own.shape[0], blocks * LANES), jnp.float32),
            pltpu.VMEM((depth, rows), jnp.bfloat16),
            pltpu.VMEM((depth, rows), jnp.bfloat16),
        ),
        in_specs=[SMEM, SMEM, VMEM, VMEM, VMEM, VMEM] + [ANY] * len(after),
        out_specs=(VMEM, VMEM, VMEM),
        compiler_params=pltpu.CompilerParams(vmem_limit_bytes=LIMIT),
        cost_estimate=cost(500, blocks * slots * LANES * LANES, 2),
        name="beside",
    )(ids, counts, own, values, coords, precision, *after)


def add_kernel(count, *refs):
    total = refs[0][...]
    for ref in refs[1:count]:
        total = total + ref[...]
    refs[-1][...] = total


def add_all(values, after):
    return pl.pallas_call(
        functools.partial(add_kernel, len(values)),
        out_shape=jax.ShapeDtypeStruct(values[0].shape, jnp.float32),
        in_specs=[VMEM] * len(values) + [ANY] * len(after),
        out_specs=VMEM,
        compiler_params=pltpu.CompilerParams(vmem_limit_bytes=LIMIT),
        name="add",
    )(*values, *after)


def butterfly_rounds(count):
    assert count & (count - 1) == 0
    bits = [1 << i for i in range(count.bit_length() - 1)]
    rounds = [(low | high, high, low) for low, high in zip(bits[0::2], bits[1::2])]
    return [(bit,) for bit in bits[len(rounds) * 2 :]] + rounds[::-1]


def butterfly_round(value, axis, turn):
    count = lax.axis_size(axis)
    return [
        lax.ppermute(value, axis, [(i, i ^ step) for i in range(count)]) for step in butterfly_rounds(count)[turn]
    ]


def shifted(value, axis, step):
    count = lax.axis_size(axis)
    if step % count == 0:
        return value
    return lax.ppermute(value, axis, [((i + step) % count, i) for i in range(count)])


def paired(value, axis, other, first):
    count, groups = lax.axis_size(axis), lax.axis_size(other)
    partner = {}
    for i in range(first, count - 1, 2):
        partner[i], partner[i + 1] = i + 1, i
    pairs = []
    for i in range(count):
        for j in range(groups):
            if i in partner:
                pairs.append((i * groups + j, partner[i] * groups + j))
            elif j ^ 1 < groups:
                pairs.append((i * groups + j, i * groups + (j ^ 1)))
    return lax.ppermute(value, (axis, other), pairs)


def shards(probes, locations, knot_locs, knot_precision, neighbours, counts):
    own_blocks = neighbours.shape[0]
    row_count = probes.shape[1]
    knot_total = knot_precision.shape[1]
    device_count = lax.axis_size(("space", "knot"))
    groups = lax.axis_size("knot")
    knot_range = KNOT_REACH * math.sqrt(own_blocks * device_count / knot_total)
    proj_scale = PROJ_GAIN * math.sqrt(knot_total / (row_count * device_count))

    stack, knots = prepare(probes, locations, knot_locs, own_blocks)
    chunks = [shifted(stack, "knot", step) for step in range(groups)]
    rate = LOG2E / knot_range
    extent = CELL * max(lax.axis_size("space"), groups * own_blocks)
    parts = []
    for chunk in chunks:
        parts.append(project(chunk, knots, rate, extent, parts[-1] if parts else None))
    stack = parts[0][4]

    strip = make_strip(chunks[-1], stack, chunks[1 % groups])
    odd = paired(strip, "space", "knot", 1)
    values, coords = assemble([strip, odd, paired(strip, "space", "knot", 0)], extent)
    projection = parts[-1][0]
    rounds = len(butterfly_rounds(lax.axis_size("space")))
    pieces = math.gcd(math.gcd(own_blocks, rounds), knot_precision.shape[0] // LANES)
    bounds = [own_blocks - own_blocks * i * (i + 2) // (pieces * (pieces + 2)) for i in range(pieces, -1, -1)]
    per_split = knot_precision.shape[0] // pieces
    base, splits = [], []
    for turn in range(rounds):
        got = butterfly_round(projection, "space", turn)
        beside = []
        for i in range(pieces):
            if i * rounds // pieces == turn:
                done = beside_round(
                    neighbours, counts, stack, values, coords, knot_precision, extent,
                    bounds[i], bounds[i + 1] - bounds[i], i * per_split, per_split, [projection],
                )
                base.append(done[0])
                splits.append(done[1:])
                beside.extend(done)
        projection = add_all([projection, *got], beside)
    factor = factored(None, projection, splits, proj_scale, 0)
    for step in range(1, groups):
        factor = factored(factor, shifted(projection, "knot", step), splits, proj_scale, step)
    total = jnp.concatenate(base, axis=1)
    for step in reversed(range(groups)):
        share = spread(factor, parts[step][1], parts[step][2], LOW_SCALE * EXPAND_GAIN)
        total = total + shifted(share, "knot", -step)
    return total


def solution(mesh):
    return jax.shard_map(
        shards,
        mesh=mesh,
        in_specs=(
            P(None, ("space", "knot")),
            P(None, ("space", "knot")),
            P(None, "knot"),
            P("knot", None),
            P(("space", "knot"), None),
            P(("space", "knot")),
        ),
        out_specs=P(None, ("space", "knot")),
        check_vma=False,
    )
```

```python
import functools
import math

import jax
import jax.numpy as jnp
from jax import lax
from jax.experimental import pallas as pl
from jax.experimental.pallas import tpu as pltpu
from jax.sharding import PartitionSpec as P

COV_RANGE = 0.05
TAPER_LEN = 0.15
KNOT_REACH = 0.15
TAPER_SCALE = 0.1
PROJ_GAIN = 0.5
EXPAND_GAIN = 0.5
LOW_SCALE = 0.5
NUGGET = 0.25
LOG2E = math.log2(math.e)
TAPER_RATE = 4.0 / TAPER_LEN
CELL = 0.1
TILE = 256
LANES = 128
HALF_GRAIN = 2.0**-24
LIMIT = 6 * 1024 * 1024
VMEM = pl.BlockSpec(memory_space=pltpu.VMEM)
HBM = pl.BlockSpec(memory_space=pltpu.HBM)
ANY = pl.BlockSpec(memory_space=pl.ANY)
SMEM = pl.BlockSpec(memory_space=pltpu.SMEM)


def halves(x):
    high = x.astype(jnp.bfloat16)
    return high, (x - high.astype(jnp.float32)).astype(jnp.bfloat16)


def stacked_halves(x):
    return jnp.concatenate(halves(x), axis=0)


def folded(x):
    rows = x.shape[0] // 2
    return x[:rows] + x[rows:]


def dot_nt(left, right):
    return lax.dot_general(
        left, right, (((1,), (1,)), ((), ())), preferred_element_type=jnp.float32
    )


def dot_nn(left, right):
    return jnp.dot(left, right, preferred_element_type=jnp.float32)


def folded_columns(x, rows):
    x = jnp.transpose(x)
    return x[:rows] + x[rows : 2 * rows]


def cost(work, pairs, transcendentals=0):
    return pl.CostEstimate(flops=work * pairs, bytes_accessed=4 * pairs, transcendentals=transcendentals * pairs)


def coordinate_rows(ref, points, axis):
    start = points + axis * LANES
    return ref[:, start : start + LANES]


def prepare_kernel(blocks, probes_ref, locations_ref, knots_ref, stack_ref, knots_out_ref, coords, sems):
    points = probes_ref.shape[1]
    block = points // blocks
    copies = [
        pltpu.make_async_copy(probes_ref, stack_ref.at[:, pl.ds(0, points)], sems.at[0]),
        pltpu.make_async_copy(locations_ref, coords, sems.at[1]),
        pltpu.make_async_copy(knots_ref, knots_out_ref, sems.at[2]),
    ]
    for copy in copies:
        copy.start()
    for copy in copies:
        copy.wait()
    stack_ref[:, points:] = jnp.zeros((stack_ref.shape[0], 2 * LANES), jnp.float32)
    for axis in range(2):
        lanes = slice(points + axis * LANES, points + (axis + 1) * LANES)
        for index in range(blocks):
            stack_ref[index : index + 1, lanes] = coords[axis : axis + 1, index * block : (index + 1) * block]


def prepare(probes, locations, knot_locs, blocks):
    rows, points = probes.shape
    assert points == blocks * LANES and blocks + 2 <= rows
    probes, locations, knot_locs = [
        pltpu.with_memory_space_constraint(x, pltpu.HBM) for x in (probes, locations, knot_locs)
    ]
    return pl.pallas_call(
        functools.partial(prepare_kernel, blocks),
        out_shape=(
            jax.ShapeDtypeStruct((rows, points + 2 * LANES), jnp.float32),
            jax.ShapeDtypeStruct(knot_locs.shape, jnp.float32),
        ),
        in_specs=[HBM, HBM, HBM],
        out_specs=(VMEM, VMEM),
        scratch_shapes=[pltpu.VMEM(locations.shape, jnp.float32), pltpu.SemaphoreType.DMA((3,))],
        compiler_params=pltpu.CompilerParams(vmem_limit_bytes=LIMIT),
        name="prepare",
    )(probes, locations, knot_locs)


def strip_kernel(below_ref, own_ref, above_ref, out_ref):
    rows, width = own_ref.shape
    points = width - 2 * LANES
    blocks = points // LANES
    out_ref[:, :LANES] = below_ref[:, points - LANES : points]
    out_ref[:, LANES : points + LANES] = own_ref[:, :points]
    out_ref[:, points + LANES : points + 2 * LANES] = above_ref[:, :LANES]
    for axis in range(2):
        lanes = slice(points + axis * LANES, points + (axis + 1) * LANES)
        target = slice(lanes.start + 2 * LANES, lanes.stop + 2 * LANES)
        out_ref[:, target] = jnp.zeros((rows, LANES), jnp.float32)
        out_ref[0:1, target] = below_ref[blocks - 1 : blocks, lanes]
        out_ref[1 : blocks + 1, target] = own_ref[:blocks, lanes]
        out_ref[blocks + 1 : blocks + 2, target] = above_ref[0:1, lanes]


def make_strip(below, own, above):
    return pl.pallas_call(
        strip_kernel,
        out_shape=jax.ShapeDtypeStruct((own.shape[0], own.shape[1] + 2 * LANES), jnp.float32),
        in_specs=[VMEM, VMEM, VMEM],
        out_specs=VMEM,
        compiler_params=pltpu.CompilerParams(vmem_limit_bytes=LIMIT),
        name="strip",
    )(below, own, above)


def assemble_kernel(grain, own_ref, odd_ref, even_ref, values_ref, coords_ref):
    probes, width = own_ref.shape
    points = width - 2 * LANES
    for turn, ref in enumerate((own_ref, odd_ref, even_ref)):
        start = turn * points
        values_ref[:, start : start + points] = stacked_halves(ref[:, :points] * (1.0 / 256.0))
        for axis in range(2):
            rows = off_grid(coordinate_rows(ref, points, axis) * TAPER_RATE, grain)
            for index in range(points // LANES):
                lanes = slice(start + index * LANES, start + (index + 1) * LANES)
                coords_ref[axis : axis + 1, lanes] = rows[index : index + 1]
    values_ref[:, 3 * points :] = jnp.zeros((2 * probes, LANES), jnp.bfloat16)


def assemble(strips, extent):
    probes, width = strips[0].shape
    near = 3 * (width - 2 * LANES)
    return pl.pallas_call(
        functools.partial(assemble_kernel, grain_of(TAPER_RATE * extent)),
        out_shape=(
            jax.ShapeDtypeStruct((2 * probes, near + LANES), jnp.bfloat16),
            jax.ShapeDtypeStruct((2, near), jnp.float32),
        ),
        in_specs=[VMEM] * 3,
        out_specs=(VMEM, VMEM),
        compiler_params=pltpu.CompilerParams(vmem_limit_bytes=LIMIT),
        name="assemble",
    )(*strips)


def grain_of(bound):
    return 2.0 ** math.ceil(math.log2(1.01 * bound))


def on_grid(x, grain):
    return (x + grain) - grain


def off_grid(x, grain):
    return (x + grain) - (grain - grain * HALF_GRAIN)


def project_kernel(scale, grain, follows, stack_ref, *rest):
    if follows:
        before_ref, columns, out_ref, high_ref, low_ref, weights = rest
    else:
        knots_ref, out_ref, high_ref, low_ref, columns, copy_ref, weights = rest
        copy_ref[...] = stack_ref[...]
    knots, points = high_ref.shape
    probes = stack_ref.shape[0]
    tile = min(TILE, knots)
    weights[...] = stacked_halves(stack_ref[:, :points])
    east, north = [on_grid(coordinate_rows(stack_ref, points, axis) * scale, grain) for axis in range(2)]

    for start in range(0, knots, tile):
        rows = slice(start, start + tile)
        if follows:
            turned = columns[rows, :]
        else:
            fill = jnp.zeros((6, tile), jnp.float32)
            turned = jnp.transpose(jnp.concatenate([off_grid(knots_ref[:, rows] * scale, grain), fill], axis=0))
            columns[rows, :] = turned
        kx, ky = [turned[:, axis : axis + 1] for axis in range(2)]
        for block in range(points // LANES):
            lanes = slice(block * LANES, (block + 1) * LANES)
            dx = east[block : block + 1, :] - kx
            dy = north[block : block + 1, :] - ky
            square = dx * dx + dy * dy
            high_ref[rows, lanes], low_ref[rows, lanes] = halves(jnp.exp2(-(square * lax.rsqrt(square))))
        total = dot_nt(high_ref[rows, :], weights[...]) + dot_nt(low_ref[rows, :], weights[...])
        found = folded_columns(total, probes)
        out_ref[:, rows] = found + before_ref[:, rows] if follows else found


def project(stack, knot_locs, scale, extent, before=None):
    probes, points, knots = stack.shape[0], stack.shape[1] - 2 * LANES, knot_locs.shape[1]
    out_shape = [
        jax.ShapeDtypeStruct((probes, knots), jnp.float32),
        pltpu.VMEM((knots, points), jnp.bfloat16),
        pltpu.VMEM((knots, points), jnp.bfloat16),
    ]
    if before is None:
        operands = (stack, knot_locs)
        out_shape += [
            jax.ShapeDtypeStruct((knots, 8), jnp.float32),
            jax.ShapeDtypeStruct(stack.shape, jnp.float32),
        ]
    else:
        operands = (stack, before[0], before[3])
    found = pl.pallas_call(
        functools.partial(project_kernel, scale, grain_of(scale * extent), before is not None),
        out_shape=out_shape,
        in_specs=[VMEM] * len(operands),
        out_specs=[VMEM] * len(out_shape),
        scratch_shapes=[pltpu.VMEM((2 * probes, points), jnp.bfloat16)],
        compiler_params=pltpu.CompilerParams(vmem_limit_bytes=LIMIT),
        cost_estimate=cost(2800, points * knots, 2),
        name="project",
    )(*operands)
    return found if before is None else [*found, *before[3:]]


def factor_kernel(scale, step, parts, before_ref, proj_ref, *rest):
    highs, lows, (out_ref, weights) = rest[:parts], rest[parts : 2 * parts], rest[-2:]
    probes, depth = proj_ref.shape
    weights[...] = stacked_halves(proj_ref[...] * scale)
    owner = lax.rem(lax.axis_index("knot") + step, lax.axis_size("knot"))
    deep = pl.ds(pl.multiple_of(owner * depth, depth), depth)
    rows = highs[0].shape[1]
    tile = min(TILE, rows)
    for part, (high_ref, low_ref) in enumerate(zip(highs, lows)):
        for start in range(0, rows, tile):
            here = slice(start, start + tile)
            found = folded(dot_nn(weights[...], high_ref[deep, here]) + dot_nn(weights[...], low_ref[deep, here]))
            target = slice(part * rows + start, part * rows + start + tile)
            if before_ref is not None:
                found = found + before_ref[:, target]
            out_ref[:, target] = found


def factored(before, projection, splits, scale, step):
    probes, depth = projection.shape
    highs, lows = [
        [pltpu.with_memory_space_constraint(split[half], pltpu.VMEM) for split in splits] for half in range(2)
    ]
    rows = sum(high.shape[1] for high in highs)
    kernel = functools.partial(factor_kernel, scale, step, len(splits))
    operands = (projection, *highs, *lows)
    if before is None:
        kernel = functools.partial(kernel, None)
    else:
        operands = (before, *operands)
    return pl.pallas_call(
        kernel,
        out_shape=jax.ShapeDtypeStruct((probes, rows), jnp.float32),
        in_specs=[VMEM] * len(operands),
        out_specs=VMEM,
        scratch_shapes=[pltpu.VMEM((2 * probes, depth), jnp.bfloat16)],
        compiler_params=pltpu.CompilerParams(vmem_limit_bytes=LIMIT),
        cost_estimate=cost(1000, rows * depth),
        name="factor",
    )(*operands)


def spread_kernel(scale, factor_ref, high_ref, low_ref, out_ref):
    points = high_ref.shape[1]
    tile = min(TILE, points)
    weights = stacked_halves(factor_ref[...] * scale)
    for start in range(0, points, tile):
        lanes = slice(start, start + tile)
        out_ref[:, lanes] = folded(dot_nn(weights, high_ref[:, lanes]) + dot_nn(weights, low_ref[:, lanes]))


def spread(factor, high, low, scale):
    (probes, knots), points = factor.shape, high.shape[1]
    high = pltpu.with_memory_space_constraint(high, pltpu.VMEM)
    low = pltpu.with_memory_space_constraint(low, pltpu.VMEM)
    return pl.pallas_call(
        functools.partial(spread_kernel, scale),
        out_shape=jax.ShapeDtypeStruct((probes, points), jnp.float32),
        in_specs=[VMEM, VMEM, VMEM],
        out_specs=VMEM,
        compiler_params=pltpu.CompilerParams(vmem_limit_bytes=LIMIT),
        cost_estimate=cost(850, knots * points),
        name="spread",
    )(factor, high, low)


def covariance(square):
    apart = square * lax.rsqrt(square)
    remain = jnp.maximum(4.0 - apart, 0.0)
    twice = remain * remain
    return (jnp.exp2(apart * (-LOG2E / (COV_RANGE * TAPER_RATE))) * (twice * twice)) * (5.0 - remain)


def beside_kernel(first, first_row, grain, ids_ref, counts_ref, own_ref, values_ref, coords_ref, precision_ref, *rest):
    out_ref, high_ref, low_ref = rest[-3:]
    own_blocks, slots = ids_ref.shape
    block = LANES
    probes = own_ref.shape[0]
    span = own_blocks + 2
    zeros_place = coords_ref.shape[1] // block
    column = lax.axis_index("space")
    north_base = lax.axis_index("knot") * own_blocks - 1
    north_cells = lax.axis_size("knot") * own_blocks
    own_columns = [
        on_grid(jnp.transpose(coordinate_rows(own_ref, own_blocks * block, axis) * TAPER_RATE), grain)
        for axis in range(2)
    ]

    def place(group, slot):
        ahead = ids_ref[group, slot] - (column - 1) * north_cells
        east = jnp.where(ahead >= north_cells, 1, 0) + jnp.where(ahead >= 2 * north_cells, 1, 0)
        strip = jnp.where(east == 1, 0, 2 - lax.rem(column + lax.div(east, 2) + 1, 2))
        index = strip * span + (ahead - east * north_cells - north_base)
        return lanes_of(index), lanes_of(jnp.where(slot < counts_ref[group], index, zeros_place))

    def lanes_of(index):
        return pl.ds(pl.multiple_of(index * block, block), block)

    depth, rows = high_ref.shape
    tile = min(TILE, rows)
    wide = min(TILE, depth)
    tiles = [(start, deep) for start in range(0, rows, tile) for deep in range(0, depth, wide)]
    groups = out_ref.shape[1] // block
    turns = groups * -(-slots // 2)

    for index in range(groups):
        group = first + index
        px, py = [turned[:, group : group + 1] for turned in own_columns]
        total = jnp.zeros((block, 2 * probes), jnp.float32)
        for pair in range(0, slots, 2):
            highs, lows, parts = [], [], []
            for slot in range(pair, min(pair + 2, slots)):
                lanes, value_lanes = place(group, slot)
                dx = px - coords_ref[0:1, lanes]
                dy = py - coords_ref[1:2, lanes]
                high, low = halves(covariance(dx * dx + dy * dy))
                highs.append(high)
                lows.append(low)
                parts.append(values_ref[:, value_lanes])
            part = jnp.concatenate(parts, axis=1)
            total = total + (
                dot_nt(jnp.concatenate(highs, axis=1), part) + dot_nt(jnp.concatenate(lows, axis=1), part)
            )
            turn = index * -(-slots // 2) + pair // 2
            for start, deep in tiles[turn * len(tiles) // turns : (turn + 1) * len(tiles) // turns]:
                from_row = first_row + start
                turned = jnp.transpose(precision_ref[from_row : from_row + tile, deep : deep + wide])
                here = slice(deep, deep + wide), slice(start, start + tile)
                high_ref[here], low_ref[here] = halves(turned)
        out_ref[:, index * block : (index + 1) * block] = (
            TAPER_SCALE * folded_columns(total, probes)
            + NUGGET * own_ref[:, group * block : (group + 1) * block]
        )


def beside_round(ids, counts, own, values, coords, precision, extent, first, blocks, first_row, rows, after):
    slots, depth = ids.shape[1], precision.shape[1]
    return pl.pallas_call(
        functools.partial(beside_kernel, first, first_row, grain_of(TAPER_RATE * extent)),
        out_shape=(
            jax.ShapeDtypeStruct((own.shape[0], blocks * LANES), jnp.float32),
            pltpu.VMEM((depth, rows), jnp.bfloat16),
            pltpu.VMEM((depth, rows), jnp.bfloat16),
        ),
        in_specs=[SMEM, SMEM, VMEM, VMEM, VMEM, VMEM] + [ANY] * len(after),
        out_specs=(VMEM, VMEM, VMEM),
        compiler_params=pltpu.CompilerParams(vmem_limit_bytes=LIMIT),
        cost_estimate=cost(500, blocks * slots * LANES * LANES, 2),
        name="beside",
    )(ids, counts, own, values, coords, precision, *after)


def add_kernel(count, *refs):
    total = refs[0][...]
    for ref in refs[1:count]:
        total = total + ref[...]
    refs[-1][...] = total


def add_all(values, after):
    return pl.pallas_call(
        functools.partial(add_kernel, len(values)),
        out_shape=jax.ShapeDtypeStruct(values[0].shape, jnp.float32),
        in_specs=[VMEM] * len(values) + [ANY] * len(after),
        out_specs=VMEM,
        compiler_params=pltpu.CompilerParams(vmem_limit_bytes=LIMIT),
        name="add",
    )(*values, *after)


def butterfly_rounds(count):
    assert count & (count - 1) == 0
    bits = [1 << i for i in range(count.bit_length() - 1)]
    rounds = [(low | high, high, low) for low, high in zip(bits[0::2], bits[1::2])]
    return rounds + [(bit,) for bit in bits[len(rounds) * 2 :]]


def butterfly_round(value, axis, turn):
    count = lax.axis_size(axis)
    return [
        lax.ppermute(value, axis, [(i, i ^ step) for i in range(count)]) for step in butterfly_rounds(count)[turn]
    ]


def shifted(value, axis, step):
    count = lax.axis_size(axis)
    if step % count == 0:
        return value
    return lax.ppermute(value, axis, [((i + step) % count, i) for i in range(count)])


def paired(value, axis, other, first):
    count, groups = lax.axis_size(axis), lax.axis_size(other)
    partner = {}
    for i in range(first, count - 1, 2):
        partner[i], partner[i + 1] = i + 1, i
    pairs = []
    for i in range(count):
        for j in range(groups):
            if i in partner:
                pairs.append((i * groups + j, partner[i] * groups + j))
            elif j ^ 1 < groups:
                pairs.append((i * groups + j, i * groups + (j ^ 1)))
    return lax.ppermute(value, (axis, other), pairs)


def shards(probes, locations, knot_locs, knot_precision, neighbours, counts):
    own_blocks = neighbours.shape[0]
    row_count = probes.shape[1]
    knot_total = knot_precision.shape[1]
    device_count = lax.axis_size(("space", "knot"))
    groups = lax.axis_size("knot")
    knot_range = KNOT_REACH * math.sqrt(own_blocks * device_count / knot_total)
    proj_scale = PROJ_GAIN * math.sqrt(knot_total / (row_count * device_count))

    stack, knots = prepare(probes, locations, knot_locs, own_blocks)
    chunks = [shifted(stack, "knot", step) for step in range(groups)]
    rate = LOG2E / knot_range
    extent = CELL * max(lax.axis_size("space"), groups * own_blocks)
    parts = []
    for chunk in chunks:
        parts.append(project(chunk, knots, rate, extent, parts[-1] if parts else None))
    stack = parts[0][4]

    strip = make_strip(chunks[-1], stack, chunks[1 % groups])
    odd = paired(strip, "space", "knot", 1)
    values, coords = assemble([strip, odd, paired(strip, "space", "knot", 0)], extent)
    projection = parts[-1][0]
    rounds = len(butterfly_rounds(lax.axis_size("space")))
    pieces = math.gcd(math.gcd(own_blocks, rounds), knot_precision.shape[0] // LANES)
    bounds = [own_blocks * i * (i + 2) // (pieces * (pieces + 2)) for i in range(pieces + 1)]
    per_split = knot_precision.shape[0] // pieces
    base, splits = [], []
    for turn in range(rounds):
        got = butterfly_round(projection, "space", turn)
        beside = []
        for i in range(pieces):
            if i * rounds // pieces == turn:
                done = beside_round(
                    neighbours, counts, stack, values, coords, knot_precision, extent,
                    bounds[i], bounds[i + 1] - bounds[i], i * per_split, per_split, [projection],
                )
                base.append(done[0])
                splits.append(done[1:])
                beside.extend(done)
        projection = add_all([projection, *got], beside)
    factor = factored(None, projection, splits, proj_scale, 0)
    for step in range(1, groups):
        factor = factored(factor, shifted(projection, "knot", step), splits, proj_scale, step)
    total = jnp.concatenate(base, axis=1)
    for step in reversed(range(groups)):
        share = spread(factor, parts[step][1], parts[step][2], LOW_SCALE * EXPAND_GAIN)
        total = total + shifted(share, "knot", -step)
    return total


def solution(mesh):
    return jax.shard_map(
        shards,
        mesh=mesh,
        in_specs=(
            P(None, ("space", "knot")),
            P(None, ("space", "knot")),
            P(None, "knot"),
            P("knot", None),
            P(("space", "knot"), None),
            P(("space", "knot")),
        ),
        out_specs=P(None, ("space", "knot")),
        check_vma=False,
    )
```

```python
import functools
import math

import jax
import jax.numpy as jnp
from jax import lax
from jax.experimental import pallas as pl
from jax.experimental.pallas import tpu as pltpu
from jax.sharding import PartitionSpec as P

COV_RANGE = 0.05
TAPER_LEN = 0.15
KNOT_REACH = 0.15
TAPER_SCALE = 0.1
PROJ_GAIN = 0.5
EXPAND_GAIN = 0.5
LOW_SCALE = 0.5
NUGGET = 0.25
LOG2E = math.log2(math.e)
TAPER_RATE = 4.0 / TAPER_LEN
CELL = 0.1
TILE = 256
LANES = 128
HALF_GRAIN = 2.0**-24
LIMIT = 6 * 1024 * 1024
VMEM = pl.BlockSpec(memory_space=pltpu.VMEM)
HBM = pl.BlockSpec(memory_space=pltpu.HBM)
ANY = pl.BlockSpec(memory_space=pl.ANY)
SMEM = pl.BlockSpec(memory_space=pltpu.SMEM)


def halves(x):
    high = x.astype(jnp.bfloat16)
    return high, (x - high.astype(jnp.float32)).astype(jnp.bfloat16)


def stacked_halves(x):
    return jnp.concatenate(halves(x), axis=0)


def folded(x):
    rows = x.shape[0] // 2
    return x[:rows] + x[rows:]


def dot_nt(left, right):
    return lax.dot_general(
        left, right, (((1,), (1,)), ((), ())), preferred_element_type=jnp.float32
    )


def dot_nn(left, right):
    return jnp.dot(left, right, preferred_element_type=jnp.float32)


def folded_columns(x, rows):
    x = jnp.transpose(x)
    return x[:rows] + x[rows : 2 * rows]


def cost(work, pairs, transcendentals=0):
    return pl.CostEstimate(flops=work * pairs, bytes_accessed=4 * pairs, transcendentals=transcendentals * pairs)


def coordinate_rows(ref, points, axis):
    start = points + axis * LANES
    return ref[:, start : start + LANES]


def prepare_kernel(blocks, probes_ref, locations_ref, knots_ref, stack_ref, knots_out_ref, coords, sems):
    points = probes_ref.shape[1]
    block = points // blocks
    copies = [
        pltpu.make_async_copy(probes_ref, stack_ref.at[:, pl.ds(0, points)], sems.at[0]),
        pltpu.make_async_copy(locations_ref, coords, sems.at[1]),
        pltpu.make_async_copy(knots_ref, knots_out_ref, sems.at[2]),
    ]
    for copy in copies:
        copy.start()
    for copy in copies:
        copy.wait()
    stack_ref[:, points:] = jnp.zeros((stack_ref.shape[0], 2 * LANES), jnp.float32)
    for axis in range(2):
        lanes = slice(points + axis * LANES, points + (axis + 1) * LANES)
        for index in range(blocks):
            stack_ref[index : index + 1, lanes] = coords[axis : axis + 1, index * block : (index + 1) * block]


def prepare(probes, locations, knot_locs, blocks):
    rows, points = probes.shape
    assert points == blocks * LANES and blocks + 2 <= rows
    probes, locations, knot_locs = [
        pltpu.with_memory_space_constraint(x, pltpu.HBM) for x in (probes, locations, knot_locs)
    ]
    return pl.pallas_call(
        functools.partial(prepare_kernel, blocks),
        out_shape=(
            jax.ShapeDtypeStruct((rows, points + 2 * LANES), jnp.float32),
            jax.ShapeDtypeStruct(knot_locs.shape, jnp.float32),
        ),
        in_specs=[HBM, HBM, HBM],
        out_specs=(VMEM, VMEM),
        scratch_shapes=[pltpu.VMEM(locations.shape, jnp.float32), pltpu.SemaphoreType.DMA((3,))],
        compiler_params=pltpu.CompilerParams(vmem_limit_bytes=LIMIT),
        name="prepare",
    )(probes, locations, knot_locs)


def strip_kernel(below_ref, own_ref, above_ref, out_ref):
    rows, width = own_ref.shape
    points = width - 2 * LANES
    blocks = points // LANES
    out_ref[:, :LANES] = below_ref[:, points - LANES : points]
    out_ref[:, LANES : points + LANES] = own_ref[:, :points]
    out_ref[:, points + LANES : points + 2 * LANES] = above_ref[:, :LANES]
    for axis in range(2):
        lanes = slice(points + axis * LANES, points + (axis + 1) * LANES)
        target = slice(lanes.start + 2 * LANES, lanes.stop + 2 * LANES)
        out_ref[:, target] = jnp.zeros((rows, LANES), jnp.float32)
        out_ref[0:1, target] = below_ref[blocks - 1 : blocks, lanes]
        out_ref[1 : blocks + 1, target] = own_ref[:blocks, lanes]
        out_ref[blocks + 1 : blocks + 2, target] = above_ref[0:1, lanes]


def make_strip(below, own, above):
    return pl.pallas_call(
        strip_kernel,
        out_shape=jax.ShapeDtypeStruct((own.shape[0], own.shape[1] + 2 * LANES), jnp.float32),
        in_specs=[VMEM, VMEM, VMEM],
        out_specs=VMEM,
        compiler_params=pltpu.CompilerParams(vmem_limit_bytes=LIMIT),
        name="strip",
    )(below, own, above)


def assemble_kernel(grain, own_ref, odd_ref, even_ref, values_ref, coords_ref):
    probes, width = own_ref.shape
    points = width - 2 * LANES
    for turn, ref in enumerate((own_ref, odd_ref, even_ref)):
        start = turn * points
        values_ref[:, start : start + points] = stacked_halves(ref[:, :points] * (1.0 / 256.0))
        for axis in range(2):
            rows = off_grid(coordinate_rows(ref, points, axis) * TAPER_RATE, grain)
            for index in range(points // LANES):
                lanes = slice(start + index * LANES, start + (index + 1) * LANES)
                coords_ref[axis : axis + 1, lanes] = rows[index : index + 1]
    values_ref[:, 3 * points :] = jnp.zeros((2 * probes, LANES), jnp.bfloat16)


def assemble(strips, extent):
    probes, width = strips[0].shape
    near = 3 * (width - 2 * LANES)
    return pl.pallas_call(
        functools.partial(assemble_kernel, grain_of(TAPER_RATE * extent)),
        out_shape=(
            jax.ShapeDtypeStruct((2 * probes, near + LANES), jnp.bfloat16),
            jax.ShapeDtypeStruct((2, near), jnp.float32),
        ),
        in_specs=[VMEM] * 3,
        out_specs=(VMEM, VMEM),
        compiler_params=pltpu.CompilerParams(vmem_limit_bytes=LIMIT),
        name="assemble",
    )(*strips)


def grain_of(bound):
    return 2.0 ** math.ceil(math.log2(1.01 * bound))


def on_grid(x, grain):
    return (x + grain) - grain


def off_grid(x, grain):
    return (x + grain) - (grain - grain * HALF_GRAIN)


def project_kernel(scale, grain, follows, stack_ref, *rest):
    if follows:
        before_ref, columns, out_ref, high_ref, low_ref, weights = rest
    else:
        knots_ref, out_ref, high_ref, low_ref, columns, copy_ref, weights = rest
        copy_ref[...] = stack_ref[...]
    knots, points = high_ref.shape
    probes = stack_ref.shape[0]
    tile = min(TILE, knots)
    weights[...] = stacked_halves(stack_ref[:, :points])
    east, north = [on_grid(coordinate_rows(stack_ref, points, axis) * scale, grain) for axis in range(2)]

    for start in range(0, knots, tile):
        rows = slice(start, start + tile)
        if follows:
            turned = columns[rows, :]
        else:
            fill = jnp.zeros((6, tile), jnp.float32)
            turned = jnp.transpose(jnp.concatenate([off_grid(knots_ref[:, rows] * scale, grain), fill], axis=0))
            columns[rows, :] = turned
        kx, ky = [turned[:, axis : axis + 1] for axis in range(2)]
        for block in range(points // LANES):
            lanes = slice(block * LANES, (block + 1) * LANES)
            dx = east[block : block + 1, :] - kx
            dy = north[block : block + 1, :] - ky
            square = dx * dx + dy * dy
            high_ref[rows, lanes], low_ref[rows, lanes] = halves(jnp.exp2(-(square * lax.rsqrt(square))))
        total = dot_nt(high_ref[rows, :], weights[...]) + dot_nt(low_ref[rows, :], weights[...])
        found = folded_columns(total, probes)
        out_ref[:, rows] = found + before_ref[:, rows] if follows else found


def project(stack, knot_locs, scale, extent, before=None):
    probes, points, knots = stack.shape[0], stack.shape[1] - 2 * LANES, knot_locs.shape[1]
    out_shape = [
        jax.ShapeDtypeStruct((probes, knots), jnp.float32),
        pltpu.VMEM((knots, points), jnp.bfloat16),
        pltpu.VMEM((knots, points), jnp.bfloat16),
    ]
    if before is None:
        operands = (stack, knot_locs)
        out_shape += [
            jax.ShapeDtypeStruct((knots, 8), jnp.float32),
            jax.ShapeDtypeStruct(stack.shape, jnp.float32),
        ]
    else:
        operands = (stack, before[0], before[3])
    found = pl.pallas_call(
        functools.partial(project_kernel, scale, grain_of(scale * extent), before is not None),
        out_shape=out_shape,
        in_specs=[VMEM] * len(operands),
        out_specs=[VMEM] * len(out_shape),
        scratch_shapes=[pltpu.VMEM((2 * probes, points), jnp.bfloat16)],
        compiler_params=pltpu.CompilerParams(vmem_limit_bytes=LIMIT),
        cost_estimate=cost(2800, points * knots, 2),
        name="project",
    )(*operands)
    return found if before is None else [*found, *before[3:]]


def factor_kernel(scale, step, parts, before_ref, proj_ref, *rest):
    highs, lows, (out_ref, weights) = rest[:parts], rest[parts : 2 * parts], rest[-2:]
    probes, depth = proj_ref.shape
    weights[...] = stacked_halves(proj_ref[...] * scale)
    owner = lax.rem(lax.axis_index("knot") + step, lax.axis_size("knot"))
    deep = pl.ds(pl.multiple_of(owner * depth, depth), depth)
    rows = highs[0].shape[1]
    tile = min(TILE, rows)
    for part, (high_ref, low_ref) in enumerate(zip(highs, lows)):
        for start in range(0, rows, tile):
            here = slice(start, start + tile)
            found = folded(dot_nn(weights[...], high_ref[deep, here]) + dot_nn(weights[...], low_ref[deep, here]))
            target = slice(part * rows + start, part * rows + start + tile)
            if before_ref is not None:
                found = found + before_ref[:, target]
            out_ref[:, target] = found


def factored(before, projection, splits, scale, step):
    probes, depth = projection.shape
    highs, lows = [
        [pltpu.with_memory_space_constraint(split[half], pltpu.VMEM) for split in splits] for half in range(2)
    ]
    rows = sum(high.shape[1] for high in highs)
    kernel = functools.partial(factor_kernel, scale, step, len(splits))
    operands = (projection, *highs, *lows)
    if before is None:
        kernel = functools.partial(kernel, None)
    else:
        operands = (before, *operands)
    return pl.pallas_call(
        kernel,
        out_shape=jax.ShapeDtypeStruct((probes, rows), jnp.float32),
        in_specs=[VMEM] * len(operands),
        out_specs=VMEM,
        scratch_shapes=[pltpu.VMEM((2 * probes, depth), jnp.bfloat16)],
        compiler_params=pltpu.CompilerParams(vmem_limit_bytes=LIMIT),
        cost_estimate=cost(1000, rows * depth),
        name="factor",
    )(*operands)


def spread_kernel(scale, factor_ref, high_ref, low_ref, out_ref):
    points = high_ref.shape[1]
    tile = min(TILE, points)
    weights = stacked_halves(factor_ref[...] * scale)
    for start in range(0, points, tile):
        lanes = slice(start, start + tile)
        out_ref[:, lanes] = folded(dot_nn(weights, high_ref[:, lanes]) + dot_nn(weights, low_ref[:, lanes]))


def spread(factor, high, low, scale):
    (probes, knots), points = factor.shape, high.shape[1]
    high = pltpu.with_memory_space_constraint(high, pltpu.VMEM)
    low = pltpu.with_memory_space_constraint(low, pltpu.VMEM)
    return pl.pallas_call(
        functools.partial(spread_kernel, scale),
        out_shape=jax.ShapeDtypeStruct((probes, points), jnp.float32),
        in_specs=[VMEM, VMEM, VMEM],
        out_specs=VMEM,
        compiler_params=pltpu.CompilerParams(vmem_limit_bytes=LIMIT),
        cost_estimate=cost(850, knots * points),
        name="spread",
    )(factor, high, low)


def covariance(square):
    apart = square * lax.rsqrt(square)
    remain = jnp.maximum(4.0 - apart, 0.0)
    twice = remain * remain
    return (jnp.exp2(apart * (-LOG2E / (COV_RANGE * TAPER_RATE))) * (twice * twice)) * (5.0 - remain)


def beside_kernel(first, first_row, grain, ids_ref, counts_ref, own_ref, values_ref, coords_ref, precision_ref, *rest):
    out_ref, high_ref, low_ref = rest[-3:]
    own_blocks, slots = ids_ref.shape
    block = LANES
    probes = own_ref.shape[0]
    span = own_blocks + 2
    zeros_place = coords_ref.shape[1] // block
    column = lax.axis_index("space")
    north_base = lax.axis_index("knot") * own_blocks - 1
    north_cells = lax.axis_size("knot") * own_blocks
    own_columns = [
        on_grid(jnp.transpose(coordinate_rows(own_ref, own_blocks * block, axis) * TAPER_RATE), grain)
        for axis in range(2)
    ]

    def place(group, slot):
        ahead = ids_ref[group, slot] - (column - 1) * north_cells
        east = jnp.where(ahead >= north_cells, 1, 0) + jnp.where(ahead >= 2 * north_cells, 1, 0)
        strip = jnp.where(east == 1, 0, 2 - lax.rem(column + lax.div(east, 2) + 1, 2))
        index = strip * span + (ahead - east * north_cells - north_base)
        return lanes_of(index), lanes_of(jnp.where(slot < counts_ref[group], index, zeros_place))

    def lanes_of(index):
        return pl.ds(pl.multiple_of(index * block, block), block)

    depth, rows = high_ref.shape
    tile = min(TILE, rows)
    wide = min(TILE, depth)
    tiles = [(start, deep) for start in range(0, rows, tile) for deep in range(0, depth, wide)]
    groups = out_ref.shape[1] // block
    turns = groups * -(-slots // 2)

    for index in range(groups):
        group = first + index
        px, py = [turned[:, group : group + 1] for turned in own_columns]
        total = jnp.zeros((block, 2 * probes), jnp.float32)
        for pair in range(0, slots, 2):
            highs, lows, parts = [], [], []
            for slot in range(pair, min(pair + 2, slots)):
                lanes, value_lanes = place(group, slot)
                dx = px - coords_ref[0:1, lanes]
                dy = py - coords_ref[1:2, lanes]
                high, low = halves(covariance(dx * dx + dy * dy))
                highs.append(high)
                lows.append(low)
                parts.append(values_ref[:, value_lanes])
            part = jnp.concatenate(parts, axis=1)
            total = total + (
                dot_nt(jnp.concatenate(highs, axis=1), part) + dot_nt(jnp.concatenate(lows, axis=1), part)
            )
            turn = index * -(-slots // 2) + pair // 2
            for start, deep in tiles[turn * len(tiles) // turns : (turn + 1) * len(tiles) // turns]:
                from_row = first_row + start
                turned = jnp.transpose(precision_ref[from_row : from_row + tile, deep : deep + wide])
                here = slice(deep, deep + wide), slice(start, start + tile)
                high_ref[here], low_ref[here] = halves(turned)
        out_ref[:, index * block : (index + 1) * block] = (
            TAPER_SCALE * folded_columns(total, probes)
            + NUGGET * own_ref[:, group * block : (group + 1) * block]
        )


def beside_round(ids, counts, own, values, coords, precision, extent, first, blocks, first_row, rows, after):
    slots, depth = ids.shape[1], precision.shape[1]
    return pl.pallas_call(
        functools.partial(beside_kernel, first, first_row, grain_of(TAPER_RATE * extent)),
        out_shape=(
            jax.ShapeDtypeStruct((own.shape[0], blocks * LANES), jnp.float32),
            pltpu.VMEM((depth, rows), jnp.bfloat16),
            pltpu.VMEM((depth, rows), jnp.bfloat16),
        ),
        in_specs=[SMEM, SMEM, VMEM, VMEM, VMEM, VMEM] + [ANY] * len(after),
        out_specs=(VMEM, VMEM, VMEM),
        compiler_params=pltpu.CompilerParams(vmem_limit_bytes=LIMIT),
        cost_estimate=cost(500, blocks * slots * LANES * LANES, 2),
        name="beside",
    )(ids, counts, own, values, coords, precision, *after)


def add_kernel(count, *refs):
    total = refs[0][...]
    for ref in refs[1:count]:
        total = total + ref[...]
    refs[-1][...] = total


def add_all(values, after):
    return pl.pallas_call(
        functools.partial(add_kernel, len(values)),
        out_shape=jax.ShapeDtypeStruct(values[0].shape, jnp.float32),
        in_specs=[VMEM] * len(values) + [ANY] * len(after),
        out_specs=VMEM,
        compiler_params=pltpu.CompilerParams(vmem_limit_bytes=LIMIT),
        name="add",
    )(*values, *after)


def butterfly_rounds(count):
    assert count & (count - 1) == 0
    bits = [1 << i for i in range(count.bit_length() - 1)]
    rounds = [(low | high, high, low) for low, high in zip(bits[0::2], bits[1::2])]
    rounds[:1] = [(high, both, low) for both, high, low in rounds[:1]]
    return rounds + [(bit,) for bit in bits[len(rounds) * 2 :]]


def butterfly_round(value, axis, turn):
    count = lax.axis_size(axis)
    return [
        lax.ppermute(value, axis, [(i, i ^ step) for i in range(count)]) for step in butterfly_rounds(count)[turn]
    ]


def shifted(value, axis, step):
    count = lax.axis_size(axis)
    if step % count == 0:
        return value
    return lax.ppermute(value, axis, [((i + step) % count, i) for i in range(count)])


def paired(value, axis, other, first):
    count, groups = lax.axis_size(axis), lax.axis_size(other)
    partner = {}
    for i in range(first, count - 1, 2):
        partner[i], partner[i + 1] = i + 1, i
    pairs = []
    for i in range(count):
        for j in range(groups):
            if i in partner:
                pairs.append((i * groups + j, partner[i] * groups + j))
            elif j ^ 1 < groups:
                pairs.append((i * groups + j, i * groups + (j ^ 1)))
    return lax.ppermute(value, (axis, other), pairs)


def shards(probes, locations, knot_locs, knot_precision, neighbours, counts):
    own_blocks = neighbours.shape[0]
    row_count = probes.shape[1]
    knot_total = knot_precision.shape[1]
    device_count = lax.axis_size(("space", "knot"))
    groups = lax.axis_size("knot")
    knot_range = KNOT_REACH * math.sqrt(own_blocks * device_count / knot_total)
    proj_scale = PROJ_GAIN * math.sqrt(knot_total / (row_count * device_count))

    stack, knots = prepare(probes, locations, knot_locs, own_blocks)
    chunks = [shifted(stack, "knot", step) for step in range(groups)]
    rate = LOG2E / knot_range
    extent = CELL * max(lax.axis_size("space"), groups * own_blocks)
    parts = []
    for chunk in chunks:
        parts.append(project(chunk, knots, rate, extent, parts[-1] if parts else None))
    stack = parts[0][4]

    strip = make_strip(chunks[-1], stack, chunks[1 % groups])
    odd = paired(strip, "space", "knot", 1)
    values, coords = assemble([strip, odd, paired(strip, "space", "knot", 0)], extent)
    projection = parts[-1][0]
    rounds = len(butterfly_rounds(lax.axis_size("space")))
    pieces = math.gcd(math.gcd(own_blocks, rounds), knot_precision.shape[0] // LANES)
    bounds = [own_blocks * i * (i + 2) // (pieces * (pieces + 2)) for i in range(pieces + 1)]
    per_split = knot_precision.shape[0] // pieces
    base, splits = [], []
    for turn in range(rounds):
        got = butterfly_round(projection, "space", turn)
        beside = []
        for i in range(pieces):
            if i * rounds // pieces == turn:
                done = beside_round(
                    neighbours, counts, stack, values, coords, knot_precision, extent,
                    bounds[i], bounds[i + 1] - bounds[i], i * per_split, per_split, [projection],
                )
                base.append(done[0])
                splits.append(done[1:])
                beside.extend(done)
        projection = add_all([projection, *got], beside)
    factor = factored(None, projection, splits, proj_scale, 0)
    for step in range(1, groups):
        factor = factored(factor, shifted(projection, "knot", step), splits, proj_scale, step)
    total = jnp.concatenate(base, axis=1)
    for step in reversed(range(groups)):
        share = spread(factor, parts[step][1], parts[step][2], LOW_SCALE * EXPAND_GAIN)
        total = total + shifted(share, "knot", -step)
    return total


def solution(mesh):
    return jax.shard_map(
        shards,
        mesh=mesh,
        in_specs=(
            P(None, ("space", "knot")),
            P(None, ("space", "knot")),
            P(None, "knot"),
            P("knot", None),
            P(("space", "knot"), None),
            P(("space", "knot")),
        ),
        out_specs=P(None, ("space", "knot")),
        check_vma=False,
    )
```

```python
import functools
import math

import jax
import jax.numpy as jnp
from jax import lax
from jax.experimental import pallas as pl
from jax.experimental.pallas import tpu as pltpu
from jax.sharding import PartitionSpec as P

COV_RANGE = 0.05
TAPER_LEN = 0.15
KNOT_REACH = 0.15
TAPER_SCALE = 0.1
PROJ_GAIN = 0.5
EXPAND_GAIN = 0.5
LOW_SCALE = 0.5
NUGGET = 0.25
LOG2E = math.log2(math.e)
TAPER_RATE = 4.0 / TAPER_LEN
CELL = 0.1
TILE = 256
LANES = 128
HALF_GRAIN = 2.0**-24
LIMIT = 6 * 1024 * 1024
VMEM = pl.BlockSpec(memory_space=pltpu.VMEM)
HBM = pl.BlockSpec(memory_space=pltpu.HBM)
ANY = pl.BlockSpec(memory_space=pl.ANY)
SMEM = pl.BlockSpec(memory_space=pltpu.SMEM)


def halves(x):
    high = x.astype(jnp.bfloat16)
    return high, (x - high.astype(jnp.float32)).astype(jnp.bfloat16)


def stacked_halves(x):
    return jnp.concatenate(halves(x), axis=0)


def folded(x):
    rows = x.shape[0] // 2
    return x[:rows] + x[rows:]


def dot_nt(left, right):
    return lax.dot_general(
        left, right, (((1,), (1,)), ((), ())), preferred_element_type=jnp.float32
    )


def dot_nn(left, right):
    return jnp.dot(left, right, preferred_element_type=jnp.float32)


def folded_columns(x, rows):
    x = jnp.transpose(x)
    return x[:rows] + x[rows : 2 * rows]


def cost(work, pairs, transcendentals=0):
    return pl.CostEstimate(flops=work * pairs, bytes_accessed=4 * pairs, transcendentals=transcendentals * pairs)


def coordinate_rows(ref, points, axis):
    start = points + axis * LANES
    return ref[:, start : start + LANES]


def prepare_kernel(blocks, probes_ref, locations_ref, knots_ref, stack_ref, knots_out_ref, coords, sems):
    points = probes_ref.shape[1]
    block = points // blocks
    copies = [
        pltpu.make_async_copy(probes_ref, stack_ref.at[:, pl.ds(0, points)], sems.at[0]),
        pltpu.make_async_copy(locations_ref, coords, sems.at[1]),
        pltpu.make_async_copy(knots_ref, knots_out_ref, sems.at[2]),
    ]
    for copy in copies:
        copy.start()
    for copy in copies:
        copy.wait()
    stack_ref[:, points:] = jnp.zeros((stack_ref.shape[0], 2 * LANES), jnp.float32)
    for axis in range(2):
        lanes = slice(points + axis * LANES, points + (axis + 1) * LANES)
        for index in range(blocks):
            stack_ref[index : index + 1, lanes] = coords[axis : axis + 1, index * block : (index + 1) * block]


def prepare(probes, locations, knot_locs, blocks):
    rows, points = probes.shape
    assert points == blocks * LANES and blocks + 2 <= rows
    probes, locations, knot_locs = [
        pltpu.with_memory_space_constraint(x, pltpu.HBM) for x in (probes, locations, knot_locs)
    ]
    return pl.pallas_call(
        functools.partial(prepare_kernel, blocks),
        out_shape=(
            jax.ShapeDtypeStruct((rows, points + 2 * LANES), jnp.float32),
            jax.ShapeDtypeStruct(knot_locs.shape, jnp.float32),
        ),
        in_specs=[HBM, HBM, HBM],
        out_specs=(VMEM, VMEM),
        scratch_shapes=[pltpu.VMEM(locations.shape, jnp.float32), pltpu.SemaphoreType.DMA((3,))],
        compiler_params=pltpu.CompilerParams(vmem_limit_bytes=LIMIT),
        name="prepare",
    )(probes, locations, knot_locs)


def strip_kernel(below_ref, own_ref, above_ref, out_ref):
    rows, width = own_ref.shape
    points = width - 2 * LANES
    blocks = points // LANES
    out_ref[:, :LANES] = below_ref[:, points - LANES : points]
    out_ref[:, LANES : points + LANES] = own_ref[:, :points]
    out_ref[:, points + LANES : points + 2 * LANES] = above_ref[:, :LANES]
    for axis in range(2):
        lanes = slice(points + axis * LANES, points + (axis + 1) * LANES)
        target = slice(lanes.start + 2 * LANES, lanes.stop + 2 * LANES)
        out_ref[:, target] = jnp.zeros((rows, LANES), jnp.float32)
        out_ref[0:1, target] = below_ref[blocks - 1 : blocks, lanes]
        out_ref[1 : blocks + 1, target] = own_ref[:blocks, lanes]
        out_ref[blocks + 1 : blocks + 2, target] = above_ref[0:1, lanes]


def make_strip(below, own, above):
    return pl.pallas_call(
        strip_kernel,
        out_shape=jax.ShapeDtypeStruct((own.shape[0], own.shape[1] + 2 * LANES), jnp.float32),
        in_specs=[VMEM, VMEM, VMEM],
        out_specs=VMEM,
        compiler_params=pltpu.CompilerParams(vmem_limit_bytes=LIMIT),
        name="strip",
    )(below, own, above)


def assemble_kernel(grain, own_ref, odd_ref, even_ref, values_ref, coords_ref):
    probes, width = own_ref.shape
    points = width - 2 * LANES
    for turn, ref in enumerate((own_ref, odd_ref, even_ref)):
        start = turn * points
        values_ref[:, start : start + points] = stacked_halves(ref[:, :points] * (1.0 / 256.0))
        for axis in range(2):
            rows = off_grid(coordinate_rows(ref, points, axis) * TAPER_RATE, grain)
            for index in range(points // LANES):
                lanes = slice(start + index * LANES, start + (index + 1) * LANES)
                coords_ref[axis : axis + 1, lanes] = rows[index : index + 1]
    values_ref[:, 3 * points :] = jnp.zeros((2 * probes, LANES), jnp.bfloat16)


def assemble(strips, extent):
    probes, width = strips[0].shape
    near = 3 * (width - 2 * LANES)
    return pl.pallas_call(
        functools.partial(assemble_kernel, grain_of(TAPER_RATE * extent)),
        out_shape=(
            jax.ShapeDtypeStruct((2 * probes, near + LANES), jnp.bfloat16),
            jax.ShapeDtypeStruct((2, near), jnp.float32),
        ),
        in_specs=[VMEM] * 3,
        out_specs=(VMEM, VMEM),
        compiler_params=pltpu.CompilerParams(vmem_limit_bytes=LIMIT),
        name="assemble",
    )(*strips)


def grain_of(bound):
    return 2.0 ** math.ceil(math.log2(1.01 * bound))


def on_grid(x, grain):
    return (x + grain) - grain


def off_grid(x, grain):
    return (x + grain) - (grain - grain * HALF_GRAIN)


def project_kernel(scale, grain, follows, stack_ref, *rest):
    if follows:
        before_ref, columns, out_ref, high_ref, low_ref, weights = rest
    else:
        knots_ref, out_ref, high_ref, low_ref, columns, copy_ref, weights = rest
        copy_ref[...] = stack_ref[...]
    knots, points = high_ref.shape
    probes = stack_ref.shape[0]
    tile = min(TILE, knots)
    weights[...] = stacked_halves(stack_ref[:, :points])
    east, north = [on_grid(coordinate_rows(stack_ref, points, axis) * scale, grain) for axis in range(2)]

    for start in range(0, knots, tile):
        rows = slice(start, start + tile)
        if follows:
            turned = columns[rows, :]
        else:
            fill = jnp.zeros((6, tile), jnp.float32)
            turned = jnp.transpose(jnp.concatenate([off_grid(knots_ref[:, rows] * scale, grain), fill], axis=0))
            columns[rows, :] = turned
        kx, ky = [turned[:, axis : axis + 1] for axis in range(2)]
        for block in range(points // LANES):
            lanes = slice(block * LANES, (block + 1) * LANES)
            dx = east[block : block + 1, :] - kx
            dy = north[block : block + 1, :] - ky
            square = dx * dx + dy * dy
            high_ref[rows, lanes], low_ref[rows, lanes] = halves(jnp.exp2(-(square * lax.rsqrt(square))))
        total = dot_nt(high_ref[rows, :], weights[...]) + dot_nt(low_ref[rows, :], weights[...])
        found = folded_columns(total, probes)
        out_ref[:, rows] = found + before_ref[:, rows] if follows else found


def project(stack, knot_locs, scale, extent, before=None):
    probes, points, knots = stack.shape[0], stack.shape[1] - 2 * LANES, knot_locs.shape[1]
    out_shape = [
        jax.ShapeDtypeStruct((probes, knots), jnp.float32),
        pltpu.VMEM((knots, points), jnp.bfloat16),
        pltpu.VMEM((knots, points), jnp.bfloat16),
    ]
    if before is None:
        operands = (stack, knot_locs)
        out_shape += [
            jax.ShapeDtypeStruct((knots, 8), jnp.float32),
            jax.ShapeDtypeStruct(stack.shape, jnp.float32),
        ]
    else:
        operands = (stack, before[0], before[3])
    found = pl.pallas_call(
        functools.partial(project_kernel, scale, grain_of(scale * extent), before is not None),
        out_shape=out_shape,
        in_specs=[VMEM] * len(operands),
        out_specs=[VMEM] * len(out_shape),
        scratch_shapes=[pltpu.VMEM((2 * probes, points), jnp.bfloat16)],
        compiler_params=pltpu.CompilerParams(vmem_limit_bytes=LIMIT),
        cost_estimate=cost(2800, points * knots, 2),
        name="project",
    )(*operands)
    return found if before is None else [*found, *before[3:]]


def factor_kernel(scale, step, parts, before_ref, proj_ref, *rest):
    highs, lows, (out_ref, weights) = rest[:parts], rest[parts : 2 * parts], rest[-2:]
    probes, depth = proj_ref.shape
    weights[...] = stacked_halves(proj_ref[...] * scale)
    owner = lax.rem(lax.axis_index("knot") + step, lax.axis_size("knot"))
    deep = pl.ds(pl.multiple_of(owner * depth, depth), depth)
    rows = highs[0].shape[1]
    tile = min(TILE, rows)
    for part, (high_ref, low_ref) in enumerate(zip(highs, lows)):
        for start in range(0, rows, tile):
            here = slice(start, start + tile)
            found = folded(dot_nn(weights[...], high_ref[deep, here]) + dot_nn(weights[...], low_ref[deep, here]))
            target = slice(part * rows + start, part * rows + start + tile)
            if before_ref is not None:
                found = found + before_ref[:, target]
            out_ref[:, target] = found


def factored(before, projection, splits, scale, step):
    probes, depth = projection.shape
    highs, lows = [
        [pltpu.with_memory_space_constraint(split[half], pltpu.VMEM) for split in splits] for half in range(2)
    ]
    rows = sum(high.shape[1] for high in highs)
    kernel = functools.partial(factor_kernel, scale, step, len(splits))
    operands = (projection, *highs, *lows)
    if before is None:
        kernel = functools.partial(kernel, None)
    else:
        operands = (before, *operands)
    return pl.pallas_call(
        kernel,
        out_shape=jax.ShapeDtypeStruct((probes, rows), jnp.float32),
        in_specs=[VMEM] * len(operands),
        out_specs=VMEM,
        scratch_shapes=[pltpu.VMEM((2 * probes, depth), jnp.bfloat16)],
        compiler_params=pltpu.CompilerParams(vmem_limit_bytes=LIMIT),
        cost_estimate=cost(1000, rows * depth),
        name="factor",
    )(*operands)


def spread_kernel(scale, factor_ref, high_ref, low_ref, *rest):
    *base, out_ref = rest
    points = high_ref.shape[1]
    tile = min(TILE, points)
    weights = stacked_halves(factor_ref[...] * scale)
    for start in range(0, points, tile):
        lanes = slice(start, start + tile)
        out_ref[:, lanes] = folded(dot_nn(weights, high_ref[:, lanes]) + dot_nn(weights, low_ref[:, lanes]))
    start = 0
    for ref in base:
        lanes = slice(start, start + ref.shape[1])
        out_ref[:, lanes] = out_ref[:, lanes] + ref[...]
        start = lanes.stop


def spread(factor, high, low, scale, base=()):
    (probes, knots), points = factor.shape, high.shape[1]
    high = pltpu.with_memory_space_constraint(high, pltpu.VMEM)
    low = pltpu.with_memory_space_constraint(low, pltpu.VMEM)
    return pl.pallas_call(
        functools.partial(spread_kernel, scale),
        out_shape=jax.ShapeDtypeStruct((probes, points), jnp.float32),
        in_specs=[VMEM] * (3 + len(base)),
        out_specs=VMEM,
        compiler_params=pltpu.CompilerParams(vmem_limit_bytes=LIMIT),
        cost_estimate=cost(850, knots * points),
        name="spread",
    )(factor, high, low, *base)


def covariance(square):
    apart = square * lax.rsqrt(square)
    remain = jnp.maximum(4.0 - apart, 0.0)
    twice = remain * remain
    return (jnp.exp2(apart * (-LOG2E / (COV_RANGE * TAPER_RATE))) * (twice * twice)) * (5.0 - remain)


def beside_kernel(first, first_row, grain, ids_ref, counts_ref, own_ref, values_ref, coords_ref, precision_ref, *rest):
    out_ref, high_ref, low_ref = rest[-3:]
    own_blocks, slots = ids_ref.shape
    block = LANES
    probes = own_ref.shape[0]
    span = own_blocks + 2
    zeros_place = coords_ref.shape[1] // block
    column = lax.axis_index("space")
    north_base = lax.axis_index("knot") * own_blocks - 1
    north_cells = lax.axis_size("knot") * own_blocks
    own_columns = [
        on_grid(jnp.transpose(coordinate_rows(own_ref, own_blocks * block, axis) * TAPER_RATE), grain)
        for axis in range(2)
    ]

    def place(group, slot):
        ahead = ids_ref[group, slot] - (column - 1) * north_cells
        east = jnp.where(ahead >= north_cells, 1, 0) + jnp.where(ahead >= 2 * north_cells, 1, 0)
        strip = jnp.where(east == 1, 0, 2 - lax.rem(column + lax.div(east, 2) + 1, 2))
        index = strip * span + (ahead - east * north_cells - north_base)
        return lanes_of(index), lanes_of(jnp.where(slot < counts_ref[group], index, zeros_place))

    def lanes_of(index):
        return pl.ds(pl.multiple_of(index * block, block), block)

    depth, rows = high_ref.shape
    tile = min(TILE, rows)
    wide = min(TILE, depth)
    tiles = [(start, deep) for start in range(0, rows, tile) for deep in range(0, depth, wide)]
    groups = out_ref.shape[1] // block
    turns = groups * -(-slots // 2)

    for index in range(groups):
        group = first + index
        px, py = [turned[:, group : group + 1] for turned in own_columns]
        total = jnp.zeros((block, 2 * probes), jnp.float32)
        for pair in range(0, slots, 2):
            highs, lows, parts = [], [], []
            for slot in range(pair, min(pair + 2, slots)):
                lanes, value_lanes = place(group, slot)
                dx = px - coords_ref[0:1, lanes]
                dy = py - coords_ref[1:2, lanes]
                high, low = halves(covariance(dx * dx + dy * dy))
                highs.append(high)
                lows.append(low)
                parts.append(values_ref[:, value_lanes])
            part = jnp.concatenate(parts, axis=1)
            total = total + (
                dot_nt(jnp.concatenate(highs, axis=1), part) + dot_nt(jnp.concatenate(lows, axis=1), part)
            )
            turn = index * -(-slots // 2) + pair // 2
            for start, deep in tiles[turn * len(tiles) // turns : (turn + 1) * len(tiles) // turns]:
                from_row = first_row + start
                turned = jnp.transpose(precision_ref[from_row : from_row + tile, deep : deep + wide])
                here = slice(deep, deep + wide), slice(start, start + tile)
                high_ref[here], low_ref[here] = halves(turned)
        out_ref[:, index * block : (index + 1) * block] = (
            TAPER_SCALE * folded_columns(total, probes)
            + NUGGET * own_ref[:, group * block : (group + 1) * block]
        )


def beside_round(ids, counts, own, values, coords, precision, extent, first, blocks, first_row, rows, after):
    slots, depth = ids.shape[1], precision.shape[1]
    return pl.pallas_call(
        functools.partial(beside_kernel, first, first_row, grain_of(TAPER_RATE * extent)),
        out_shape=(
            jax.ShapeDtypeStruct((own.shape[0], blocks * LANES), jnp.float32),
            pltpu.VMEM((depth, rows), jnp.bfloat16),
            pltpu.VMEM((depth, rows), jnp.bfloat16),
        ),
        in_specs=[SMEM, SMEM, VMEM, VMEM, VMEM, VMEM] + [ANY] * len(after),
        out_specs=(VMEM, VMEM, VMEM),
        compiler_params=pltpu.CompilerParams(vmem_limit_bytes=LIMIT),
        cost_estimate=cost(500, blocks * slots * LANES * LANES, 2),
        name="beside",
    )(ids, counts, own, values, coords, precision, *after)


def add_kernel(count, *refs):
    total = refs[0][...]
    for ref in refs[1:count]:
        total = total + ref[...]
    refs[-1][...] = total


def add_all(values, after):
    return pl.pallas_call(
        functools.partial(add_kernel, len(values)),
        out_shape=jax.ShapeDtypeStruct(values[0].shape, jnp.float32),
        in_specs=[VMEM] * len(values) + [ANY] * len(after),
        out_specs=VMEM,
        compiler_params=pltpu.CompilerParams(vmem_limit_bytes=LIMIT),
        name="add",
    )(*values, *after)


def butterfly_rounds(count):
    assert count & (count - 1) == 0
    bits = [1 << i for i in range(count.bit_length() - 1)]
    rounds = [(low | high, high, low) for low, high in zip(bits[0::2], bits[1::2])]
    return rounds + [(bit,) for bit in bits[len(rounds) * 2 :]]


def butterfly_round(value, axis, turn):
    count = lax.axis_size(axis)
    return [
        lax.ppermute(value, axis, [(i, i ^ step) for i in range(count)]) for step in butterfly_rounds(count)[turn]
    ]


def shifted(value, axis, step):
    count = lax.axis_size(axis)
    if step % count == 0:
        return value
    return lax.ppermute(value, axis, [((i + step) % count, i) for i in range(count)])


def paired(value, axis, other, first):
    count, groups = lax.axis_size(axis), lax.axis_size(other)
    partner = {}
    for i in range(first, count - 1, 2):
        partner[i], partner[i + 1] = i + 1, i
    pairs = []
    for i in range(count):
        for j in range(groups):
            if i in partner:
                pairs.append((i * groups + j, partner[i] * groups + j))
            elif j ^ 1 < groups:
                pairs.append((i * groups + j, i * groups + (j ^ 1)))
    return lax.ppermute(value, (axis, other), pairs)


def shards(probes, locations, knot_locs, knot_precision, neighbours, counts):
    own_blocks = neighbours.shape[0]
    row_count = probes.shape[1]
    knot_total = knot_precision.shape[1]
    device_count = lax.axis_size(("space", "knot"))
    groups = lax.axis_size("knot")
    knot_range = KNOT_REACH * math.sqrt(own_blocks * device_count / knot_total)
    proj_scale = PROJ_GAIN * math.sqrt(knot_total / (row_count * device_count))

    stack, knots = prepare(probes, locations, knot_locs, own_blocks)
    chunks = [shifted(stack, "knot", step) for step in range(groups)]
    rate = LOG2E / knot_range
    extent = CELL * max(lax.axis_size("space"), groups * own_blocks)
    parts = []
    for chunk in chunks:
        parts.append(project(chunk, knots, rate, extent, parts[-1] if parts else None))
    stack = parts[0][4]

    strip = make_strip(chunks[-1], stack, chunks[1 % groups])
    odd = paired(strip, "space", "knot", 1)
    values, coords = assemble([strip, odd, paired(strip, "space", "knot", 0)], extent)
    projection = parts[-1][0]
    rounds = len(butterfly_rounds(lax.axis_size("space")))
    pieces = math.gcd(math.gcd(own_blocks, rounds), knot_precision.shape[0] // LANES)
    bounds = [own_blocks * i * (i + 2) // (pieces * (pieces + 2)) for i in range(pieces + 1)]
    per_split = knot_precision.shape[0] // pieces
    base, splits = [], []
    for turn in range(rounds):
        got = butterfly_round(projection, "space", turn)
        beside = []
        for i in range(pieces):
            if i * rounds // pieces == turn:
                done = beside_round(
                    neighbours, counts, stack, values, coords, knot_precision, extent,
                    bounds[i], bounds[i + 1] - bounds[i], i * per_split, per_split, [projection],
                )
                base.append(done[0])
                splits.append(done[1:])
                beside.extend(done)
        projection = add_all([projection, *got], beside)
    factor = factored(None, projection, splits, proj_scale, 0)
    for step in range(1, groups):
        factor = factored(factor, shifted(projection, "knot", step), splits, proj_scale, step)
    gain = LOW_SCALE * EXPAND_GAIN
    shares = []
    for step in reversed(range(1, groups)):
        shares.append(shifted(spread(factor, parts[step][1], parts[step][2], gain), "knot", -step))
    return sum(shares, spread(factor, parts[0][1], parts[0][2], gain, base))


def solution(mesh):
    return jax.shard_map(
        shards,
        mesh=mesh,
        in_specs=(
            P(None, ("space", "knot")),
            P(None, ("space", "knot")),
            P(None, "knot"),
            P("knot", None),
            P(("space", "knot"), None),
            P(("space", "knot")),
        ),
        out_specs=P(None, ("space", "knot")),
        check_vma=False,
    )
```
